32 devices in a mesh: lat: 4 (over y, x), lon: 8 (over z, core).
Axes of the slice: x: 2, y: 2, z: 4, core: 2. Of those that a mesh axis runs over, the one named last changes fastest.
Arguments:
- conc: bfloat16 [128, 64, 2048], P('lat', None, 'lon'), may hold values from -6 to 6
- dep_owner: int32 [8, 128, 4], P('lon', 'lat'), may hold values from 0 to 14, all different within a row; in each aligned block of 32 rows (0 to 31, 32 to 63, ..., all dimensions but the last counted through in order) at most 17 rows name the same one
- dep_row: int32 [8, 128, 4], P('lon', 'lat'), may hold values from 0 to 31
- dep_weight: float32 [8, 128, 4], P('lon', 'lat'), may hold values from 0.05 to 0.5
- dep_count: int32 [8, 128], P('lon', 'lat'), may hold values from 1 to 4
- zonal_offset: int32 [128], P('lat'), may hold values from -2 to 2
- agg_rates: float32 [4, 128, 2048], P(None, 'lat', 'lon'), may hold values from 0.1 to 1
- toeplitz: bfloat16 [4, 127], replicated, may hold values from -0.75 to 0.75
- settle: float32 [64], replicated, may hold values from 0.05 to 0.5
- kappa: float32 [128, 2048], P('lat', 'lon'), may hold values from 0.02 to 0.2
Outputs:
- updated: float32 [128, 64, 2048], P('lat', None, 'lon')
The draws below stay inside these ranges and needn't reach their ends.
Inputs may be any that keep to these rules, and one draw needn't show every extreme that they name: `dep_owner`: the 4 entries of a row name different neighbour blocks; among the rows of one device no neighbour block is named by more than 17 entries, and in some device's rows one is named exactly 17 times; every value is named somewhere. `dep_count`: entries of a row at or past its count are padding.
All inputs are finite; a program needn't handle non-finite values.
Results may differ from the reference program's by a relative error of at most 0.00092.
Values may be sent and summed in bfloat16 or wider, within the bound.
No kernel may reach another device: no remote copies, remote signals or barrier semaphores. Data moves between devices by JAX's collectives and lax.ppermute only.
A program may use at most 64 MiB of HBM per device.

```python
import math
import jax
import jax.numpy as jnp
import numpy as np
from jax import lax

B = 64
RANK = 4
KS = 4
NEAR = 15
LAT_DEV = 32
LON_DEV = 256
LAT = 128
NLON = 2048
CAP = 17
N_LAT = 4
N_LON = 8


def with_ends(values, own_key, low, top_value):
    index_at = [jax.random.randint(jax.random.fold_in(own_key, axis), (), 0, length) for axis, length in enumerate(values.shape)]
    widest = values.shape.index(max(values.shape))
    beside = index_at[:widest] + [(index_at[widest] + 1) % values.shape[widest]] + index_at[widest + 1:]
    return values.at[tuple(index_at)].set(low).at[tuple(beside)].set(top_value)


def block_levels(key, dims, shards, least, top_value):
    level = 1.0
    for position, blocks in shards:
        steps = jax.random.uniform(jax.random.fold_in(jax.random.fold_in(key, 6), position), (blocks,), jnp.float32, least / len(shards), top_value / len(shards))
        level = level * jnp.repeat(jnp.exp(steps), dims[position] // blocks).reshape((-1,) + (1,) * (len(dims) - 1 - position))
    return level


def assign_block(own_key, own, number, rows, amount, top, bound, skew):
    order = jax.random.permutation(own_key, amount)
    crowded, common = portions_of(amount, rows * top, bound, skew, True), portions_of(amount, rows * top, bound, skew, False)
    places = jnp.arange(amount)

    def named(lengths, rotation):
        used = int((lengths > 0).sum())
        fixed = max(1, used // 4)
        passed = fixed + (places - fixed + rotation * (used - fixed)) % max(1, amount - fixed)
        return jnp.zeros((amount,), jnp.int32).at[order[jnp.where(places < fixed, places, passed)]].set(jnp.asarray(lengths, jnp.int32))

    lengths = jnp.where(number % 4 == 0, named(crowded, number // 4), named(common, number - number // 4 - 1))
    mixed = jax.random.permutation(jax.random.fold_in(own, 3), amount)
    source_of, receiver = mixed[0:amount // 2 * 2:2], mixed[1:amount // 2 * 2:2]
    room = jnp.minimum(lengths[source_of] - 1, bound - lengths[receiver]) // 2
    room = jnp.where((source_of == order[0]) | (receiver == order[0]) | (lengths[receiver] == 0), 0, jnp.maximum(room, 0))
    passed = jax.random.randint(jax.random.fold_in(own, 4), (amount // 2,), 0, 1 << 20) % (room + 1)
    lengths = lengths.at[source_of].add(-passed).at[receiver].add(passed)
    items = jnp.searchsorted(jnp.cumsum(lengths), jnp.arange(rows * top), side="right").astype(jnp.int32)
    grid = items.reshape(top, rows).T
    grid = grid[jax.random.permutation(jax.random.fold_in(own, 1), rows)]
    rotation = jax.random.randint(jax.random.fold_in(own, 2), (rows, 1), 0, top)
    return jnp.take_along_axis(grid, (jnp.arange(top)[None, :] + rotation) % top, axis=1)


def portions_of(amount, total, limit, skew, full):
    weights = [(1 << 20) // math.isqrt(standing ** skew) + 1 for standing in range(1, amount + 1)]
    largest = limit if full else min(limit, max(-(-total // amount), total * weights[0] // sum(weights)))
    least = 1 if total - largest >= amount - 1 else 0
    counts, spare = [largest] + [least] * (amount - 1), total - largest - least * (amount - 1)
    while spare > 0:
        movable = [i for i in range(1, amount) if counts[i] < largest] or [i for i in range(1, amount) if counts[i] < limit]
        whole, budget = sum([weights[i] for i in movable]), spare
        for i in movable:
            more = min(limit - counts[i], max(1, budget * weights[i] // whole), spare)
            counts[i] = counts[i] + more
            spare = spare - more
    return np.array(counts)


def scatter_about(rng, extent, width, bound, cuts=(), held_as=jnp.bfloat16):
    drawn = width * jax.random.normal(rng, extent, jnp.float32)
    if cuts:
        drawn = drawn * block_levels(rng, extent, cuts, -0.22, 0.18)
    return jnp.clip(drawn, -bound, bound).astype(held_as)


def setup_inputs(seed: int = 0) -> dict:
    streams_of = jax.random.split(jax.random.key(seed), 11)
    conc = scatter_about(streams_of[0], (LAT, B, NLON), 1.0, 6.0, ((0, 4), (2, 8)))
    dep_owner_keys = jax.random.split(jax.random.fold_in(streams_of[1], 1), N_LON * LAT // LAT_DEV)
    dep_owner_turns = jax.random.permutation(jax.random.fold_in(streams_of[1], 3), N_LON * LAT // LAT_DEV)
    dep_owner = jax.vmap(lambda own, number: assign_block(jax.random.fold_in(streams_of[1], 2), own, number, LAT_DEV, NEAR, KS, CAP, 2))(dep_owner_keys, dep_owner_turns).reshape((N_LON, LAT, KS))
    dep_row = with_ends(jax.random.randint(streams_of[2], (N_LON, LAT, KS), 0, LAT_DEV), jax.random.fold_in(streams_of[2], 1), 0, LAT_DEV - 1).astype(jnp.int32)
    dep_weight = jnp.clip(0.05 + 0.45 * jax.random.uniform(streams_of[3], (N_LON, LAT, KS), jnp.float32) ** block_levels(streams_of[3], (N_LON, LAT, KS), ((0, 8), (1, 4)), -0.2, 0.2), 0.05, 0.5)
    dep_count = with_ends(jax.random.randint(streams_of[4], (N_LON, LAT), 1, KS + 1), jax.random.fold_in(streams_of[4], 1), 1, KS).astype(jnp.int32)
    zonal_offset = with_ends(jax.random.randint(streams_of[5], (LAT,), -2, 3), jax.random.fold_in(streams_of[5], 1), -2, 2).astype(jnp.int32)
    agg_rates = jnp.clip(jnp.exp(math.log(1.0) - 2.3025851 * jax.random.uniform(streams_of[6], (RANK, LAT, NLON), jnp.float32) ** block_levels(streams_of[6], (RANK, LAT, NLON), ((1, 4), (2, 8)), -0.2, 0.2)), 0.1, 1.0)
    toeplitz = scatter_about(streams_of[7], (RANK, 2 * B - 1), B ** -0.5, 0.75)
    settle = jnp.clip(jnp.exp(jax.random.uniform(streams_of[8], (B,), jnp.float32, math.log(0.05), math.log(0.5))), 0.05, 0.5)
    kappa = jnp.clip(jnp.exp(math.log(0.2) - 2.3025851 * jax.random.uniform(streams_of[9], (LAT, NLON), jnp.float32) ** block_levels(streams_of[9], (LAT, NLON), ((0, 4), (1, 8)), -0.2, 0.2)), 0.02, 0.2)
    return dict(conc=conc, dep_owner=dep_owner, dep_row=dep_row, dep_weight=dep_weight, dep_count=dep_count, zonal_offset=zonal_offset, agg_rates=agg_rates, toeplitz=toeplitz, settle=settle, kappa=kappa)


def toeplitz_stack(toeplitz, bins):
    flipped = toeplitz[:, ::-1]
    return jnp.stack([flipped[:, bins - 1 - i: 2 * bins - 1 - i] for i in range(bins)], axis=1)


def reference(conc, dep_owner, dep_row, dep_weight, dep_count, zonal_offset, agg_rates, toeplitz, settle, kappa):
    band_field = conc.reshape(LAT, B, N_LON, LON_DEV)
    entry_ids = jnp.arange(KS, dtype=jnp.int32)
    lat_block = (jnp.arange(LAT, dtype=jnp.int32) // LAT_DEV).astype(jnp.int32)

    def remap_block(inputs):
        block_index, owner, source_row, weight, count = inputs
        source_block = (lat_block[:, None] + owner // 5 - 1).astype(jnp.int32)
        inside = (source_block >= 0) & (source_block < N_LAT)
        source_lat = jnp.clip(source_block * LAT_DEV + source_row, 0, LAT - 1).astype(jnp.int32)
        source_lon = ((block_index + owner % 5 - 2) % N_LON).astype(jnp.int32)
        keep = (entry_ids[None, :] < count[:, None]) & inside
        live_weight = jnp.where(keep, weight, jnp.float32(0.0))
        summed = jnp.zeros((LAT, B, LON_DEV), jnp.float32)
        for k in range(KS):
            row_data = band_field[source_lat[:, k], :, source_lon[:, k], :]
            summed = summed + live_weight[:, k, None, None] * row_data.astype(jnp.float32)
        return summed.astype(jnp.bfloat16)

    block_ids = jnp.arange(N_LON, dtype=jnp.int32)
    blocks = lax.map(remap_block, (block_ids, dep_owner, dep_row, dep_weight, dep_count))
    remapped = jnp.transpose(blocks, (1, 2, 0, 3)).reshape(LAT, B, NLON)
    displace = zonal_offset[:, None, None]
    shifted = jnp.zeros_like(remapped)
    for step in range(-2, 3):
        shifted = shifted + jnp.where(displace == step, jnp.roll(remapped, step, axis=2), jnp.zeros_like(remapped))
    center = shifted.astype(jnp.float32)
    padded = jnp.pad(center, ((1, 1), (0, 0), (0, 0)))
    neighbours = padded[2:] + padded[:-2] + jnp.roll(center, -1, axis=2) + jnp.roll(center, 1, axis=2)
    diffusion = kappa[:, None, :] * (neighbours - 4.0 * center)
    matrices = toeplitz_stack(toeplitz, B).astype(jnp.float32)
    conc_wide = conc.astype(jnp.float32)
    growth = jnp.zeros((LAT, B, NLON), jnp.float32)
    for q in range(RANK):
        growth = growth + agg_rates[q][:, None, :] * jnp.einsum("ij,ljx->lix", matrices[q], conc_wide)
    return center + diffusion + growth - settle[None, :, None] * conc_wide
```

```python
import functools

import jax
import jax.numpy as jnp
from jax import lax
from jax.experimental import pallas as pl
from jax.experimental.pallas import tpu as pltpu
from jax.sharding import PartitionSpec as P

REACH = 2
NEAR_LON = 5
VMEM_BYTES = 24 * 1024 * 1024


def permute_lon(value, steps):
    count = lax.axis_size("lon")
    return lax.ppermute(value, "lon", [(i, (i + steps) % count) for i in range(count)])


def swap_lon(value):
    count = lax.axis_size("lon")
    return lax.ppermute(value, "lon", [(i, i ^ 1) for i in range(count)])


def permute_lat(value, steps):
    count = lax.axis_size("lat")
    pairs = [(i, i + steps) for i in range(count) if 0 <= i + steps < count]
    return lax.ppermute(value, "lat", pairs)


def whole_vmem():
    return pl.BlockSpec(memory_space=pltpu.VMEM)


def whole_smem():
    return pl.BlockSpec(memory_space=pltpu.SMEM)


def growth_kernel(flip_ref, settle_ref, conc_ref, rates_ref, out_ref, mat_ref):
    ranks, rows_step = rates_ref.shape[0], conc_ref.shape[0]
    bins, width = conc_ref.shape[1:]

    @pl.when(pl.program_id(0) == 0)
    def _():
        for q in range(ranks):
            spread = jnp.broadcast_to(flip_ref[q : q + 1, :], (bins, 2 * bins))
            turned = pltpu.roll(spread, bins + 1, 1, stride=1, stride_axis=0)
            mat_ref[q * bins : (q + 1) * bins, :] = turned[:, :bins].astype(jnp.bfloat16)

    settle = jnp.broadcast_to(settle_ref[...], (bins, width))
    for r in range(rows_step):
        cells = conc_ref[r]
        product = jnp.dot(mat_ref[...], cells, preferred_element_type=jnp.float32)
        total = -settle * cells.astype(jnp.float32)
        for q in range(ranks):
            total = total + rates_ref[q, r : r + 1, :] * product[q * bins : (q + 1) * bins]
        out_ref[r] = total


def local_terms(conc, agg_rates, toeplitz, settle):
    rows, bins, width = conc.shape
    ranks = agg_rates.shape[0]
    step = 8
    flipped = jnp.pad(toeplitz[:, ::-1].astype(jnp.float32), ((0, 0), (0, 1)))
    return pl.pallas_call(
        growth_kernel,
        grid=(rows // step,),
        in_specs=[
            pl.BlockSpec((ranks, 2 * bins), lambda i: (0, 0)),
            pl.BlockSpec((bins, 1), lambda i: (0, 0)),
            pl.BlockSpec((step, bins, width), lambda i: (i, 0, 0)),
            pl.BlockSpec((ranks, step, width), lambda i: (0, i, 0)),
        ],
        out_specs=pl.BlockSpec((step, bins, width), lambda i: (i, 0, 0)),
        out_shape=jax.ShapeDtypeStruct(conc.shape, jnp.float32),
        scratch_shapes=[pltpu.VMEM((ranks * bins, bins), jnp.bfloat16)],
        cost_estimate=pl.CostEstimate(
            flops=2 * ranks * bins * bins * rows * width, bytes_accessed=8 * conc.size, transcendentals=0
        ),
        name="growth",
    )(flipped, settle[:, None], conc, agg_rates)


def gather_kernel(spans, tables, entries, *refs):
    index_ref, weight_ref = refs[:2]
    sources = refs[2 : 2 + tables]
    outs = refs[2 + tables : -2]
    table, sems = refs[-2:]
    per = table.shape[0] // tables
    copies = [
        pltpu.make_async_copy(sources[i], table.at[pl.ds(i * per, per)], sems.at[i]) for i in range(tables)
    ]
    for copy in copies:
        copy.start()
    for copy in copies:
        copy.wait()
    for first, last, targets in spans:

        def one(r, carry, targets=targets):
            total = jnp.zeros(table.shape[1:], jnp.float32)
            for k in range(entries):
                at = r * entries + k
                total = total + weight_ref[at] * table[index_ref[at]].astype(jnp.float32)
            for which, base in targets:
                outs[which][r - base] = total.astype(outs[which].dtype)
            return carry

        lax.fori_loop(first, last, one, 0)


def gather_sums(index, weight, sources, spans, outs, entries):
    tables = len(sources)
    per, bins, width = sources[0].shape
    total_rows = index.shape[0] // entries
    return pl.pallas_call(
        functools.partial(gather_kernel, spans, tables, entries),
        in_specs=[whole_smem(), whole_smem()] + [pl.BlockSpec(memory_space=pl.ANY)] * tables,
        out_specs=[whole_vmem() for _ in outs],
        out_shape=[jax.ShapeDtypeStruct((n, bins, width), dtype) for n, dtype in outs],
        scratch_shapes=[
            pltpu.VMEM((tables * per, bins, width), sources[0].dtype),
            pltpu.SemaphoreType.DMA((tables,)),
        ],
        compiler_params=pltpu.CompilerParams(vmem_limit_bytes=VMEM_BYTES),
        cost_estimate=pl.CostEstimate(
            flops=2 * total_rows * entries * bins * width,
            bytes_accessed=2 * tables * per * bins * width + 4 * total_rows * bins * width,
            transcendentals=0,
        ),
        name="row_sums",
    )(index, weight, *sources)


def combine_kernel(
    own0, from_south, from_north, far_south, far_north, own1, from_west, from_east, out_ref, first_ref, last_ref
):
    rows = out_ref.shape[0]
    half = own0.shape[1]
    bins, width = out_ref.shape[1:]
    lane = lax.broadcasted_iota(jnp.int32, (bins, 128), 1)
    wide = lambda ref, r: ref[r].astype(jnp.float32)
    out_ref[0, :half] = own0[0] + wide(from_south, 0) + wide(far_south, 0)
    out_ref[rows - 1, :half] = own0[rows - 1] + wide(from_north, rows - 2) + wide(far_north, 0)

    def inner(r, carry):
        out_ref[r, :half] = own0[r] + wide(from_south, r) + wide(from_north, r - 1)
        return carry

    lax.fori_loop(1, rows - 1, inner, 0)

    def other(r, carry):
        first, last = carry
        out_ref[r, half:] = own1[r] + wide(from_west, r) + wide(from_east, r)
        spot = (lane >= 3 * r) & (lane < 3 * r + 3)
        first = jnp.where(spot, pltpu.roll(out_ref[r, :, :128], 3 * r, 1), first)
        last = jnp.where(spot, pltpu.roll(out_ref[r, :, width - 128 :], 3 * r + 3, 1), last)
        return first, last

    blank = jnp.zeros((bins, 128), jnp.float32)
    first, last = lax.fori_loop(0, rows, other, (blank, blank))
    first_ref[...] = first.astype(first_ref.dtype)
    last_ref[...] = last.astype(last_ref.dtype)


def combine(*parts):
    rows, half, width = parts[0].shape
    bins = 2 * half
    return pl.pallas_call(
        combine_kernel,
        in_specs=[whole_vmem() for _ in parts],
        out_specs=[whole_vmem() for _ in range(3)],
        out_shape=[
            jax.ShapeDtypeStruct((rows, bins, width), jnp.float32),
            jax.ShapeDtypeStruct((bins, 128), jnp.bfloat16),
            jax.ShapeDtypeStruct((bins, 128), jnp.bfloat16),
        ],
        compiler_params=pltpu.CompilerParams(vmem_limit_bytes=VMEM_BYTES),
        name="combine",
    )(*parts)


def final_kernel(offset_ref, remap_ref, west_ref, east_ref, kappa_ref, local_ref, out_ref, shifted_ref):
    rows = remap_ref.shape[0]
    bins, width = remap_ref.shape[1:]
    lane = lax.broadcasted_iota(jnp.int32, (bins, 128), 1)
    tiles = width // 128

    def moved(tile_list, amount):
        turned = [pltpu.roll(tile, lax.rem(amount + 128, 128), 1) for tile in tile_list]
        count = len(turned)
        return [
            jnp.where(
                lane < amount,
                turned[t - 1],
                jnp.where(lane >= 128 + amount, turned[(t + 1) % count], turned[t]),
            )
            for t in range(count)
        ]

    def shifted_row(r):
        east = pltpu.roll(east_ref[...].astype(jnp.float32), lax.rem(128 - 3 * r + 128, 128), 1)
        west = pltpu.roll(west_ref[...].astype(jnp.float32), lax.rem(125 - 3 * r + 128, 128), 1)
        edge = jnp.where(lane < 64, east, west)
        row = [remap_ref[r, :, 128 * t : 128 * t + 128] for t in range(tiles)]
        return moved(row + [edge], offset_ref[r])

    def outer(r):
        row = shifted_row(r)
        shifted_ref[r] = jnp.concatenate(row[:tiles], axis=1)

    outer(0)
    outer(rows - 1)

    def inner(r, carry):
        row = shifted_row(r)
        count = len(row)
        eastern = [pltpu.roll(tile, 127, 1) for tile in row]
        western = [pltpu.roll(tile, 1, 1) for tile in row]
        for t in range(tiles):
            at = slice(128 * t, 128 * t + 128)
            east = jnp.where(lane == 127, eastern[(t + 1) % count], eastern[t])
            west = jnp.where(lane == 0, western[t - 1], western[t])
            kappa = kappa_ref[r - 1, :, at]
            shifted_ref[r, :, at] = row[t]
            out_ref[r - 1, :, at] = local_ref[r - 1, :, at] + row[t] + kappa * (east + west - 4.0 * row[t])
        return carry

    lax.fori_loop(1, rows - 1, inner, 0)

    def last(r, carry):
        kappa = kappa_ref[r]
        out_ref[r] = out_ref[r] + kappa * (shifted_ref[r] + shifted_ref[r + 2])
        return carry

    lax.fori_loop(0, rows - 2, last, 0)


def final(offset, remapped, west, east, kappa, local):
    rows, bins, width = remapped.shape
    return pl.pallas_call(
        final_kernel,
        in_specs=[whole_smem()] + [whole_vmem() for _ in range(5)],
        out_specs=whole_vmem(),
        out_shape=jax.ShapeDtypeStruct((rows - 2, bins, width), jnp.float32),
        scratch_shapes=[pltpu.VMEM((rows, bins, width), jnp.float32)],
        compiler_params=pltpu.CompilerParams(vmem_limit_bytes=VMEM_BYTES),
        name="final",
    )(offset, remapped, west, east, kappa, local)


def body(
    conc,
    dep_owner,
    dep_row,
    dep_weight,
    dep_count,
    zonal_offset,
    agg_rates,
    toeplitz,
    settle,
    kappa,
):
    rows, bins, width = conc.shape
    entries = dep_owner.shape[2]
    n_lat, n_lon = lax.axis_size("lat"), lax.axis_size("lon")
    my_lat, my_lon = lax.axis_index("lat"), lax.axis_index("lon")
    half = bins // 2
    low, high = conc[:, :half], conc[:, half:]

    live = jnp.where(
        jnp.arange(entries, dtype=jnp.int32)[None, :] < dep_count[0][:, None], dep_weight[0], jnp.float32(0.0)
    )
    code = (dep_owner[0] * rows + dep_row[0]).astype(jnp.float32)
    size = rows * entries
    meta = jnp.concatenate([code.reshape(size), live.reshape(size), zonal_offset.astype(jnp.float32)])
    meta = jnp.pad(meta, (0, -meta.shape[0] % 128))
    known = lax.all_gather(meta, ("lat", "lon")).reshape(n_lat, n_lon, meta.shape[0])

    behind = permute_lon(low, 2)
    ahead = permute_lon(low, -2)
    beside = swap_lon(low)
    column = lax.all_gather(high, "lat")
    local = local_terms(conc, agg_rates, toeplitz, settle)

    odd = my_lon % 2
    toward = 1 - 2 * odd
    known = jnp.concatenate([known[:, n_lon - 2 :], known, known[:, :2]], axis=1)
    known = jnp.pad(known, ((1, 1), (0, 0), (0, 0)))
    known = lax.dynamic_slice(known, (my_lat, my_lon, 0), (3, 5, known.shape[2]))
    codes = known[:, ::2, :size].astype(jnp.int32).reshape(3, 3, rows, entries)
    lives = known[:, ::2, size : 2 * size].reshape(3, 3, rows, entries)
    turns = known[:, 2, 2 * size : 2 * size + rows].astype(jnp.int32)
    owner, source = codes // rows, codes % rows
    lat_step, lon_step = owner // NEAR_LON - 1, owner % NEAR_LON - REACH
    block = jnp.arange(-1, 2, dtype=jnp.int32)

    here = block[:, None, None] + lat_step[:, 1] == 0
    step = lon_step[:, 1]
    slot = jnp.where(step == 0, 0, jnp.where(step == 2, 2, jnp.where(step == -2, 3, jnp.where(step == toward, 1, 4))))
    index0 = jnp.where(here, slot * rows + source[:, 1], 0).reshape(-1)
    weight0 = jnp.where(here, lives[:, 1], 0.0).reshape(-1)

    def with_halo(value):
        return jnp.concatenate([value[0, :, rows - 1 :], value[1], value[2, :, :1]], axis=1)

    lat_from = my_lat + with_halo(block[:, None, None, None] + lat_step)
    lon_from = with_halo(2 * block[None, :, None, None] + lon_step)
    pair = jnp.where(lon_from == 0, 0, 1)
    here = (lat_from >= 0) & (lat_from < n_lat) & ((lon_from == 0) | (lon_from == toward))
    index1 = jnp.where(here, (pair * n_lat + lat_from) * rows + with_halo(source), 0).reshape(-1)
    weight1 = jnp.where(here, with_halo(lives), 0.0).reshape(-1)
    offset = jnp.concatenate([turns[0, rows - 1 :], turns[1], turns[2, :1]])

    passed = swap_lon(jnp.where(odd == 1, behind, ahead))
    count = rows + 2
    down, own0, up, down2, up2 = gather_sums(
        index0,
        weight0,
        [low, beside, ahead, behind, passed],
        (
            (0, 1, ((0, 0), (3, 0))),
            (1, rows - 1, ((0, 0),)),
            (rows - 1, rows + 1, ((0, 0), (1, rows - 1))),
            (rows + 1, 2 * rows - 1, ((1, rows - 1),)),
            (2 * rows - 1, 2 * rows + 1, ((1, rows - 1), (2, 2 * rows - 1))),
            (2 * rows + 1, 3 * rows - 1, ((2, 2 * rows - 1),)),
            (3 * rows - 1, 3 * rows, ((2, 2 * rows - 1), (4, 3 * rows - 1))),
        ),
        ((rows + 1, jnp.bfloat16), (count, jnp.float32), (rows + 1, jnp.bfloat16), (1, jnp.bfloat16), (1, jnp.bfloat16)),
        entries,
    )
    from_south = permute_lat(up, 1)
    from_north = permute_lat(down, -1)
    far_south = permute_lat(up2, 2)
    far_north = permute_lat(down2, -2)

    column = column.reshape(n_lat * rows, half, width)
    beside_column = swap_lon(column)
    to_west, own1, to_east = gather_sums(
        index1,
        weight1,
        [column, beside_column],
        (
            (0, count, ((0, 0),)),
            (count, 2 * count, ((1, count),)),
            (2 * count, 3 * count, ((2, 2 * count),)),
        ),
        ((count, jnp.bfloat16), (count, jnp.float32), (count, jnp.bfloat16)),
        entries,
    )
    from_west = permute_lon(to_east, 2)
    from_east = permute_lon(to_west, -2)

    remapped, first, last = combine(
        own0, from_south, from_north, far_south, far_north, own1, from_west, from_east
    )
    west = permute_lon(last, 1)
    east = permute_lon(first, -1)
    return final(offset, remapped, west, east, kappa[:, None, :], local)


def solution(mesh):
    return jax.shard_map(
        body,
        mesh=mesh,
        in_specs=(
            P("lat", None, "lon"),
            P("lon", "lat", None),
            P("lon", "lat", None),
            P("lon", "lat", None),
            P("lon", "lat"),
            P("lat"),
            P(None, "lat", "lon"),
            P(),
            P(),
            P("lat", "lon"),
        ),
        out_specs=P("lat", None, "lon"),
        check_vma=False,
    )
```

```python
import functools

import jax
import jax.numpy as jnp
from jax import lax
from jax.experimental import pallas as pl
from jax.experimental.pallas import tpu as pltpu
from jax.sharding import PartitionSpec as P

REACH = 2
NEAR_LON = 5
TILE = 16
UNROLL = 4
VMEM_BYTES = 24 * 1024 * 1024


def permute_lon(value, steps):
    count = lax.axis_size("lon")
    return lax.ppermute(value, "lon", [(i, (i + steps) % count) for i in range(count)])


def swap_lon(value):
    count = lax.axis_size("lon")
    return lax.ppermute(value, "lon", [(i, i ^ 1) for i in range(count)])


def permute_lat(value, steps):
    count = lax.axis_size("lat")
    pairs = [(i, i + steps) for i in range(count) if 0 <= i + steps < count]
    return lax.ppermute(value, "lat", pairs)


def in_smem():
    return pl.BlockSpec(memory_space=pltpu.SMEM)


def in_place():
    return pl.BlockSpec(memory_space=pl.ANY)


def for_rows(first, last, one):
    groups = (last - first) // UNROLL

    def some(g, carry):
        for u in range(UNROLL):
            one(first + g * UNROLL + u)
        return carry

    if groups:
        lax.fori_loop(0, groups, some, 0)
    for r in range(first + groups * UNROLL, last):
        one(r)


def growth_kernel(flip_ref, settle_ref, conc_ref, rates_ref, out_ref, mat_ref):
    ranks, rows_step = rates_ref.shape[0], conc_ref.shape[0]
    bins, width = conc_ref.shape[1:]

    @pl.when(pl.program_id(0) == 0)
    def _():
        for q in range(ranks):
            spread = jnp.broadcast_to(flip_ref[q : q + 1, :], (bins, 2 * bins))
            turned = pltpu.roll(spread, bins + 1, 1, stride=1, stride_axis=0)
            mat_ref[q * bins : (q + 1) * bins, :] = turned[:, :bins].astype(jnp.bfloat16)

    settle = jnp.broadcast_to(settle_ref[...], (bins, width))
    for r in range(rows_step):
        cells = conc_ref[r]
        product = jnp.dot(mat_ref[...], cells, preferred_element_type=jnp.float32)
        total = -settle * cells.astype(jnp.float32)
        for q in range(ranks):
            total = total + rates_ref[q, r : r + 1, :] * product[q * bins : (q + 1) * bins]
        out_ref[r] = total


def local_terms(conc, agg_rates, toeplitz, settle):
    rows, bins, width = conc.shape
    ranks = agg_rates.shape[0]
    step = 8
    flipped = jnp.pad(toeplitz[:, ::-1].astype(jnp.float32), ((0, 0), (0, 1)))
    return pl.pallas_call(
        growth_kernel,
        grid=(rows // step,),
        in_specs=[
            pl.BlockSpec((ranks, 2 * bins), lambda i: (0, 0)),
            pl.BlockSpec((bins, 1), lambda i: (0, 0)),
            pl.BlockSpec((step, bins, width), lambda i: (i, 0, 0)),
            pl.BlockSpec((ranks, step, width), lambda i: (0, i, 0)),
        ],
        out_specs=pl.BlockSpec((step, bins, width), lambda i: (i, 0, 0)),
        out_shape=jax.ShapeDtypeStruct(conc.shape, jnp.float32),
        scratch_shapes=[pltpu.VMEM((ranks * bins, bins), jnp.bfloat16)],
        cost_estimate=pl.CostEstimate(
            flops=2 * ranks * bins * bins * rows * width, bytes_accessed=8 * conc.size, transcendentals=0
        ),
        name="growth",
    )(flipped, settle[:, None], conc, agg_rates)


def row_sums_kernel(bases, spans, entries, *refs):
    tables = len(bases)
    index_ref, weight_ref = refs[:2]
    sources = refs[2 : 2 + tables]
    outs = refs[2 + tables : -2]
    table, sems = refs[-2:]
    steps, every, tile, width = table.shape
    per = every // tables
    now = pl.program_id(0)

    def copy(step, i):
        return pltpu.make_async_copy(
            sources[i].at[:, pl.ds(bases[i] + step * tile, tile), :],
            table.at[step, pl.ds(i * per, per)],
            sems.at[step, i],
        )

    @pl.when(now == 0)
    def _():
        for step in range(steps):
            for i in range(tables):
                copy(step, i).start()

    for step in range(steps):

        @pl.when(now == step)
        def _(step=step):
            for i in range(tables):
                copy(step, i).wait()

    for group, first, last, targets in spans:

        def one(r, group=group, targets=targets):
            total = jnp.zeros((tile, width), jnp.float32)
            for k in range(entries):
                row = group * entries + k
                total = total + weight_ref[row, r] * table[now, index_ref[row, r]].astype(jnp.float32)
            for which, base in targets:
                outs[which][r + base] = total.astype(outs[which].dtype)

        for_rows(first, last, one)


def row_sums(index, weight, sources, half, spans, outs, entries):
    tables = len(sources)
    per, width = sources[0][0].shape[0], sources[0][0].shape[2]
    steps = half // TILE
    terms = sum(last - first for _, first, last, _ in spans) * entries
    return pl.pallas_call(
        functools.partial(row_sums_kernel, tuple(base for _, base in sources), spans, entries),
        grid=(steps,),
        in_specs=[in_smem(), in_smem()] + [in_place()] * tables,
        out_specs=[pl.BlockSpec((n, TILE, width), lambda t: (0, t, 0)) for n, _ in outs],
        out_shape=[jax.ShapeDtypeStruct((n, half, width), dtype) for n, dtype in outs],
        scratch_shapes=[
            pltpu.VMEM((steps, tables * per, TILE, width), jnp.bfloat16),
            pltpu.SemaphoreType.DMA((steps, tables)),
        ],
        compiler_params=pltpu.CompilerParams(vmem_limit_bytes=VMEM_BYTES),
        cost_estimate=pl.CostEstimate(
            flops=2 * terms * half * width,
            bytes_accessed=2 * tables * per * half * width + sum(n * half * width * 2 for n, _ in outs),
            transcendentals=0,
        ),
        name="row_sums",
    )(index, weight, *[source for source, _ in sources])


def edges_kernel(along_lat, *refs):
    first_ref, last_ref = refs[-2:]
    count = (len(refs) - 2) // 2
    rows = refs[0].shape[0]
    bins = first_ref.shape[0]
    lane = lax.broadcasted_iota(jnp.int32, (bins, 128), 1)
    for parts, out_ref, extra in ((refs[:count], first_ref, 0), (refs[count : 2 * count], last_ref, 3)):
        packed = jnp.zeros((bins, 128), jnp.float32)
        for r in range(rows):
            cells = total_row(parts, r, rows, along_lat)
            spot = (lane >= 3 * r) & (lane < 3 * r + 3)
            packed = jnp.where(spot, pltpu.roll(cells, (3 * r + extra) % 128, 1), packed)
        out_ref[...] = packed.astype(out_ref.dtype)


def total_row(parts, r, rows, along_lat):
    wide = lambda ref, i: ref[i].astype(jnp.float32)
    if not along_lat:
        return parts[0][r] + wide(parts[1], r) + wide(parts[2], r)
    if r == 0:
        return parts[0][r] + wide(parts[1], 0) + wide(parts[3], 0)
    if r == rows - 1:
        return parts[0][r] + wide(parts[2], rows - 2) + wide(parts[4], 0)
    return parts[0][r] + wide(parts[1], r) + wide(parts[2], r - 1)


def edges(along_lat, parts):
    half, width = parts[0].shape[1:]
    specs = [
        pl.BlockSpec((part.shape[0], half, 128), lambda t, at=at: (0, 0, at))
        for at in (0, width // 128 - 1)
        for part in parts
    ]
    return pl.pallas_call(
        functools.partial(edges_kernel, along_lat),
        grid=(1,),
        in_specs=specs,
        out_specs=[pl.BlockSpec((half, 128), lambda t: (0, 0))] * 2,
        out_shape=[jax.ShapeDtypeStruct((half, 128), jnp.bfloat16)] * 2,
        compiler_params=pltpu.CompilerParams(vmem_limit_bytes=VMEM_BYTES),
        cost_estimate=pl.CostEstimate(flops=8 * half * 128 * 68, bytes_accessed=8 * half * 128 * 68, transcendentals=0),
        name="edges",
    )(*parts, *parts)


def combine_kernel(along_lat, *refs):
    out_ref = refs[-1]
    rows = out_ref.shape[0]
    out_ref[0] = total_row(refs[:-1], 0, rows, along_lat)
    out_ref[rows - 1] = total_row(refs[:-1], rows - 1, rows, along_lat)
    for r in range(1, rows - 1):
        out_ref[r] = total_row(refs[:-1], r, rows, along_lat)


def combine(along_lat, parts):
    rows, half, width = parts[0].shape
    return pl.pallas_call(
        functools.partial(combine_kernel, along_lat),
        grid=(half // TILE,),
        in_specs=[pl.BlockSpec((part.shape[0], TILE, width), lambda t: (0, t, 0)) for part in parts],
        out_specs=pl.BlockSpec((rows, TILE, width), lambda t: (0, t, 0)),
        out_shape=jax.ShapeDtypeStruct((rows, half, width), jnp.float32),
        compiler_params=pltpu.CompilerParams(vmem_limit_bytes=VMEM_BYTES),
        cost_estimate=pl.CostEstimate(flops=2 * parts[0].size, bytes_accessed=12 * parts[0].size, transcendentals=0),
        name="combine",
    )(*parts)


def final_kernel(offset_ref, remap_ref, west_ref, east_ref, kappa_ref, local_ref, *refs):
    out_ref, shifted_ref = refs[-2:]
    rows = remap_ref.shape[0]
    bins, width = remap_ref.shape[1:]
    lane = lax.broadcasted_iota(jnp.int32, (bins, 128), 1)
    tiles = width // 128
    eastern_cells = east_ref[...].astype(jnp.float32)
    western_cells = west_ref[...].astype(jnp.float32)

    def shifted_row(r):
        amount = offset_ref[r]
        east = pltpu.roll(eastern_cells, lax.rem(256 - 3 * r, 128), 1)
        west = pltpu.roll(western_cells, lax.rem(253 - 3 * r, 128), 1)
        row = [remap_ref[r, :, 128 * t : 128 * t + 128] for t in range(tiles)]
        row.append(jnp.where(lane < 64, east, west))
        turned = [pltpu.roll(tile, lax.rem(amount + 128, 128), 1) for tile in row]
        before, after = lane < amount, lane >= 128 + amount
        count = tiles + 1
        return [
            jnp.where(before, turned[t - 1], jnp.where(after, turned[(t + 1) % count], turned[t]))
            for t in range(count)
        ]

    for r in (0, rows - 1):
        row = shifted_row(r)
        for t in range(tiles):
            shifted_ref[r, :, 128 * t : 128 * t + 128] = row[t]

    def inner(r):
        row = shifted_row(r)
        count = tiles + 1
        eastern = [pltpu.roll(tile, 127, 1) for tile in row]
        western = [pltpu.roll(tile, 1, 1) for tile in row]
        for t in range(tiles):
            at = slice(128 * t, 128 * t + 128)
            east = jnp.where(lane == 127, eastern[(t + 1) % count], eastern[t])
            west = jnp.where(lane == 0, western[t - 1], western[t])
            kappa = kappa_ref[r - 1, :, at]
            shifted_ref[r, :, at] = row[t]
            out_ref[r - 1, :, at] = local_ref[r - 1, :, at] + row[t] + kappa * (east + west - 4.0 * row[t])

    for_rows(1, rows - 1, inner)

    def add_rows(r):
        out_ref[r] = out_ref[r] + kappa_ref[r] * (shifted_ref[r] + shifted_ref[r + 2])

    for_rows(0, rows - 2, add_rows)


def final(offset, remapped, west, east, kappa, local, base, earlier):
    rows, half, width = remapped.shape
    first = base // TILE
    block = pl.BlockSpec((rows - 2, TILE, width), lambda t: (0, first + t, 0))
    packed = pl.BlockSpec((TILE, 128), lambda t: (t, 0))
    return pl.pallas_call(
        final_kernel,
        grid=(half // TILE,),
        in_specs=[
            in_smem(),
            pl.BlockSpec((rows, TILE, width), lambda t: (0, t, 0)),
            packed,
            packed,
            pl.BlockSpec(kappa.shape, lambda t: (0, 0, 0)),
            block,
        ]
        + [in_place()] * len(earlier),
        out_specs=block,
        out_shape=jax.ShapeDtypeStruct(local.shape, jnp.float32),
        scratch_shapes=[pltpu.VMEM((rows, TILE, width), jnp.float32)],
        input_output_aliases={6: 0} if earlier else {},
        compiler_params=pltpu.CompilerParams(vmem_limit_bytes=VMEM_BYTES),
        cost_estimate=pl.CostEstimate(flops=30 * remapped.size, bytes_accessed=12 * remapped.size, transcendentals=0),
        name="final",
    )(offset, remapped, west, east, kappa, local, *earlier)


def body(
    conc,
    dep_owner,
    dep_row,
    dep_weight,
    dep_count,
    zonal_offset,
    agg_rates,
    toeplitz,
    settle,
    kappa,
):
    rows, bins, width = conc.shape
    entries = dep_owner.shape[2]
    my_lon = lax.axis_index("lon")
    half = bins // 2
    low, high = conc[:, :half], conc[:, half:]

    live = jnp.where(
        jnp.arange(entries, dtype=jnp.int32)[:, None] < dep_count, dep_weight[0].T, jnp.float32(0.0)
    )
    code = (dep_owner[0].T * rows + dep_row[0].T).astype(jnp.float32)
    meta = jnp.concatenate([code, live, zonal_offset.astype(jnp.float32)[None, :]])
    column = jnp.stack([permute_lat(meta, 1), meta, permute_lat(meta, -1)])
    known = jnp.stack([permute_lon(column, -2), column, permute_lon(column, 2)])

    ahead = permute_lon(low, -2)
    behind = permute_lon(low, 2)
    beside = swap_lon(conc)
    from_lat = {step: permute_lat(high, -step) for step in (-1, 1, -2, 2)}
    local = local_terms(conc, agg_rates, toeplitz, settle)

    odd = my_lon % 2
    toward = 1 - 2 * odd
    codes = known[:, :, :entries].astype(jnp.int32)
    lives = known[:, :, entries : 2 * entries]
    turns = column[:, 2 * entries].astype(jnp.int32)
    offset = jnp.concatenate([turns[0, rows - 1 :], turns[1], turns[2, :1]])
    owner, source = codes // rows, codes % rows
    lat_step, lon_step = owner // NEAR_LON - 1, owner % NEAR_LON - REACH
    block = jnp.arange(-1, 2, dtype=jnp.int32)
    lat_from = block[None, :, None, None] + lat_step
    lon_from = 2 * (-block)[:, None, None, None] + lon_step

    here = lat_from[1] == 0
    step = lon_step[1]
    slot = jnp.where(step == 0, 0, jnp.where(step == 2, 2, jnp.where(step == -2, 3, jnp.where(step == toward, 1, 4))))
    index0 = jnp.where(here, slot * rows + source[1], 0).reshape(3 * entries, rows)
    weight0 = jnp.where(here, lives[1], 0.0).reshape(3 * entries, rows)

    pair = jnp.where(lon_from == 0, 0, 1)
    here = (lon_from == 0) | (lon_from == toward)
    near = (lat_from >= -2) & (lat_from <= 2)
    index1 = jnp.where(here & near, (pair * 5 + lat_from + 2) * rows + source, 0).reshape(9 * entries, rows)
    weight1 = jnp.where(here & near, lives, 0.0).reshape(9 * entries, rows)

    passed = swap_lon(jnp.where(odd == 1, behind, ahead))
    index0, local = lax.optimization_barrier((index0, local))
    count = rows + 2
    end = rows - 1
    down, own0, up, down2, up2 = row_sums(
        index0,
        weight0,
        [(conc, 0), (beside, 0), (ahead, 0), (behind, 0), (passed, 0)],
        half,
        (
            (0, 0, 1, ((0, 0), (3, 0))),
            (0, 1, end, ((0, 0),)),
            (0, end, rows, ((0, 0), (1, -end))),
            (1, 0, 1, ((0, rows), (1, 1))),
            (1, 1, end, ((1, 1),)),
            (1, end, rows, ((1, 1), (2, -end))),
            (2, 0, 1, ((1, rows + 1), (2, 1))),
            (2, 1, end, ((2, 1),)),
            (2, end, rows, ((2, 1), (4, -end))),
        ),
        (
            (rows + 1, jnp.bfloat16),
            (count, jnp.float32),
            (rows + 1, jnp.bfloat16),
            (1, jnp.bfloat16),
            (1, jnp.bfloat16),
        ),
        entries,
    )
    parts0 = [own0, permute_lat(up, 1), permute_lat(down, -1), permute_lat(up2, 2), permute_lat(down2, -2)]

    tables = []
    for step in range(-2, 3):
        tables.append((conc, half) if step == 0 else (from_lat[step], 0))
    for step in range(-2, 3):
        tables.append((beside, half) if step == 0 else (swap_lon(from_lat[step]), 0))
    spans = []
    for which in range(3):
        spans.append((3 * which, end, rows, ((which, -end),)))
        spans.append((3 * which + 1, 0, rows, ((which, 1),)))
        spans.append((3 * which + 2, 0, 1, ((which, rows + 1),)))
    to_east, own1, to_west = row_sums(
        index1,
        weight1,
        tables,
        half,
        tuple(spans),
        ((count, jnp.bfloat16), (count, jnp.float32), (count, jnp.bfloat16)),
        entries,
    )
    parts1 = [own1, permute_lon(to_east, 2), permute_lon(to_west, -2)]

    result = []
    for along_lat, parts, base in ((True, parts0, 0), (False, parts1, half)):
        first, last = edges(along_lat, parts)
        east, west = permute_lon(first, -1), permute_lon(last, 1)
        remapped = combine(along_lat, parts)
        result = [final(offset, remapped, west, east, kappa[:, None, :], local, base, result)]
    return result[0]


def solution(mesh):
    return jax.shard_map(
        body,
        mesh=mesh,
        in_specs=(
            P("lat", None, "lon"),
            P("lon", "lat", None),
            P("lon", "lat", None),
            P("lon", "lat", None),
            P("lon", "lat"),
            P("lat"),
            P(None, "lat", "lon"),
            P(),
            P(),
            P("lat", "lon"),
        ),
        out_specs=P("lat", None, "lon"),
        check_vma=False,
    )
```

```python
import functools

import jax
import jax.numpy as jnp
from jax import lax
from jax.experimental import pallas as pl
from jax.experimental.pallas import tpu as pltpu
from jax.sharding import PartitionSpec as P

REACH = 2
NEAR_LON = 5
TILE = 16
UNROLL = 4
VMEM_BYTES = 24 * 1024 * 1024


def permute_lon(value, steps):
    count = lax.axis_size("lon")
    return lax.ppermute(value, "lon", [(i, (i + steps) % count) for i in range(count)])


def swap_lon(value):
    count = lax.axis_size("lon")
    return lax.ppermute(value, "lon", [(i, i ^ 1) for i in range(count)])


def permute_lat(value, steps):
    count = lax.axis_size("lat")
    pairs = [(i, i + steps) for i in range(count) if 0 <= i + steps < count]
    return lax.ppermute(value, "lat", pairs)


def in_smem():
    return pl.BlockSpec(memory_space=pltpu.SMEM)


def in_place():
    return pl.BlockSpec(memory_space=pl.ANY)


def for_rows(count, one):
    def some(g, carry):
        stores = []
        for u in range(UNROLL):
            stores += one(g * UNROLL + u)
        for ref, at, value in stores:
            ref[at] = value.astype(ref.dtype)
        return carry

    lax.fori_loop(0, count // UNROLL, some, 0)


def growth_kernel(flip_ref, settle_ref, conc_ref, rates_ref, out_ref, mat_ref):
    ranks, rows_step = rates_ref.shape[0], conc_ref.shape[0]
    bins, width = conc_ref.shape[1:]

    @pl.when(pl.program_id(0) == 0)
    def _():
        for q in range(ranks):
            spread = jnp.broadcast_to(flip_ref[q : q + 1, :], (bins, 2 * bins))
            turned = pltpu.roll(spread, bins + 1, 1, stride=1, stride_axis=0)
            mat_ref[q * bins : (q + 1) * bins, :] = turned[:, :bins].astype(jnp.bfloat16)

    settle = jnp.broadcast_to(settle_ref[...], (bins, width))
    for r in range(rows_step):
        cells = conc_ref[r]
        product = jnp.dot(mat_ref[...], cells, preferred_element_type=jnp.float32)
        total = -settle * cells.astype(jnp.float32)
        for q in range(ranks):
            total = total + rates_ref[q, r : r + 1, :] * product[q * bins : (q + 1) * bins]
        out_ref[r] = total


def local_terms(conc, agg_rates, toeplitz, settle):
    rows, bins, width = conc.shape
    ranks = agg_rates.shape[0]
    step = 8
    flipped = jnp.pad(toeplitz[:, ::-1].astype(jnp.float32), ((0, 0), (0, 1)))
    return pl.pallas_call(
        growth_kernel,
        grid=(rows // step,),
        in_specs=[
            pl.BlockSpec((ranks, 2 * bins), lambda i: (0, 0)),
            pl.BlockSpec((bins, 1), lambda i: (0, 0)),
            pl.BlockSpec((step, bins, width), lambda i: (i, 0, 0)),
            pl.BlockSpec((ranks, step, width), lambda i: (0, i, 0)),
        ],
        out_specs=pl.BlockSpec((step, bins, width), lambda i: (i, 0, 0)),
        out_shape=jax.ShapeDtypeStruct(conc.shape, jnp.float32),
        scratch_shapes=[pltpu.VMEM((ranks * bins, bins), jnp.bfloat16)],
        cost_estimate=pl.CostEstimate(
            flops=2 * ranks * bins * bins * rows * width, bytes_accessed=8 * conc.size, transcendentals=0
        ),
        name="growth",
    )(flipped, settle[:, None], conc, agg_rates)


def row_sums_kernel(bases, entries, *refs):
    tables = len(bases)
    index_ref, weight_ref = refs[:2]
    sources = refs[2 : 2 + tables]
    outs = refs[2 + tables : -2]
    table, sems = refs[-2:]
    steps, every, tile, width = table.shape
    rows = every // tables
    now = pl.program_id(0)

    def copy(step, i):
        return pltpu.make_async_copy(
            sources[i].at[pl.ds(0, rows), pl.ds(bases[i] + step * tile, tile), :],
            table.at[step, pl.ds(i * rows, rows)],
            sems.at[step, i],
        )

    @pl.when(now == 0)
    def _():
        for step in range(steps):
            for i in range(tables):
                copy(step, i).start()

    for step in range(steps):

        @pl.when(now == step)
        def _(step=step):
            for i in range(tables):
                copy(step, i).wait()

    for group, out in enumerate(outs):

        def one(r, group=group, out=out):
            total = jnp.zeros((tile, width), jnp.float32)
            for k in range(entries):
                row = group * entries + k
                total = total + weight_ref[row, r] * table[now, index_ref[row, r]].astype(jnp.float32)
            return [(out, r, total)]

        for_rows(rows, one)


def row_sums(index, weight, sources, rows, half, dtypes, entries):
    tables = len(sources)
    width = sources[0][0].shape[2]
    steps = half // TILE
    count = len(dtypes)
    return pl.pallas_call(
        functools.partial(row_sums_kernel, tuple(base for _, base in sources), entries),
        grid=(steps,),
        in_specs=[in_smem(), in_smem()] + [in_place()] * tables,
        out_specs=[pl.BlockSpec((rows, TILE, width), lambda t: (0, t, 0))] * count,
        out_shape=[jax.ShapeDtypeStruct((rows, half, width), dtype) for dtype in dtypes],
        scratch_shapes=[
            pltpu.VMEM((steps, tables * rows, TILE, width), jnp.bfloat16),
            pltpu.SemaphoreType.DMA((steps, tables)),
        ],
        compiler_params=pltpu.CompilerParams(vmem_limit_bytes=VMEM_BYTES),
        cost_estimate=pl.CostEstimate(
            flops=2 * count * rows * entries * half * width,
            bytes_accessed=2 * (tables + count) * rows * half * width,
            transcendentals=0,
        ),
        name="row_sums",
    )(index, weight, *[source for source, _ in sources])


def edges_kernel(*refs):
    first_ref, last_ref = refs[-2:]
    halves = (len(refs) - 2) // 6
    rows = refs[0].shape[0]
    half = refs[0].shape[1]
    per = 128 // 8
    lane = lax.broadcasted_iota(jnp.int32, (half, 128), 1)
    for side, out_ref in ((0, first_ref), (1, last_ref)):
        for h in range(halves):
            parts = refs[6 * h + 3 * side : 6 * h + 3 * side + 3]
            for j in range(rows // per):
                packed = jnp.zeros((half, 128), jnp.float32)
                for i in range(per):
                    r = j * per + i
                    cells = parts[0][r] + parts[1][r].astype(jnp.float32) + parts[2][r].astype(jnp.float32)
                    at = 8 * i + 3 * (1 - side)
                    spot = (lane >= at) & (lane < at + 3)
                    packed = jnp.where(spot, pltpu.roll(cells, 8 * i + 3, 1), packed)
                out_ref[j, h * half : (h + 1) * half] = packed.astype(out_ref.dtype)


def edges(parts0, parts1):
    rows, half, width = parts0[0].shape
    specs, operands = [], []
    for parts in (parts0, parts1):
        for at in (0, width // 128 - 1):
            specs += [pl.BlockSpec((rows, half, 128), lambda t, at=at: (0, 0, at))] * 3
            operands += parts
    packed = (rows // 16, 2 * half, 128)
    return pl.pallas_call(
        edges_kernel,
        grid=(1,),
        in_specs=specs,
        out_specs=[pl.BlockSpec(packed, lambda t: (0, 0, 0))] * 2,
        out_shape=[jax.ShapeDtypeStruct(packed, jnp.bfloat16)] * 2,
        compiler_params=pltpu.CompilerParams(vmem_limit_bytes=VMEM_BYTES),
        cost_estimate=pl.CostEstimate(flops=8 * half * 256 * rows, bytes_accessed=16 * half * 256 * rows, transcendentals=0),
        name="edges",
    )(*operands)


def combine_kernel(own0, a0, b0, own1, a1, b1, out_ref):
    rows, half = own0.shape[:2]
    for r in range(rows):
        out_ref[r, :half] = own0[r] + a0[r].astype(jnp.float32) + b0[r].astype(jnp.float32)
        out_ref[r, half:] = own1[r] + a1[r].astype(jnp.float32) + b1[r].astype(jnp.float32)


def combine(parts0, parts1):
    rows, half, width = parts0[0].shape
    step = 8
    return pl.pallas_call(
        combine_kernel,
        grid=(rows // step,),
        in_specs=[pl.BlockSpec((step, half, width), lambda t: (t, 0, 0))] * 6,
        out_specs=pl.BlockSpec((step, 2 * half, width), lambda t: (t, 0, 0)),
        out_shape=jax.ShapeDtypeStruct((rows, 2 * half, width), jnp.float32),
        compiler_params=pltpu.CompilerParams(vmem_limit_bytes=VMEM_BYTES),
        cost_estimate=pl.CostEstimate(
            flops=4 * rows * half * width, bytes_accessed=24 * rows * half * width, transcendentals=0
        ),
        name="combine",
    )(*parts0, *parts1)


def moved_row(row, edge, amount, lane):
    tiles = row + [edge]
    count = len(tiles)
    turned = [pltpu.roll(tile, lax.rem(amount + 128, 128), 1) for tile in tiles]
    before, after = lane < amount, lane >= 128 + amount
    return [
        jnp.where(before, turned[t - 1], jnp.where(after, turned[(t + 1) % count], turned[t])) for t in range(count)
    ]


def edge_tile(west_ref, east_ref, r):
    per = 128 // 8
    both = west_ref[r // per].astype(jnp.float32) + east_ref[r // per].astype(jnp.float32)
    return pltpu.roll(both, lax.rem(125 - 8 * lax.rem(r, per) + 128, 128), 1)


def rows_kernel(offset_ref, remap0_ref, remap1_ref, west_ref, east_ref, first_ref, last_ref):
    bins, width = remap0_ref.shape[1:]
    lane = lax.broadcasted_iota(jnp.int32, (bins, 128), 1)
    end = offset_ref.shape[0] - 1
    for r, remap_ref, out_ref in ((0, remap0_ref, first_ref), (end, remap1_ref, last_ref)):
        row = [remap_ref[0, :, 128 * t : 128 * t + 128] for t in range(width // 128)]
        row = moved_row(row, edge_tile(west_ref, east_ref, r), offset_ref[r], lane)
        for t in range(width // 128):
            out_ref[0, :, 128 * t : 128 * t + 128] = row[t].astype(out_ref.dtype)


def outer_rows(offset, remapped, west, east):
    rows, bins, width = remapped.shape
    row = lambda at: pl.BlockSpec((1, bins, width), lambda t: (at, 0, 0))
    whole = pl.BlockSpec(west.shape, lambda t: (0, 0, 0))
    return pl.pallas_call(
        rows_kernel,
        grid=(1,),
        in_specs=[in_smem(), row(0), row(rows - 1), whole, whole],
        out_specs=[row(0), row(0)],
        out_shape=[jax.ShapeDtypeStruct((1, bins, width), jnp.bfloat16)] * 2,
        cost_estimate=pl.CostEstimate(flops=20 * bins * width, bytes_accessed=12 * bins * width, transcendentals=0),
        name="outer_rows",
    )(offset, remapped, remapped, west, east)


def final_kernel(offset_ref, remap_ref, west_ref, east_ref, kappa_ref, local_ref, out_ref):
    rows, bins, width = remap_ref.shape
    lane = lax.broadcasted_iota(jnp.int32, (bins, 128), 1)
    tiles = width // 128
    spots = [slice(128 * t, 128 * t + 128) for t in range(tiles)]

    def group(g, carry):
        before, now, base = carry
        stores = []
        for u in range(UNROLL):
            r = g * UNROLL + u
            row = moved_row(
                [remap_ref[r, :, at] for at in spots], edge_tile(west_ref, east_ref, r), offset_ref[r], lane
            )
            eastern = [pltpu.roll(tile, 127, 1) for tile in row]
            western = [pltpu.roll(tile, 1, 1) for tile in row]
            fresh = []
            above = jnp.maximum(r - 1, 0)
            for t in range(tiles):
                east = jnp.where(lane == 127, eastern[t + 1], eastern[t])
                west = jnp.where(lane == 0, western[t - 1], western[t])
                kappa = kappa_ref[r, :, spots[t]]
                fresh.append(local_ref[r, :, spots[t]] + row[t] + kappa * (east + west - 4.0 * row[t]))
                stores.append((above, t, base[t] + kappa_ref[above, :, spots[t]] * (before[t] + row[t])))
            before, now, base = now, row[:tiles], fresh
        for r, t, value in stores:
            out_ref[r, :, spots[t]] = value
        return before, now, base

    blank = [jnp.zeros((bins, 128), jnp.float32)] * tiles
    before, now, base = lax.fori_loop(0, rows // UNROLL, group, (blank, blank, blank))
    for t in range(tiles):
        out_ref[rows - 1, :, spots[t]] = base[t] + kappa_ref[rows - 1, :, spots[t]] * before[t]


def final(offset, remapped, west, east, kappa, local):
    rows, bins, width = remapped.shape
    block = pl.BlockSpec((rows, TILE, width), lambda t: (0, t, 0))
    packed = pl.BlockSpec((west.shape[0], TILE, 128), lambda t: (0, t, 0))
    return pl.pallas_call(
        final_kernel,
        grid=(bins // TILE,),
        in_specs=[in_smem(), block, packed, packed, pl.BlockSpec(kappa.shape, lambda t: (0, 0, 0)), block],
        out_specs=block,
        out_shape=jax.ShapeDtypeStruct(local.shape, jnp.float32),
        compiler_params=pltpu.CompilerParams(vmem_limit_bytes=VMEM_BYTES),
        cost_estimate=pl.CostEstimate(flops=30 * remapped.size, bytes_accessed=12 * remapped.size, transcendentals=0),
        name="final",
    )(offset, remapped, west, east, kappa, local)


def halo_kernel(before_ref, after_ref, kappa_ref, in_ref, out_ref):
    side = pl.program_id(0)
    value = jnp.where(side == 0, before_ref[0].astype(jnp.float32), after_ref[0].astype(jnp.float32))
    out_ref[0] = in_ref[0] + kappa_ref[0] * value


def add_halo(before, after, kappa, partial):
    rows, bins, width = partial.shape
    whole = pl.BlockSpec((1, bins, width), lambda i: (0, 0, 0))
    row = pl.BlockSpec((1, bins, width), lambda i: (i * (rows - 1), 0, 0))
    return pl.pallas_call(
        halo_kernel,
        grid=(2,),
        in_specs=[whole, whole, pl.BlockSpec((1, 1, width), lambda i: (i * (rows - 1), 0, 0)), row],
        out_specs=row,
        out_shape=jax.ShapeDtypeStruct(partial.shape, jnp.float32),
        input_output_aliases={3: 0},
        cost_estimate=pl.CostEstimate(flops=4 * bins * width, bytes_accessed=20 * bins * width, transcendentals=0),
        name="add_halo",
    )(before, after, kappa, partial)


def body(
    conc,
    dep_owner,
    dep_row,
    dep_weight,
    dep_count,
    zonal_offset,
    agg_rates,
    toeplitz,
    settle,
    kappa,
):
    rows, bins, width = conc.shape
    entries = dep_owner.shape[2]
    odd = lax.axis_index("lon") % 2
    toward = 1 - 2 * odd
    half = bins // 2

    live = jnp.where(
        jnp.arange(entries, dtype=jnp.int32)[:, None] < dep_count, dep_weight[0].T, jnp.float32(0.0)
    )
    top = lax.reduce_precision(live, 8, 7)
    middle = lax.reduce_precision(live - top, 8, 7)
    asked = [dep_owner[0].T.astype(jnp.float32), dep_row[0].T.astype(jnp.float32), top, middle, live - top - middle]
    meta = jnp.concatenate(asked).astype(jnp.bfloat16)
    extra = jnp.pad(meta, ((0, half - 5 * entries), (0, width - rows)))[None]
    low = jnp.concatenate([conc[:, :half], extra])
    high = jnp.concatenate([conc[:, half:], extra])

    ahead = permute_lon(low, -2)
    behind = permute_lon(low, 2)
    south = permute_lat(high, 1)
    north = permute_lat(high, -1)
    beside = swap_lon(conc)
    local = local_terms(conc, agg_rates, toeplitz, settle)

    def asked_by(blocks):
        parts = jnp.stack([block[: 5 * entries, :rows] for block in blocks]).astype(jnp.float32)
        parts = parts.reshape(3, 5, entries, rows)
        owner, source = parts[:, 0].astype(jnp.int32), parts[:, 1].astype(jnp.int32)
        weight = parts[:, 2] + parts[:, 3] + parts[:, 4]
        return owner // NEAR_LON - 1, owner % NEAR_LON - REACH, source, weight

    block = jnp.arange(-1, 2, dtype=jnp.int32)[:, None, None]

    lat_step, lon_step, source, weight = asked_by([south[rows], extra[0], north[rows]])
    slot = jnp.where(
        lon_step == 0,
        0,
        jnp.where(lon_step == 2, 2, jnp.where(lon_step == -2, 3, jnp.where(lon_step == toward, 1, 4))),
    )
    here = block + lat_step == 0
    index0 = jnp.where(here, slot * rows + source, 0).reshape(3 * entries, rows)
    weight0 = jnp.where(here, weight, 0.0).reshape(3 * entries, rows)
    passed = swap_lon(jnp.where(odd == 1, behind, ahead))
    down, own0, up = row_sums(
        index0,
        weight0,
        [(conc, 0), (beside, 0), (ahead, 0), (behind, 0), (passed, 0)],
        rows,
        half,
        (jnp.bfloat16, jnp.float32, jnp.bfloat16),
        entries,
    )
    parts0 = [own0, permute_lat(up, 1), permute_lat(down, -1)]

    lat_step, lon_step, source, weight = asked_by([behind[rows], extra[0], ahead[rows]])
    lon_from = 2 * block + lon_step
    pair = jnp.where(lon_from == 0, 0, 1)
    here = (lon_from == 0) | (lon_from == toward)
    index1 = jnp.where(here, (pair * 3 + lat_step + 1) * rows + source, 0).reshape(3 * entries, rows)
    weight1 = jnp.where(here, weight, 0.0).reshape(3 * entries, rows)
    to_west, own1, to_east = row_sums(
        index1,
        weight1,
        [(south, 0), (conc, half), (north, 0), (swap_lon(south), 0), (beside, half), (swap_lon(north), 0)],
        rows,
        half,
        (jnp.bfloat16, jnp.float32, jnp.bfloat16),
        entries,
    )
    parts1 = [own1, permute_lon(to_east, 2), permute_lon(to_west, -2)]

    first, last = edges(parts0, parts1)
    east, west = permute_lon(first, -1), permute_lon(last, 1)
    remapped = combine(parts0, parts1)
    top_row, end_row = outer_rows(zonal_offset, remapped, west, east)
    before, after = permute_lat(end_row, 1), permute_lat(top_row, -1)
    kappa = kappa[:, None, :]
    partial = final(zonal_offset, remapped, west, east, kappa, local)
    return add_halo(before, after, kappa, partial)


def solution(mesh):
    return jax.shard_map(
        body,
        mesh=mesh,
        in_specs=(
            P("lat", None, "lon"),
            P("lon", "lat", None),
            P("lon", "lat", None),
            P("lon", "lat", None),
            P("lon", "lat"),
            P("lat"),
            P(None, "lat", "lon"),
            P(),
            P(),
            P("lat", "lon"),
        ),
        out_specs=P("lat", None, "lon"),
        check_vma=False,
    )
```

```python
import functools

import jax
import jax.numpy as jnp
from jax import lax
from jax.experimental import pallas as pl
from jax.experimental.pallas import tpu as pltpu
from jax.sharding import PartitionSpec as P

REACH = 2
NEAR_LON = 5
TILE = 16
UNROLL = 4
VMEM_BYTES = 12 * 1024 * 1024
TABLE_BYTES = 20 * 1024 * 1024
QUICK = 2


def permute_lon(value, steps):
    count = lax.axis_size("lon")
    return lax.ppermute(value, "lon", [(i, (i + steps) % count) for i in range(count)])


def swap_lon(value):
    count = lax.axis_size("lon")
    return lax.ppermute(value, "lon", [(i, i ^ 1) for i in range(count)])


def permute_lat(value, steps):
    count = lax.axis_size("lat")
    pairs = [(i, i + steps) for i in range(count) if 0 <= i + steps < count]
    return lax.ppermute(value, "lat", pairs)


def in_smem():
    return pl.BlockSpec(memory_space=pltpu.SMEM)


def in_place():
    return pl.BlockSpec(memory_space=pl.ANY)


def for_rows(count, one):
    def some(g, carry):
        stores = []
        for u in range(UNROLL):
            stores += one(g * UNROLL + u)
        for ref, at, value in stores:
            ref[at] = value.astype(ref.dtype)
        return carry

    lax.fori_loop(0, count // UNROLL, some, 0)


def growth_kernel(flip_ref, settle_ref, conc_ref, rates_ref, out_ref, mat_ref):
    ranks, rows_step = rates_ref.shape[0], conc_ref.shape[0]
    bins, width = conc_ref.shape[1:]

    @pl.when(pl.program_id(0) == 0)
    def _():
        for q in range(ranks):
            spread = jnp.broadcast_to(flip_ref[q : q + 1, :], (bins, 2 * bins))
            turned = pltpu.roll(spread, bins + 1, 1, stride=1, stride_axis=0)
            mat_ref[q * bins : (q + 1) * bins, :] = turned[:, :bins].astype(jnp.bfloat16)

    settle = jnp.broadcast_to(settle_ref[...], (bins, width))
    for r in range(rows_step):
        cells = conc_ref[r]
        product = jnp.dot(mat_ref[...], cells, preferred_element_type=jnp.float32)
        total = -settle * cells.astype(jnp.float32)
        for q in range(ranks):
            total = total + rates_ref[q, r : r + 1, :] * product[q * bins : (q + 1) * bins]
        out_ref[r] = total


def local_terms(conc, agg_rates, toeplitz, settle):
    rows, bins, width = conc.shape
    ranks = agg_rates.shape[0]
    step = 8
    flipped = jnp.pad(toeplitz[:, ::-1].astype(jnp.float32), ((0, 0), (0, 1)))
    return pl.pallas_call(
        growth_kernel,
        grid=(rows // step,),
        in_specs=[
            pl.BlockSpec((ranks, 2 * bins), lambda i: (0, 0)),
            pl.BlockSpec((bins, 1), lambda i: (0, 0)),
            pl.BlockSpec((step, bins, width), lambda i: (i, 0, 0)),
            pl.BlockSpec((ranks, step, width), lambda i: (0, i, 0)),
        ],
        out_specs=pl.BlockSpec((step, bins, width), lambda i: (i, 0, 0)),
        out_shape=jax.ShapeDtypeStruct(conc.shape, jnp.float32),
        scratch_shapes=[pltpu.VMEM((ranks * bins, bins), jnp.bfloat16)],
        compiler_params=pltpu.CompilerParams(vmem_limit_bytes=VMEM_BYTES),
        cost_estimate=pl.CostEstimate(
            flops=2 * ranks * bins * bins * rows * width, bytes_accessed=8 * conc.size, transcendentals=0
        ),
        name="growth",
    )(flipped, settle[:, None], conc, agg_rates)


def row_sums_kernel(bases, entries, *refs):
    tables = len(bases)
    index_ref, weight_ref, more_ref = refs[:3]
    sources = refs[3 : 3 + tables]
    outs = refs[3 + tables : -2]
    table, sems = refs[-2:]
    every, half, width = table.shape
    rows = every // tables
    copies = [
        pltpu.make_async_copy(
            sources[i].at[pl.ds(0, rows), pl.ds(bases[i], half), :], table.at[pl.ds(i * rows, rows)], sems.at[i]
        )
        for i in range(tables)
    ]
    for copy in copies:
        copy.start()
    for copy in copies:
        copy.wait()

    for group, out in enumerate(outs):

        def some(g, carry, group=group, out=out):
            def sums(terms):
                totals = []
                for u in range(UNROLL):
                    r = g * UNROLL + u
                    total = jnp.zeros((half, width), jnp.float32)
                    for k in range(terms):
                        row = group * entries + k
                        total = total + weight_ref[row, r] * table[index_ref[row, r]].astype(jnp.float32)
                    totals.append(total)
                for u in range(UNROLL):
                    out[g * UNROLL + u] = totals[u].astype(out.dtype)

            sums(min(QUICK, entries))

            @pl.when(more_ref[group, g] > 0)
            def _():
                sums(entries)

            return carry

        lax.fori_loop(0, rows // UNROLL, some, 0)


def packed_terms(here, index, weight):
    groups, entries, rows = index.shape
    rank = jnp.cumsum(here.astype(jnp.int32), axis=1) - here.astype(jnp.int32)
    indices, weights = [], []
    for place in range(entries):
        taken = here & (rank == place)
        indices.append(jnp.sum(jnp.where(taken, index, 0), axis=1))
        weights.append(jnp.sum(jnp.where(taken, weight, 0.0), axis=1))
    count = jnp.sum(here.astype(jnp.int32), axis=1).reshape(groups, rows // UNROLL, UNROLL)
    more = (jnp.max(count, axis=2) > QUICK).astype(jnp.int32)
    shape = (groups * entries, rows)
    return jnp.stack(indices, axis=1).reshape(shape), jnp.stack(weights, axis=1).reshape(shape), more


def row_sums(terms, sources, rows, half, dtypes, entries):
    tables = len(sources)
    width = sources[0][0].shape[2]
    count = len(dtypes)
    return pl.pallas_call(
        functools.partial(row_sums_kernel, tuple(base for _, base in sources), entries),
        in_specs=[in_smem()] * 3 + [in_place()] * tables,
        out_specs=[pl.BlockSpec(memory_space=pltpu.VMEM)] * count,
        out_shape=[jax.ShapeDtypeStruct((rows, half, width), dtype) for dtype in dtypes],
        scratch_shapes=[
            pltpu.VMEM((tables * rows, half, width), jnp.bfloat16),
            pltpu.SemaphoreType.DMA((tables,)),
        ],
        compiler_params=pltpu.CompilerParams(vmem_limit_bytes=TABLE_BYTES),
        cost_estimate=pl.CostEstimate(
            flops=2 * count * rows * entries * half * width,
            bytes_accessed=2 * (tables + count) * rows * half * width,
            transcendentals=0,
        ),
        name="row_sums",
    )(*terms, *[source for source, _ in sources])


def edges_kernel(*refs):
    first_ref, last_ref = refs[-2:]
    halves = (len(refs) - 2) // 6
    rows = refs[0].shape[0]
    half = refs[0].shape[1]
    per = 128 // 8
    lane = lax.broadcasted_iota(jnp.int32, (half, 128), 1)
    for side, out_ref in ((0, first_ref), (1, last_ref)):
        for h in range(halves):
            parts = refs[6 * h + 3 * side : 6 * h + 3 * side + 3]
            for j in range(rows // per):
                packed = jnp.zeros((half, 128), jnp.float32)
                for i in range(per):
                    r = j * per + i
                    cells = parts[0][r] + parts[1][r].astype(jnp.float32) + parts[2][r].astype(jnp.float32)
                    at = 8 * i + 3 * (1 - side)
                    spot = (lane >= at) & (lane < at + 3)
                    packed = jnp.where(spot, pltpu.roll(cells, 8 * i + 3, 1), packed)
                out_ref[j, h * half : (h + 1) * half] = packed.astype(out_ref.dtype)


def edges(parts0, parts1):
    rows, half, width = parts0[0].shape
    specs, operands = [], []
    for parts in (parts0, parts1):
        for at in (0, width // 128 - 1):
            specs += [pl.BlockSpec((rows, half, 128), lambda t, at=at: (0, 0, at))] * 3
            operands += parts
    packed = (rows // 16, 2 * half, 128)
    return pl.pallas_call(
        edges_kernel,
        grid=(1,),
        in_specs=specs,
        out_specs=[pl.BlockSpec(packed, lambda t: (0, 0, 0))] * 2,
        out_shape=[jax.ShapeDtypeStruct(packed, jnp.bfloat16)] * 2,
        compiler_params=pltpu.CompilerParams(vmem_limit_bytes=VMEM_BYTES),
        cost_estimate=pl.CostEstimate(flops=8 * half * 256 * rows, bytes_accessed=16 * half * 256 * rows, transcendentals=0),
        name="edges",
    )(*operands)


def combine_kernel(own0, a0, b0, own1, a1, b1, out_ref):
    rows, half = own0.shape[:2]
    for r in range(rows):
        out_ref[r, :half] = own0[r] + a0[r].astype(jnp.float32) + b0[r].astype(jnp.float32)
        out_ref[r, half:] = own1[r] + a1[r].astype(jnp.float32) + b1[r].astype(jnp.float32)


def combine(parts0, parts1):
    rows, half, width = parts0[0].shape
    step = 8
    return pl.pallas_call(
        combine_kernel,
        grid=(rows // step,),
        in_specs=[pl.BlockSpec((step, half, width), lambda t: (t, 0, 0))] * 6,
        out_specs=pl.BlockSpec((step, 2 * half, width), lambda t: (t, 0, 0)),
        out_shape=jax.ShapeDtypeStruct((rows, 2 * half, width), jnp.float32),
        compiler_params=pltpu.CompilerParams(vmem_limit_bytes=VMEM_BYTES),
        cost_estimate=pl.CostEstimate(
            flops=4 * rows * half * width, bytes_accessed=24 * rows * half * width, transcendentals=0
        ),
        name="combine",
    )(*parts0, *parts1)


def moved_row(row, edge, amount, lane):
    tiles = row + [edge]
    count = len(tiles)
    index = (lane + (128 - amount)) & 127
    turned = [jnp.take_along_axis(tile, index, axis=1) for tile in tiles]
    before, after = lane < amount, lane >= 128 + amount
    return [
        jnp.where(before, turned[t - 1], jnp.where(after, turned[(t + 1) % count], turned[t])) for t in range(count)
    ]


def edge_tile(west_ref, east_ref, j, i):
    both = west_ref[j].astype(jnp.float32) + east_ref[j].astype(jnp.float32)
    return pltpu.roll(both, (125 - 8 * i) % 128, 1)


def rows_kernel(offset_ref, remap0_ref, remap1_ref, west_ref, east_ref, first_ref, last_ref):
    bins, width = remap0_ref.shape[1:]
    lane = lax.broadcasted_iota(jnp.int32, (bins, 128), 1)
    end = offset_ref.shape[0] - 1
    for r, remap_ref, out_ref in ((0, remap0_ref, first_ref), (end, remap1_ref, last_ref)):
        row = [remap_ref[0, :, 128 * t : 128 * t + 128] for t in range(width // 128)]
        row = moved_row(row, edge_tile(west_ref, east_ref, r // 16, r % 16), offset_ref[r], lane)
        for t in range(width // 128):
            out_ref[0, :, 128 * t : 128 * t + 128] = row[t].astype(out_ref.dtype)


def outer_rows(offset, remapped, west, east):
    rows, bins, width = remapped.shape
    row = lambda at: pl.BlockSpec((1, bins, width), lambda t: (at, 0, 0))
    whole = pl.BlockSpec(west.shape, lambda t: (0, 0, 0))
    return pl.pallas_call(
        rows_kernel,
        grid=(1,),
        in_specs=[in_smem(), row(0), row(rows - 1), whole, whole],
        out_specs=[row(0), row(0)],
        out_shape=[jax.ShapeDtypeStruct((1, bins, width), jnp.bfloat16)] * 2,
        compiler_params=pltpu.CompilerParams(vmem_limit_bytes=VMEM_BYTES),
        cost_estimate=pl.CostEstimate(flops=20 * bins * width, bytes_accessed=12 * bins * width, transcendentals=0),
        name="outer_rows",
    )(offset, remapped, remapped, west, east)


def final_kernel(offset_ref, remap_ref, west_ref, east_ref, kappa_ref, local_ref, out_ref):
    rows, bins, width = remap_ref.shape
    lane = lax.broadcasted_iota(jnp.int32, (bins, 128), 1)
    tiles = width // 128
    per = 128 // 8
    spots = [slice(128 * t, 128 * t + 128) for t in range(tiles)]

    def group(j, carry):
        before, now, base = carry
        stores = []
        for i in range(per):
            r = j * per + i
            row = moved_row(
                [remap_ref[r, :, at] for at in spots], edge_tile(west_ref, east_ref, j, i), offset_ref[r], lane
            )
            eastern = [pltpu.roll(tile, 127, 1) for tile in row]
            western = [pltpu.roll(tile, 1, 1) for tile in row]
            fresh = []
            above = jnp.maximum(r - 1, 0)
            for t in range(tiles):
                east = jnp.where(lane == 127, eastern[t + 1], eastern[t])
                west = jnp.where(lane == 0, western[t - 1], western[t])
                kappa = kappa_ref[r, :, spots[t]]
                fresh.append(local_ref[r, :, spots[t]] + row[t] + kappa * (east + west - 4.0 * row[t]))
                stores.append((above, t, base[t] + kappa_ref[above, :, spots[t]] * (before[t] + row[t])))
            before, now, base = now, row[:tiles], fresh
            if i % UNROLL == UNROLL - 1:
                for at, t, value in stores:
                    out_ref[at, :, spots[t]] = value
                stores = []
        return before, now, base

    blank = [jnp.zeros((bins, 128), jnp.float32)] * tiles
    before, now, base = lax.fori_loop(0, rows // per, group, (blank, blank, blank))
    for t in range(tiles):
        out_ref[rows - 1, :, spots[t]] = base[t] + kappa_ref[rows - 1, :, spots[t]] * before[t]


def final(offset, remapped, west, east, kappa, local):
    rows, bins, width = remapped.shape
    block = pl.BlockSpec((rows, TILE, width), lambda t: (0, t, 0))
    packed = pl.BlockSpec((west.shape[0], TILE, 128), lambda t: (0, t, 0))
    return pl.pallas_call(
        final_kernel,
        grid=(bins // TILE,),
        in_specs=[in_smem(), block, packed, packed, pl.BlockSpec(kappa.shape, lambda t: (0, 0, 0)), block],
        out_specs=block,
        out_shape=jax.ShapeDtypeStruct(local.shape, jnp.float32),
        compiler_params=pltpu.CompilerParams(vmem_limit_bytes=VMEM_BYTES),
        cost_estimate=pl.CostEstimate(flops=30 * remapped.size, bytes_accessed=12 * remapped.size, transcendentals=0),
        name="final",
    )(offset, remapped, west, east, kappa, local)


def halo_kernel(before_ref, after_ref, kappa_ref, in_ref, out_ref):
    side = pl.program_id(0)
    value = jnp.where(side == 0, before_ref[0].astype(jnp.float32), after_ref[0].astype(jnp.float32))
    out_ref[0] = in_ref[0] + kappa_ref[0] * value


def add_halo(before, after, kappa, partial):
    rows, bins, width = partial.shape
    whole = pl.BlockSpec((1, bins, width), lambda i: (0, 0, 0))
    row = pl.BlockSpec((1, bins, width), lambda i: (i * (rows - 1), 0, 0))
    return pl.pallas_call(
        halo_kernel,
        grid=(2,),
        in_specs=[whole, whole, pl.BlockSpec((1, 1, width), lambda i: (i * (rows - 1), 0, 0)), row],
        out_specs=row,
        out_shape=jax.ShapeDtypeStruct(partial.shape, jnp.float32),
        input_output_aliases={3: 0},
        compiler_params=pltpu.CompilerParams(vmem_limit_bytes=VMEM_BYTES),
        cost_estimate=pl.CostEstimate(flops=4 * bins * width, bytes_accessed=20 * bins * width, transcendentals=0),
        name="add_halo",
    )(before, after, kappa, partial)


def body(
    conc,
    dep_owner,
    dep_row,
    dep_weight,
    dep_count,
    zonal_offset,
    agg_rates,
    toeplitz,
    settle,
    kappa,
):
    rows, bins, width = conc.shape
    entries = dep_owner.shape[2]
    odd = lax.axis_index("lon") % 2
    toward = 1 - 2 * odd
    half = bins // 2

    live = jnp.where(
        jnp.arange(entries, dtype=jnp.int32)[:, None] < dep_count, dep_weight[0].T, jnp.float32(0.0)
    )
    top = lax.reduce_precision(live, 8, 7)
    middle = lax.reduce_precision(live - top, 8, 7)
    asked = [dep_owner[0].T.astype(jnp.float32), dep_row[0].T.astype(jnp.float32), top, middle, live - top - middle]
    meta = jnp.concatenate(asked).astype(jnp.bfloat16)
    extra = jnp.pad(meta, ((0, half - 5 * entries), (0, width - rows)))[None]
    low = jnp.concatenate([conc[:, :half], extra])
    high = jnp.concatenate([conc[:, half:], extra])

    ahead = permute_lon(low, -2)
    behind = permute_lon(low, 2)
    south = permute_lat(high, 1)
    north = permute_lat(high, -1)
    beside = swap_lon(conc)
    local = local_terms(conc, agg_rates, toeplitz, settle)

    def asked_by(blocks):
        parts = jnp.stack([block[: 5 * entries, :rows] for block in blocks]).astype(jnp.float32)
        parts = parts.reshape(3, 5, entries, rows)
        owner, source = parts[:, 0].astype(jnp.int32), parts[:, 1].astype(jnp.int32)
        weight = parts[:, 2] + parts[:, 3] + parts[:, 4]
        return owner // NEAR_LON - 1, owner % NEAR_LON - REACH, source, weight

    block = jnp.arange(-1, 2, dtype=jnp.int32)[:, None, None]

    lat_step, lon_step, source, weight = asked_by([south[rows], extra[0], north[rows]])
    slot = jnp.where(
        lon_step == 0,
        0,
        jnp.where(lon_step == 2, 2, jnp.where(lon_step == -2, 3, jnp.where(lon_step == toward, 1, 4))),
    )
    here = block + lat_step == 0
    terms0 = packed_terms(here & (weight != 0.0), slot * rows + source, weight)
    terms0, local = lax.optimization_barrier((terms0, local))
    passed = swap_lon(jnp.where(odd == 1, behind, ahead))
    down, own0, up = row_sums(
        terms0,
        [(conc, 0), (beside, 0), (ahead, 0), (behind, 0), (passed, 0)],
        rows,
        half,
        (jnp.bfloat16, jnp.float32, jnp.bfloat16),
        entries,
    )
    parts0 = [own0, permute_lat(up, 1), permute_lat(down, -1)]

    lat_step, lon_step, source, weight = asked_by([behind[rows], extra[0], ahead[rows]])
    lon_from = 2 * block + lon_step
    pair = jnp.where(lon_from == 0, 0, 1)
    here = (lon_from == 0) | (lon_from == toward)
    terms1 = packed_terms(here & (weight != 0.0), (pair * 3 + lat_step + 1) * rows + source, weight)
    to_west, own1, to_east = row_sums(
        terms1,
        [(south, 0), (conc, half), (north, 0), (swap_lon(south), 0), (beside, half), (swap_lon(north), 0)],
        rows,
        half,
        (jnp.bfloat16, jnp.float32, jnp.bfloat16),
        entries,
    )
    parts1 = [own1, permute_lon(to_east, 2), permute_lon(to_west, -2)]

    first, last = edges(parts0, parts1)
    east, west = permute_lon(first, -1), permute_lon(last, 1)
    remapped = combine(parts0, parts1)
    top_row, end_row = outer_rows(zonal_offset, remapped, west, east)
    before, after = permute_lat(end_row, 1), permute_lat(top_row, -1)
    kappa = kappa[:, None, :]
    partial = final(zonal_offset, remapped, west, east, kappa, local)
    return add_halo(before, after, kappa, partial)


def solution(mesh):
    return jax.shard_map(
        body,
        mesh=mesh,
        in_specs=(
            P("lat", None, "lon"),
            P("lon", "lat", None),
            P("lon", "lat", None),
            P("lon", "lat", None),
            P("lon", "lat"),
            P("lat"),
            P(None, "lat", "lon"),
            P(),
            P(),
            P("lat", "lon"),
        ),
        out_specs=P("lat", None, "lon"),
        check_vma=False,
    )
```

```python
import functools

import jax
import jax.numpy as jnp
from jax import lax
from jax.experimental import pallas as pl
from jax.experimental.pallas import tpu as pltpu
from jax.sharding import PartitionSpec as P

REACH = 2
NEAR_LON = 5
TILE = 16
UNROLL = 4
VMEM_BYTES = 12 * 1024 * 1024
TABLE_BYTES = 20 * 1024 * 1024
QUICK = 2
FIELDS = ((0, 0), (0, 128), (8, 0), (8, 128), (16, 0))


def permute_lon(value, steps):
    count = lax.axis_size("lon")
    return lax.ppermute(value, "lon", [(i, (i + steps) % count) for i in range(count)])


def swap_lon(value):
    count = lax.axis_size("lon")
    return lax.ppermute(value, "lon", [(i, i ^ 1) for i in range(count)])


def permute_lat(value, steps):
    count = lax.axis_size("lat")
    pairs = [(i, i + steps) for i in range(count) if 0 <= i + steps < count]
    return lax.ppermute(value, "lat", pairs)


def in_smem():
    return pl.BlockSpec(memory_space=pltpu.SMEM)


def in_place():
    return pl.BlockSpec(memory_space=pl.ANY)


def for_rows(count, one):
    def some(g, carry):
        stores = []
        for u in range(UNROLL):
            stores += one(g * UNROLL + u)
        for ref, at, value in stores:
            ref[at] = value.astype(ref.dtype)
        return carry

    lax.fori_loop(0, count // UNROLL, some, 0)


def growth_kernel(flip_ref, settle_ref, conc_ref, rates_ref, out_ref, mat_ref):
    ranks, rows_step = rates_ref.shape[0], conc_ref.shape[0]
    bins, width = conc_ref.shape[1:]

    @pl.when(pl.program_id(0) == 0)
    def _():
        for q in range(ranks):
            spread = jnp.broadcast_to(flip_ref[q : q + 1, :], (bins, 2 * bins))
            turned = pltpu.roll(spread, bins + 1, 1, stride=1, stride_axis=0)
            mat_ref[q * bins : (q + 1) * bins, :] = turned[:, :bins].astype(jnp.bfloat16)

    settle = jnp.broadcast_to(settle_ref[...], (bins, width))
    for r in range(rows_step):
        cells = conc_ref[r]
        product = jnp.dot(mat_ref[...], cells, preferred_element_type=jnp.float32)
        total = -settle * cells.astype(jnp.float32)
        for q in range(ranks):
            total = total + rates_ref[q, r : r + 1, :] * product[q * bins : (q + 1) * bins]
        out_ref[r] = total


def local_terms(conc, agg_rates, toeplitz, settle):
    rows, bins, width = conc.shape
    ranks = agg_rates.shape[0]
    step = 8
    flipped = jnp.pad(toeplitz[:, ::-1].astype(jnp.float32), ((0, 0), (0, 1)))
    return pl.pallas_call(
        growth_kernel,
        grid=(rows // step,),
        in_specs=[
            pl.BlockSpec((ranks, 2 * bins), lambda i: (0, 0)),
            pl.BlockSpec((bins, 1), lambda i: (0, 0)),
            pl.BlockSpec((step, bins, width), lambda i: (i, 0, 0)),
            pl.BlockSpec((ranks, step, width), lambda i: (0, i, 0)),
        ],
        out_specs=pl.BlockSpec((step, bins, width), lambda i: (i, 0, 0)),
        out_shape=jax.ShapeDtypeStruct(conc.shape, jnp.float32),
        scratch_shapes=[pltpu.VMEM((ranks * bins, bins), jnp.bfloat16)],
        compiler_params=pltpu.CompilerParams(vmem_limit_bytes=VMEM_BYTES),
        cost_estimate=pl.CostEstimate(
            flops=2 * ranks * bins * bins * rows * width, bytes_accessed=8 * conc.size, transcendentals=0
        ),
        name="growth",
    )(flipped, settle[:, None], conc, agg_rates)


def message_kernel(conc_ref, owner_ref, source_ref, weight_ref, count_ref, low_ref, high_ref, meta_ref, sems):
    rows, bins, _ = conc_ref.shape
    half = bins // 2
    entries = owner_ref.shape[0]
    copies = [
        pltpu.make_async_copy(conc_ref.at[:, pl.ds(0, half), :], low_ref.at[pl.ds(0, rows)], sems.at[0]),
        pltpu.make_async_copy(conc_ref.at[:, pl.ds(half, half), :], high_ref.at[pl.ds(0, rows)], sems.at[1]),
    ]
    for copy in copies:
        copy.start()
    meta_ref[...] = jnp.zeros(meta_ref.shape, meta_ref.dtype)
    wide = lambda value: value.astype(jnp.float32)
    entry = lax.broadcasted_iota(jnp.int32, owner_ref.shape, 0)
    live = jnp.where(entry < count_ref[...], weight_ref[...], 0.0)
    top = live.astype(jnp.bfloat16)
    middle = (live - wide(top)).astype(jnp.bfloat16)
    bottom = (live - wide(top) - wide(middle)).astype(jnp.bfloat16)
    fields = (wide(owner_ref[...]), wide(source_ref[...]), wide(top), wide(middle), wide(bottom))
    for field, (at, lane) in zip(fields, FIELDS):
        meta_ref[0, at : at + entries, lane : lane + rows] = field.astype(jnp.bfloat16)
    more = [
        pltpu.make_async_copy(meta_ref, low_ref.at[pl.ds(rows, 1)], sems.at[2]),
        pltpu.make_async_copy(meta_ref, high_ref.at[pl.ds(rows, 1)], sems.at[3]),
    ]
    for copy in more:
        copy.start()
    for copy in copies + more:
        copy.wait()


def messages(conc, owner, source, weight, count):
    rows, bins, width = conc.shape
    half = bins // 2
    vmem = pl.BlockSpec(memory_space=pltpu.VMEM)
    return pl.pallas_call(
        message_kernel,
        in_specs=[in_place(), vmem, vmem, vmem, vmem],
        out_specs=[in_place(), in_place()],
        out_shape=[jax.ShapeDtypeStruct((rows + 1, half, width), conc.dtype)] * 2,
        scratch_shapes=[pltpu.VMEM((1, half, width), jnp.bfloat16), pltpu.SemaphoreType.DMA((4,))],
        compiler_params=pltpu.CompilerParams(vmem_limit_bytes=VMEM_BYTES),
        cost_estimate=pl.CostEstimate(flops=0, bytes_accessed=4 * conc.size, transcendentals=0),
        name="messages",
    )(conc, owner, source, weight, count)


def lat_slots(rows, group, lat_step, lon_step, odd):
    toward = 1.0 - 2.0 * odd
    slot = jnp.where(
        lon_step == 0.0,
        0.0,
        jnp.where(lon_step == 2.0, 2.0, jnp.where(lon_step == -2.0, 3.0, jnp.where(lon_step == toward, 1.0, 5.0 - odd))),
    )
    return lat_step == 1.0 - group, slot * rows


def lon_slots(rows, group, lat_step, lon_step, odd):
    toward = 1.0 - 2.0 * odd
    lon_from = 2.0 * (group - 1.0) + lon_step
    slot = jnp.where(lon_from == 0.0, 0.0, 3.0) + lat_step + 1.0
    return (lon_from == 0.0) | (lon_from == toward), slot * rows


def row_sums_kernel(bases, slots, entries, *refs):
    tables = len(bases)
    odd_ref = refs[0]
    asked = refs[1:4]
    sources = refs[4 : 4 + tables]
    outs = refs[4 + tables : 7 + tables]
    table, meta_ref, index_vec, weight_vec, index_ref, weight_ref, sems = refs[7 + tables :]
    every, half, width = table.shape
    rows = every // tables
    metas = [
        pltpu.make_async_copy(asked[g].at[pl.ds(rows, 1)], meta_ref.at[pl.ds(g, 1)], sems.at[tables + g])
        for g in range(3)
    ]
    copies = [
        pltpu.make_async_copy(
            sources[i].at[pl.ds(0, rows), pl.ds(bases[i], half), :], table.at[pl.ds(i * rows, rows)], sems.at[i]
        )
        for i in range(tables)
    ]
    for copy in metas + copies:
        copy.start()
    for copy in metas:
        copy.wait()

    odd = odd_ref[0].astype(jnp.float32)
    for g in range(3):
        owner, source, top, middle, bottom = [
            meta_ref[g, at : at + entries, lane : lane + 128].astype(jnp.float32) for at, lane in FIELDS
        ]
        weight = top + middle + bottom
        band = jnp.where(owner >= NEAR_LON, 1.0, 0.0) + jnp.where(owner >= 2 * NEAR_LON, 1.0, 0.0)
        here, base = slots(rows, float(g), band - 1.0, owner - NEAR_LON * band - REACH, odd)
        here = jnp.where(here & (weight != 0.0), 1.0, 0.0)
        index = base + source
        packed = [[jnp.zeros((1, 128), jnp.float32)] * 2 for _ in range(entries)]
        rank = jnp.zeros((1, 128), jnp.float32)
        for k in range(entries):
            taken = here[k : k + 1]
            for place in range(k + 1):
                spot = (taken > 0.0) & (rank == place)
                packed[place] = [
                    jnp.where(spot, index[k : k + 1], packed[place][0]),
                    jnp.where(spot, weight[k : k + 1], packed[place][1]),
                ]
            rank = rank + taken
        for place in range(entries):
            at = g * entries + place
            index_vec[at : at + 1, :] = packed[place][0].astype(jnp.int32)
            weight_vec[at : at + 1, :] = packed[place][1]
        at = 3 * entries + g
        index_vec[at : at + 1, :] = rank.astype(jnp.int32)
    to_scalar = [
        pltpu.make_async_copy(index_vec, index_ref, sems.at[tables + 3]),
        pltpu.make_async_copy(weight_vec, weight_ref, sems.at[tables + 4]),
    ]
    for copy in to_scalar:
        copy.start()
    for copy in to_scalar + copies:
        copy.wait()

    for group, out in enumerate(outs):

        def some(g, carry, group=group, out=out):
            def sums(terms):
                totals = []
                for u in range(UNROLL):
                    r = g * UNROLL + u
                    total = jnp.zeros((half, width), jnp.float32)
                    for k in range(terms):
                        row = group * entries + k
                        total = total + weight_ref[row, r] * table[index_ref[row, r]].astype(jnp.float32)
                    totals.append(total)
                for u in range(UNROLL):
                    out[g * UNROLL + u] = totals[u].astype(out.dtype)

            most = index_ref[3 * entries + group, g * UNROLL]
            for u in range(1, UNROLL):
                most = jnp.maximum(most, index_ref[3 * entries + group, g * UNROLL + u])
            sums(min(QUICK, entries))

            @pl.when(most > QUICK)
            def _():
                sums(entries)

            return carry

        lax.fori_loop(0, rows // UNROLL, some, 0)


def row_sums(odd, asked, slots, sources, rows, half, entries):
    tables = len(sources)
    width = sources[0][0].shape[2]
    vectors = -(-3 * (entries + 1) // 8) * 8
    return pl.pallas_call(
        functools.partial(row_sums_kernel, tuple(base for _, base in sources), slots, entries),
        in_specs=[in_smem()] + [in_place()] * (3 + tables),
        out_specs=[pl.BlockSpec(memory_space=pltpu.VMEM)] * 3,
        out_shape=[
            jax.ShapeDtypeStruct((rows, half, width), dtype) for dtype in (jnp.bfloat16, jnp.float32, jnp.bfloat16)
        ],
        scratch_shapes=[
            pltpu.VMEM((tables * rows, half, width), jnp.bfloat16),
            pltpu.VMEM((3, half, width), jnp.bfloat16),
            pltpu.VMEM((vectors, 128), jnp.int32),
            pltpu.VMEM((vectors, 128), jnp.float32),
            pltpu.SMEM((vectors, 128), jnp.int32),
            pltpu.SMEM((vectors, 128), jnp.float32),
            pltpu.SemaphoreType.DMA((tables + 5,)),
        ],
        compiler_params=pltpu.CompilerParams(vmem_limit_bytes=TABLE_BYTES),
        cost_estimate=pl.CostEstimate(
            flops=6 * rows * entries * half * width,
            bytes_accessed=2 * (tables + 3) * rows * half * width,
            transcendentals=0,
        ),
        name="row_sums",
    )(odd, *asked, *[source for source, _ in sources])


def edges_kernel(*refs):
    first_ref, last_ref = refs[-2:]
    halves = (len(refs) - 2) // 6
    rows = refs[0].shape[0]
    half = refs[0].shape[1]
    per = 128 // 8
    lane = lax.broadcasted_iota(jnp.int32, (half, 128), 1)
    for side, out_ref in ((0, first_ref), (1, last_ref)):
        for h in range(halves):
            parts = refs[6 * h + 3 * side : 6 * h + 3 * side + 3]
            for j in range(rows // per):
                packed = jnp.zeros((half, 128), jnp.float32)
                for i in range(per):
                    r = j * per + i
                    cells = parts[0][r] + parts[1][r].astype(jnp.float32) + parts[2][r].astype(jnp.float32)
                    at = 8 * i + 3 * (1 - side)
                    spot = (lane >= at) & (lane < at + 3)
                    packed = jnp.where(spot, pltpu.roll(cells, 8 * i + 3, 1), packed)
                out_ref[j, h * half : (h + 1) * half] = packed.astype(out_ref.dtype)


def edges(parts0, parts1):
    rows, half, width = parts0[0].shape
    specs, operands = [], []
    for parts in (parts0, parts1):
        for at in (0, width // 128 - 1):
            specs += [pl.BlockSpec((rows, half, 128), lambda t, at=at: (0, 0, at))] * 3
            operands += parts
    packed = (rows // 16, 2 * half, 128)
    return pl.pallas_call(
        edges_kernel,
        grid=(1,),
        in_specs=specs,
        out_specs=[pl.BlockSpec(packed, lambda t: (0, 0, 0))] * 2,
        out_shape=[jax.ShapeDtypeStruct(packed, jnp.bfloat16)] * 2,
        compiler_params=pltpu.CompilerParams(vmem_limit_bytes=VMEM_BYTES),
        cost_estimate=pl.CostEstimate(flops=8 * half * 256 * rows, bytes_accessed=16 * half * 256 * rows, transcendentals=0),
        name="edges",
    )(*operands)


def combine_kernel(own0, a0, b0, own1, a1, b1, out_ref):
    rows, half = own0.shape[:2]
    for r in range(rows):
        out_ref[r, :half] = own0[r] + a0[r].astype(jnp.float32) + b0[r].astype(jnp.float32)
        out_ref[r, half:] = own1[r] + a1[r].astype(jnp.float32) + b1[r].astype(jnp.float32)


def combine(parts0, parts1):
    rows, half, width = parts0[0].shape
    step = 8
    return pl.pallas_call(
        combine_kernel,
        grid=(rows // step,),
        in_specs=[pl.BlockSpec((step, half, width), lambda t: (t, 0, 0))] * 6,
        out_specs=pl.BlockSpec((step, 2 * half, width), lambda t: (t, 0, 0)),
        out_shape=jax.ShapeDtypeStruct((rows, 2 * half, width), jnp.float32),
        compiler_params=pltpu.CompilerParams(vmem_limit_bytes=VMEM_BYTES),
        cost_estimate=pl.CostEstimate(
            flops=4 * rows * half * width, bytes_accessed=24 * rows * half * width, transcendentals=0
        ),
        name="combine",
    )(*parts0, *parts1)


def shifted_by(row, edge, amount, lane):
    count = len(row)
    if amount == 0:
        return row
    if amount > 0:
        row = row[:-1] + [jnp.where(lane >= 128 - amount, edge, row[-1])]
        turned = [pltpu.roll(tile, amount, 1) for tile in row]
        return [jnp.where(lane < amount, turned[t - 1], turned[t]) for t in range(count)]
    row = [jnp.where(lane < -amount, edge, row[0])] + row[1:]
    turned = [pltpu.roll(tile, 128 + amount, 1) for tile in row]
    return [jnp.where(lane >= 128 + amount, turned[(t + 1) % count], turned[t]) for t in range(count)]


def edge_tile(west_ref, east_ref, r):
    per = 128 // 8
    both = west_ref[r // per].astype(jnp.float32) + east_ref[r // per].astype(jnp.float32)
    return pltpu.roll(both, (125 - 8 * (r % per)) % 128, 1)


def rows_kernel(offset_ref, remap0_ref, remap1_ref, west_ref, east_ref, first_ref, last_ref):
    bins, width = remap0_ref.shape[1:]
    lane = lax.broadcasted_iota(jnp.int32, (bins, 128), 1)
    spots = [slice(128 * t, 128 * t + 128) for t in range(width // 128)]
    end = offset_ref.shape[0] - 1
    for r, remap_ref, out_ref in ((0, remap0_ref, first_ref), (end, remap1_ref, last_ref)):
        for amount in range(-REACH, REACH + 1):

            @pl.when(offset_ref[r] == amount)
            def _(r=r, remap_ref=remap_ref, out_ref=out_ref, amount=amount):
                row = [remap_ref[0, :, at] for at in spots]
                row = shifted_by(row, edge_tile(west_ref, east_ref, r), amount, lane)
                for at, tile in zip(spots, row):
                    out_ref[0, :, at] = tile.astype(out_ref.dtype)


def outer_rows(offset, remapped, west, east):
    rows, bins, width = remapped.shape
    row = lambda at: pl.BlockSpec((1, bins, width), lambda t: (at, 0, 0))
    whole = pl.BlockSpec(west.shape, lambda t: (0, 0, 0))
    return pl.pallas_call(
        rows_kernel,
        grid=(1,),
        in_specs=[in_smem(), row(0), row(rows - 1), whole, whole],
        out_specs=[row(0), row(0)],
        out_shape=[jax.ShapeDtypeStruct((1, bins, width), jnp.bfloat16)] * 2,
        compiler_params=pltpu.CompilerParams(vmem_limit_bytes=VMEM_BYTES),
        cost_estimate=pl.CostEstimate(flops=20 * bins * width, bytes_accessed=12 * bins * width, transcendentals=0),
        name="outer_rows",
    )(offset, remapped, remapped, west, east)


def final_kernel(offset_ref, remap_ref, west_ref, east_ref, kappa_ref, local_ref, out_ref, edge_ref, shifted_ref):
    rows, bins, width = remap_ref.shape
    lane = lax.broadcasted_iota(jnp.int32, (bins, 128), 1)
    spots = [slice(128 * t, 128 * t + 128) for t in range(width // 128)]
    for r in range(rows):
        edge_ref[r] = edge_tile(west_ref, east_ref, r)
    shifted_ref[0] = jnp.zeros((bins, width), jnp.float32)
    shifted_ref[rows + 1] = jnp.zeros((bins, width), jnp.float32)

    def one(r, carry):
        offset = offset_ref[r]
        for amount in range(-REACH, REACH + 1):

            @pl.when(offset == amount)
            def _(amount=amount):
                row = [remap_ref[r, :, at] for at in spots]
                edge = edge_ref[r]
                center = shifted_by(row, edge, amount, lane)
                east = shifted_by(row, edge, amount - 1, lane)
                west = shifted_by(row, edge, amount + 1, lane)
                values = []
                for t, at in enumerate(spots):
                    around = kappa_ref[r, :, at] * (east[t] + west[t] - 4.0 * center[t])
                    values.append(local_ref[r, :, at] + center[t] + around)
                for t, at in enumerate(spots):
                    shifted_ref[r + 1, :, at] = center[t]
                    out_ref[r, :, at] = values[t]

        return carry

    lax.fori_loop(0, rows, one, 0)

    def beside(r):
        return [(out_ref, r, out_ref[r] + kappa_ref[r] * (shifted_ref[r] + shifted_ref[r + 2]))]

    for_rows(rows, beside)


def final(offset, remapped, west, east, kappa, local):
    rows, bins, width = remapped.shape
    tile = bins // 2
    block = pl.BlockSpec((rows, tile, width), lambda t: (0, t, 0))
    packed = pl.BlockSpec((west.shape[0], tile, 128), lambda t: (0, t, 0))
    return pl.pallas_call(
        final_kernel,
        grid=(bins // tile,),
        in_specs=[in_smem(), block, packed, packed, pl.BlockSpec(kappa.shape, lambda t: (0, 0, 0)), block],
        out_specs=block,
        out_shape=jax.ShapeDtypeStruct(local.shape, jnp.float32),
        scratch_shapes=[
            pltpu.VMEM((rows, tile, 128), jnp.float32),
            pltpu.VMEM((rows + 2, tile, width), jnp.float32),
        ],
        compiler_params=pltpu.CompilerParams(vmem_limit_bytes=TABLE_BYTES),
        cost_estimate=pl.CostEstimate(flops=30 * remapped.size, bytes_accessed=12 * remapped.size, transcendentals=0),
        name="final",
    )(offset, remapped, west, east, kappa, local)


def halo_kernel(before_ref, after_ref, kappa_ref, in_ref, out_ref):
    side = pl.program_id(0)
    value = jnp.where(side == 0, before_ref[0].astype(jnp.float32), after_ref[0].astype(jnp.float32))
    out_ref[0] = in_ref[0] + kappa_ref[0] * value


def add_halo(before, after, kappa, partial):
    rows, bins, width = partial.shape
    whole = pl.BlockSpec((1, bins, width), lambda i: (0, 0, 0))
    row = pl.BlockSpec((1, bins, width), lambda i: (i * (rows - 1), 0, 0))
    return pl.pallas_call(
        halo_kernel,
        grid=(2,),
        in_specs=[whole, whole, pl.BlockSpec((1, 1, width), lambda i: (i * (rows - 1), 0, 0)), row],
        out_specs=row,
        out_shape=jax.ShapeDtypeStruct(partial.shape, jnp.float32),
        input_output_aliases={3: 0},
        compiler_params=pltpu.CompilerParams(vmem_limit_bytes=VMEM_BYTES),
        cost_estimate=pl.CostEstimate(flops=4 * bins * width, bytes_accessed=20 * bins * width, transcendentals=0),
        name="add_halo",
    )(before, after, kappa, partial)


def body(
    conc,
    dep_owner,
    dep_row,
    dep_weight,
    dep_count,
    zonal_offset,
    agg_rates,
    toeplitz,
    settle,
    kappa,
):
    rows, bins, width = conc.shape
    entries = dep_owner.shape[2]
    odd = (lax.axis_index("lon") % 2).astype(jnp.int32).reshape(1)
    half = bins // 2
    low, high = messages(conc, dep_owner[0].T, dep_row[0].T, dep_weight[0].T, dep_count)

    ahead = permute_lon(low, -2)
    behind = permute_lon(low, 2)
    south = permute_lat(high, 1)
    north = permute_lat(high, -1)
    beside = swap_lon(conc)
    local = local_terms(conc, agg_rates, toeplitz, settle)
    odd, local = lax.optimization_barrier((odd, local))

    down, own0, up = row_sums(
        odd,
        [south, low, north],
        lat_slots,
        [(conc, 0), (beside, 0), (ahead, 0), (behind, 0), (swap_lon(ahead), 0), (swap_lon(behind), 0)],
        rows,
        half,
        entries,
    )
    parts0 = [own0, permute_lat(up, 1), permute_lat(down, -1)]

    to_west, own1, to_east = row_sums(
        odd,
        [behind, high, ahead],
        lon_slots,
        [(south, 0), (conc, half), (north, 0), (swap_lon(south), 0), (beside, half), (swap_lon(north), 0)],
        rows,
        half,
        entries,
    )
    parts1 = [own1, permute_lon(to_east, 2), permute_lon(to_west, -2)]

    first, last = edges(parts0, parts1)
    east, west = permute_lon(first, -1), permute_lon(last, 1)
    remapped = combine(parts0, parts1)
    top_row, end_row = outer_rows(zonal_offset, remapped, west, east)
    before, after = permute_lat(end_row, 1), permute_lat(top_row, -1)
    kappa = kappa[:, None, :]
    partial = final(zonal_offset, remapped, west, east, kappa, local)
    return add_halo(before, after, kappa, partial)


def solution(mesh):
    return jax.shard_map(
        body,
        mesh=mesh,
        in_specs=(
            P("lat", None, "lon"),
            P("lon", "lat", None),
            P("lon", "lat", None),
            P("lon", "lat", None),
            P("lon", "lat"),
            P("lat"),
            P(None, "lat", "lon"),
            P(),
            P(),
            P("lat", "lon"),
        ),
        out_specs=P("lat", None, "lon"),
        check_vma=False,
    )
```

```python
import functools

import jax
import jax.numpy as jnp
from jax import lax
from jax.experimental import pallas as pl
from jax.experimental.pallas import tpu as pltpu
from jax.sharding import PartitionSpec as P

REACH = 2
NEAR_LON = 5
TILE = 16
UNROLL = 4
VMEM_BYTES = 12 * 1024 * 1024
MOST_BYTES = 60 * 1024 * 1024
TABLE_BYTES = 20 * 1024 * 1024
QUICK = 2
FIELDS = ((0, 0), (0, 128), (8, 0), (8, 128), (16, 0))


def permute_lon(value, steps):
    count = lax.axis_size("lon")
    return lax.ppermute(value, "lon", [(i, (i + steps) % count) for i in range(count)])


def swap_lon(value):
    count = lax.axis_size("lon")
    return lax.ppermute(value, "lon", [(i, i ^ 1) for i in range(count)])


def permute_lat(value, steps):
    count = lax.axis_size("lat")
    pairs = [(i, i + steps) for i in range(count) if 0 <= i + steps < count]
    return lax.ppermute(value, "lat", pairs)


def in_smem():
    return pl.BlockSpec(memory_space=pltpu.SMEM)


def in_place():
    return pl.BlockSpec(memory_space=pl.ANY)


def for_rows(count, one):
    def some(g, carry):
        stores = []
        for u in range(UNROLL):
            stores += one(g * UNROLL + u)
        for ref, at, value in stores:
            ref[at] = value.astype(ref.dtype)
        return carry

    lax.fori_loop(0, count // UNROLL, some, 0)


def growth_kernel(flip_ref, settle_ref, conc_ref, rates_ref, out_ref, mat_ref):
    ranks, rows_step = rates_ref.shape[0], conc_ref.shape[0]
    bins, width = conc_ref.shape[1:]

    @pl.when(pl.program_id(0) == 0)
    def _():
        for q in range(ranks):
            spread = jnp.broadcast_to(flip_ref[q : q + 1, :], (bins, 2 * bins))
            turned = pltpu.roll(spread, bins + 1, 1, stride=1, stride_axis=0)
            mat_ref[q * bins : (q + 1) * bins, :] = turned[:, :bins].astype(jnp.bfloat16)

    settle = jnp.broadcast_to(settle_ref[...], (bins, width))
    for r in range(rows_step):
        cells = conc_ref[r]
        product = jnp.dot(mat_ref[...], cells, preferred_element_type=jnp.float32)
        total = -settle * cells.astype(jnp.float32)
        for q in range(ranks):
            total = total + rates_ref[q, r : r + 1, :] * product[q * bins : (q + 1) * bins]
        out_ref[r] = total


def local_terms(conc, agg_rates, toeplitz, settle):
    rows, bins, width = conc.shape
    ranks = agg_rates.shape[0]
    step = 8
    flipped = jnp.pad(toeplitz[:, ::-1].astype(jnp.float32), ((0, 0), (0, 1)))
    return pl.pallas_call(
        growth_kernel,
        grid=(rows // step,),
        in_specs=[
            pl.BlockSpec((ranks, 2 * bins), lambda i: (0, 0)),
            pl.BlockSpec((bins, 1), lambda i: (0, 0)),
            pl.BlockSpec((step, bins, width), lambda i: (i, 0, 0)),
            pl.BlockSpec((ranks, step, width), lambda i: (0, i, 0)),
        ],
        out_specs=pl.BlockSpec((step, bins, width), lambda i: (i, 0, 0)),
        out_shape=jax.ShapeDtypeStruct(conc.shape, jnp.float32),
        scratch_shapes=[pltpu.VMEM((ranks * bins, bins), jnp.bfloat16)],
        compiler_params=pltpu.CompilerParams(vmem_limit_bytes=VMEM_BYTES),
        cost_estimate=pl.CostEstimate(
            flops=2 * ranks * bins * bins * rows * width, bytes_accessed=8 * conc.size, transcendentals=0
        ),
        name="growth",
    )(flipped, settle[:, None], conc, agg_rates)


def message_kernel(
    conc_ref, owner_hbm, source_hbm, weight_hbm, count_hbm, low_ref, high_ref,
    owner_ref, source_ref, weight_ref, count_ref, meta_ref, sems,
):
    rows, bins, _ = conc_ref.shape
    half = bins // 2
    entries = owner_ref.shape[0]
    small = [
        pltpu.make_async_copy(hbm, ref, sems.at[4 + i])
        for i, (hbm, ref) in enumerate(
            ((owner_hbm, owner_ref), (source_hbm, source_ref), (weight_hbm, weight_ref), (count_hbm, count_ref))
        )
    ]
    copies = [
        pltpu.make_async_copy(conc_ref.at[:, pl.ds(0, half), :], low_ref.at[pl.ds(0, rows)], sems.at[0]),
        pltpu.make_async_copy(conc_ref.at[:, pl.ds(half, half), :], high_ref.at[pl.ds(0, rows)], sems.at[1]),
    ]
    for copy in small + copies:
        copy.start()
    for copy in small:
        copy.wait()
    meta_ref[...] = jnp.zeros(meta_ref.shape, meta_ref.dtype)
    wide = lambda value: value.astype(jnp.float32)
    entry = lax.broadcasted_iota(jnp.int32, owner_ref.shape, 0)
    live = jnp.where(entry < count_ref[...], weight_ref[...], 0.0)
    top = live.astype(jnp.bfloat16)
    middle = (live - wide(top)).astype(jnp.bfloat16)
    bottom = (live - wide(top) - wide(middle)).astype(jnp.bfloat16)
    fields = (wide(owner_ref[...]), wide(source_ref[...]), wide(top), wide(middle), wide(bottom))
    for field, (at, lane) in zip(fields, FIELDS):
        meta_ref[0, at : at + entries, lane : lane + rows] = field.astype(jnp.bfloat16)
    more = [
        pltpu.make_async_copy(meta_ref, low_ref.at[pl.ds(rows, 1)], sems.at[2]),
        pltpu.make_async_copy(meta_ref, high_ref.at[pl.ds(rows, 1)], sems.at[3]),
    ]
    for copy in more:
        copy.start()
    for copy in copies + more:
        copy.wait()


def messages(conc, owner, source, weight, count):
    rows, bins, width = conc.shape
    half = bins // 2
    return pl.pallas_call(
        message_kernel,
        in_specs=[in_place()] * 5,
        out_specs=[in_place(), in_place()],
        out_shape=[jax.ShapeDtypeStruct((rows + 1, half, width), conc.dtype)] * 2,
        scratch_shapes=[pltpu.VMEM(small.shape, small.dtype) for small in (owner, source, weight, count)]
        + [pltpu.VMEM((1, half, width), jnp.bfloat16), pltpu.SemaphoreType.DMA((8,))],
        compiler_params=pltpu.CompilerParams(vmem_limit_bytes=MOST_BYTES),
        cost_estimate=pl.CostEstimate(flops=0, bytes_accessed=4 * conc.size, transcendentals=0),
        name="messages",
    )(conc, owner, source, weight, count)


def lat_slots(rows, group, lat_step, lon_step, odd):
    toward = 1.0 - 2.0 * odd
    slot = jnp.where(
        lon_step == 0.0,
        0.0,
        jnp.where(lon_step == 2.0, 2.0, jnp.where(lon_step == -2.0, 3.0, jnp.where(lon_step == toward, 1.0, 5.0 - odd))),
    )
    return lat_step == 1.0 - group, slot * rows


def lon_slots(rows, group, lat_step, lon_step, odd):
    toward = 1.0 - 2.0 * odd
    lon_from = 2.0 * (group - 1.0) + lon_step
    slot = jnp.where(lon_from == 0.0, 0.0, 3.0) + lat_step + 1.0
    return (lon_from == 0.0) | (lon_from == toward), slot * rows


def row_sums_kernel(bases, slots, entries, *refs):
    tables = len(bases)
    odd_ref = refs[0]
    asked = refs[1:4]
    sources = refs[4 : 4 + tables]
    outs = refs[4 + tables : 7 + tables]
    table, meta_ref, index_vec, weight_vec, index_ref, weight_ref, sems = refs[7 + tables :]
    every, half, width = table.shape
    rows = every // tables
    metas = [
        pltpu.make_async_copy(asked[g].at[pl.ds(rows, 1)], meta_ref.at[pl.ds(g, 1)], sems.at[tables + g])
        for g in range(3)
    ]
    copies = [
        pltpu.make_async_copy(
            sources[i].at[pl.ds(0, rows), pl.ds(bases[i], half), :], table.at[pl.ds(i * rows, rows)], sems.at[i]
        )
        for i in range(tables)
    ]
    for copy in metas + copies:
        copy.start()
    for copy in metas:
        copy.wait()

    odd = odd_ref[0].astype(jnp.float32)
    for g in range(3):
        owner, source, top, middle, bottom = [
            meta_ref[g, at : at + entries, lane : lane + 128].astype(jnp.float32) for at, lane in FIELDS
        ]
        weight = top + middle + bottom
        band = jnp.where(owner >= NEAR_LON, 1.0, 0.0) + jnp.where(owner >= 2 * NEAR_LON, 1.0, 0.0)
        here, base = slots(rows, float(g), band - 1.0, owner - NEAR_LON * band - REACH, odd)
        here = jnp.where(here & (weight != 0.0), 1.0, 0.0)
        index = base + source
        packed = [[jnp.zeros((1, 128), jnp.float32)] * 2 for _ in range(entries)]
        rank = jnp.zeros((1, 128), jnp.float32)
        for k in range(entries):
            taken = here[k : k + 1]
            for place in range(k + 1):
                spot = (taken > 0.0) & (rank == place)
                packed[place] = [
                    jnp.where(spot, index[k : k + 1], packed[place][0]),
                    jnp.where(spot, weight[k : k + 1], packed[place][1]),
                ]
            rank = rank + taken
        for place in range(entries):
            at = g * entries + place
            index_vec[at : at + 1, :] = packed[place][0].astype(jnp.int32)
            weight_vec[at : at + 1, :] = packed[place][1]
        at = 3 * entries + g
        index_vec[at : at + 1, :] = rank.astype(jnp.int32)
    to_scalar = [
        pltpu.make_async_copy(index_vec, index_ref, sems.at[tables + 3]),
        pltpu.make_async_copy(weight_vec, weight_ref, sems.at[tables + 4]),
    ]
    for copy in to_scalar:
        copy.start()
    for copy in to_scalar + copies:
        copy.wait()

    for group, out in enumerate(outs):

        def some(g, carry, group=group, out=out):
            def sums(terms):
                totals = []
                for u in range(UNROLL):
                    r = g * UNROLL + u
                    total = jnp.zeros((half, width), jnp.float32)
                    for k in range(terms):
                        row = group * entries + k
                        total = total + weight_ref[row, r] * table[index_ref[row, r]].astype(jnp.float32)
                    totals.append(total)
                for u in range(UNROLL):
                    out[g * UNROLL + u] = totals[u].astype(out.dtype)

            most = index_ref[3 * entries + group, g * UNROLL]
            for u in range(1, UNROLL):
                most = jnp.maximum(most, index_ref[3 * entries + group, g * UNROLL + u])
            sums(min(QUICK, entries))

            @pl.when(most > QUICK)
            def _():
                sums(entries)

            return carry

        lax.fori_loop(0, rows // UNROLL, some, 0)


def row_sums(odd, asked, slots, sources, rows, half, entries):
    tables = len(sources)
    width = sources[0][0].shape[2]
    vectors = -(-3 * (entries + 1) // 8) * 8
    return pl.pallas_call(
        functools.partial(row_sums_kernel, tuple(base for _, base in sources), slots, entries),
        in_specs=[in_smem()] + [in_place()] * (3 + tables),
        out_specs=[pl.BlockSpec(memory_space=pltpu.VMEM)] * 3,
        out_shape=[
            jax.ShapeDtypeStruct((rows, half, width), dtype) for dtype in (jnp.bfloat16, jnp.float32, jnp.bfloat16)
        ],
        scratch_shapes=[
            pltpu.VMEM((tables * rows, half, width), jnp.bfloat16),
            pltpu.VMEM((3, half, width), jnp.bfloat16),
            pltpu.VMEM((vectors, 128), jnp.int32),
            pltpu.VMEM((vectors, 128), jnp.float32),
            pltpu.SMEM((vectors, 128), jnp.int32),
            pltpu.SMEM((vectors, 128), jnp.float32),
            pltpu.SemaphoreType.DMA((tables + 5,)),
        ],
        compiler_params=pltpu.CompilerParams(vmem_limit_bytes=TABLE_BYTES),
        cost_estimate=pl.CostEstimate(
            flops=6 * rows * entries * half * width,
            bytes_accessed=2 * (tables + 3) * rows * half * width,
            transcendentals=0,
        ),
        name="row_sums",
    )(odd, *asked, *[source for source, _ in sources])


def edges_kernel(*refs):
    first_ref, last_ref = refs[-2:]
    halves = (len(refs) - 2) // 6
    rows = refs[0].shape[0]
    half = refs[0].shape[1]
    per = 128 // 8
    lane = lax.broadcasted_iota(jnp.int32, (half, 128), 1)
    for side, out_ref in ((0, first_ref), (1, last_ref)):
        for h in range(halves):
            parts = refs[6 * h + 3 * side : 6 * h + 3 * side + 3]
            for j in range(rows // per):
                packed = jnp.zeros((half, 128), jnp.float32)
                for i in range(per):
                    r = j * per + i
                    cells = parts[0][r] + parts[1][r].astype(jnp.float32) + parts[2][r].astype(jnp.float32)
                    at = 8 * i + 3 * (1 - side)
                    spot = (lane >= at) & (lane < at + 3)
                    packed = jnp.where(spot, pltpu.roll(cells, 8 * i + 3, 1), packed)
                out_ref[j, h * half : (h + 1) * half] = packed.astype(out_ref.dtype)


def edges(parts0, parts1):
    rows, half, width = parts0[0].shape
    specs, operands = [], []
    for parts in (parts0, parts1):
        for at in (0, width // 128 - 1):
            specs += [pl.BlockSpec((rows, half, 128), lambda t, at=at: (0, 0, at))] * 3
            operands += parts
    packed = (rows // 16, 2 * half, 128)
    return pl.pallas_call(
        edges_kernel,
        grid=(1,),
        in_specs=specs,
        out_specs=[pl.BlockSpec(packed, lambda t: (0, 0, 0))] * 2,
        out_shape=[jax.ShapeDtypeStruct(packed, jnp.bfloat16)] * 2,
        compiler_params=pltpu.CompilerParams(vmem_limit_bytes=VMEM_BYTES),
        cost_estimate=pl.CostEstimate(flops=8 * half * 256 * rows, bytes_accessed=16 * half * 256 * rows, transcendentals=0),
        name="edges",
    )(*operands)


def combine_kernel(own0, a0, b0, own1, a1, b1, out_ref):
    rows, half = own0.shape[:2]
    for r in range(rows):
        out_ref[r, :half] = own0[r] + a0[r].astype(jnp.float32) + b0[r].astype(jnp.float32)
        out_ref[r, half:] = own1[r] + a1[r].astype(jnp.float32) + b1[r].astype(jnp.float32)


def combine(parts0, parts1):
    rows, half, width = parts0[0].shape
    step = 8
    return pl.pallas_call(
        combine_kernel,
        grid=(rows // step,),
        in_specs=[pl.BlockSpec((step, half, width), lambda t: (t, 0, 0))] * 6,
        out_specs=pl.BlockSpec((step, 2 * half, width), lambda t: (t, 0, 0)),
        out_shape=jax.ShapeDtypeStruct((rows, 2 * half, width), jnp.float32),
        compiler_params=pltpu.CompilerParams(vmem_limit_bytes=VMEM_BYTES),
        cost_estimate=pl.CostEstimate(
            flops=4 * rows * half * width, bytes_accessed=24 * rows * half * width, transcendentals=0
        ),
        name="combine",
    )(*parts0, *parts1)


def shifted_by(row, edge, amount, lane):
    count = len(row)
    if amount == 0:
        return row
    if amount > 0:
        row = row[:-1] + [jnp.where(lane >= 128 - amount, edge, row[-1])]
        turned = [pltpu.roll(tile, amount, 1) for tile in row]
        return [jnp.where(lane < amount, turned[t - 1], turned[t]) for t in range(count)]
    row = [jnp.where(lane < -amount, edge, row[0])] + row[1:]
    turned = [pltpu.roll(tile, 128 + amount, 1) for tile in row]
    return [jnp.where(lane >= 128 + amount, turned[(t + 1) % count], turned[t]) for t in range(count)]


def edge_tile(west_ref, east_ref, r):
    per = 128 // 8
    both = west_ref[r // per].astype(jnp.float32) + east_ref[r // per].astype(jnp.float32)
    return pltpu.roll(both, (125 - 8 * (r % per)) % 128, 1)


def rows_kernel(offset_ref, remap0_ref, remap1_ref, west_ref, east_ref, first_ref, last_ref):
    bins, width = remap0_ref.shape[1:]
    lane = lax.broadcasted_iota(jnp.int32, (bins, 128), 1)
    spots = [slice(128 * t, 128 * t + 128) for t in range(width // 128)]
    end = offset_ref.shape[0] - 1
    for r, remap_ref, out_ref in ((0, remap0_ref, first_ref), (end, remap1_ref, last_ref)):
        for amount in range(-REACH, REACH + 1):

            @pl.when(offset_ref[r] == amount)
            def _(r=r, remap_ref=remap_ref, out_ref=out_ref, amount=amount):
                row = [remap_ref[0, :, at] for at in spots]
                row = shifted_by(row, edge_tile(west_ref, east_ref, r), amount, lane)
                for at, tile in zip(spots, row):
                    out_ref[0, :, at] = tile.astype(out_ref.dtype)


def outer_rows(offset, remapped, west, east):
    rows, bins, width = remapped.shape
    row = lambda at: pl.BlockSpec((1, bins, width), lambda t: (at, 0, 0))
    whole = pl.BlockSpec(west.shape, lambda t: (0, 0, 0))
    return pl.pallas_call(
        rows_kernel,
        grid=(1,),
        in_specs=[in_smem(), row(0), row(rows - 1), whole, whole],
        out_specs=[row(0), row(0)],
        out_shape=[jax.ShapeDtypeStruct((1, bins, width), jnp.bfloat16)] * 2,
        compiler_params=pltpu.CompilerParams(vmem_limit_bytes=VMEM_BYTES),
        cost_estimate=pl.CostEstimate(flops=20 * bins * width, bytes_accessed=12 * bins * width, transcendentals=0),
        name="outer_rows",
    )(offset, remapped, remapped, west, east)


def final_kernel(offset_ref, remap_ref, west_ref, east_ref, kappa_ref, local_ref, out_ref, edge_ref):
    rows, bins, width = remap_ref.shape
    count = width // 128
    lane = lax.broadcasted_iota(jnp.int32, (8, 128), 1)
    spots = [slice(128 * t, 128 * t + 128) for t in range(count)]
    for r in range(rows):
        edge_ref[r] = edge_tile(west_ref, east_ref, r)

    def moved(row, edge, amount):
        row = [jnp.where(lane < -amount, edge, row[0])] + row[1:]
        row = row[:-1] + [jnp.where(lane >= 128 - amount, edge, row[-1])]
        turned = [pltpu.roll(tile, (amount + 128) & 127, 1) for tile in row]
        before, after = lane < amount, lane >= 128 + amount
        return [
            jnp.where(before, turned[t - 1], jnp.where(after, turned[(t + 1) % count], turned[t])) for t in range(count)
        ]

    for b in range(bins // 8):
        at = slice(8 * b, 8 * b + 8)
        blank = [jnp.zeros((8, 128), jnp.float32)] * count
        before, now, base = blank, blank, None
        stores = []
        for r in range(rows):
            amount = offset_ref[r]
            row = [remap_ref[r, at, spot] for spot in spots]
            edge = edge_ref[r, at]
            center = moved(row, edge, amount)
            east = moved(row, edge, amount - 1)
            west = moved(row, edge, amount + 1)
            fresh = []
            for t, spot in enumerate(spots):
                kappa = kappa_ref[r, :, spot]
                fresh.append(local_ref[r, at, spot] + center[t] + kappa * (east[t] + west[t] - 4.0 * center[t]))
                if r:
                    stores.append((r - 1, spot, base[t] + kappa_ref[r - 1, :, spot] * (before[t] + center[t])))
            before, now, base = now, center, fresh
            if r % 4 == 3:
                for which, spot, value in stores:
                    out_ref[which, at, spot] = value
                stores = []
        for t, spot in enumerate(spots):
            out_ref[rows - 1, at, spot] = base[t] + kappa_ref[rows - 1, :, spot] * before[t]


def final(offset, remapped, west, east, kappa, local):
    rows, bins, width = remapped.shape
    block = pl.BlockSpec((rows, TILE, width), lambda t: (0, t, 0))
    packed = pl.BlockSpec((west.shape[0], TILE, 128), lambda t: (0, t, 0))
    return pl.pallas_call(
        final_kernel,
        grid=(bins // TILE,),
        in_specs=[in_smem(), block, packed, packed, pl.BlockSpec(kappa.shape, lambda t: (0, 0, 0)), block],
        out_specs=block,
        out_shape=jax.ShapeDtypeStruct(local.shape, jnp.float32),
        scratch_shapes=[pltpu.VMEM((rows, TILE, 128), jnp.float32)],
        compiler_params=pltpu.CompilerParams(vmem_limit_bytes=VMEM_BYTES),
        cost_estimate=pl.CostEstimate(flops=30 * remapped.size, bytes_accessed=12 * remapped.size, transcendentals=0),
        name="final",
    )(offset, remapped, west, east, kappa, local)


def halo_kernel(before_ref, after_ref, kappa_ref, in_ref, out_ref):
    side = pl.program_id(0)
    value = jnp.where(side == 0, before_ref[0].astype(jnp.float32), after_ref[0].astype(jnp.float32))
    out_ref[0] = in_ref[0] + kappa_ref[0] * value


def add_halo(before, after, kappa, partial):
    rows, bins, width = partial.shape
    whole = pl.BlockSpec((1, bins, width), lambda i: (0, 0, 0))
    row = pl.BlockSpec((1, bins, width), lambda i: (i * (rows - 1), 0, 0))
    return pl.pallas_call(
        halo_kernel,
        grid=(2,),
        in_specs=[whole, whole, pl.BlockSpec((1, 1, width), lambda i: (i * (rows - 1), 0, 0)), row],
        out_specs=row,
        out_shape=jax.ShapeDtypeStruct(partial.shape, jnp.float32),
        input_output_aliases={3: 0},
        compiler_params=pltpu.CompilerParams(vmem_limit_bytes=VMEM_BYTES),
        cost_estimate=pl.CostEstimate(flops=4 * bins * width, bytes_accessed=20 * bins * width, transcendentals=0),
        name="add_halo",
    )(before, after, kappa, partial)


def body(
    conc,
    dep_owner,
    dep_row,
    dep_weight,
    dep_count,
    zonal_offset,
    agg_rates,
    toeplitz,
    settle,
    kappa,
):
    rows, bins, width = conc.shape
    entries = dep_owner.shape[2]
    odd = (lax.axis_index("lon") % 2).astype(jnp.int32).reshape(1)
    half = bins // 2
    low, high = messages(conc, dep_owner[0].T, dep_row[0].T, dep_weight[0].T, dep_count)

    ahead = permute_lon(low, -2)
    behind = permute_lon(low, 2)
    south = permute_lat(high, 1)
    north = permute_lat(high, -1)
    beside = swap_lon(conc)
    local = local_terms(conc, agg_rates, toeplitz, settle)
    south, north, local = lax.optimization_barrier((south, north, local))

    down, own0, up = row_sums(
        odd,
        [south, low, north],
        lat_slots,
        [(conc, 0), (beside, 0), (ahead, 0), (behind, 0), (swap_lon(ahead), 0), (swap_lon(behind), 0)],
        rows,
        half,
        entries,
    )
    parts0 = [own0, permute_lat(up, 1), permute_lat(down, -1)]

    to_west, own1, to_east = row_sums(
        odd,
        [behind, high, ahead],
        lon_slots,
        [(south, 0), (conc, half), (north, 0), (swap_lon(south), 0), (beside, half), (swap_lon(north), 0)],
        rows,
        half,
        entries,
    )
    parts1 = [own1, permute_lon(to_east, 2), permute_lon(to_west, -2)]

    first, last = edges(parts0, parts1)
    east, west = permute_lon(first, -1), permute_lon(last, 1)
    remapped = combine(parts0, parts1)
    top_row, end_row = outer_rows(zonal_offset, remapped, west, east)
    before, after = permute_lat(end_row, 1), permute_lat(top_row, -1)
    kappa = kappa[:, None, :]
    partial = final(zonal_offset, remapped, west, east, kappa, local)
    return add_halo(before, after, kappa, partial)


def solution(mesh):
    return jax.shard_map(
        body,
        mesh=mesh,
        in_specs=(
            P("lat", None, "lon"),
            P("lon", "lat", None),
            P("lon", "lat", None),
            P("lon", "lat", None),
            P("lon", "lat"),
            P("lat"),
            P(None, "lat", "lon"),
            P(),
            P(),
            P("lat", "lon"),
        ),
        out_specs=P("lat", None, "lon"),
        check_vma=False,
    )
```

```python
import functools

import jax
import jax.numpy as jnp
from jax import lax
from jax.experimental import pallas as pl
from jax.experimental.pallas import tpu as pltpu
from jax.sharding import PartitionSpec as P

REACH = 2
NEAR_LON = 5
TILE = 16
UNROLL = 4
VMEM_BYTES = 12 * 1024 * 1024
MOST_BYTES = 60 * 1024 * 1024
TABLE_BYTES = 20 * 1024 * 1024
QUICK = 2
FIELDS = ((0, 0), (0, 128), (8, 0), (8, 128), (16, 0))


def permute_lon(value, steps):
    count = lax.axis_size("lon")
    return lax.ppermute(value, "lon", [(i, (i + steps) % count) for i in range(count)])


def swap_lon(value):
    count = lax.axis_size("lon")
    return lax.ppermute(value, "lon", [(i, i ^ 1) for i in range(count)])


def permute_lat(value, steps):
    count = lax.axis_size("lat")
    pairs = [(i, i + steps) for i in range(count) if 0 <= i + steps < count]
    return lax.ppermute(value, "lat", pairs)


def in_smem():
    return pl.BlockSpec(memory_space=pltpu.SMEM)


def in_place():
    return pl.BlockSpec(memory_space=pl.ANY)


def for_rows(count, one):
    def some(g, carry):
        stores = []
        for u in range(UNROLL):
            stores += one(g * UNROLL + u)
        for ref, at, value in stores:
            ref[at] = value.astype(ref.dtype)
        return carry

    lax.fori_loop(0, count // UNROLL, some, 0)


def growth_kernel(flip_ref, settle_ref, conc_ref, rates_ref, out_ref, mat_ref):
    ranks, rows_step = rates_ref.shape[0], conc_ref.shape[0]
    bins, width = conc_ref.shape[1:]

    @pl.when(pl.program_id(0) == 0)
    def _():
        for q in range(ranks):
            spread = jnp.broadcast_to(flip_ref[q : q + 1, :], (bins, 2 * bins))
            turned = pltpu.roll(spread, bins + 1, 1, stride=1, stride_axis=0)
            mat_ref[q * bins : (q + 1) * bins, :] = turned[:, :bins].astype(jnp.bfloat16)

    settle = jnp.broadcast_to(settle_ref[...], (bins, width))
    for r in range(rows_step):
        cells = conc_ref[r]
        product = jnp.dot(mat_ref[...], cells, preferred_element_type=jnp.float32)
        total = -settle * cells.astype(jnp.float32)
        for q in range(ranks):
            total = total + rates_ref[q, r : r + 1, :] * product[q * bins : (q + 1) * bins]
        out_ref[r] = total


def local_terms(conc, agg_rates, toeplitz, settle):
    rows, bins, width = conc.shape
    ranks = agg_rates.shape[0]
    step = 8
    flipped = jnp.pad(toeplitz[:, ::-1].astype(jnp.float32), ((0, 0), (0, 1)))
    return pl.pallas_call(
        growth_kernel,
        grid=(rows // step,),
        in_specs=[
            pl.BlockSpec((ranks, 2 * bins), lambda i: (0, 0)),
            pl.BlockSpec((bins, 1), lambda i: (0, 0)),
            pl.BlockSpec((step, bins, width), lambda i: (i, 0, 0)),
            pl.BlockSpec((ranks, step, width), lambda i: (0, i, 0)),
        ],
        out_specs=pl.BlockSpec((step, bins, width), lambda i: (i, 0, 0)),
        out_shape=jax.ShapeDtypeStruct(conc.shape, jnp.float32),
        scratch_shapes=[pltpu.VMEM((ranks * bins, bins), jnp.bfloat16)],
        compiler_params=pltpu.CompilerParams(vmem_limit_bytes=VMEM_BYTES),
        cost_estimate=pl.CostEstimate(
            flops=2 * ranks * bins * bins * rows * width, bytes_accessed=8 * conc.size, transcendentals=0
        ),
        name="growth",
    )(flipped, settle[:, None], conc, agg_rates)


def low_kernel(
    conc_ref, owner_hbm, source_hbm, weight_hbm, count_hbm, low_ref, meta_ref,
    owner_ref, source_ref, weight_ref, count_ref, sems,
):
    rows = conc_ref.shape[0]
    half = low_ref.shape[1]
    entries = owner_ref.shape[0]
    small = [
        pltpu.make_async_copy(hbm, ref, sems.at[1 + i])
        for i, (hbm, ref) in enumerate(
            ((owner_hbm, owner_ref), (source_hbm, source_ref), (weight_hbm, weight_ref), (count_hbm, count_ref))
        )
    ]
    large = pltpu.make_async_copy(conc_ref.at[:, pl.ds(0, half), :], low_ref.at[pl.ds(0, rows)], sems.at[0])
    for copy in small + [large]:
        copy.start()
    meta_ref[...] = jnp.zeros(meta_ref.shape, meta_ref.dtype)
    for copy in small:
        copy.wait()
    wide = lambda value: value.astype(jnp.float32)
    entry = lax.broadcasted_iota(jnp.int32, owner_ref.shape, 0)
    live = jnp.where(entry < count_ref[...], weight_ref[...], 0.0)
    top = live.astype(jnp.bfloat16)
    middle = (live - wide(top)).astype(jnp.bfloat16)
    bottom = (live - wide(top) - wide(middle)).astype(jnp.bfloat16)
    fields = (wide(owner_ref[...]), wide(source_ref[...]), wide(top), wide(middle), wide(bottom))
    for field, (at, lane) in zip(fields, FIELDS):
        meta_ref[0, at : at + entries, lane : lane + rows] = field.astype(jnp.bfloat16)
    low_ref[rows] = meta_ref[0]
    large.wait()


def low_message(conc, owner, source, weight, count):
    rows, bins, width = conc.shape
    half = bins // 2
    return pl.pallas_call(
        low_kernel,
        in_specs=[in_place()] * 5,
        out_specs=[pl.BlockSpec(memory_space=pltpu.VMEM)] * 2,
        out_shape=[
            jax.ShapeDtypeStruct((rows + 1, half, width), conc.dtype),
            jax.ShapeDtypeStruct((1, half, width), conc.dtype),
        ],
        scratch_shapes=[pltpu.VMEM(small.shape, small.dtype) for small in (owner, source, weight, count)]
        + [pltpu.SemaphoreType.DMA((5,))],
        compiler_params=pltpu.CompilerParams(vmem_limit_bytes=MOST_BYTES),
        cost_estimate=pl.CostEstimate(flops=0, bytes_accessed=2 * conc.size, transcendentals=0),
        name="low_message",
    )(conc, owner, source, weight, count)


def high_kernel(conc_ref, meta_ref, _, high_ref, sem):
    rows = conc_ref.shape[0]
    half = high_ref.shape[1]
    copy = pltpu.make_async_copy(conc_ref.at[:, pl.ds(half, half), :], high_ref.at[pl.ds(0, rows)], sem)
    copy.start()
    high_ref[rows] = meta_ref[0]
    copy.wait()


def high_message(conc, meta, earlier):
    rows, bins, width = conc.shape
    half = bins // 2
    vmem = pl.BlockSpec(memory_space=pltpu.VMEM)
    return pl.pallas_call(
        high_kernel,
        in_specs=[in_place(), vmem, in_place()],
        out_specs=vmem,
        out_shape=jax.ShapeDtypeStruct((rows + 1, half, width), conc.dtype),
        scratch_shapes=[pltpu.SemaphoreType.DMA],
        compiler_params=pltpu.CompilerParams(vmem_limit_bytes=VMEM_BYTES),
        cost_estimate=pl.CostEstimate(flops=0, bytes_accessed=2 * conc.size, transcendentals=0),
        name="high_message",
    )(conc, meta, earlier)


def lat_slots(rows, group, lat_step, lon_step, odd):
    toward = 1.0 - 2.0 * odd
    slot = jnp.where(
        lon_step == 0.0,
        0.0,
        jnp.where(lon_step == 2.0, 2.0, jnp.where(lon_step == -2.0, 3.0, jnp.where(lon_step == toward, 1.0, 5.0 - odd))),
    )
    return lat_step == 1.0 - group, slot * rows


def lon_slots(rows, group, lat_step, lon_step, odd):
    toward = 1.0 - 2.0 * odd
    lon_from = 2.0 * (group - 1.0) + lon_step
    slot = jnp.where(lon_from == 0.0, 0.0, 3.0) + lat_step + 1.0
    return (lon_from == 0.0) | (lon_from == toward), slot * rows


def row_sums_kernel(bases, slots, entries, *refs):
    tables = len(bases)
    odd_ref = refs[0]
    asked = refs[1:4]
    sources = refs[4 : 4 + tables]
    outs = refs[4 + tables : 7 + tables]
    table, meta_ref, index_vec, weight_vec, index_ref, weight_ref, sems = refs[7 + tables :]
    every, half, width = table.shape
    rows = every // tables
    metas = [
        pltpu.make_async_copy(
            asked[g].at[pl.ds(asked[g].shape[0] - 1, 1)], meta_ref.at[pl.ds(g, 1)], sems.at[tables + g]
        )
        for g in range(3)
    ]
    copies = [
        pltpu.make_async_copy(
            sources[i].at[pl.ds(0, rows), pl.ds(bases[i], half), :], table.at[pl.ds(i * rows, rows)], sems.at[i]
        )
        for i in range(tables)
    ]
    for copy in metas + copies:
        copy.start()
    for copy in metas:
        copy.wait()

    odd = odd_ref[0].astype(jnp.float32)
    for g in range(3):
        owner, source, top, middle, bottom = [
            meta_ref[g, at : at + entries, lane : lane + 128].astype(jnp.float32) for at, lane in FIELDS
        ]
        weight = top + middle + bottom
        band = jnp.where(owner >= NEAR_LON, 1.0, 0.0) + jnp.where(owner >= 2 * NEAR_LON, 1.0, 0.0)
        here, base = slots(rows, float(g), band - 1.0, owner - NEAR_LON * band - REACH, odd)
        here = jnp.where(here & (weight != 0.0), 1.0, 0.0)
        index = base + source
        packed = [[jnp.zeros((1, 128), jnp.float32)] * 2 for _ in range(entries)]
        rank = jnp.zeros((1, 128), jnp.float32)
        for k in range(entries):
            taken = here[k : k + 1]
            for place in range(k + 1):
                spot = (taken > 0.0) & (rank == place)
                packed[place] = [
                    jnp.where(spot, index[k : k + 1], packed[place][0]),
                    jnp.where(spot, weight[k : k + 1], packed[place][1]),
                ]
            rank = rank + taken
        for place in range(entries):
            at = g * entries + place
            index_vec[at : at + 1, :] = packed[place][0].astype(jnp.int32)
            weight_vec[at : at + 1, :] = packed[place][1]
        at = 3 * entries + g
        index_vec[at : at + 1, :] = rank.astype(jnp.int32)
    to_scalar = [
        pltpu.make_async_copy(index_vec, index_ref, sems.at[tables + 3]),
        pltpu.make_async_copy(weight_vec, weight_ref, sems.at[tables + 4]),
    ]
    for copy in to_scalar:
        copy.start()
    for copy in to_scalar + copies:
        copy.wait()

    for group, out in enumerate(outs):

        def some(g, carry, group=group, out=out):
            def sums(terms):
                totals = []
                for u in range(UNROLL):
                    r = g * UNROLL + u
                    total = jnp.zeros((half, width), jnp.float32)
                    for k in range(terms):
                        row = group * entries + k
                        total = total + weight_ref[row, r] * table[index_ref[row, r]].astype(jnp.float32)
                    totals.append(total)
                for u in range(UNROLL):
                    out[g * UNROLL + u] = totals[u].astype(out.dtype)

            most = index_ref[3 * entries + group, g * UNROLL]
            for u in range(1, UNROLL):
                most = jnp.maximum(most, index_ref[3 * entries + group, g * UNROLL + u])
            sums(min(QUICK, entries))

            @pl.when(most > QUICK)
            def _():
                sums(entries)

            return carry

        lax.fori_loop(0, rows // UNROLL, some, 0)


def row_sums(odd, asked, slots, sources, rows, half, entries):
    tables = len(sources)
    width = sources[0][0].shape[2]
    vectors = -(-3 * (entries + 1) // 8) * 8
    return pl.pallas_call(
        functools.partial(row_sums_kernel, tuple(base for _, base in sources), slots, entries),
        in_specs=[in_smem()] + [in_place()] * (3 + tables),
        out_specs=[pl.BlockSpec(memory_space=pltpu.VMEM)] * 3,
        out_shape=[
            jax.ShapeDtypeStruct((rows, half, width), dtype) for dtype in (jnp.bfloat16, jnp.float32, jnp.bfloat16)
        ],
        scratch_shapes=[
            pltpu.VMEM((tables * rows, half, width), jnp.bfloat16),
            pltpu.VMEM((3, half, width), jnp.bfloat16),
            pltpu.VMEM((vectors, 128), jnp.int32),
            pltpu.VMEM((vectors, 128), jnp.float32),
            pltpu.SMEM((vectors, 128), jnp.int32),
            pltpu.SMEM((vectors, 128), jnp.float32),
            pltpu.SemaphoreType.DMA((tables + 5,)),
        ],
        compiler_params=pltpu.CompilerParams(vmem_limit_bytes=TABLE_BYTES),
        cost_estimate=pl.CostEstimate(
            flops=6 * rows * entries * half * width,
            bytes_accessed=2 * (tables + 3) * rows * half * width,
            transcendentals=0,
        ),
        name="row_sums",
    )(odd, *asked, *[source for source, _ in sources])


def edges_kernel(*refs):
    first_ref, last_ref = refs[-2:]
    halves = (len(refs) - 2) // 6
    rows = refs[0].shape[0]
    half = refs[0].shape[1]
    per = 128 // 8
    lane = lax.broadcasted_iota(jnp.int32, (half, 128), 1)
    for side, out_ref in ((0, first_ref), (1, last_ref)):
        for h in range(halves):
            parts = refs[6 * h + 3 * side : 6 * h + 3 * side + 3]
            for j in range(rows // per):
                packed = jnp.zeros((half, 128), jnp.float32)
                for i in range(per):
                    r = j * per + i
                    cells = parts[0][r] + parts[1][r].astype(jnp.float32) + parts[2][r].astype(jnp.float32)
                    at = 8 * i + 3 * (1 - side)
                    spot = (lane >= at) & (lane < at + 3)
                    packed = jnp.where(spot, pltpu.roll(cells, 8 * i + 3, 1), packed)
                out_ref[j, h * half : (h + 1) * half] = packed.astype(out_ref.dtype)


def edges(parts0, parts1):
    rows, half, width = parts0[0].shape
    specs, operands = [], []
    for parts in (parts0, parts1):
        for at in (0, width // 128 - 1):
            specs += [pl.BlockSpec((rows, half, 128), lambda t, at=at: (0, 0, at))] * 3
            operands += parts
    packed = (rows // 16, 2 * half, 128)
    return pl.pallas_call(
        edges_kernel,
        grid=(1,),
        in_specs=specs,
        out_specs=[pl.BlockSpec(packed, lambda t: (0, 0, 0))] * 2,
        out_shape=[jax.ShapeDtypeStruct(packed, jnp.bfloat16)] * 2,
        compiler_params=pltpu.CompilerParams(vmem_limit_bytes=VMEM_BYTES),
        cost_estimate=pl.CostEstimate(flops=8 * half * 256 * rows, bytes_accessed=16 * half * 256 * rows, transcendentals=0),
        name="edges",
    )(*operands)


def combine_kernel(own0, a0, b0, own1, a1, b1, out_ref):
    rows, half = own0.shape[:2]
    for r in range(rows):
        out_ref[r, :half] = own0[r] + a0[r].astype(jnp.float32) + b0[r].astype(jnp.float32)
        out_ref[r, half:] = own1[r] + a1[r].astype(jnp.float32) + b1[r].astype(jnp.float32)


def combine(parts0, parts1):
    rows, half, width = parts0[0].shape
    step = 8
    return pl.pallas_call(
        combine_kernel,
        grid=(rows // step,),
        in_specs=[pl.BlockSpec((step, half, width), lambda t: (t, 0, 0))] * 6,
        out_specs=pl.BlockSpec((step, 2 * half, width), lambda t: (t, 0, 0)),
        out_shape=jax.ShapeDtypeStruct((rows, 2 * half, width), jnp.float32),
        compiler_params=pltpu.CompilerParams(vmem_limit_bytes=VMEM_BYTES),
        cost_estimate=pl.CostEstimate(
            flops=4 * rows * half * width, bytes_accessed=24 * rows * half * width, transcendentals=0
        ),
        name="combine",
    )(*parts0, *parts1)


def shifted_by(row, edge, amount, lane):
    count = len(row)
    if amount == 0:
        return row
    if amount > 0:
        row = row[:-1] + [jnp.where(lane >= 128 - amount, edge, row[-1])]
        turned = [pltpu.roll(tile, amount, 1) for tile in row]
        return [jnp.where(lane < amount, turned[t - 1], turned[t]) for t in range(count)]
    row = [jnp.where(lane < -amount, edge, row[0])] + row[1:]
    turned = [pltpu.roll(tile, 128 + amount, 1) for tile in row]
    return [jnp.where(lane >= 128 + amount, turned[(t + 1) % count], turned[t]) for t in range(count)]


def edge_tile(west_ref, east_ref, r):
    per = 128 // 8
    both = west_ref[r // per].astype(jnp.float32) + east_ref[r // per].astype(jnp.float32)
    return pltpu.roll(both, (125 - 8 * (r % per)) % 128, 1)


def rows_kernel(offset_ref, remap0_ref, remap1_ref, west_ref, east_ref, first_ref, last_ref):
    bins, width = remap0_ref.shape[1:]
    lane = lax.broadcasted_iota(jnp.int32, (bins, 128), 1)
    spots = [slice(128 * t, 128 * t + 128) for t in range(width // 128)]
    end = offset_ref.shape[0] - 1
    for r, remap_ref, out_ref in ((0, remap0_ref, first_ref), (end, remap1_ref, last_ref)):
        for amount in range(-REACH, REACH + 1):

            @pl.when(offset_ref[r] == amount)
            def _(r=r, remap_ref=remap_ref, out_ref=out_ref, amount=amount):
                row = [remap_ref[0, :, at] for at in spots]
                row = shifted_by(row, edge_tile(west_ref, east_ref, r), amount, lane)
                for at, tile in zip(spots, row):
                    out_ref[0, :, at] = tile.astype(out_ref.dtype)


def outer_rows(offset, remapped, west, east):
    rows, bins, width = remapped.shape
    row = lambda at: pl.BlockSpec((1, bins, width), lambda t: (at, 0, 0))
    whole = pl.BlockSpec(west.shape, lambda t: (0, 0, 0))
    return pl.pallas_call(
        rows_kernel,
        grid=(1,),
        in_specs=[in_smem(), row(0), row(rows - 1), whole, whole],
        out_specs=[row(0), row(0)],
        out_shape=[jax.ShapeDtypeStruct((1, bins, width), jnp.bfloat16)] * 2,
        compiler_params=pltpu.CompilerParams(vmem_limit_bytes=VMEM_BYTES),
        cost_estimate=pl.CostEstimate(flops=20 * bins * width, bytes_accessed=12 * bins * width, transcendentals=0),
        name="outer_rows",
    )(offset, remapped, remapped, west, east)


def final_kernel(offset_ref, remap_ref, west_ref, east_ref, kappa_ref, local_ref, out_ref, outer_ref, edge_ref):
    rows, bins, width = remap_ref.shape
    count = width // 128
    lane = lax.broadcasted_iota(jnp.int32, (8, 128), 1)
    spots = [slice(128 * t, 128 * t + 128) for t in range(count)]
    for r in range(rows):
        edge_ref[r] = edge_tile(west_ref, east_ref, r)

    def moved(row, edge, amount):
        row = [jnp.where(lane < -amount, edge, row[0])] + row[1:]
        row = row[:-1] + [jnp.where(lane >= 128 - amount, edge, row[-1])]
        turned = [pltpu.roll(tile, (amount + 128) & 127, 1) for tile in row]
        before, after = lane < amount, lane >= 128 + amount
        return [
            jnp.where(before, turned[t - 1], jnp.where(after, turned[(t + 1) % count], turned[t])) for t in range(count)
        ]

    for b in range(bins // 8):
        at = slice(8 * b, 8 * b + 8)
        blank = [jnp.zeros((8, 128), jnp.float32)] * count
        before, now, base = blank, blank, None
        stores = []
        for r in range(rows):
            amount = offset_ref[r]
            row = [remap_ref[r, at, spot] for spot in spots]
            edge = edge_ref[r, at]
            center = moved(row, edge, amount)
            east = moved(row, edge, amount - 1)
            west = moved(row, edge, amount + 1)
            fresh = []
            for t, spot in enumerate(spots):
                kappa = kappa_ref[r, :, spot]
                fresh.append(local_ref[r, at, spot] + center[t] + kappa * (east[t] + west[t] - 4.0 * center[t]))
                if r:
                    stores.append((r - 1, spot, base[t] + kappa_ref[r - 1, :, spot] * (before[t] + center[t])))
            before, now, base = now, center, fresh
            if r % 4 == 3:
                for which, spot, value in stores:
                    if which:
                        out_ref[which, at, spot] = value
                    else:
                        outer_ref[0, at, spot] = value
                stores = []
        for t, spot in enumerate(spots):
            outer_ref[1, at, spot] = base[t] + kappa_ref[rows - 1, :, spot] * before[t]


def final(offset, remapped, west, east, kappa, local):
    rows, bins, width = remapped.shape
    block = pl.BlockSpec((rows, TILE, width), lambda t: (0, t, 0))
    packed = pl.BlockSpec((west.shape[0], TILE, 128), lambda t: (0, t, 0))
    return pl.pallas_call(
        final_kernel,
        grid=(bins // TILE,),
        in_specs=[in_smem(), block, packed, packed, pl.BlockSpec(kappa.shape, lambda t: (0, 0, 0)), block],
        out_specs=[block, pl.BlockSpec((2, TILE, width), lambda t: (0, t, 0))],
        out_shape=[
            jax.ShapeDtypeStruct(local.shape, jnp.float32),
            jax.ShapeDtypeStruct((2, bins, width), jnp.float32),
        ],
        scratch_shapes=[pltpu.VMEM((rows, TILE, 128), jnp.float32)],
        compiler_params=pltpu.CompilerParams(vmem_limit_bytes=VMEM_BYTES),
        cost_estimate=pl.CostEstimate(flops=30 * remapped.size, bytes_accessed=12 * remapped.size, transcendentals=0),
        name="final",
    )(offset, remapped, west, east, kappa, local)


def halo_kernel(before_ref, after_ref, kappa_ref, outer_ref, _, out_ref, sums_ref, sems):
    rows = out_ref.shape[0]
    copies = []
    for side, (value_ref, at) in enumerate(((before_ref, 0), (after_ref, rows - 1))):
        sums_ref[side] = outer_ref[side] + kappa_ref[at] * value_ref[0].astype(jnp.float32)
        copy = pltpu.make_async_copy(sums_ref.at[pl.ds(side, 1)], out_ref.at[pl.ds(at, 1)], sems.at[side])
        copy.start()
        copies.append(copy)
    for copy in copies:
        copy.wait()


def add_halo(before, after, kappa, outer, partial):
    vmem = pl.BlockSpec(memory_space=pltpu.VMEM)
    return pl.pallas_call(
        halo_kernel,
        in_specs=[vmem, vmem, vmem, vmem, in_place()],
        out_specs=in_place(),
        out_shape=jax.ShapeDtypeStruct(partial.shape, jnp.float32),
        scratch_shapes=[pltpu.VMEM(outer.shape, jnp.float32), pltpu.SemaphoreType.DMA((2,))],
        input_output_aliases={4: 0},
        compiler_params=pltpu.CompilerParams(vmem_limit_bytes=VMEM_BYTES),
        cost_estimate=pl.CostEstimate(flops=4 * outer.size, bytes_accessed=20 * outer.size, transcendentals=0),
        name="add_halo",
    )(before, after, kappa, outer, partial)


def body(
    conc,
    dep_owner,
    dep_row,
    dep_weight,
    dep_count,
    zonal_offset,
    agg_rates,
    toeplitz,
    settle,
    kappa,
):
    rows, bins, width = conc.shape
    entries = dep_owner.shape[2]
    odd = (lax.axis_index("lon") % 2).astype(jnp.int32).reshape(1)
    half = bins // 2
    low, meta = low_message(conc, dep_owner[0].T, dep_row[0].T, dep_weight[0].T, dep_count)
    ahead = permute_lon(low, -2)
    behind = permute_lon(low, 2)
    high = high_message(conc, meta, swap_lon(meta))
    beside = swap_lon(conc)
    rates, high = lax.optimization_barrier((agg_rates, high))
    south = permute_lat(high, 1)
    north = permute_lat(high, -1)
    local = local_terms(conc, rates, toeplitz, settle)
    ahead, behind, local = lax.optimization_barrier((ahead, behind, local))
    south, north, ahead, behind = lax.optimization_barrier((south, north, ahead, behind))

    to_west, own1, to_east = row_sums(
        odd,
        [behind, meta, ahead],
        lon_slots,
        [(south, 0), (conc, half), (north, 0), (swap_lon(south), 0), (beside, half), (swap_lon(north), 0)],
        rows,
        half,
        entries,
    )
    parts1 = [own1, permute_lon(to_east, 2), permute_lon(to_west, -2)]

    down, own0, up = row_sums(
        odd,
        [south, meta, north],
        lat_slots,
        [(conc, 0), (beside, 0), (ahead, 0), (behind, 0), (swap_lon(ahead), 0), (swap_lon(behind), 0)],
        rows,
        half,
        entries,
    )
    parts0 = [own0, permute_lat(up, 1), permute_lat(down, -1)]

    first, last = edges(parts0, parts1)
    east, west = permute_lon(first, -1), permute_lon(last, 1)
    remapped = combine(parts0, parts1)
    top_row, end_row = outer_rows(zonal_offset, remapped, west, east)
    before, after = permute_lat(end_row, 1), permute_lat(top_row, -1)
    kappa = kappa[:, None, :]
    partial, outer = final(zonal_offset, remapped, west, east, kappa, local)
    return add_halo(before, after, kappa, outer, partial)


def solution(mesh):
    return jax.shard_map(
        body,
        mesh=mesh,
        in_specs=(
            P("lat", None, "lon"),
            P("lon", "lat", None),
            P("lon", "lat", None),
            P("lon", "lat", None),
            P("lon", "lat"),
            P("lat"),
            P(None, "lat", "lon"),
            P(),
            P(),
            P("lat", "lon"),
        ),
        out_specs=P("lat", None, "lon"),
        check_vma=False,
    )
```

```python
import functools

import jax
import jax.numpy as jnp
from jax import lax
from jax.experimental import pallas as pl
from jax.experimental.pallas import tpu as pltpu
from jax.sharding import PartitionSpec as P

REACH = 2
NEAR_LON = 5
UNROLL = 4
VMEM_BYTES = 12 * 1024 * 1024
MOST_BYTES = 60 * 1024 * 1024
TABLE_BYTES = 20 * 1024 * 1024
QUICK = 2
FIELDS = ((0, 0), (0, 128), (8, 0), (8, 128), (16, 0))


def permute_lon(value, steps):
    count = lax.axis_size("lon")
    return lax.ppermute(value, "lon", [(i, (i + steps) % count) for i in range(count)])


def swap_lon(value):
    count = lax.axis_size("lon")
    return lax.ppermute(value, "lon", [(i, i ^ 1) for i in range(count)])


def permute_lat(value, steps):
    count = lax.axis_size("lat")
    pairs = [(i, i + steps) for i in range(count) if 0 <= i + steps < count]
    return lax.ppermute(value, "lat", pairs)


def in_smem():
    return pl.BlockSpec(memory_space=pltpu.SMEM)


def in_place():
    return pl.BlockSpec(memory_space=pl.ANY)


def for_rows(count, one):
    def some(g, carry):
        stores = []
        for u in range(UNROLL):
            stores += one(g * UNROLL + u)
        for ref, at, value in stores:
            ref[at] = value.astype(ref.dtype)
        return carry

    lax.fori_loop(0, count // UNROLL, some, 0)


def growth_kernel(flip_ref, settle_ref, conc_ref, rates_ref, out_ref, mat_ref):
    ranks, rows_step = rates_ref.shape[0], conc_ref.shape[0]
    bins, width = conc_ref.shape[1:]

    @pl.when(pl.program_id(0) == 0)
    def _():
        for q in range(ranks):
            spread = jnp.broadcast_to(flip_ref[q : q + 1, :], (bins, 2 * bins))
            turned = pltpu.roll(spread, bins + 1, 1, stride=1, stride_axis=0)
            mat_ref[q * bins : (q + 1) * bins, :] = turned[:, :bins].astype(jnp.bfloat16)

    settle = jnp.broadcast_to(settle_ref[...], (bins, width))
    for r in range(rows_step):
        cells = conc_ref[r]
        product = jnp.dot(mat_ref[...], cells, preferred_element_type=jnp.float32)
        total = -settle * cells.astype(jnp.float32)
        for q in range(ranks):
            total = total + rates_ref[q, r : r + 1, :] * product[q * bins : (q + 1) * bins]
        out_ref[r] = total


def local_terms(conc, agg_rates, toeplitz, settle):
    rows, bins, width = conc.shape
    ranks = agg_rates.shape[0]
    step = 8
    flipped = jnp.pad(toeplitz[:, ::-1].astype(jnp.float32), ((0, 0), (0, 1)))
    return pl.pallas_call(
        growth_kernel,
        grid=(rows // step,),
        in_specs=[
            pl.BlockSpec((ranks, 2 * bins), lambda i: (0, 0)),
            pl.BlockSpec((bins, 1), lambda i: (0, 0)),
            pl.BlockSpec((step, bins, width), lambda i: (i, 0, 0)),
            pl.BlockSpec((ranks, step, width), lambda i: (0, i, 0)),
        ],
        out_specs=pl.BlockSpec((step, bins, width), lambda i: (i, 0, 0)),
        out_shape=jax.ShapeDtypeStruct(conc.shape, jnp.float32),
        scratch_shapes=[pltpu.VMEM((ranks * bins, bins), jnp.bfloat16)],
        compiler_params=pltpu.CompilerParams(vmem_limit_bytes=VMEM_BYTES),
        cost_estimate=pl.CostEstimate(
            flops=2 * ranks * bins * bins * rows * width, bytes_accessed=8 * conc.size, transcendentals=0
        ),
        name="growth",
    )(flipped, settle[:, None], conc, agg_rates)


def messages_kernel(
    conc_ref, owner_hbm, source_hbm, weight_hbm, count_hbm, low_ref, high_ref, meta_ref,
    owner_ref, source_ref, weight_ref, count_ref, sems,
):
    rows = conc_ref.shape[0]
    half = low_ref.shape[1]
    entries = owner_ref.shape[0]
    small = [
        pltpu.make_async_copy(hbm, ref, sems.at[2 + i])
        for i, (hbm, ref) in enumerate(
            ((owner_hbm, owner_ref), (source_hbm, source_ref), (weight_hbm, weight_ref), (count_hbm, count_ref))
        )
    ]
    large = [
        pltpu.make_async_copy(conc_ref.at[:, pl.ds(i * half, half), :], ref.at[pl.ds(0, rows)], sems.at[i])
        for i, ref in enumerate((low_ref, high_ref))
    ]
    for copy in small + large:
        copy.start()
    meta_ref[...] = jnp.zeros(meta_ref.shape, meta_ref.dtype)
    for copy in small:
        copy.wait()
    wide = lambda value: value.astype(jnp.float32)
    entry = lax.broadcasted_iota(jnp.int32, owner_ref.shape, 0)
    live = jnp.where(entry < count_ref[...], weight_ref[...], 0.0)
    top = live.astype(jnp.bfloat16)
    middle = (live - wide(top)).astype(jnp.bfloat16)
    bottom = (live - wide(top) - wide(middle)).astype(jnp.bfloat16)
    fields = (wide(owner_ref[...]), wide(source_ref[...]), wide(top), wide(middle), wide(bottom))
    for field, (at, lane) in zip(fields, FIELDS):
        meta_ref[0, at : at + entries, lane : lane + rows] = field.astype(jnp.bfloat16)
    low_ref[rows] = meta_ref[0]
    high_ref[rows] = meta_ref[0]
    for copy in large:
        copy.wait()


def messages(conc, owner, source, weight, count):
    rows, bins, width = conc.shape
    half = bins // 2
    return pl.pallas_call(
        messages_kernel,
        in_specs=[in_place()] * 5,
        out_specs=[pl.BlockSpec(memory_space=pltpu.VMEM)] * 3,
        out_shape=[
            jax.ShapeDtypeStruct((rows + 1, half, width), conc.dtype),
            jax.ShapeDtypeStruct((rows + 1, half, width), conc.dtype),
            jax.ShapeDtypeStruct((1, half, width), conc.dtype),
        ],
        scratch_shapes=[pltpu.VMEM(small.shape, small.dtype) for small in (owner, source, weight, count)]
        + [pltpu.SemaphoreType.DMA((6,))],
        compiler_params=pltpu.CompilerParams(vmem_limit_bytes=MOST_BYTES),
        cost_estimate=pl.CostEstimate(flops=0, bytes_accessed=4 * conc.size, transcendentals=0),
        name="messages",
    )(conc, owner, source, weight, count)


def lat_slots(rows, group, lat_step, lon_step, odd):
    toward = 1.0 - 2.0 * odd
    slot = jnp.where(
        lon_step == 0.0,
        0.0,
        jnp.where(lon_step == 2.0, 2.0, jnp.where(lon_step == -2.0, 3.0, jnp.where(lon_step == toward, 1.0, 5.0 - odd))),
    )
    return lat_step == 1.0 - group, slot * rows


def lon_slots(rows, group, lat_step, lon_step, odd):
    toward = 1.0 - 2.0 * odd
    lon_from = 2.0 * (group - 1.0) + lon_step
    slot = jnp.where(lon_from == 0.0, 0.0, 3.0) + lat_step + 1.0
    return (lon_from == 0.0) | (lon_from == toward), slot * rows


def row_sums_kernel(bases, slots, entries, *refs):
    tables = len(bases)
    odd_ref = refs[0]
    asked = refs[1:4]
    sources = refs[4 : 4 + tables]
    outs = refs[4 + tables : 7 + tables]
    table, meta_ref, index_vec, weight_vec, index_ref, weight_ref, sems = refs[7 + tables :]
    every, half, width = table.shape
    rows = every // tables
    metas = [
        pltpu.make_async_copy(
            asked[g].at[pl.ds(asked[g].shape[0] - 1, 1)], meta_ref.at[pl.ds(g, 1)], sems.at[tables + g]
        )
        for g in range(3)
    ]
    copies = [
        pltpu.make_async_copy(
            sources[i].at[pl.ds(0, rows), pl.ds(bases[i], half), :], table.at[pl.ds(i * rows, rows)], sems.at[i]
        )
        for i in range(tables)
    ]
    for copy in metas + copies:
        copy.start()
    for copy in metas:
        copy.wait()

    odd = odd_ref[0].astype(jnp.float32)
    for g in range(3):
        owner, source, top, middle, bottom = [
            meta_ref[g, at : at + entries, lane : lane + 128].astype(jnp.float32) for at, lane in FIELDS
        ]
        weight = top + middle + bottom
        band = jnp.where(owner >= NEAR_LON, 1.0, 0.0) + jnp.where(owner >= 2 * NEAR_LON, 1.0, 0.0)
        here, base = slots(rows, float(g), band - 1.0, owner - NEAR_LON * band - REACH, odd)
        here = jnp.where(here & (weight != 0.0), 1.0, 0.0)
        index = base + source
        packed = [[jnp.zeros((1, 128), jnp.float32)] * 2 for _ in range(entries)]
        rank = jnp.zeros((1, 128), jnp.float32)
        for k in range(entries):
            taken = here[k : k + 1]
            for place in range(k + 1):
                spot = (taken > 0.0) & (rank == place)
                packed[place] = [
                    jnp.where(spot, index[k : k + 1], packed[place][0]),
                    jnp.where(spot, weight[k : k + 1], packed[place][1]),
                ]
            rank = rank + taken
        for place in range(entries):
            at = g * entries + place
            index_vec[at : at + 1, :] = packed[place][0].astype(jnp.int32)
            weight_vec[at : at + 1, :] = packed[place][1]
        at = 3 * entries + g
        index_vec[at : at + 1, :] = rank.astype(jnp.int32)
    to_scalar = [
        pltpu.make_async_copy(index_vec, index_ref, sems.at[tables + 3]),
        pltpu.make_async_copy(weight_vec, weight_ref, sems.at[tables + 4]),
    ]
    for copy in to_scalar:
        copy.start()
    for copy in to_scalar + copies:
        copy.wait()

    for group, out in enumerate(outs):

        def some(g, carry, group=group, out=out):
            def sums(terms):
                totals = []
                for u in range(UNROLL):
                    r = g * UNROLL + u
                    total = jnp.zeros((half, width), jnp.float32)
                    for k in range(terms):
                        row = group * entries + k
                        total = total + weight_ref[row, r] * table[index_ref[row, r]].astype(jnp.float32)
                    totals.append(total)
                for u in range(UNROLL):
                    out[g * UNROLL + u] = totals[u].astype(out.dtype)

            most = index_ref[3 * entries + group, g * UNROLL]
            for u in range(1, UNROLL):
                most = jnp.maximum(most, index_ref[3 * entries + group, g * UNROLL + u])
            sums(min(QUICK, entries))

            @pl.when(most > QUICK)
            def _():
                sums(entries)

            return carry

        lax.fori_loop(0, rows // UNROLL, some, 0)


def row_sums(odd, asked, slots, sources, rows, half, entries):
    tables = len(sources)
    width = sources[0][0].shape[2]
    vectors = -(-3 * (entries + 1) // 8) * 8
    return pl.pallas_call(
        functools.partial(row_sums_kernel, tuple(base for _, base in sources), slots, entries),
        in_specs=[in_smem()] + [in_place()] * (3 + tables),
        out_specs=[pl.BlockSpec(memory_space=pltpu.VMEM)] * 3,
        out_shape=[
            jax.ShapeDtypeStruct((rows, half, width), dtype) for dtype in (jnp.bfloat16, jnp.float32, jnp.bfloat16)
        ],
        scratch_shapes=[
            pltpu.VMEM((tables * rows, half, width), jnp.bfloat16),
            pltpu.VMEM((3, half, width), jnp.bfloat16),
            pltpu.VMEM((vectors, 128), jnp.int32),
            pltpu.VMEM((vectors, 128), jnp.float32),
            pltpu.SMEM((vectors, 128), jnp.int32),
            pltpu.SMEM((vectors, 128), jnp.float32),
            pltpu.SemaphoreType.DMA((tables + 5,)),
        ],
        compiler_params=pltpu.CompilerParams(vmem_limit_bytes=TABLE_BYTES),
        cost_estimate=pl.CostEstimate(
            flops=6 * rows * entries * half * width,
            bytes_accessed=2 * (tables + 3) * rows * half * width,
            transcendentals=0,
        ),
        name="row_sums",
    )(odd, *asked, *[source for source, _ in sources])


def edges_kernel(*refs):
    first_ref, last_ref = refs[-2:]
    halves = (len(refs) - 2) // 6
    rows = refs[0].shape[0]
    half = refs[0].shape[1]
    per = 128 // 8
    lane = lax.broadcasted_iota(jnp.int32, (half, 128), 1)
    for side, out_ref in ((0, first_ref), (1, last_ref)):
        for h in range(halves):
            parts = refs[6 * h + 3 * side : 6 * h + 3 * side + 3]
            for j in range(rows // per):
                packed = jnp.zeros((half, 128), jnp.float32)
                for i in range(per):
                    r = j * per + i
                    cells = parts[0][r] + parts[1][r].astype(jnp.float32) + parts[2][r].astype(jnp.float32)
                    at = 8 * i + 3 * (1 - side)
                    spot = (lane >= at) & (lane < at + 3)
                    packed = jnp.where(spot, pltpu.roll(cells, 8 * i + 3, 1), packed)
                out_ref[j, h * half : (h + 1) * half] = packed.astype(out_ref.dtype)


def edges(parts0, parts1):
    rows, half, width = parts0[0].shape
    specs, operands = [], []
    for parts in (parts0, parts1):
        for at in (0, width // 128 - 1):
            specs += [pl.BlockSpec((rows, half, 128), lambda t, at=at: (0, 0, at))] * 3
            operands += parts
    packed = (rows // 16, 2 * half, 128)
    return pl.pallas_call(
        edges_kernel,
        grid=(1,),
        in_specs=specs,
        out_specs=[pl.BlockSpec(packed, lambda t: (0, 0, 0))] * 2,
        out_shape=[jax.ShapeDtypeStruct(packed, jnp.bfloat16)] * 2,
        compiler_params=pltpu.CompilerParams(vmem_limit_bytes=VMEM_BYTES),
        cost_estimate=pl.CostEstimate(flops=8 * half * 256 * rows, bytes_accessed=16 * half * 256 * rows, transcendentals=0),
        name="edges",
    )(*operands)


def combine_kernel(own0, a0, b0, own1, a1, b1, out_ref):
    rows, half = own0.shape[:2]
    for r in range(rows):
        out_ref[r, :half] = own0[r] + a0[r].astype(jnp.float32) + b0[r].astype(jnp.float32)
        out_ref[r, half:] = own1[r] + a1[r].astype(jnp.float32) + b1[r].astype(jnp.float32)


def combine(parts0, parts1):
    rows, half, width = parts0[0].shape
    step = 8
    return pl.pallas_call(
        combine_kernel,
        grid=(rows // step,),
        in_specs=[pl.BlockSpec((step, half, width), lambda t: (t, 0, 0))] * 6,
        out_specs=pl.BlockSpec((step, 2 * half, width), lambda t: (t, 0, 0)),
        out_shape=jax.ShapeDtypeStruct((rows, 2 * half, width), jnp.float32),
        compiler_params=pltpu.CompilerParams(vmem_limit_bytes=VMEM_BYTES),
        cost_estimate=pl.CostEstimate(
            flops=4 * rows * half * width, bytes_accessed=24 * rows * half * width, transcendentals=0
        ),
        name="combine",
    )(*parts0, *parts1)


def shifted_by(row, edge, amount, lane):
    count = len(row)
    if amount == 0:
        return row
    if amount > 0:
        row = row[:-1] + [jnp.where(lane >= 128 - amount, edge, row[-1])]
        turned = [pltpu.roll(tile, amount, 1) for tile in row]
        return [jnp.where(lane < amount, turned[t - 1], turned[t]) for t in range(count)]
    row = [jnp.where(lane < -amount, edge, row[0])] + row[1:]
    turned = [pltpu.roll(tile, 128 + amount, 1) for tile in row]
    return [jnp.where(lane >= 128 + amount, turned[(t + 1) % count], turned[t]) for t in range(count)]


def edge_tile(west_ref, east_ref, r):
    per = 128 // 8
    both = west_ref[r // per].astype(jnp.float32) + east_ref[r // per].astype(jnp.float32)
    return pltpu.roll(both, (125 - 8 * (r % per)) % 128, 1)


def rows_kernel(offset_ref, remap0_ref, remap1_ref, west_ref, east_ref, first_ref, last_ref):
    bins, width = remap0_ref.shape[1:]
    lane = lax.broadcasted_iota(jnp.int32, (bins, 128), 1)
    spots = [slice(128 * t, 128 * t + 128) for t in range(width // 128)]
    end = offset_ref.shape[0] - 1
    for r, remap_ref, out_ref in ((0, remap0_ref, first_ref), (end, remap1_ref, last_ref)):
        for amount in range(-REACH, REACH + 1):

            @pl.when(offset_ref[r] == amount)
            def _(r=r, remap_ref=remap_ref, out_ref=out_ref, amount=amount):
                row = [remap_ref[0, :, at] for at in spots]
                row = shifted_by(row, edge_tile(west_ref, east_ref, r), amount, lane)
                for at, tile in zip(spots, row):
                    out_ref[0, :, at] = tile.astype(out_ref.dtype)


def outer_rows(offset, remapped, west, east):
    rows, bins, width = remapped.shape
    row = lambda at: pl.BlockSpec((1, bins, width), lambda t: (at, 0, 0))
    whole = pl.BlockSpec(west.shape, lambda t: (0, 0, 0))
    return pl.pallas_call(
        rows_kernel,
        grid=(1,),
        in_specs=[in_smem(), row(0), row(rows - 1), whole, whole],
        out_specs=[row(0), row(0)],
        out_shape=[jax.ShapeDtypeStruct((1, bins, width), jnp.bfloat16)] * 2,
        compiler_params=pltpu.CompilerParams(vmem_limit_bytes=VMEM_BYTES),
        cost_estimate=pl.CostEstimate(flops=20 * bins * width, bytes_accessed=12 * bins * width, transcendentals=0),
        name="outer_rows",
    )(offset, remapped, remapped, west, east)


def final_kernel(offset_ref, remap_ref, west_ref, east_ref, kappa_ref, local_ref, out_ref, outer_ref, edge_ref):
    rows, bins, width = remap_ref.shape
    count = width // 128
    lane = lax.broadcasted_iota(jnp.int32, (8, 128), 1)
    spots = [slice(128 * t, 128 * t + 128) for t in range(count)]
    for r in range(rows):
        edge_ref[r] = edge_tile(west_ref, east_ref, r)

    def moved(row, edge, amount):
        row = [jnp.where(lane < -amount, edge, row[0])] + row[1:]
        row = row[:-1] + [jnp.where(lane >= 128 - amount, edge, row[-1])]
        turned = [pltpu.roll(tile, (amount + 128) & 127, 1) for tile in row]
        before, after = lane < amount, lane >= 128 + amount
        return [
            jnp.where(before, turned[t - 1], jnp.where(after, turned[(t + 1) % count], turned[t])) for t in range(count)
        ]

    pieces = [slice(8 * b, 8 * b + 8) for b in range(bins // 8)]
    before, now, base = {}, {}, {}
    stores = []
    for r in range(rows):
        amount = offset_ref[r]
        kappa = [kappa_ref[r, :, spot] for spot in spots]
        above = [kappa_ref[max(r - 1, 0), :, spot] for spot in spots]
        for at in pieces:
            row = [remap_ref[r, at, spot] for spot in spots]
            edge = edge_ref[r, at]
            center = moved(row, edge, amount)
            east = moved(row, edge, amount - 1)
            west = moved(row, edge, amount + 1)
            key = at.start
            fresh = []
            for t, spot in enumerate(spots):
                around = kappa[t] * (east[t] + west[t] - 4.0 * center[t])
                fresh.append(local_ref[r, at, spot] + center[t] + around)
                if r == 1:
                    stores.append((r - 1, at, spot, base[key][t] + above[t] * center[t]))
                elif r:
                    stores.append((r - 1, at, spot, base[key][t] + above[t] * (before[key][t] + center[t])))
            if r:
                before[key] = now[key]
            now[key], base[key] = center, fresh
        if r % 2:
            for which, at, spot, value in stores:
                if which:
                    out_ref[which, at, spot] = value
                else:
                    outer_ref[0, at, spot] = value
            stores = []
    for at in pieces:
        for t, spot in enumerate(spots):
            outer_ref[1, at, spot] = base[at.start][t] + kappa_ref[rows - 1, :, spot] * before[at.start][t]


def final(offset, remapped, west, east, kappa, local):
    rows, bins, width = remapped.shape
    tile = bins // 2
    block = pl.BlockSpec((rows, tile, width), lambda t: (0, t, 0))
    packed = pl.BlockSpec((west.shape[0], tile, 128), lambda t: (0, t, 0))
    return pl.pallas_call(
        final_kernel,
        grid=(bins // tile,),
        in_specs=[in_smem(), block, packed, packed, pl.BlockSpec(kappa.shape, lambda t: (0, 0, 0)), block],
        out_specs=[block, pl.BlockSpec((2, tile, width), lambda t: (0, t, 0))],
        out_shape=[
            jax.ShapeDtypeStruct(local.shape, jnp.float32),
            jax.ShapeDtypeStruct((2, bins, width), jnp.float32),
        ],
        scratch_shapes=[pltpu.VMEM((rows, tile, 128), jnp.float32)],
        compiler_params=pltpu.CompilerParams(vmem_limit_bytes=VMEM_BYTES),
        cost_estimate=pl.CostEstimate(flops=30 * remapped.size, bytes_accessed=12 * remapped.size, transcendentals=0),
        name="final",
    )(offset, remapped, west, east, kappa, local)


def halo_kernel(before_ref, after_ref, kappa_ref, outer_ref, _, out_ref, sums_ref, sems):
    rows = out_ref.shape[0]
    copies = []
    for side, (value_ref, at) in enumerate(((before_ref, 0), (after_ref, rows - 1))):
        sums_ref[side] = outer_ref[side] + kappa_ref[at] * value_ref[0].astype(jnp.float32)
        copy = pltpu.make_async_copy(sums_ref.at[pl.ds(side, 1)], out_ref.at[pl.ds(at, 1)], sems.at[side])
        copy.start()
        copies.append(copy)
    for copy in copies:
        copy.wait()


def add_halo(before, after, kappa, outer, partial):
    vmem = pl.BlockSpec(memory_space=pltpu.VMEM)
    return pl.pallas_call(
        halo_kernel,
        in_specs=[vmem, vmem, vmem, vmem, in_place()],
        out_specs=in_place(),
        out_shape=jax.ShapeDtypeStruct(partial.shape, jnp.float32),
        scratch_shapes=[pltpu.VMEM(outer.shape, jnp.float32), pltpu.SemaphoreType.DMA((2,))],
        input_output_aliases={4: 0},
        compiler_params=pltpu.CompilerParams(vmem_limit_bytes=VMEM_BYTES),
        cost_estimate=pl.CostEstimate(flops=4 * outer.size, bytes_accessed=20 * outer.size, transcendentals=0),
        name="add_halo",
    )(before, after, kappa, outer, partial)


def body(
    conc,
    dep_owner,
    dep_row,
    dep_weight,
    dep_count,
    zonal_offset,
    agg_rates,
    toeplitz,
    settle,
    kappa,
):
    rows, bins, width = conc.shape
    entries = dep_owner.shape[2]
    odd = (lax.axis_index("lon") % 2).astype(jnp.int32).reshape(1)
    half = bins // 2
    low, high, meta = messages(conc, dep_owner[0].T, dep_row[0].T, dep_weight[0].T, dep_count)
    south = permute_lat(high, 1)
    north = permute_lat(high, -1)
    ahead = permute_lon(low, -2)
    behind = permute_lon(low, 2)
    beside = swap_lon(conc)
    rates, meta = lax.optimization_barrier((agg_rates, meta))
    local = local_terms(conc, rates, toeplitz, settle)
    south, north, local = lax.optimization_barrier((south, north, local))

    to_west, own1, to_east = row_sums(
        odd,
        [behind, meta, ahead],
        lon_slots,
        [(south, 0), (conc, half), (north, 0), (swap_lon(south), 0), (beside, half), (swap_lon(north), 0)],
        rows,
        half,
        entries,
    )
    parts1 = [own1, permute_lon(to_east, 2), permute_lon(to_west, -2)]

    down, own0, up = row_sums(
        odd,
        [south, meta, north],
        lat_slots,
        [(conc, 0), (beside, 0), (ahead, 0), (behind, 0), (swap_lon(ahead), 0), (swap_lon(behind), 0)],
        rows,
        half,
        entries,
    )
    parts0 = [own0, permute_lat(up, 1), permute_lat(down, -1)]

    first, last = edges(parts0, parts1)
    east, west = permute_lon(first, -1), permute_lon(last, 1)
    remapped = combine(parts0, parts1)
    top_row, end_row = outer_rows(zonal_offset, remapped, west, east)
    before, after = permute_lat(end_row, 1), permute_lat(top_row, -1)
    kappa = kappa[:, None, :]
    partial, outer = final(zonal_offset, remapped, west, east, kappa, local)
    return add_halo(before, after, kappa, outer, partial)


def solution(mesh):
    return jax.shard_map(
        body,
        mesh=mesh,
        in_specs=(
            P("lat", None, "lon"),
            P("lon", "lat", None),
            P("lon", "lat", None),
            P("lon", "lat", None),
            P("lon", "lat"),
            P("lat"),
            P(None, "lat", "lon"),
            P(),
            P(),
            P("lat", "lon"),
        ),
        out_specs=P("lat", None, "lon"),
        check_vma=False,
    )
```

```python
import functools

import jax
import jax.numpy as jnp
from jax import lax
from jax.experimental import pallas as pl
from jax.experimental.pallas import tpu as pltpu
from jax.sharding import PartitionSpec as P

REACH = 2
NEAR_LON = 5
UNROLL = 4
VMEM_BYTES = 12 * 1024 * 1024
MOST_BYTES = 60 * 1024 * 1024
TABLE_BYTES = 20 * 1024 * 1024
QUICK = 2
FIELDS = ((0, 0), (0, 128), (8, 0), (8, 128), (16, 0))


def permute_lon(value, steps):
    count = lax.axis_size("lon")
    return lax.ppermute(value, "lon", [(i, (i + steps) % count) for i in range(count)])


def swap_lon(value):
    count = lax.axis_size("lon")
    return lax.ppermute(value, "lon", [(i, i ^ 1) for i in range(count)])


def permute_lat(value, steps):
    count = lax.axis_size("lat")
    pairs = [(i, i + steps) for i in range(count) if 0 <= i + steps < count]
    return lax.ppermute(value, "lat", pairs)


def in_smem():
    return pl.BlockSpec(memory_space=pltpu.SMEM)


def in_place():
    return pl.BlockSpec(memory_space=pl.ANY)


def for_rows(count, one):
    def some(g, carry):
        stores = []
        for u in range(UNROLL):
            stores += one(g * UNROLL + u)
        for ref, at, value in stores:
            ref[at] = value.astype(ref.dtype)
        return carry

    lax.fori_loop(0, count // UNROLL, some, 0)


def growth_kernel(flip_ref, settle_ref, conc_ref, rates_ref, low_ref, high_ref, mat_ref):
    ranks, rows_step = rates_ref.shape[0], conc_ref.shape[0]
    bins, width = conc_ref.shape[1:]

    @pl.when(pl.program_id(0) == 0)
    def _():
        for q in range(ranks):
            spread = jnp.broadcast_to(flip_ref[q : q + 1, :], (bins, 2 * bins))
            turned = pltpu.roll(spread, bins + 1, 1, stride=1, stride_axis=0)
            mat_ref[q * bins : (q + 1) * bins, :] = turned[:, :bins].astype(jnp.bfloat16)

    settle = jnp.broadcast_to(settle_ref[...], (bins, width))
    for r in range(rows_step):
        cells = conc_ref[r]
        product = jnp.dot(mat_ref[...], cells, preferred_element_type=jnp.float32)
        total = -settle * cells.astype(jnp.float32)
        for q in range(ranks):
            total = total + rates_ref[q, r : r + 1, :] * product[q * bins : (q + 1) * bins]
        low_ref[r] = total[: bins // 2]
        high_ref[r] = total[bins // 2 :]


def local_terms(conc, agg_rates, toeplitz, settle):
    rows, bins, width = conc.shape
    ranks = agg_rates.shape[0]
    step = 8
    flipped = jnp.pad(toeplitz[:, ::-1].astype(jnp.float32), ((0, 0), (0, 1)))
    return pl.pallas_call(
        growth_kernel,
        grid=(rows // step,),
        in_specs=[
            pl.BlockSpec((ranks, 2 * bins), lambda i: (0, 0)),
            pl.BlockSpec((bins, 1), lambda i: (0, 0)),
            pl.BlockSpec((step, bins, width), lambda i: (i, 0, 0)),
            pl.BlockSpec((ranks, step, width), lambda i: (0, i, 0)),
        ],
        out_specs=[pl.BlockSpec((step, bins // 2, width), lambda i: (i, 0, 0))] * 2,
        out_shape=[jax.ShapeDtypeStruct((rows, bins // 2, width), jnp.float32)] * 2,
        scratch_shapes=[pltpu.VMEM((ranks * bins, bins), jnp.bfloat16)],
        compiler_params=pltpu.CompilerParams(vmem_limit_bytes=VMEM_BYTES),
        cost_estimate=pl.CostEstimate(
            flops=2 * ranks * bins * bins * rows * width, bytes_accessed=8 * conc.size, transcendentals=0
        ),
        name="growth",
    )(flipped, settle[:, None], conc, agg_rates)


def messages_kernel(
    conc_ref, owner_hbm, source_hbm, weight_hbm, count_hbm, low_ref, high_ref, meta_ref,
    owner_ref, source_ref, weight_ref, count_ref, sems,
):
    rows = conc_ref.shape[0]
    half = low_ref.shape[1]
    entries = owner_ref.shape[0]
    small = [
        pltpu.make_async_copy(hbm, ref, sems.at[2 + i])
        for i, (hbm, ref) in enumerate(
            ((owner_hbm, owner_ref), (source_hbm, source_ref), (weight_hbm, weight_ref), (count_hbm, count_ref))
        )
    ]
    large = [
        pltpu.make_async_copy(conc_ref.at[:, pl.ds(i * half, half), :], ref.at[pl.ds(0, rows)], sems.at[i])
        for i, ref in enumerate((low_ref, high_ref))
    ]
    for copy in small + large:
        copy.start()
    meta_ref[...] = jnp.zeros(meta_ref.shape, meta_ref.dtype)
    for copy in small:
        copy.wait()
    wide = lambda value: value.astype(jnp.float32)
    entry = lax.broadcasted_iota(jnp.int32, owner_ref.shape, 0)
    live = jnp.where(entry < count_ref[...], weight_ref[...], 0.0)
    top = live.astype(jnp.bfloat16)
    middle = (live - wide(top)).astype(jnp.bfloat16)
    bottom = (live - wide(top) - wide(middle)).astype(jnp.bfloat16)
    fields = (wide(owner_ref[...]), wide(source_ref[...]), wide(top), wide(middle), wide(bottom))
    for field, (at, lane) in zip(fields, FIELDS):
        meta_ref[0, at : at + entries, lane : lane + rows] = field.astype(jnp.bfloat16)
    low_ref[rows] = meta_ref[0]
    high_ref[rows] = meta_ref[0]
    for copy in large:
        copy.wait()


def messages(conc, owner, source, weight, count):
    rows, bins, width = conc.shape
    half = bins // 2
    return pl.pallas_call(
        messages_kernel,
        in_specs=[in_place()] * 5,
        out_specs=[pl.BlockSpec(memory_space=pltpu.VMEM)] * 3,
        out_shape=[
            jax.ShapeDtypeStruct((rows + 1, half, width), conc.dtype),
            jax.ShapeDtypeStruct((rows + 1, half, width), conc.dtype),
            jax.ShapeDtypeStruct((1, half, width), conc.dtype),
        ],
        scratch_shapes=[pltpu.VMEM(small.shape, small.dtype) for small in (owner, source, weight, count)]
        + [pltpu.SemaphoreType.DMA((6,))],
        compiler_params=pltpu.CompilerParams(vmem_limit_bytes=MOST_BYTES),
        cost_estimate=pl.CostEstimate(flops=0, bytes_accessed=4 * conc.size, transcendentals=0),
        name="messages",
    )(conc, owner, source, weight, count)


def lat_slots(rows, group, lat_step, lon_step, odd):
    toward = 1.0 - 2.0 * odd
    slot = jnp.where(
        lon_step == 0.0,
        0.0,
        jnp.where(lon_step == 2.0, 2.0, jnp.where(lon_step == -2.0, 3.0, jnp.where(lon_step == toward, 1.0, 5.0 - odd))),
    )
    return lat_step == 1.0 - group, slot * rows


def lon_slots(rows, group, lat_step, lon_step, odd):
    toward = 1.0 - 2.0 * odd
    lon_from = 2.0 * (group - 1.0) + lon_step
    slot = jnp.where(lon_from == 0.0, 0.0, 3.0) + lat_step + 1.0
    return (lon_from == 0.0) | (lon_from == toward), slot * rows


def decode(slots, rows, entries, odd, meta_ref, index_ref, weight_ref):
    for g in range(3):
        owner, source, top, middle, bottom = [
            meta_ref[g, at : at + entries, lane : lane + 128].astype(jnp.float32) for at, lane in FIELDS
        ]
        weight = top + middle + bottom
        band = jnp.where(owner >= NEAR_LON, 1.0, 0.0) + jnp.where(owner >= 2 * NEAR_LON, 1.0, 0.0)
        here, base = slots(rows, float(g), band - 1.0, owner - NEAR_LON * band - REACH, odd)
        here = jnp.where(here & (weight != 0.0), 1.0, 0.0)
        index = base + source
        packed = [[jnp.zeros((1, 128), jnp.float32)] * 2 for _ in range(entries)]
        rank = jnp.zeros((1, 128), jnp.float32)
        for k in range(entries):
            taken = here[k : k + 1]
            for place in range(k + 1):
                spot = (taken > 0.0) & (rank == place)
                packed[place] = [
                    jnp.where(spot, index[k : k + 1], packed[place][0]),
                    jnp.where(spot, weight[k : k + 1], packed[place][1]),
                ]
            rank = rank + taken
        for place in range(entries):
            at = g * entries + place
            index_ref[at : at + 1, :] = packed[place][0].astype(jnp.int32)
            weight_ref[at : at + 1, :] = packed[place][1]
        at = 3 * entries + g
        index_ref[at : at + 1, :] = rank.astype(jnp.int32)


def read_metas(asked, meta_ref, sems, first):
    return [
        pltpu.make_async_copy(ref.at[pl.ds(ref.shape[0] - 1, 1)], meta_ref.at[pl.ds(g, 1)], sems.at[first + g])
        for g, ref in enumerate(asked)
    ]


def decode_kernel(slots, rows, entries, odd_ref, south_ref, own_ref, north_ref, index_ref, weight_ref, meta_ref, sems):
    copies = read_metas((south_ref, own_ref, north_ref), meta_ref, sems, 0)
    for copy in copies:
        copy.start()
    for copy in copies:
        copy.wait()
    decode(slots, rows, entries, odd_ref[0].astype(jnp.float32), meta_ref, index_ref, weight_ref)


def decoded(odd, asked, slots, rows, half, entries):
    width = asked[1].shape[2]
    vectors = -(-3 * (entries + 1) // 8) * 8
    return pl.pallas_call(
        functools.partial(decode_kernel, slots, rows, entries),
        in_specs=[in_smem()] + [in_place()] * 3,
        out_specs=[pl.BlockSpec(memory_space=pltpu.VMEM)] * 2,
        out_shape=[
            jax.ShapeDtypeStruct((vectors, 128), jnp.int32),
            jax.ShapeDtypeStruct((vectors, 128), jnp.float32),
        ],
        scratch_shapes=[pltpu.VMEM((3, half, width), jnp.bfloat16), pltpu.SemaphoreType.DMA((3,))],
        compiler_params=pltpu.CompilerParams(vmem_limit_bytes=VMEM_BYTES),
        cost_estimate=pl.CostEstimate(flops=0, bytes_accessed=6 * half * width, transcendentals=0),
        name="decode",
    )(odd, *asked)


def table_copies(bases, rows, sources, table, sems):
    half = table.shape[1]
    return [
        pltpu.make_async_copy(
            source.at[pl.ds(0, rows), pl.ds(base, half), :], table.at[pl.ds(i * rows, rows)], sems.at[i]
        )
        for i, (source, base) in enumerate(zip(sources, bases))
    ]


def add_terms(rows, entries, index_ref, weight_ref, table, outs):
    half, width = table.shape[1:]
    for group, out in enumerate(outs):

        def some(g, carry, group=group, out=out):
            def sums(terms):
                totals = []
                for u in range(UNROLL):
                    r = g * UNROLL + u
                    total = jnp.zeros((half, width), jnp.float32)
                    for k in range(terms):
                        row = group * entries + k
                        total = total + weight_ref[row, r] * table[index_ref[row, r]].astype(jnp.float32)
                    totals.append(total)
                for u in range(UNROLL):
                    out[g * UNROLL + u] = totals[u].astype(out.dtype)

            most = index_ref[3 * entries + group, g * UNROLL]
            for u in range(1, UNROLL):
                most = jnp.maximum(most, index_ref[3 * entries + group, g * UNROLL + u])
            sums(min(QUICK, entries))

            @pl.when(most > QUICK)
            def _():
                sums(entries)

            return carry

        lax.fori_loop(0, rows // UNROLL, some, 0)


def lat_sums_kernel(bases, entries, odd_ref, index_ref, weight_ref, *refs):
    tables = len(bases)
    sources, outs = refs[:tables], refs[tables : tables + 3]
    table, sems = refs[tables + 3 :]
    rows = table.shape[0] // tables
    copies = table_copies(bases, rows, sources, table, sems)
    even = odd_ref[0] == 0
    for copy in copies[:-2]:
        copy.start()
    pl.when(even)(copies[-1].start)
    pl.when(jnp.logical_not(even))(copies[-2].start)
    for copy in copies[:-2]:
        copy.wait()
    pl.when(even)(copies[-1].wait)
    pl.when(jnp.logical_not(even))(copies[-2].wait)
    add_terms(rows, entries, index_ref, weight_ref, table, outs)


def lon_sums_kernel(bases, slots, entries, odd_ref, *refs):
    tables = len(bases)
    asked, sources, outs = refs[:3], refs[3 : 3 + tables], refs[3 + tables : 6 + tables]
    table, meta_ref, index_vec, weight_vec, index_ref, weight_ref, sems = refs[6 + tables :]
    rows = table.shape[0] // tables
    metas = read_metas(asked, meta_ref, sems, tables)
    copies = table_copies(bases, rows, sources, table, sems)
    for copy in metas + copies:
        copy.start()
    for copy in metas:
        copy.wait()
    decode(slots, rows, entries, odd_ref[0].astype(jnp.float32), meta_ref, index_vec, weight_vec)
    to_scalar = [
        pltpu.make_async_copy(index_vec, index_ref, sems.at[tables + 3]),
        pltpu.make_async_copy(weight_vec, weight_ref, sems.at[tables + 4]),
    ]
    for copy in to_scalar:
        copy.start()
    for copy in to_scalar + copies:
        copy.wait()
    add_terms(rows, entries, index_ref, weight_ref, table, outs)


def sums_call(kernel, operands, smem, sources, scratch, rows, half, entries, name):
    tables = len(sources)
    width = sources[0][0].shape[2]
    return pl.pallas_call(
        kernel,
        in_specs=[in_smem()] * smem + [in_place()] * (len(operands) - smem + tables),
        out_specs=[pl.BlockSpec(memory_space=pltpu.VMEM)] * 3,
        out_shape=[
            jax.ShapeDtypeStruct((rows, half, width), dtype) for dtype in (jnp.bfloat16, jnp.float32, jnp.bfloat16)
        ],
        scratch_shapes=[pltpu.VMEM((tables * rows, half, width), jnp.bfloat16)] + scratch,
        compiler_params=pltpu.CompilerParams(vmem_limit_bytes=TABLE_BYTES),
        cost_estimate=pl.CostEstimate(
            flops=6 * rows * entries * half * width,
            bytes_accessed=2 * (tables + 3) * rows * half * width,
            transcendentals=0,
        ),
        name=name,
    )(*operands, *[source for source, _ in sources])


def lat_sums(odd, terms, sources, rows, half, entries):
    kernel = functools.partial(lat_sums_kernel, tuple(base for _, base in sources), entries)
    scratch = [pltpu.SemaphoreType.DMA((len(sources),))]
    return sums_call(kernel, [odd, *terms], 3, sources, scratch, rows, half, entries, "lat_sums")


def lon_sums(odd, asked, slots, sources, rows, half, entries):
    kernel = functools.partial(lon_sums_kernel, tuple(base for _, base in sources), slots, entries)
    vectors = -(-3 * (entries + 1) // 8) * 8
    scratch = [pltpu.VMEM((3, half, asked[1].shape[2]), jnp.bfloat16)]
    scratch += [space((vectors, 128), dtype) for space in (pltpu.VMEM, pltpu.SMEM) for dtype in (jnp.int32, jnp.float32)]
    scratch += [pltpu.SemaphoreType.DMA((len(sources) + 5,))]
    return sums_call(kernel, [odd, *asked], 1, sources, scratch, rows, half, entries, "lon_sums")


def edges_kernel(*refs):
    first_ref, last_ref = refs[-2:]
    rows, half = refs[0].shape[:2]
    per = 128 // 8
    lane = lax.broadcasted_iota(jnp.int32, (half, 128), 1)
    for side, out_ref in ((0, first_ref), (1, last_ref)):
        parts = refs[3 * side : 3 * side + 3]
        for j in range(rows // per):
            packed = jnp.zeros((half, 128), jnp.float32)
            for i in range(per):
                r = j * per + i
                cells = parts[0][r] + parts[1][r].astype(jnp.float32) + parts[2][r].astype(jnp.float32)
                at = 8 * i + 3 * (1 - side)
                spot = (lane >= at) & (lane < at + 3)
                packed = jnp.where(spot, pltpu.roll(cells, 8 * i + 3, 1), packed)
            out_ref[j] = packed.astype(out_ref.dtype)


def edges(parts):
    rows, half, width = parts[0].shape
    specs = [
        pl.BlockSpec((rows, half, 128), lambda t, at=at: (0, 0, at)) for at in (0, width // 128 - 1) for _ in parts
    ]
    packed = (rows // 16, half, 128)
    return pl.pallas_call(
        edges_kernel,
        grid=(1,),
        in_specs=specs,
        out_specs=[pl.BlockSpec(packed, lambda t: (0, 0, 0))] * 2,
        out_shape=[jax.ShapeDtypeStruct(packed, jnp.bfloat16)] * 2,
        compiler_params=pltpu.CompilerParams(vmem_limit_bytes=VMEM_BYTES),
        cost_estimate=pl.CostEstimate(flops=8 * half * 256 * rows, bytes_accessed=16 * half * 256 * rows, transcendentals=0),
        name="edges",
    )(*parts, *parts)


def combine_kernel(own, a, b, out_ref):
    for r in range(own.shape[0]):
        out_ref[r] = own[r] + a[r].astype(jnp.float32) + b[r].astype(jnp.float32)


def combine(parts):
    rows, half, width = parts[0].shape
    step = 8
    block = pl.BlockSpec((step, half, width), lambda t: (t, 0, 0))
    return pl.pallas_call(
        combine_kernel,
        grid=(rows // step,),
        in_specs=[block] * 3,
        out_specs=block,
        out_shape=jax.ShapeDtypeStruct((rows, half, width), jnp.float32),
        compiler_params=pltpu.CompilerParams(vmem_limit_bytes=VMEM_BYTES),
        cost_estimate=pl.CostEstimate(
            flops=2 * rows * half * width, bytes_accessed=12 * rows * half * width, transcendentals=0
        ),
        name="combine",
    )(*parts)


def shifted_by(row, edge, amount, lane):
    count = len(row)
    if amount == 0:
        return row
    if amount > 0:
        row = row[:-1] + [jnp.where(lane >= 128 - amount, edge, row[-1])]
        turned = [pltpu.roll(tile, amount, 1) for tile in row]
        return [jnp.where(lane < amount, turned[t - 1], turned[t]) for t in range(count)]
    row = [jnp.where(lane < -amount, edge, row[0])] + row[1:]
    turned = [pltpu.roll(tile, 128 + amount, 1) for tile in row]
    return [jnp.where(lane >= 128 + amount, turned[(t + 1) % count], turned[t]) for t in range(count)]


def edge_tile(west_ref, east_ref, r):
    per = 128 // 8
    both = west_ref[r // per].astype(jnp.float32) + east_ref[r // per].astype(jnp.float32)
    return pltpu.roll(both, (125 - 8 * (r % per)) % 128, 1)


def rows_kernel(offset_ref, *refs):
    outs = refs[-2:]
    half, width = refs[0].shape[1:]
    lane = lax.broadcasted_iota(jnp.int32, (half, 128), 1)
    spots = [slice(128 * t, 128 * t + 128) for t in range(width // 128)]
    end = offset_ref.shape[0] - 1
    for side, r in enumerate((0, end)):
        for amount in range(-REACH, REACH + 1):

            @pl.when(offset_ref[r] == amount)
            def _(side=side, r=r, amount=amount):
                for h in range(2):
                    remap_ref, west_ref, east_ref = refs[4 * h + side], refs[4 * h + 2], refs[4 * h + 3]
                    row = [remap_ref[0, :, at] for at in spots]
                    row = shifted_by(row, edge_tile(west_ref, east_ref, r), amount, lane)
                    for at, tile in zip(spots, row):
                        outs[side][0, h * half : (h + 1) * half, at] = tile.astype(outs[side].dtype)


def outer_rows(offset, halves):
    rows, half, width = halves[0][0].shape
    row = lambda at: pl.BlockSpec((1, half, width), lambda t: (at, 0, 0))
    whole = pl.BlockSpec(halves[0][1].shape, lambda t: (0, 0, 0))
    out = pl.BlockSpec((1, 2 * half, width), lambda t: (0, 0, 0))
    operands = [array for remapped, west, east in halves for array in (remapped, remapped, west, east)]
    return pl.pallas_call(
        rows_kernel,
        grid=(1,),
        in_specs=[in_smem()] + [row(0), row(rows - 1), whole, whole] * 2,
        out_specs=[out, out],
        out_shape=[jax.ShapeDtypeStruct((1, 2 * half, width), jnp.bfloat16)] * 2,
        compiler_params=pltpu.CompilerParams(vmem_limit_bytes=VMEM_BYTES),
        cost_estimate=pl.CostEstimate(flops=40 * half * width, bytes_accessed=24 * half * width, transcendentals=0),
        name="outer_rows",
    )(offset, *operands)


def final_kernel(offset_ref, remap_ref, west_ref, east_ref, kappa_ref, local_ref, *refs):
    out_ref, outer_ref, edge_ref = refs[-3:]
    rows, bins, width = remap_ref.shape
    count = width // 128
    lane = lax.broadcasted_iota(jnp.int32, (8, 128), 1)
    spots = [slice(128 * t, 128 * t + 128) for t in range(count)]
    for r in range(rows):
        edge_ref[r] = edge_tile(west_ref, east_ref, r)

    def moved(row, edge, amount):
        row = [jnp.where(lane < -amount, edge, row[0])] + row[1:]
        row = row[:-1] + [jnp.where(lane >= 128 - amount, edge, row[-1])]
        turned = [pltpu.roll(tile, (amount + 128) & 127, 1) for tile in row]
        before, after = lane < amount, lane >= 128 + amount
        return [
            jnp.where(before, turned[t - 1], jnp.where(after, turned[(t + 1) % count], turned[t])) for t in range(count)
        ]

    pieces = [slice(8 * b, 8 * b + 8) for b in range(bins // 8)]
    before, now, base = {}, {}, {}
    stores = []
    for r in range(rows):
        amount = offset_ref[r]
        kappa = [kappa_ref[r, :, spot] for spot in spots]
        above = [kappa_ref[max(r - 1, 0), :, spot] for spot in spots]
        for at in pieces:
            row = [remap_ref[r, at, spot] for spot in spots]
            edge = edge_ref[r, at]
            center = moved(row, edge, amount)
            east = moved(row, edge, amount - 1)
            west = moved(row, edge, amount + 1)
            key = at.start
            fresh = []
            for t, spot in enumerate(spots):
                around = kappa[t] * (east[t] + west[t] - 4.0 * center[t])
                fresh.append(local_ref[r, at, spot] + center[t] + around)
                if r == 1:
                    stores.append((r - 1, at, spot, base[key][t] + above[t] * center[t]))
                elif r:
                    stores.append((r - 1, at, spot, base[key][t] + above[t] * (before[key][t] + center[t])))
            if r:
                before[key] = now[key]
            now[key], base[key] = center, fresh
        if r % 2:
            for which, at, spot, value in stores:
                if which:
                    out_ref[which, at, spot] = value
                else:
                    outer_ref[0, at, spot] = value
            stores = []
    for at in pieces:
        for t, spot in enumerate(spots):
            outer_ref[1, at, spot] = base[at.start][t] + kappa_ref[rows - 1, :, spot] * before[at.start][t]


def final(offset, remapped, west, east, kappa, local, which, earlier):
    rows, half, width = remapped.shape
    steps = 2
    tile = half // steps
    block = pl.BlockSpec((rows, tile, width), lambda t: (0, t, 0))
    packed = pl.BlockSpec((west.shape[0], tile, 128), lambda t: (0, t, 0))
    return pl.pallas_call(
        final_kernel,
        grid=(steps,),
        in_specs=[in_smem(), block, packed, packed, pl.BlockSpec(kappa.shape, lambda t: (0, 0, 0)), block]
        + [in_place()] * len(earlier),
        out_specs=[
            pl.BlockSpec((rows, tile, width), lambda t: (0, which * steps + t, 0)),
            pl.BlockSpec((2, tile, width), lambda t: (0, t, 0)),
        ],
        out_shape=[
            jax.ShapeDtypeStruct((rows, 2 * half, width), jnp.float32),
            jax.ShapeDtypeStruct((2, half, width), jnp.float32),
        ],
        scratch_shapes=[pltpu.VMEM((rows, tile, 128), jnp.float32)],
        input_output_aliases={6: 0} if earlier else {},
        compiler_params=pltpu.CompilerParams(vmem_limit_bytes=VMEM_BYTES),
        cost_estimate=pl.CostEstimate(flops=30 * remapped.size, bytes_accessed=40 * remapped.size, transcendentals=0),
        name="final",
    )(offset, remapped, west, east, kappa, local, *earlier)


def halo_kernel(before_ref, after_ref, kappa_ref, outer0_ref, outer1_ref, _, out_ref, sums_ref, sems):
    rows = out_ref.shape[0]
    half = outer0_ref.shape[1]
    copies = []
    for side, (value_ref, at) in enumerate(((before_ref, 0), (after_ref, rows - 1))):
        for h, outer_ref in enumerate((outer0_ref, outer1_ref)):
            bins = slice(h * half, (h + 1) * half)
            sums_ref[side, bins] = outer_ref[side] + kappa_ref[at] * value_ref[0, bins].astype(jnp.float32)
        copy = pltpu.make_async_copy(sums_ref.at[pl.ds(side, 1)], out_ref.at[pl.ds(at, 1)], sems.at[side])
        copy.start()
        copies.append(copy)
    for copy in copies:
        copy.wait()


def add_halo(before, after, kappa, outers, partial):
    vmem = pl.BlockSpec(memory_space=pltpu.VMEM)
    sides, half, width = outers[0].shape
    return pl.pallas_call(
        halo_kernel,
        in_specs=[vmem] * 5 + [in_place()],
        out_specs=in_place(),
        out_shape=jax.ShapeDtypeStruct(partial.shape, jnp.float32),
        scratch_shapes=[pltpu.VMEM((sides, 2 * half, width), jnp.float32), pltpu.SemaphoreType.DMA((2,))],
        input_output_aliases={5: 0},
        compiler_params=pltpu.CompilerParams(vmem_limit_bytes=VMEM_BYTES),
        cost_estimate=pl.CostEstimate(flops=4 * partial.size // 16, bytes_accessed=partial.size, transcendentals=0),
        name="add_halo",
    )(before, after, kappa, *outers, partial)


def body(
    conc,
    dep_owner,
    dep_row,
    dep_weight,
    dep_count,
    zonal_offset,
    agg_rates,
    toeplitz,
    settle,
    kappa,
):
    rows, bins, width = conc.shape
    entries = dep_owner.shape[2]
    odd = (lax.axis_index("lon") % 2).astype(jnp.int32).reshape(1)
    half = bins // 2
    low, high, meta = messages(conc, dep_owner[0].T, dep_row[0].T, dep_weight[0].T, dep_count)
    south = permute_lat(high, 1)
    north = permute_lat(high, -1)
    ahead = permute_lon(low, -2)
    behind = permute_lon(low, 2)
    beside = swap_lon(conc)
    rates, meta = lax.optimization_barrier((agg_rates, meta))
    local0, local1 = local_terms(conc, rates, toeplitz, settle)
    terms = decoded(odd, [south, meta, north], lat_slots, rows, half, entries)
    south, north, local0, terms = lax.optimization_barrier((south, north, local0, terms))

    to_west, own1, to_east = lon_sums(
        odd,
        [behind, meta, ahead],
        lon_slots,
        [(south, 0), (conc, half), (north, 0), (swap_lon(south), 0), (beside, half), (swap_lon(north), 0)],
        rows,
        half,
        entries,
    )
    from_west, from_east = permute_lon(to_east, 2), permute_lon(to_west, -2)
    own1, odd = lax.optimization_barrier((own1, odd))
    parts1 = [own1, from_west, from_east]

    down, own0, up = lat_sums(
        odd,
        terms,
        [(conc, 0), (beside, 0), (ahead, 0), (behind, 0), (swap_lon(ahead), 0), (swap_lon(behind), 0)],
        rows,
        half,
        entries,
    )
    parts0 = [own0, permute_lat(up, 1), permute_lat(down, -1)]

    kappa = kappa[:, None, :]

    def with_edges(parts):
        first, last = edges(parts)
        return combine(parts), permute_lon(last, 1), permute_lon(first, -1)

    half1, half0 = with_edges(parts1), with_edges(parts0)
    partial, outer1 = final(zonal_offset, *half1, kappa, local1, 1, [])
    offset, outer1 = lax.optimization_barrier((zonal_offset, outer1))
    top_row, end_row = outer_rows(offset, [half0, half1])
    before, after = permute_lat(end_row, 1), permute_lat(top_row, -1)
    partial, outer0 = final(zonal_offset, *half0, kappa, local0, 0, [partial])
    return add_halo(before, after, kappa, [outer0, outer1], partial)


def solution(mesh):
    return jax.shard_map(
        body,
        mesh=mesh,
        in_specs=(
            P("lat", None, "lon"),
            P("lon", "lat", None),
            P("lon", "lat", None),
            P("lon", "lat", None),
            P("lon", "lat"),
            P("lat"),
            P(None, "lat", "lon"),
            P(),
            P(),
            P("lat", "lon"),
        ),
        out_specs=P("lat", None, "lon"),
        check_vma=False,
    )
```

```python
import functools

import jax
import jax.numpy as jnp
from jax import lax
from jax.experimental import pallas as pl
from jax.experimental.pallas import tpu as pltpu
from jax.sharding import PartitionSpec as P

REACH = 2
NEAR_LON = 5
UNROLL = 4
VMEM_BYTES = 12 * 1024 * 1024
MOST_BYTES = 60 * 1024 * 1024
TABLE_BYTES = 20 * 1024 * 1024
QUICK = 2
FIELDS = ((0, 0), (0, 128), (8, 0), (8, 128), (16, 0))


def permute_lon(value, steps):
    count = lax.axis_size("lon")
    return lax.ppermute(value, "lon", [(i, (i + steps) % count) for i in range(count)])


def swap_lon(value):
    count = lax.axis_size("lon")
    return lax.ppermute(value, "lon", [(i, i ^ 1) for i in range(count)])


def permute_lat(value, steps):
    count = lax.axis_size("lat")
    pairs = [(i, i + steps) for i in range(count) if 0 <= i + steps < count]
    return lax.ppermute(value, "lat", pairs)


def in_smem():
    return pl.BlockSpec(memory_space=pltpu.SMEM)


def in_place():
    return pl.BlockSpec(memory_space=pl.ANY)


def for_rows(count, one):
    def some(g, carry):
        stores = []
        for u in range(UNROLL):
            stores += one(g * UNROLL + u)
        for ref, at, value in stores:
            ref[at] = value.astype(ref.dtype)
        return carry

    lax.fori_loop(0, count // UNROLL, some, 0)


def growth_kernel(flip_ref, settle_ref, conc_ref, rates_ref, low_ref, high_ref, mat_ref):
    ranks, rows_step = rates_ref.shape[0], conc_ref.shape[0]
    bins, width = conc_ref.shape[1:]

    @pl.when(pl.program_id(0) == 0)
    def _():
        for q in range(ranks):
            spread = jnp.broadcast_to(flip_ref[q : q + 1, :], (bins, 2 * bins))
            turned = pltpu.roll(spread, bins + 1, 1, stride=1, stride_axis=0)
            mat_ref[q * bins : (q + 1) * bins, :] = turned[:, :bins].astype(jnp.bfloat16)

    settle = jnp.broadcast_to(settle_ref[...], (bins, width))
    for r in range(rows_step):
        cells = conc_ref[r]
        product = jnp.dot(mat_ref[...], cells, preferred_element_type=jnp.float32)
        total = -settle * cells.astype(jnp.float32)
        for q in range(ranks):
            total = total + rates_ref[q, r : r + 1, :] * product[q * bins : (q + 1) * bins]
        low_ref[r] = total[: bins // 2]
        high_ref[r] = total[bins // 2 :]


def local_terms(conc, agg_rates, toeplitz, settle):
    rows, bins, width = conc.shape
    ranks = agg_rates.shape[0]
    step = 8
    flipped = jnp.pad(toeplitz[:, ::-1].astype(jnp.float32), ((0, 0), (0, 1)))
    return pl.pallas_call(
        growth_kernel,
        grid=(rows // step,),
        in_specs=[
            pl.BlockSpec((ranks, 2 * bins), lambda i: (0, 0)),
            pl.BlockSpec((bins, 1), lambda i: (0, 0)),
            pl.BlockSpec((step, bins, width), lambda i: (i, 0, 0)),
            pl.BlockSpec((ranks, step, width), lambda i: (0, i, 0)),
        ],
        out_specs=[pl.BlockSpec((step, bins // 2, width), lambda i: (i, 0, 0))] * 2,
        out_shape=[jax.ShapeDtypeStruct((rows, bins // 2, width), jnp.float32)] * 2,
        scratch_shapes=[pltpu.VMEM((ranks * bins, bins), jnp.bfloat16)],
        compiler_params=pltpu.CompilerParams(vmem_limit_bytes=VMEM_BYTES),
        cost_estimate=pl.CostEstimate(
            flops=2 * ranks * bins * bins * rows * width, bytes_accessed=8 * conc.size, transcendentals=0
        ),
        name="growth",
    )(flipped, settle[:, None], conc, agg_rates)


def messages_kernel(
    conc_ref, owner_hbm, source_hbm, weight_hbm, count_hbm, low_ref, high_ref, meta_ref,
    owner_ref, source_ref, weight_ref, count_ref, sems,
):
    rows = conc_ref.shape[0]
    half = low_ref.shape[1]
    entries = owner_ref.shape[0]
    small = [
        pltpu.make_async_copy(hbm, ref, sems.at[2 + i])
        for i, (hbm, ref) in enumerate(
            ((owner_hbm, owner_ref), (source_hbm, source_ref), (weight_hbm, weight_ref), (count_hbm, count_ref))
        )
    ]
    large = [
        pltpu.make_async_copy(conc_ref.at[:, pl.ds(i * half, half), :], ref.at[pl.ds(0, rows)], sems.at[i])
        for i, ref in enumerate((low_ref, high_ref))
    ]
    for copy in small + large:
        copy.start()
    meta_ref[...] = jnp.zeros(meta_ref.shape, meta_ref.dtype)
    for copy in small:
        copy.wait()
    wide = lambda value: value.astype(jnp.float32)
    entry = lax.broadcasted_iota(jnp.int32, owner_ref.shape, 0)
    live = jnp.where(entry < count_ref[...], weight_ref[...], 0.0)
    top = live.astype(jnp.bfloat16)
    middle = (live - wide(top)).astype(jnp.bfloat16)
    bottom = (live - wide(top) - wide(middle)).astype(jnp.bfloat16)
    fields = (wide(owner_ref[...]), wide(source_ref[...]), wide(top), wide(middle), wide(bottom))
    for field, (at, lane) in zip(fields, FIELDS):
        meta_ref[0, at : at + entries, lane : lane + rows] = field.astype(jnp.bfloat16)
    low_ref[rows] = meta_ref[0]
    high_ref[rows] = meta_ref[0]
    for copy in large:
        copy.wait()


def messages(conc, owner, source, weight, count):
    rows, bins, width = conc.shape
    half = bins // 2
    return pl.pallas_call(
        messages_kernel,
        in_specs=[in_place()] * 5,
        out_specs=[pl.BlockSpec(memory_space=pltpu.VMEM)] * 3,
        out_shape=[
            jax.ShapeDtypeStruct((rows + 1, half, width), conc.dtype),
            jax.ShapeDtypeStruct((rows + 1, half, width), conc.dtype),
            jax.ShapeDtypeStruct((1, half, width), conc.dtype),
        ],
        scratch_shapes=[pltpu.VMEM(small.shape, small.dtype) for small in (owner, source, weight, count)]
        + [pltpu.SemaphoreType.DMA((6,))],
        compiler_params=pltpu.CompilerParams(vmem_limit_bytes=MOST_BYTES),
        cost_estimate=pl.CostEstimate(flops=0, bytes_accessed=4 * conc.size, transcendentals=0),
        name="messages",
    )(conc, owner, source, weight, count)


def lat_slots(rows, group, lat_step, lon_step, odd):
    toward = 1.0 - 2.0 * odd
    slot = jnp.where(
        lon_step == 0.0,
        0.0,
        jnp.where(lon_step == 2.0, 2.0, jnp.where(lon_step == -2.0, 3.0, jnp.where(lon_step == toward, 1.0, 5.0 - odd))),
    )
    return lat_step == 1.0 - group, slot * rows


def lon_slots(rows, group, lat_step, lon_step, odd):
    toward = 1.0 - 2.0 * odd
    lon_from = 2.0 * (group - 1.0) + lon_step
    slot = jnp.where(lon_from == 0.0, 0.0, 3.0) + lat_step + 1.0
    return (lon_from == 0.0) | (lon_from == toward), slot * rows


def decode(slots, rows, entries, odd, meta_ref, index_ref, weight_ref):
    for g in range(3):
        owner, source, top, middle, bottom = [
            meta_ref[g, at : at + entries, lane : lane + 128].astype(jnp.float32) for at, lane in FIELDS
        ]
        weight = top + middle + bottom
        band = jnp.where(owner >= NEAR_LON, 1.0, 0.0) + jnp.where(owner >= 2 * NEAR_LON, 1.0, 0.0)
        here, base = slots(rows, float(g), band - 1.0, owner - NEAR_LON * band - REACH, odd)
        here = jnp.where(here & (weight != 0.0), 1.0, 0.0)
        index = base + source
        packed = [[jnp.zeros((1, 128), jnp.float32)] * 2 for _ in range(entries)]
        rank = jnp.zeros((1, 128), jnp.float32)
        for k in range(entries):
            taken = here[k : k + 1]
            for place in range(k + 1):
                spot = (taken > 0.0) & (rank == place)
                packed[place] = [
                    jnp.where(spot, index[k : k + 1], packed[place][0]),
                    jnp.where(spot, weight[k : k + 1], packed[place][1]),
                ]
            rank = rank + taken
        for place in range(entries):
            at = g * entries + place
            index_ref[at : at + 1, :] = packed[place][0].astype(jnp.int32)
            weight_ref[at : at + 1, :] = packed[place][1]
        at = 3 * entries + g
        index_ref[at : at + 1, :] = rank.astype(jnp.int32)


def read_metas(asked, meta_ref, sems, first):
    return [
        pltpu.make_async_copy(ref.at[pl.ds(ref.shape[0] - 1, 1)], meta_ref.at[pl.ds(g, 1)], sems.at[first + g])
        for g, ref in enumerate(asked)
    ]


def decode_kernel(slots, rows, entries, odd_ref, south_ref, own_ref, north_ref, index_ref, weight_ref, meta_ref, sems):
    copies = read_metas((south_ref, own_ref, north_ref), meta_ref, sems, 0)
    for copy in copies:
        copy.start()
    for copy in copies:
        copy.wait()
    decode(slots, rows, entries, odd_ref[0].astype(jnp.float32), meta_ref, index_ref, weight_ref)


def decoded(odd, asked, slots, rows, half, entries):
    width = asked[1].shape[2]
    vectors = -(-3 * (entries + 1) // 8) * 8
    return pl.pallas_call(
        functools.partial(decode_kernel, slots, rows, entries),
        in_specs=[in_smem()] + [in_place()] * 3,
        out_specs=[pl.BlockSpec(memory_space=pltpu.VMEM)] * 2,
        out_shape=[
            jax.ShapeDtypeStruct((vectors, 128), jnp.int32),
            jax.ShapeDtypeStruct((vectors, 128), jnp.float32),
        ],
        scratch_shapes=[pltpu.VMEM((3, half, width), jnp.bfloat16), pltpu.SemaphoreType.DMA((3,))],
        compiler_params=pltpu.CompilerParams(vmem_limit_bytes=VMEM_BYTES),
        cost_estimate=pl.CostEstimate(flops=0, bytes_accessed=6 * half * width, transcendentals=0),
        name="decode",
    )(odd, *asked)


def table_copies(bases, rows, sources, table, sems):
    half = table.shape[1]
    return [
        pltpu.make_async_copy(
            source.at[pl.ds(0, rows), pl.ds(base, half), :], table.at[pl.ds(i * rows, rows)], sems.at[i]
        )
        for i, (source, base) in enumerate(zip(sources, bases))
    ]


def add_terms(rows, entries, index_ref, weight_ref, table, outs):
    half, width = table.shape[1:]
    for group, out in enumerate(outs):

        def some(g, carry, group=group, out=out):
            def sums(terms):
                totals = []
                for u in range(UNROLL):
                    r = g * UNROLL + u
                    total = jnp.zeros((half, width), jnp.float32)
                    for k in range(terms):
                        row = group * entries + k
                        total = total + weight_ref[row, r] * table[index_ref[row, r]].astype(jnp.float32)
                    totals.append(total)
                for u in range(UNROLL):
                    out[g * UNROLL + u] = totals[u].astype(out.dtype)

            most = index_ref[3 * entries + group, g * UNROLL]
            for u in range(1, UNROLL):
                most = jnp.maximum(most, index_ref[3 * entries + group, g * UNROLL + u])
            sums(min(QUICK, entries))

            @pl.when(most > QUICK)
            def _():
                sums(entries)

            return carry

        lax.fori_loop(0, rows // UNROLL, some, 0)


def lat_sums_kernel(bases, entries, odd_ref, index_ref, weight_ref, *refs):
    tables = len(bases)
    sources, outs = refs[:tables], refs[tables : tables + 3]
    table, sems = refs[tables + 3 :]
    rows = table.shape[0] // tables
    copies = table_copies(bases, rows, sources, table, sems)
    even = odd_ref[0] == 0
    for copy in copies[:-2]:
        copy.start()
    pl.when(even)(copies[-1].start)
    pl.when(jnp.logical_not(even))(copies[-2].start)
    for copy in copies[:-2]:
        copy.wait()
    pl.when(even)(copies[-1].wait)
    pl.when(jnp.logical_not(even))(copies[-2].wait)
    add_terms(rows, entries, index_ref, weight_ref, table, outs)


def lon_sums_kernel(bases, slots, entries, odd_ref, *refs):
    tables = len(bases)
    asked, sources, outs = refs[:3], refs[3 : 3 + tables], refs[3 + tables : 6 + tables]
    table, meta_ref, index_vec, weight_vec, index_ref, weight_ref, sems = refs[6 + tables :]
    rows = table.shape[0] // tables
    metas = read_metas(asked, meta_ref, sems, tables)
    copies = table_copies(bases, rows, sources, table, sems)
    for copy in metas + copies:
        copy.start()
    for copy in metas:
        copy.wait()
    decode(slots, rows, entries, odd_ref[0].astype(jnp.float32), meta_ref, index_vec, weight_vec)
    to_scalar = [
        pltpu.make_async_copy(index_vec, index_ref, sems.at[tables + 3]),
        pltpu.make_async_copy(weight_vec, weight_ref, sems.at[tables + 4]),
    ]
    for copy in to_scalar:
        copy.start()
    for copy in to_scalar + copies:
        copy.wait()
    add_terms(rows, entries, index_ref, weight_ref, table, outs)


def sums_call(kernel, operands, smem, sources, scratch, rows, half, entries, name):
    tables = len(sources)
    width = sources[0][0].shape[2]
    return pl.pallas_call(
        kernel,
        in_specs=[in_smem()] * smem + [in_place()] * (len(operands) - smem + tables),
        out_specs=[pl.BlockSpec(memory_space=pltpu.VMEM)] * 3,
        out_shape=[
            jax.ShapeDtypeStruct((rows, half, width), dtype) for dtype in (jnp.bfloat16, jnp.float32, jnp.bfloat16)
        ],
        scratch_shapes=[pltpu.VMEM((tables * rows, half, width), jnp.bfloat16)] + scratch,
        compiler_params=pltpu.CompilerParams(vmem_limit_bytes=TABLE_BYTES),
        cost_estimate=pl.CostEstimate(
            flops=6 * rows * entries * half * width,
            bytes_accessed=2 * (tables + 3) * rows * half * width,
            transcendentals=0,
        ),
        name=name,
    )(*operands, *[source for source, _ in sources])


def lat_sums(odd, terms, sources, rows, half, entries):
    kernel = functools.partial(lat_sums_kernel, tuple(base for _, base in sources), entries)
    scratch = [pltpu.SemaphoreType.DMA((len(sources),))]
    return sums_call(kernel, [odd, *terms], 3, sources, scratch, rows, half, entries, "lat_sums")


def lon_sums(odd, asked, slots, sources, rows, half, entries):
    kernel = functools.partial(lon_sums_kernel, tuple(base for _, base in sources), slots, entries)
    vectors = -(-3 * (entries + 1) // 8) * 8
    scratch = [pltpu.VMEM((3, half, asked[1].shape[2]), jnp.bfloat16)]
    scratch += [space((vectors, 128), dtype) for space in (pltpu.VMEM, pltpu.SMEM) for dtype in (jnp.int32, jnp.float32)]
    scratch += [pltpu.SemaphoreType.DMA((len(sources) + 5,))]
    return sums_call(kernel, [odd, *asked], 1, sources, scratch, rows, half, entries, "lon_sums")


def edges_kernel(*refs):
    first_ref, last_ref = refs[-2:]
    rows, half = refs[0].shape[:2]
    per = 128 // 8
    lane = lax.broadcasted_iota(jnp.int32, (half, 128), 1)
    for side, out_ref in ((0, first_ref), (1, last_ref)):
        parts = refs[3 * side : 3 * side + 3]
        for j in range(rows // per):
            packed = jnp.zeros((half, 128), jnp.float32)
            for i in range(per):
                r = j * per + i
                cells = parts[0][r] + parts[1][r].astype(jnp.float32) + parts[2][r].astype(jnp.float32)
                at = 8 * i + 3 * (1 - side)
                spot = (lane >= at) & (lane < at + 3)
                packed = jnp.where(spot, pltpu.roll(cells, 8 * i + 3, 1), packed)
            out_ref[j] = packed.astype(out_ref.dtype)


def edges(parts):
    rows, half, width = parts[0].shape
    specs = [
        pl.BlockSpec((rows, half, 128), lambda t, at=at: (0, 0, at)) for at in (0, width // 128 - 1) for _ in parts
    ]
    packed = (rows // 16, half, 128)
    return pl.pallas_call(
        edges_kernel,
        grid=(1,),
        in_specs=specs,
        out_specs=[pl.BlockSpec(packed, lambda t: (0, 0, 0))] * 2,
        out_shape=[jax.ShapeDtypeStruct(packed, jnp.bfloat16)] * 2,
        compiler_params=pltpu.CompilerParams(vmem_limit_bytes=VMEM_BYTES),
        cost_estimate=pl.CostEstimate(flops=8 * half * 256 * rows, bytes_accessed=16 * half * 256 * rows, transcendentals=0),
        name="edges",
    )(*parts, *parts)


def combine_kernel(own, a, b, out_ref):
    for r in range(own.shape[0]):
        out_ref[r] = own[r] + a[r].astype(jnp.float32) + b[r].astype(jnp.float32)


def combine(parts):
    rows, half, width = parts[0].shape
    step = 8
    block = pl.BlockSpec((step, half, width), lambda t: (t, 0, 0))
    return pl.pallas_call(
        combine_kernel,
        grid=(rows // step,),
        in_specs=[block] * 3,
        out_specs=block,
        out_shape=jax.ShapeDtypeStruct((rows, half, width), jnp.float32),
        compiler_params=pltpu.CompilerParams(vmem_limit_bytes=VMEM_BYTES),
        cost_estimate=pl.CostEstimate(
            flops=2 * rows * half * width, bytes_accessed=12 * rows * half * width, transcendentals=0
        ),
        name="combine",
    )(*parts)


def shifted_by(row, edge, amount, lane):
    count = len(row)
    if amount == 0:
        return row
    if amount > 0:
        row = row[:-1] + [jnp.where(lane >= 128 - amount, edge, row[-1])]
        turned = [pltpu.roll(tile, amount, 1) for tile in row]
        return [jnp.where(lane < amount, turned[t - 1], turned[t]) for t in range(count)]
    row = [jnp.where(lane < -amount, edge, row[0])] + row[1:]
    turned = [pltpu.roll(tile, 128 + amount, 1) for tile in row]
    return [jnp.where(lane >= 128 + amount, turned[(t + 1) % count], turned[t]) for t in range(count)]


def edge_tile(west_ref, east_ref, r):
    per = 128 // 8
    both = west_ref[r // per].astype(jnp.float32) + east_ref[r // per].astype(jnp.float32)
    return pltpu.roll(both, (125 - 8 * (r % per)) % 128, 1)


def rows_kernel(offset_ref, *refs):
    outs = refs[-2:]
    half, width = refs[0].shape[1:]
    lane = lax.broadcasted_iota(jnp.int32, (half, 128), 1)
    spots = [slice(128 * t, 128 * t + 128) for t in range(width // 128)]
    end = offset_ref.shape[0] - 1
    for side, r in enumerate((0, end)):
        for amount in range(-REACH, REACH + 1):

            @pl.when(offset_ref[r] == amount)
            def _(side=side, r=r, amount=amount):
                for h in range(2):
                    remap_ref, west_ref, east_ref = refs[4 * h + side], refs[4 * h + 2], refs[4 * h + 3]
                    row = [remap_ref[0, :, at] for at in spots]
                    row = shifted_by(row, edge_tile(west_ref, east_ref, r), amount, lane)
                    for at, tile in zip(spots, row):
                        outs[side][0, h * half : (h + 1) * half, at] = tile.astype(outs[side].dtype)


def outer_rows(offset, halves):
    rows, half, width = halves[0][0].shape
    row = lambda at: pl.BlockSpec((1, half, width), lambda t: (at, 0, 0))
    whole = pl.BlockSpec(halves[0][1].shape, lambda t: (0, 0, 0))
    out = pl.BlockSpec((1, 2 * half, width), lambda t: (0, 0, 0))
    operands = [array for remapped, west, east in halves for array in (remapped, remapped, west, east)]
    return pl.pallas_call(
        rows_kernel,
        grid=(1,),
        in_specs=[in_smem()] + [row(0), row(rows - 1), whole, whole] * 2,
        out_specs=[out, out],
        out_shape=[jax.ShapeDtypeStruct((1, 2 * half, width), jnp.bfloat16)] * 2,
        compiler_params=pltpu.CompilerParams(vmem_limit_bytes=VMEM_BYTES),
        cost_estimate=pl.CostEstimate(flops=40 * half * width, bytes_accessed=24 * half * width, transcendentals=0),
        name="outer_rows",
    )(offset, *operands)


def final_kernel(offset_ref, remap_ref, west_ref, east_ref, kappa_ref, local_ref, *refs):
    out_ref, outer_ref, edge_ref = refs[-3:]
    rows, bins, width = remap_ref.shape
    count = width // 128
    lane = lax.broadcasted_iota(jnp.int32, (8, 128), 1)
    spots = [slice(128 * t, 128 * t + 128) for t in range(count)]
    for r in range(rows):
        edge_ref[r] = edge_tile(west_ref, east_ref, r)

    def moved(row, edge, amount):
        row = [jnp.where(lane < -amount, edge, row[0])] + row[1:]
        row = row[:-1] + [jnp.where(lane >= 128 - amount, edge, row[-1])]
        turned = [pltpu.roll(tile, (amount + 128) & 127, 1) for tile in row]
        before, after = lane < amount, lane >= 128 + amount
        return [
            jnp.where(before, turned[t - 1], jnp.where(after, turned[(t + 1) % count], turned[t])) for t in range(count)
        ]

    pieces = [slice(8 * b, 8 * b + 8) for b in range(bins // 8)]
    before, now, base = {}, {}, {}
    stores = []
    for r in range(rows):
        amount = offset_ref[r]
        kappa = [kappa_ref[r, :, spot] for spot in spots]
        above = [kappa_ref[max(r - 1, 0), :, spot] for spot in spots]
        for at in pieces:
            row = [remap_ref[r, at, spot] for spot in spots]
            edge = edge_ref[r, at]
            center = moved(row, edge, amount)
            east = moved(row, edge, amount - 1)
            west = moved(row, edge, amount + 1)
            key = at.start
            fresh = []
            for t, spot in enumerate(spots):
                around = kappa[t] * (east[t] + west[t] - 4.0 * center[t])
                fresh.append(local_ref[r, at, spot] + center[t] + around)
                if r == 1:
                    stores.append((r - 1, at, spot, base[key][t] + above[t] * center[t]))
                elif r:
                    stores.append((r - 1, at, spot, base[key][t] + above[t] * (before[key][t] + center[t])))
            if r:
                before[key] = now[key]
            now[key], base[key] = center, fresh
        if r % 2:
            for which, at, spot, value in stores:
                if which:
                    out_ref[which, at, spot] = value
                else:
                    outer_ref[0, at, spot] = value
            stores = []
    for at in pieces:
        for t, spot in enumerate(spots):
            outer_ref[1, at, spot] = base[at.start][t] + kappa_ref[rows - 1, :, spot] * before[at.start][t]


def final(offset, remapped, west, east, kappa, local, which, earlier):
    rows, half, width = remapped.shape
    steps = 1
    tile = half // steps
    block = pl.BlockSpec((rows, tile, width), lambda t: (0, t, 0))
    packed = pl.BlockSpec((west.shape[0], tile, 128), lambda t: (0, t, 0))
    return pl.pallas_call(
        final_kernel,
        grid=(steps,),
        in_specs=[in_smem(), block, packed, packed, pl.BlockSpec(kappa.shape, lambda t: (0, 0, 0)), block]
        + [in_place()] * len(earlier),
        out_specs=[
            pl.BlockSpec((rows, tile, width), lambda t: (0, which * steps + t, 0)),
            pl.BlockSpec((2, tile, width), lambda t: (0, t, 0)),
        ],
        out_shape=[
            jax.ShapeDtypeStruct((rows, 2 * half, width), jnp.float32),
            jax.ShapeDtypeStruct((2, half, width), jnp.float32),
        ],
        scratch_shapes=[pltpu.VMEM((rows, tile, 128), jnp.float32)],
        input_output_aliases={6: 0} if earlier else {},
        compiler_params=pltpu.CompilerParams(vmem_limit_bytes=VMEM_BYTES),
        cost_estimate=pl.CostEstimate(flops=30 * remapped.size, bytes_accessed=40 * remapped.size, transcendentals=0),
        name="final",
    )(offset, remapped, west, east, kappa, local, *earlier)


def halo_kernel(before_ref, after_ref, kappa_ref, outer0_ref, outer1_ref, _, out_ref, sums_ref, sems):
    rows = out_ref.shape[0]
    half = outer0_ref.shape[1]
    copies = []
    for side, (value_ref, at) in enumerate(((before_ref, 0), (after_ref, rows - 1))):
        for h, outer_ref in enumerate((outer0_ref, outer1_ref)):
            bins = slice(h * half, (h + 1) * half)
            sums_ref[side, bins] = outer_ref[side] + kappa_ref[at] * value_ref[0, bins].astype(jnp.float32)
        copy = pltpu.make_async_copy(sums_ref.at[pl.ds(side, 1)], out_ref.at[pl.ds(at, 1)], sems.at[side])
        copy.start()
        copies.append(copy)
    for copy in copies:
        copy.wait()


def add_halo(before, after, kappa, outers, partial):
    vmem = pl.BlockSpec(memory_space=pltpu.VMEM)
    sides, half, width = outers[0].shape
    return pl.pallas_call(
        halo_kernel,
        in_specs=[vmem] * 5 + [in_place()],
        out_specs=in_place(),
        out_shape=jax.ShapeDtypeStruct(partial.shape, jnp.float32),
        scratch_shapes=[pltpu.VMEM((sides, 2 * half, width), jnp.float32), pltpu.SemaphoreType.DMA((2,))],
        input_output_aliases={5: 0},
        compiler_params=pltpu.CompilerParams(vmem_limit_bytes=VMEM_BYTES),
        cost_estimate=pl.CostEstimate(flops=4 * partial.size // 16, bytes_accessed=partial.size, transcendentals=0),
        name="add_halo",
    )(before, after, kappa, *outers, partial)


def body(
    conc,
    dep_owner,
    dep_row,
    dep_weight,
    dep_count,
    zonal_offset,
    agg_rates,
    toeplitz,
    settle,
    kappa,
):
    rows, bins, width = conc.shape
    entries = dep_owner.shape[2]
    odd = (lax.axis_index("lon") % 2).astype(jnp.int32).reshape(1)
    half = bins // 2
    low, high, meta = messages(conc, dep_owner[0].T, dep_row[0].T, dep_weight[0].T, dep_count)
    south = permute_lat(high, 1)
    north = permute_lat(high, -1)
    ahead = permute_lon(low, -2)
    behind = permute_lon(low, 2)
    beside = swap_lon(conc)
    rates, meta = lax.optimization_barrier((agg_rates, meta))
    local0, local1 = local_terms(conc, rates, toeplitz, settle)
    terms = decoded(odd, [south, meta, north], lat_slots, rows, half, entries)
    south, north, local0, terms = lax.optimization_barrier((south, north, local0, terms))

    to_west, own1, to_east = lon_sums(
        odd,
        [behind, meta, ahead],
        lon_slots,
        [(south, 0), (conc, half), (north, 0), (swap_lon(south), 0), (beside, half), (swap_lon(north), 0)],
        rows,
        half,
        entries,
    )
    from_west, from_east = permute_lon(to_east, 2), permute_lon(to_west, -2)
    own1, odd = lax.optimization_barrier((own1, odd))
    parts1 = [own1, from_west, from_east]

    down, own0, up = lat_sums(
        odd,
        terms,
        [(conc, 0), (beside, 0), (ahead, 0), (behind, 0), (swap_lon(ahead), 0), (swap_lon(behind), 0)],
        rows,
        half,
        entries,
    )
    parts0 = [own0, permute_lat(up, 1), permute_lat(down, -1)]

    kappa = kappa[:, None, :]

    def with_edges(parts):
        first, last = edges(parts)
        return combine(parts), permute_lon(last, 1), permute_lon(first, -1)

    half1 = with_edges(parts1)
    partial, outer1 = final(zonal_offset, *half1, kappa, local1, 1, [])
    parts0, outer1 = lax.optimization_barrier((parts0, outer1))
    half0 = with_edges(parts0)
    top_row, end_row = outer_rows(zonal_offset, [half0, half1])
    before, after = permute_lat(end_row, 1), permute_lat(top_row, -1)
    partial, outer0 = final(zonal_offset, *half0, kappa, local0, 0, [partial])
    return add_halo(before, after, kappa, [outer0, outer1], partial)


def solution(mesh):
    return jax.shard_map(
        body,
        mesh=mesh,
        in_specs=(
            P("lat", None, "lon"),
            P("lon", "lat", None),
            P("lon", "lat", None),
            P("lon", "lat", None),
            P("lon", "lat"),
            P("lat"),
            P(None, "lat", "lon"),
            P(),
            P(),
            P("lat", "lon"),
        ),
        out_specs=P("lat", None, "lon"),
        check_vma=False,
    )
```

```python
import functools

import jax
import jax.numpy as jnp
from jax import lax
from jax.experimental import pallas as pl
from jax.experimental.pallas import tpu as pltpu
from jax.sharding import PartitionSpec as P

REACH = 2
NEAR_LON = 5
UNROLL = 4
VMEM_BYTES = 12 * 1024 * 1024
MOST_BYTES = 60 * 1024 * 1024
TABLE_BYTES = 20 * 1024 * 1024
QUICK = 2
FIELDS = ((0, 0), (0, 128), (8, 0), (8, 128), (16, 0))


def exchange(value, axis, pairs):
    return lax.ppermute(value, axis, [(i, j) for i, j in pairs] + [(j, i) for i, j in pairs])


def swap_core(value):
    return exchange(value, "lon", [(i, i + 1) for i in range(0, lax.axis_size("lon"), 2)])


def swap_across(value):
    count = lax.axis_size("lon")
    return exchange(value, "lon", [(i, (i + 1) % count) for i in range(1, count, 2)])


def swap_chip(value, second):
    count = lax.axis_size("lon")
    firsts = [i for i in range(count) if (i // 2) % 2 == second]
    return exchange(value, "lon", [(i, (i + 2) % count) for i in firsts])


def swap_lat(value, second):
    count = lax.axis_size("lat")
    return exchange(value, "lat", [(i, i + 1) for i in range(second, count - 1, 2)])


def in_smem():
    return pl.BlockSpec(memory_space=pltpu.SMEM)


def in_place():
    return pl.BlockSpec(memory_space=pl.ANY)


def for_rows(count, one):
    def some(g, carry):
        stores = []
        for u in range(UNROLL):
            stores += one(g * UNROLL + u)
        for ref, at, value in stores:
            ref[at] = value.astype(ref.dtype)
        return carry

    lax.fori_loop(0, count // UNROLL, some, 0)


def growth_kernel(flip_ref, settle_ref, conc_ref, rates_ref, low_ref, high_ref, mat_ref):
    ranks, rows_step = rates_ref.shape[0], conc_ref.shape[0]
    bins, width = conc_ref.shape[1:]

    @pl.when(pl.program_id(0) == 0)
    def _():
        for q in range(ranks):
            spread = jnp.broadcast_to(flip_ref[q : q + 1, :], (bins, 2 * bins))
            turned = pltpu.roll(spread, bins + 1, 1, stride=1, stride_axis=0)
            mat_ref[q * bins : (q + 1) * bins, :] = turned[:, :bins].astype(jnp.bfloat16)

    settle = jnp.broadcast_to(settle_ref[...], (bins, width))
    for r in range(rows_step):
        cells = conc_ref[r]
        product = jnp.dot(mat_ref[...], cells, preferred_element_type=jnp.float32)
        total = -settle * cells.astype(jnp.float32)
        for q in range(ranks):
            total = total + rates_ref[q, r : r + 1, :] * product[q * bins : (q + 1) * bins]
        low_ref[r] = total[: bins // 2]
        high_ref[r] = total[bins // 2 :]


def local_terms(conc, agg_rates, toeplitz, settle):
    rows, bins, width = conc.shape
    ranks = agg_rates.shape[0]
    step = 8
    flipped = jnp.pad(toeplitz[:, ::-1].astype(jnp.float32), ((0, 0), (0, 1)))
    return pl.pallas_call(
        growth_kernel,
        grid=(rows // step,),
        in_specs=[
            pl.BlockSpec((ranks, 2 * bins), lambda i: (0, 0)),
            pl.BlockSpec((bins, 1), lambda i: (0, 0)),
            pl.BlockSpec((step, bins, width), lambda i: (i, 0, 0)),
            pl.BlockSpec((ranks, step, width), lambda i: (0, i, 0)),
        ],
        out_specs=[pl.BlockSpec((step, bins // 2, width), lambda i: (i, 0, 0))] * 2,
        out_shape=[jax.ShapeDtypeStruct((rows, bins // 2, width), jnp.float32)] * 2,
        scratch_shapes=[pltpu.VMEM((ranks * bins, bins), jnp.bfloat16)],
        compiler_params=pltpu.CompilerParams(vmem_limit_bytes=VMEM_BYTES),
        cost_estimate=pl.CostEstimate(
            flops=2 * ranks * bins * bins * rows * width, bytes_accessed=8 * conc.size, transcendentals=0
        ),
        name="growth",
    )(flipped, settle[:, None], conc, agg_rates)


def messages_kernel(
    conc_ref, owner_hbm, source_hbm, weight_hbm, count_hbm, low_ref, high_ref, meta_ref,
    owner_ref, source_ref, weight_ref, count_ref, sems,
):
    rows = conc_ref.shape[0]
    half = low_ref.shape[1]
    entries = owner_ref.shape[0]
    small = [
        pltpu.make_async_copy(hbm, ref, sems.at[2 + i])
        for i, (hbm, ref) in enumerate(
            ((owner_hbm, owner_ref), (source_hbm, source_ref), (weight_hbm, weight_ref), (count_hbm, count_ref))
        )
    ]
    large = [
        pltpu.make_async_copy(conc_ref.at[:, pl.ds(i * half, half), :], ref.at[pl.ds(0, rows)], sems.at[i])
        for i, ref in enumerate((low_ref, high_ref))
    ]
    for copy in small + large:
        copy.start()
    meta_ref[...] = jnp.zeros(meta_ref.shape, meta_ref.dtype)
    for copy in small:
        copy.wait()
    wide = lambda value: value.astype(jnp.float32)
    entry = lax.broadcasted_iota(jnp.int32, owner_ref.shape, 0)
    live = jnp.where(entry < count_ref[...], weight_ref[...], 0.0)
    top = live.astype(jnp.bfloat16)
    middle = (live - wide(top)).astype(jnp.bfloat16)
    bottom = (live - wide(top) - wide(middle)).astype(jnp.bfloat16)
    fields = (wide(owner_ref[...]), wide(source_ref[...]), wide(top), wide(middle), wide(bottom))
    for field, (at, lane) in zip(fields, FIELDS):
        meta_ref[0, at : at + entries, lane : lane + rows] = field.astype(jnp.bfloat16)
    low_ref[rows] = meta_ref[0]
    high_ref[rows] = meta_ref[0]
    for copy in large:
        copy.wait()


def messages(conc, owner, source, weight, count):
    rows, bins, width = conc.shape
    half = bins // 2
    return pl.pallas_call(
        messages_kernel,
        in_specs=[in_place()] * 5,
        out_specs=[pl.BlockSpec(memory_space=pltpu.VMEM)] * 3,
        out_shape=[
            jax.ShapeDtypeStruct((rows + 1, half, width), conc.dtype),
            jax.ShapeDtypeStruct((rows + 1, half, width), conc.dtype),
            jax.ShapeDtypeStruct((1, half, width), conc.dtype),
        ],
        scratch_shapes=[pltpu.VMEM(small.shape, small.dtype) for small in (owner, source, weight, count)]
        + [pltpu.SemaphoreType.DMA((6,))],
        compiler_params=pltpu.CompilerParams(vmem_limit_bytes=MOST_BYTES),
        cost_estimate=pl.CostEstimate(flops=0, bytes_accessed=4 * conc.size, transcendentals=0),
        name="messages",
    )(conc, owner, source, weight, count)


def signs(flags_ref):
    return [1.0 - 2.0 * flags_ref[i].astype(jnp.float32) for i in range(3)]


def lat_slots(rows, group, lat_step, lon_step, flags_ref):
    core, chip, lat = signs(flags_ref)
    far = jnp.where(core * chip < 0.0, 4.0, 5.0)
    slot = jnp.where(
        lon_step == 0.0,
        0.0,
        jnp.where(
            lon_step == 2.0 * chip, 2.0, jnp.where(lon_step == -2.0 * chip, 3.0, jnp.where(lon_step == core, 1.0, far))
        ),
    )
    return lat_step == (group - 1.0) * lat, slot * rows


def lon_slots(rows, group, lat_step, lon_step, flags_ref):
    core, chip, lat = signs(flags_ref)
    lon_from = 2.0 * (1.0 - group) * chip + lon_step
    slot = jnp.where(lon_from == 0.0, 1.0, 4.0) - lat_step * lat
    return (lon_from == 0.0) | (lon_from == core), slot * rows


def decode(slots, rows, entries, flags_ref, meta_ref, index_ref, weight_ref):
    for g in range(3):
        owner, source, top, middle, bottom = [
            meta_ref[g, at : at + entries, lane : lane + 128].astype(jnp.float32) for at, lane in FIELDS
        ]
        weight = top + middle + bottom
        band = jnp.where(owner >= NEAR_LON, 1.0, 0.0) + jnp.where(owner >= 2 * NEAR_LON, 1.0, 0.0)
        here, base = slots(rows, float(g), band - 1.0, owner - NEAR_LON * band - REACH, flags_ref)
        here = jnp.where(here & (weight != 0.0), 1.0, 0.0)
        index = base + source
        packed = [[jnp.zeros((1, 128), jnp.float32)] * 2 for _ in range(entries)]
        rank = jnp.zeros((1, 128), jnp.float32)
        for k in range(entries):
            taken = here[k : k + 1]
            for place in range(k + 1):
                spot = (taken > 0.0) & (rank == place)
                packed[place] = [
                    jnp.where(spot, index[k : k + 1], packed[place][0]),
                    jnp.where(spot, weight[k : k + 1], packed[place][1]),
                ]
            rank = rank + taken
        for place in range(entries):
            at = g * entries + place
            index_ref[at : at + 1, :] = packed[place][0].astype(jnp.int32)
            weight_ref[at : at + 1, :] = packed[place][1]
        at = 3 * entries + g
        index_ref[at : at + 1, :] = rank.astype(jnp.int32)


def read_metas(asked, meta_ref, sems, first):
    return [
        pltpu.make_async_copy(ref.at[pl.ds(ref.shape[0] - 1, 1)], meta_ref.at[pl.ds(g, 1)], sems.at[first + g])
        for g, ref in enumerate(asked)
    ]


def decode_kernel(slots, rows, entries, flags_ref, first_ref, own_ref, second_ref, index_ref, weight_ref, meta_ref, sems):
    copies = read_metas((first_ref, own_ref, second_ref), meta_ref, sems, 0)
    for copy in copies:
        copy.start()
    for copy in copies:
        copy.wait()
    decode(slots, rows, entries, flags_ref, meta_ref, index_ref, weight_ref)


def decoded(flags, asked, slots, rows, half, entries):
    width = asked[1].shape[2]
    vectors = -(-3 * (entries + 1) // 8) * 8
    return pl.pallas_call(
        functools.partial(decode_kernel, slots, rows, entries),
        in_specs=[in_smem()] + [in_place()] * 3,
        out_specs=[pl.BlockSpec(memory_space=pltpu.VMEM)] * 2,
        out_shape=[
            jax.ShapeDtypeStruct((vectors, 128), jnp.int32),
            jax.ShapeDtypeStruct((vectors, 128), jnp.float32),
        ],
        scratch_shapes=[pltpu.VMEM((3, half, width), jnp.bfloat16), pltpu.SemaphoreType.DMA((3,))],
        compiler_params=pltpu.CompilerParams(vmem_limit_bytes=VMEM_BYTES),
        cost_estimate=pl.CostEstimate(flops=0, bytes_accessed=6 * half * width, transcendentals=0),
        name="decode",
    )(flags, *asked)


def table_copies(bases, rows, sources, table, sems):
    half = table.shape[1]
    return [
        pltpu.make_async_copy(
            source.at[pl.ds(0, rows), pl.ds(base, half), :], table.at[pl.ds(i * rows, rows)], sems.at[i]
        )
        for i, (source, base) in enumerate(zip(sources, bases))
    ]


def add_terms(rows, entries, index_ref, weight_ref, table, outs):
    half, width = table.shape[1:]
    for group, out in enumerate(outs):

        def some(g, carry, group=group, out=out):
            def sums(terms):
                totals = []
                for u in range(UNROLL):
                    r = g * UNROLL + u
                    total = jnp.zeros((half, width), jnp.float32)
                    for k in range(terms):
                        row = group * entries + k
                        total = total + weight_ref[row, r] * table[index_ref[row, r]].astype(jnp.float32)
                    totals.append(total)
                for u in range(UNROLL):
                    out[g * UNROLL + u] = totals[u].astype(out.dtype)

            most = index_ref[3 * entries + group, g * UNROLL]
            for u in range(1, UNROLL):
                most = jnp.maximum(most, index_ref[3 * entries + group, g * UNROLL + u])
            sums(min(QUICK, entries))

            @pl.when(most > QUICK)
            def _():
                sums(entries)

            return carry

        lax.fori_loop(0, rows // UNROLL, some, 0)


def lat_sums_kernel(bases, entries, flags_ref, index_ref, weight_ref, *refs):
    tables = len(bases)
    sources, outs = refs[:tables], refs[tables : tables + 3]
    table, sems = refs[tables + 3 :]
    rows = table.shape[0] // tables
    copies = table_copies(bases, rows, sources, table, sems)
    first = flags_ref[0] != flags_ref[1]
    for copy in copies[:-2]:
        copy.start()
    pl.when(first)(copies[-2].start)
    pl.when(jnp.logical_not(first))(copies[-1].start)
    for copy in copies[:-2]:
        copy.wait()
    pl.when(first)(copies[-2].wait)
    pl.when(jnp.logical_not(first))(copies[-1].wait)
    add_terms(rows, entries, index_ref, weight_ref, table, outs)


def lon_sums_kernel(bases, slots, entries, flags_ref, *refs):
    tables = len(bases)
    asked, sources, outs = refs[:3], refs[3 : 3 + tables], refs[3 + tables : 6 + tables]
    table, meta_ref, index_vec, weight_vec, index_ref, weight_ref, sems = refs[6 + tables :]
    rows = table.shape[0] // tables
    metas = read_metas(asked, meta_ref, sems, tables)
    copies = table_copies(bases, rows, sources, table, sems)
    for copy in metas + copies:
        copy.start()
    for copy in metas:
        copy.wait()
    decode(slots, rows, entries, flags_ref, meta_ref, index_vec, weight_vec)
    to_scalar = [
        pltpu.make_async_copy(index_vec, index_ref, sems.at[tables + 3]),
        pltpu.make_async_copy(weight_vec, weight_ref, sems.at[tables + 4]),
    ]
    for copy in to_scalar:
        copy.start()
    for copy in to_scalar + copies:
        copy.wait()
    add_terms(rows, entries, index_ref, weight_ref, table, outs)


def sums_call(kernel, operands, smem, sources, scratch, rows, half, entries, name):
    tables = len(sources)
    width = sources[0][0].shape[2]
    return pl.pallas_call(
        kernel,
        in_specs=[in_smem()] * smem + [in_place()] * (len(operands) - smem + tables),
        out_specs=[pl.BlockSpec(memory_space=pltpu.VMEM)] * 3,
        out_shape=[
            jax.ShapeDtypeStruct((rows, half, width), dtype) for dtype in (jnp.bfloat16, jnp.float32, jnp.bfloat16)
        ],
        scratch_shapes=[pltpu.VMEM((tables * rows, half, width), jnp.bfloat16)] + scratch,
        compiler_params=pltpu.CompilerParams(vmem_limit_bytes=TABLE_BYTES),
        cost_estimate=pl.CostEstimate(
            flops=6 * rows * entries * half * width,
            bytes_accessed=2 * (tables + 3) * rows * half * width,
            transcendentals=0,
        ),
        name=name,
    )(*operands, *[source for source, _ in sources])


def lat_sums(flags, terms, sources, rows, half, entries):
    kernel = functools.partial(lat_sums_kernel, tuple(base for _, base in sources), entries)
    scratch = [pltpu.SemaphoreType.DMA((len(sources),))]
    return sums_call(kernel, [flags, *terms], 3, sources, scratch, rows, half, entries, "lat_sums")


def lon_sums(flags, asked, slots, sources, rows, half, entries):
    kernel = functools.partial(lon_sums_kernel, tuple(base for _, base in sources), slots, entries)
    vectors = -(-3 * (entries + 1) // 8) * 8
    scratch = [pltpu.VMEM((3, half, asked[1].shape[2]), jnp.bfloat16)]
    scratch += [space((vectors, 128), dtype) for space in (pltpu.VMEM, pltpu.SMEM) for dtype in (jnp.int32, jnp.float32)]
    scratch += [pltpu.SemaphoreType.DMA((len(sources) + 5,))]
    return sums_call(kernel, [flags, *asked], 1, sources, scratch, rows, half, entries, "lon_sums")


def edges_kernel(flags_ref, *refs):
    rows, half = refs[0].shape[:2]
    per = 128 // 8
    lane = lax.broadcasted_iota(jnp.int32, (half, 128), 1)
    odd = flags_ref[0] == 1
    for j in range(rows // per):
        ends = []
        for side in range(2):
            parts = refs[3 * side : 3 * side + 3]
            packed = jnp.zeros((half, 128), jnp.float32)
            for i in range(per):
                r = j * per + i
                cells = parts[0][r] + parts[1][r].astype(jnp.float32) + parts[2][r].astype(jnp.float32)
                at = 8 * i + 3 * (1 - side)
                spot = (lane >= at) & (lane < at + 3)
                packed = jnp.where(spot, pltpu.roll(cells, 8 * i + 3, 1), packed)
            ends.append(packed)
        for out_ref, value in zip(refs[-2:], (jnp.where(odd, *ends), jnp.where(odd, *ends[::-1]))):
            out_ref[j] = value.astype(out_ref.dtype)


def edges(flags, parts):
    rows, half, width = parts[0].shape
    specs = [
        pl.BlockSpec((rows, half, 128), lambda t, at=at: (0, 0, at)) for at in (0, width // 128 - 1) for _ in parts
    ]
    packed = (rows // 16, half, 128)
    return pl.pallas_call(
        edges_kernel,
        grid=(1,),
        in_specs=[in_smem()] + specs,
        out_specs=[pl.BlockSpec(packed, lambda t: (0, 0, 0))] * 2,
        out_shape=[jax.ShapeDtypeStruct(packed, jnp.bfloat16)] * 2,
        compiler_params=pltpu.CompilerParams(vmem_limit_bytes=VMEM_BYTES),
        cost_estimate=pl.CostEstimate(flops=8 * half * 256 * rows, bytes_accessed=16 * half * 256 * rows, transcendentals=0),
        name="edges",
    )(flags, *parts, *parts)


def combine_kernel(own, a, b, out_ref):
    for r in range(own.shape[0]):
        out_ref[r] = own[r] + a[r].astype(jnp.float32) + b[r].astype(jnp.float32)


def combine(parts):
    rows, half, width = parts[0].shape
    step = 8
    block = pl.BlockSpec((step, half, width), lambda t: (t, 0, 0))
    return pl.pallas_call(
        combine_kernel,
        grid=(rows // step,),
        in_specs=[block] * 3,
        out_specs=block,
        out_shape=jax.ShapeDtypeStruct((rows, half, width), jnp.float32),
        compiler_params=pltpu.CompilerParams(vmem_limit_bytes=VMEM_BYTES),
        cost_estimate=pl.CostEstimate(
            flops=2 * rows * half * width, bytes_accessed=12 * rows * half * width, transcendentals=0
        ),
        name="combine",
    )(*parts)


def shifted_by(row, edge, amount, lane):
    count = len(row)
    if amount == 0:
        return row
    if amount > 0:
        row = row[:-1] + [jnp.where(lane >= 128 - amount, edge, row[-1])]
        turned = [pltpu.roll(tile, amount, 1) for tile in row]
        return [jnp.where(lane < amount, turned[t - 1], turned[t]) for t in range(count)]
    row = [jnp.where(lane < -amount, edge, row[0])] + row[1:]
    turned = [pltpu.roll(tile, 128 + amount, 1) for tile in row]
    return [jnp.where(lane >= 128 + amount, turned[(t + 1) % count], turned[t]) for t in range(count)]


def edge_tile(west_ref, east_ref, r):
    per = 128 // 8
    both = west_ref[r // per].astype(jnp.float32) + east_ref[r // per].astype(jnp.float32)
    return pltpu.roll(both, (125 - 8 * (r % per)) % 128, 1)


def rows_kernel(flags_ref, offset_ref, *refs):
    outs = refs[-2:]
    half, width = refs[0].shape[1:]
    lane = lax.broadcasted_iota(jnp.int32, (half, 128), 1)
    spots = [slice(128 * t, 128 * t + 128) for t in range(width // 128)]
    end = offset_ref.shape[0] - 1
    odd = flags_ref[2] == 1
    for out_ref, first in ((outs[0], odd), (outs[1], jnp.logical_not(odd))):
        offset = jnp.where(first, offset_ref[0], offset_ref[end])
        for amount in range(-REACH, REACH + 1):

            @pl.when(offset == amount)
            def _(out_ref=out_ref, first=first, amount=amount):
                for h in range(2):
                    first_row, last_row, one_ref, other_ref = refs[4 * h : 4 * h + 4]
                    row = [jnp.where(first, first_row[0, :, at], last_row[0, :, at]) for at in spots]
                    edge = jnp.where(first, edge_tile(one_ref, other_ref, 0), edge_tile(one_ref, other_ref, end))
                    for at, tile in zip(spots, shifted_by(row, edge, amount, lane)):
                        out_ref[0, h * half : (h + 1) * half, at] = tile.astype(out_ref.dtype)


def outer_rows(flags, offset, halves):
    rows, half, width = halves[0][0].shape
    row = lambda at: pl.BlockSpec((1, half, width), lambda t: (at, 0, 0))
    whole = pl.BlockSpec(halves[0][1].shape, lambda t: (0, 0, 0))
    out = pl.BlockSpec((1, 2 * half, width), lambda t: (0, 0, 0))
    operands = [array for remapped, west, east in halves for array in (remapped, remapped, west, east)]
    return pl.pallas_call(
        rows_kernel,
        grid=(1,),
        in_specs=[in_smem()] * 2 + [row(0), row(rows - 1), whole, whole] * 2,
        out_specs=[out, out],
        out_shape=[jax.ShapeDtypeStruct((1, 2 * half, width), jnp.bfloat16)] * 2,
        compiler_params=pltpu.CompilerParams(vmem_limit_bytes=VMEM_BYTES),
        cost_estimate=pl.CostEstimate(flops=40 * half * width, bytes_accessed=24 * half * width, transcendentals=0),
        name="outer_rows",
    )(flags, offset, *operands)


def final_kernel(offset_ref, remap_ref, west_ref, east_ref, kappa_ref, local_ref, *refs):
    out_ref, outer_ref, edge_ref = refs[-3:]
    rows, bins, width = remap_ref.shape
    count = width // 128
    lane = lax.broadcasted_iota(jnp.int32, (8, 128), 1)
    spots = [slice(128 * t, 128 * t + 128) for t in range(count)]
    for r in range(rows):
        edge_ref[r] = edge_tile(west_ref, east_ref, r)

    def moved(row, edge, amount):
        row = [jnp.where(lane < -amount, edge, row[0])] + row[1:]
        row = row[:-1] + [jnp.where(lane >= 128 - amount, edge, row[-1])]
        turned = [pltpu.roll(tile, (amount + 128) & 127, 1) for tile in row]
        before, after = lane < amount, lane >= 128 + amount
        return [
            jnp.where(before, turned[t - 1], jnp.where(after, turned[(t + 1) % count], turned[t])) for t in range(count)
        ]

    pieces = [slice(8 * b, 8 * b + 8) for b in range(bins // 8)]
    before, now, base = {}, {}, {}
    stores = []
    for r in range(rows):
        amount = offset_ref[r]
        kappa = [kappa_ref[r, :, spot] for spot in spots]
        above = [kappa_ref[max(r - 1, 0), :, spot] for spot in spots]
        for at in pieces:
            row = [remap_ref[r, at, spot] for spot in spots]
            edge = edge_ref[r, at]
            center = moved(row, edge, amount)
            east = moved(row, edge, amount - 1)
            west = moved(row, edge, amount + 1)
            key = at.start
            fresh = []
            for t, spot in enumerate(spots):
                around = kappa[t] * (east[t] + west[t] - 4.0 * center[t])
                fresh.append(local_ref[r, at, spot] + center[t] + around)
                if r == 1:
                    stores.append((r - 1, at, spot, base[key][t] + above[t] * center[t]))
                elif r:
                    stores.append((r - 1, at, spot, base[key][t] + above[t] * (before[key][t] + center[t])))
            if r:
                before[key] = now[key]
            now[key], base[key] = center, fresh
        if r % 2:
            for which, at, spot, value in stores:
                if which:
                    out_ref[which, at, spot] = value
                else:
                    outer_ref[0, at, spot] = value
            stores = []
    for at in pieces:
        for t, spot in enumerate(spots):
            outer_ref[1, at, spot] = base[at.start][t] + kappa_ref[rows - 1, :, spot] * before[at.start][t]


def final(offset, remapped, west, east, kappa, local, which, earlier):
    rows, half, width = remapped.shape
    steps = 1
    tile = half // steps
    block = pl.BlockSpec((rows, tile, width), lambda t: (0, t, 0))
    packed = pl.BlockSpec((west.shape[0], tile, 128), lambda t: (0, t, 0))
    return pl.pallas_call(
        final_kernel,
        grid=(steps,),
        in_specs=[in_smem(), block, packed, packed, pl.BlockSpec(kappa.shape, lambda t: (0, 0, 0)), block]
        + [in_place()] * len(earlier),
        out_specs=[
            pl.BlockSpec((rows, tile, width), lambda t: (0, which * steps + t, 0)),
            pl.BlockSpec((2, tile, width), lambda t: (0, t, 0)),
        ],
        out_shape=[
            jax.ShapeDtypeStruct((rows, 2 * half, width), jnp.float32),
            jax.ShapeDtypeStruct((2, half, width), jnp.float32),
        ],
        scratch_shapes=[pltpu.VMEM((rows, tile, 128), jnp.float32)],
        input_output_aliases={6: 0} if earlier else {},
        compiler_params=pltpu.CompilerParams(vmem_limit_bytes=VMEM_BYTES),
        cost_estimate=pl.CostEstimate(flops=30 * remapped.size, bytes_accessed=40 * remapped.size, transcendentals=0),
        name="final",
    )(offset, remapped, west, east, kappa, local, *earlier)


def halo_kernel(flags_ref, one_ref, other_ref, kappa_ref, outer0_ref, outer1_ref, _, out_ref, sums_ref, sems):
    odd = flags_ref[2] == 1
    rows = out_ref.shape[0]
    half = outer0_ref.shape[1]
    copies = []
    for side, (first, at) in enumerate(((odd, 0), (jnp.logical_not(odd), rows - 1))):
        value = jnp.where(first, one_ref[0].astype(jnp.float32), other_ref[0].astype(jnp.float32))
        for h, outer_ref in enumerate((outer0_ref, outer1_ref)):
            bins = slice(h * half, (h + 1) * half)
            sums_ref[side, bins] = outer_ref[side] + kappa_ref[at] * value[bins]
        copy = pltpu.make_async_copy(sums_ref.at[pl.ds(side, 1)], out_ref.at[pl.ds(at, 1)], sems.at[side])
        copy.start()
        copies.append(copy)
    for copy in copies:
        copy.wait()


def add_halo(flags, one, other, kappa, outers, partial):
    vmem = pl.BlockSpec(memory_space=pltpu.VMEM)
    sides, half, width = outers[0].shape
    return pl.pallas_call(
        halo_kernel,
        in_specs=[in_smem()] + [vmem] * 5 + [in_place()],
        out_specs=in_place(),
        out_shape=jax.ShapeDtypeStruct(partial.shape, jnp.float32),
        scratch_shapes=[pltpu.VMEM((sides, 2 * half, width), jnp.float32), pltpu.SemaphoreType.DMA((2,))],
        input_output_aliases={6: 0},
        compiler_params=pltpu.CompilerParams(vmem_limit_bytes=VMEM_BYTES),
        cost_estimate=pl.CostEstimate(flops=4 * partial.size // 16, bytes_accessed=partial.size, transcendentals=0),
        name="add_halo",
    )(flags, one, other, kappa, *outers, partial)


def body(
    conc,
    dep_owner,
    dep_row,
    dep_weight,
    dep_count,
    zonal_offset,
    agg_rates,
    toeplitz,
    settle,
    kappa,
):
    rows, bins, width = conc.shape
    entries = dep_owner.shape[2]
    my_lat, my_lon = lax.axis_index("lat"), lax.axis_index("lon")
    flags = jnp.stack([my_lon % 2, my_lon // 2 % 2, my_lat % 2]).astype(jnp.int32)
    half = bins // 2
    low, high, meta = messages(conc, dep_owner[0].T, dep_row[0].T, dep_weight[0].T, dep_count)
    lat1, lat2 = swap_lat(high, 0), swap_lat(high, 1)
    lon1, lon2 = swap_chip(low, 0), swap_chip(low, 1)
    beside = swap_core(conc)
    rates, meta = lax.optimization_barrier((agg_rates, meta))
    local0, local1 = local_terms(conc, rates, toeplitz, settle)
    terms = decoded(flags, [lat1, meta, lat2], lat_slots, rows, half, entries)
    lat1, lat2, local0, terms = lax.optimization_barrier((lat1, lat2, local0, terms))

    to_lon1, own1, to_lon2 = lon_sums(
        flags,
        [lon1, meta, lon2],
        lon_slots,
        [(lat1, 0), (conc, half), (lat2, 0), (swap_core(lat1), 0), (beside, half), (swap_core(lat2), 0)],
        rows,
        half,
        entries,
    )
    parts1 = [swap_chip(to_lon1, 0), swap_chip(to_lon2, 1)]
    own1, flags = lax.optimization_barrier((own1, flags))
    parts1 = [own1] + parts1

    to_lat1, own0, to_lat2 = lat_sums(
        flags,
        terms,
        [(conc, 0), (beside, 0), (lon1, 0), (lon2, 0), (swap_core(lon1), 0), (swap_core(lon2), 0)],
        rows,
        half,
        entries,
    )
    parts0 = [own0, swap_lat(to_lat1, 0), swap_lat(to_lat2, 1)]

    kappa = kappa[:, None, :]

    def with_edges(parts):
        to_core, to_across = edges(flags, parts)
        return combine(parts), swap_core(to_core), swap_across(to_across)

    half1 = with_edges(parts1)
    partial, outer1 = final(zonal_offset, *half1, kappa, local1, 1, [])
    parts0, outer1 = lax.optimization_barrier((parts0, outer1))
    half0 = with_edges(parts0)
    row1, row2 = outer_rows(flags, zonal_offset, [half0, half1])
    row1, row2 = swap_lat(row1, 0), swap_lat(row2, 1)
    partial, outer0 = final(zonal_offset, *half0, kappa, local0, 0, [partial])
    return add_halo(flags, row1, row2, kappa, [outer0, outer1], partial)


def solution(mesh):
    return jax.shard_map(
        body,
        mesh=mesh,
        in_specs=(
            P("lat", None, "lon"),
            P("lon", "lat", None),
            P("lon", "lat", None),
            P("lon", "lat", None),
            P("lon", "lat"),
            P("lat"),
            P(None, "lat", "lon"),
            P(),
            P(),
            P("lat", "lon"),
        ),
        out_specs=P("lat", None, "lon"),
        check_vma=False,
    )
```

```python
import functools

import jax
import jax.numpy as jnp
from jax import lax
from jax.experimental import pallas as pl
from jax.experimental.pallas import tpu as pltpu
from jax.sharding import PartitionSpec as P

REACH = 2
NEAR_LON = 5
UNROLL = 4
VMEM_BYTES = 12 * 1024 * 1024
MOST_BYTES = 60 * 1024 * 1024
TABLE_BYTES = 20 * 1024 * 1024
QUICK = 2
FIELDS = ((0, 0), (0, 128), (8, 0), (8, 128), (16, 0))


def exchange(value, axis, pairs):
    return lax.ppermute(value, axis, [(i, j) for i, j in pairs] + [(j, i) for i, j in pairs])


def swap_core(value):
    return exchange(value, "lon", [(i, i + 1) for i in range(0, lax.axis_size("lon"), 2)])


def swap_across(value):
    count = lax.axis_size("lon")
    return exchange(value, "lon", [(i, (i + 1) % count) for i in range(1, count, 2)])


def swap_chip(value, second):
    count = lax.axis_size("lon")
    firsts = [i for i in range(count) if (i // 2) % 2 == second]
    return exchange(value, "lon", [(i, (i + 2) % count) for i in firsts])


def swap_lat(value, second):
    count = lax.axis_size("lat")
    return exchange(value, "lat", [(i, i + 1) for i in range(second, count - 1, 2)])


def in_smem():
    return pl.BlockSpec(memory_space=pltpu.SMEM)


def in_place():
    return pl.BlockSpec(memory_space=pl.ANY)


def for_rows(count, one):
    def some(g, carry):
        stores = []
        for u in range(UNROLL):
            stores += one(g * UNROLL + u)
        for ref, at, value in stores:
            ref[at] = value.astype(ref.dtype)
        return carry

    lax.fori_loop(0, count // UNROLL, some, 0)


def growth_kernel(flip_ref, settle_ref, conc_ref, rates_ref, out_ref, mat_ref):
    ranks, rows_step = rates_ref.shape[0], conc_ref.shape[0]
    bins, width = conc_ref.shape[1:]

    @pl.when(pl.program_id(0) == 0)
    def _():
        for q in range(ranks):
            spread = jnp.broadcast_to(flip_ref[q : q + 1, :], (bins, 2 * bins))
            turned = pltpu.roll(spread, bins + 1, 1, stride=1, stride_axis=0)
            mat_ref[q * bins : (q + 1) * bins, :] = turned[:, :bins].astype(jnp.bfloat16)

    settle = jnp.broadcast_to(settle_ref[...], (bins, width))
    for r in range(rows_step):
        cells = conc_ref[r]
        product = jnp.dot(mat_ref[...], cells, preferred_element_type=jnp.float32)
        total = -settle * cells.astype(jnp.float32)
        for q in range(ranks):
            total = total + rates_ref[q, r : r + 1, :] * product[q * bins : (q + 1) * bins]
        out_ref[r] = total


def local_terms(conc, agg_rates, toeplitz, settle):
    rows, bins, width = conc.shape
    ranks = agg_rates.shape[0]
    step = 8
    flipped = jnp.pad(toeplitz[:, ::-1].astype(jnp.float32), ((0, 0), (0, 1)))
    return pl.pallas_call(
        growth_kernel,
        grid=(rows // step,),
        in_specs=[
            pl.BlockSpec((ranks, 2 * bins), lambda i: (0, 0)),
            pl.BlockSpec((bins, 1), lambda i: (0, 0)),
            pl.BlockSpec((step, bins, width), lambda i: (i, 0, 0)),
            pl.BlockSpec((ranks, step, width), lambda i: (0, i, 0)),
        ],
        out_specs=pl.BlockSpec((step, bins, width), lambda i: (i, 0, 0)),
        out_shape=jax.ShapeDtypeStruct(conc.shape, jnp.float32),
        scratch_shapes=[pltpu.VMEM((ranks * bins, bins), jnp.bfloat16)],
        compiler_params=pltpu.CompilerParams(vmem_limit_bytes=VMEM_BYTES),
        cost_estimate=pl.CostEstimate(
            flops=2 * ranks * bins * bins * rows * width, bytes_accessed=8 * conc.size, transcendentals=0
        ),
        name="growth",
    )(flipped, settle[:, None], conc, agg_rates)


def messages_kernel(
    conc_ref, owner_hbm, source_hbm, weight_hbm, count_hbm, low_ref, high_ref, meta_ref,
    owner_ref, source_ref, weight_ref, count_ref, sems,
):
    rows = conc_ref.shape[0]
    half = low_ref.shape[1]
    entries = owner_ref.shape[0]
    small = [
        pltpu.make_async_copy(hbm, ref, sems.at[2 + i])
        for i, (hbm, ref) in enumerate(
            ((owner_hbm, owner_ref), (source_hbm, source_ref), (weight_hbm, weight_ref), (count_hbm, count_ref))
        )
    ]
    large = [
        pltpu.make_async_copy(conc_ref.at[:, pl.ds(i * half, half), :], ref.at[pl.ds(0, rows)], sems.at[i])
        for i, ref in enumerate((low_ref, high_ref))
    ]
    for copy in small + large:
        copy.start()
    meta_ref[...] = jnp.zeros(meta_ref.shape, meta_ref.dtype)
    for copy in small:
        copy.wait()
    wide = lambda value: value.astype(jnp.float32)
    entry = lax.broadcasted_iota(jnp.int32, owner_ref.shape, 0)
    live = jnp.where(entry < count_ref[...], weight_ref[...], 0.0)
    top = live.astype(jnp.bfloat16)
    middle = (live - wide(top)).astype(jnp.bfloat16)
    bottom = (live - wide(top) - wide(middle)).astype(jnp.bfloat16)
    fields = (wide(owner_ref[...]), wide(source_ref[...]), wide(top), wide(middle), wide(bottom))
    for field, (at, lane) in zip(fields, FIELDS):
        meta_ref[0, at : at + entries, lane : lane + rows] = field.astype(jnp.bfloat16)
    low_ref[rows] = meta_ref[0]
    high_ref[rows] = meta_ref[0]
    for copy in large:
        copy.wait()


def messages(conc, owner, source, weight, count):
    rows, bins, width = conc.shape
    half = bins // 2
    return pl.pallas_call(
        messages_kernel,
        in_specs=[in_place()] * 5,
        out_specs=[pl.BlockSpec(memory_space=pltpu.VMEM)] * 3,
        out_shape=[
            jax.ShapeDtypeStruct((rows + 1, half, width), conc.dtype),
            jax.ShapeDtypeStruct((rows + 1, half, width), conc.dtype),
            jax.ShapeDtypeStruct((1, half, width), conc.dtype),
        ],
        scratch_shapes=[pltpu.VMEM(small.shape, small.dtype) for small in (owner, source, weight, count)]
        + [pltpu.SemaphoreType.DMA((6,))],
        compiler_params=pltpu.CompilerParams(vmem_limit_bytes=MOST_BYTES),
        cost_estimate=pl.CostEstimate(flops=0, bytes_accessed=4 * conc.size, transcendentals=0),
        name="messages",
    )(conc, owner, source, weight, count)


def signs(flags):
    return [1.0 - 2.0 * ref[0].astype(jnp.float32) for ref in flags]


def lat_slots(rows, group, lat_step, lon_step, flags):
    core, chip, lat = signs(flags)
    far = jnp.where(core * chip < 0.0, 4.0, 5.0)
    slot = jnp.where(
        lon_step == 0.0,
        0.0,
        jnp.where(
            lon_step == 2.0 * chip, 2.0, jnp.where(lon_step == -2.0 * chip, 3.0, jnp.where(lon_step == core, 1.0, far))
        ),
    )
    return lat_step == (group - 1.0) * lat, slot * rows


def lon_slots(rows, group, lat_step, lon_step, flags):
    core, chip, lat = signs(flags)
    lon_from = 2.0 * (1.0 - group) * chip + lon_step
    slot = jnp.where(lon_from == 0.0, 1.0, 4.0) - lat_step * lat
    return (lon_from == 0.0) | (lon_from == core), slot * rows


def decode(slots, rows, entries, flags, meta_ref, index_ref, weight_ref):
    for g in range(3):
        owner, source, top, middle, bottom = [
            meta_ref[g, at : at + entries, lane : lane + 128].astype(jnp.float32) for at, lane in FIELDS
        ]
        weight = top + middle + bottom
        band = jnp.where(owner >= NEAR_LON, 1.0, 0.0) + jnp.where(owner >= 2 * NEAR_LON, 1.0, 0.0)
        here, base = slots(rows, float(g), band - 1.0, owner - NEAR_LON * band - REACH, flags)
        here = jnp.where(here & (weight != 0.0), 1.0, 0.0)
        index = base + source
        packed = [[jnp.zeros((1, 128), jnp.float32)] * 2 for _ in range(entries)]
        rank = jnp.zeros((1, 128), jnp.float32)
        for k in range(entries):
            taken = here[k : k + 1]
            for place in range(k + 1):
                spot = (taken > 0.0) & (rank == place)
                packed[place] = [
                    jnp.where(spot, index[k : k + 1], packed[place][0]),
                    jnp.where(spot, weight[k : k + 1], packed[place][1]),
                ]
            rank = rank + taken
        for place in range(entries):
            at = g * entries + place
            index_ref[at : at + 1, :] = packed[place][0].astype(jnp.int32)
            weight_ref[at : at + 1, :] = packed[place][1]
        at = 3 * entries + g
        index_ref[at : at + 1, :] = rank.astype(jnp.int32)


def read_metas(asked, meta_ref, sems, first):
    return [
        pltpu.make_async_copy(ref.at[pl.ds(ref.shape[0] - 1, 1)], meta_ref.at[pl.ds(g, 1)], sems.at[first + g])
        for g, ref in enumerate(asked)
    ]


def decode_kernel(slots, rows, entries, *refs):
    flags, asked, (index_ref, weight_ref, meta_ref, sems) = refs[:3], refs[3:6], refs[6:]
    copies = read_metas(asked, meta_ref, sems, 0)
    for copy in copies:
        copy.start()
    for copy in copies:
        copy.wait()
    decode(slots, rows, entries, flags, meta_ref, index_ref, weight_ref)


def decoded(flags, asked, slots, rows, half, entries):
    width = asked[1].shape[2]
    vectors = -(-3 * (entries + 1) // 8) * 8
    return pl.pallas_call(
        functools.partial(decode_kernel, slots, rows, entries),
        in_specs=[in_smem()] * 3 + [in_place()] * 3,
        out_specs=[pl.BlockSpec(memory_space=pltpu.VMEM)] * 2,
        out_shape=[
            jax.ShapeDtypeStruct((vectors, 128), jnp.int32),
            jax.ShapeDtypeStruct((vectors, 128), jnp.float32),
        ],
        scratch_shapes=[pltpu.VMEM((3, half, width), jnp.bfloat16), pltpu.SemaphoreType.DMA((3,))],
        compiler_params=pltpu.CompilerParams(vmem_limit_bytes=VMEM_BYTES),
        cost_estimate=pl.CostEstimate(flops=0, bytes_accessed=6 * half * width, transcendentals=0),
        name="decode",
    )(*flags, *asked)


def table_copies(bases, rows, sources, table, sems):
    half = table.shape[1]
    return [
        pltpu.make_async_copy(
            source.at[pl.ds(0, rows), pl.ds(base, half), :], table.at[pl.ds(i * rows, rows)], sems.at[i]
        )
        for i, (source, base) in enumerate(zip(sources, bases))
    ]


def add_terms(rows, entries, index_ref, weight_ref, table, outs):
    half, width = table.shape[1:]
    for group, out in enumerate(outs):

        def some(g, carry, group=group, out=out):
            def sums(terms):
                totals = []
                for u in range(UNROLL):
                    r = g * UNROLL + u
                    total = jnp.zeros((half, width), jnp.float32)
                    for k in range(terms):
                        row = group * entries + k
                        total = total + weight_ref[row, r] * table[index_ref[row, r]].astype(jnp.float32)
                    totals.append(total)
                for u in range(UNROLL):
                    out[g * UNROLL + u] = totals[u].astype(out.dtype)

            most = index_ref[3 * entries + group, g * UNROLL]
            for u in range(1, UNROLL):
                most = jnp.maximum(most, index_ref[3 * entries + group, g * UNROLL + u])
            sums(min(QUICK, entries))

            @pl.when(most > QUICK)
            def _():
                sums(entries)

            return carry

        lax.fori_loop(0, rows // UNROLL, some, 0)


def lat_sums_kernel(bases, entries, core_ref, chip_ref, index_ref, weight_ref, *refs):
    tables = len(bases)
    sources, outs = refs[:tables], refs[tables : tables + 3]
    table, sems = refs[tables + 3 :]
    rows = table.shape[0] // tables
    copies = table_copies(bases, rows, sources, table, sems)
    first = core_ref[0] != chip_ref[0]
    for copy in copies[:-2]:
        copy.start()
    pl.when(first)(copies[-2].start)
    pl.when(jnp.logical_not(first))(copies[-1].start)
    for copy in copies[:-2]:
        copy.wait()
    pl.when(first)(copies[-2].wait)
    pl.when(jnp.logical_not(first))(copies[-1].wait)
    add_terms(rows, entries, index_ref, weight_ref, table, outs)


def lon_sums_kernel(bases, slots, entries, *refs):
    tables = len(bases)
    flags, refs = refs[:3], refs[3:]
    asked, sources, outs = refs[:3], refs[3 : 3 + tables], refs[3 + tables : 6 + tables]
    table, meta_ref, index_vec, weight_vec, index_ref, weight_ref, sems = refs[6 + tables :]
    rows = table.shape[0] // tables
    metas = read_metas(asked, meta_ref, sems, tables)
    copies = table_copies(bases, rows, sources, table, sems)
    for copy in metas + copies:
        copy.start()
    for copy in metas:
        copy.wait()
    decode(slots, rows, entries, flags, meta_ref, index_vec, weight_vec)
    to_scalar = [
        pltpu.make_async_copy(index_vec, index_ref, sems.at[tables + 3]),
        pltpu.make_async_copy(weight_vec, weight_ref, sems.at[tables + 4]),
    ]
    for copy in to_scalar:
        copy.start()
    for copy in to_scalar + copies:
        copy.wait()
    add_terms(rows, entries, index_ref, weight_ref, table, outs)


def sums_call(kernel, operands, smem, sources, scratch, rows, half, entries, name):
    tables = len(sources)
    width = sources[0][0].shape[2]
    return pl.pallas_call(
        kernel,
        in_specs=[in_smem()] * smem + [in_place()] * (len(operands) - smem + tables),
        out_specs=[pl.BlockSpec(memory_space=pltpu.VMEM)] * 3,
        out_shape=[
            jax.ShapeDtypeStruct((rows, half, width), dtype) for dtype in (jnp.bfloat16, jnp.float32, jnp.bfloat16)
        ],
        scratch_shapes=[pltpu.VMEM((tables * rows, half, width), jnp.bfloat16)] + scratch,
        compiler_params=pltpu.CompilerParams(vmem_limit_bytes=TABLE_BYTES),
        cost_estimate=pl.CostEstimate(
            flops=6 * rows * entries * half * width,
            bytes_accessed=2 * (tables + 3) * rows * half * width,
            transcendentals=0,
        ),
        name=name,
    )(*operands, *[source for source, _ in sources])


def lat_sums(flags, terms, sources, rows, half, entries):
    kernel = functools.partial(lat_sums_kernel, tuple(base for _, base in sources), entries)
    scratch = [pltpu.SemaphoreType.DMA((len(sources),))]
    return sums_call(kernel, [*flags[:2], *terms], 4, sources, scratch, rows, half, entries, "lat_sums")


def lon_sums(flags, asked, slots, sources, rows, half, entries):
    kernel = functools.partial(lon_sums_kernel, tuple(base for _, base in sources), slots, entries)
    vectors = -(-3 * (entries + 1) // 8) * 8
    scratch = [pltpu.VMEM((3, half, asked[1].shape[2]), jnp.bfloat16)]
    scratch += [space((vectors, 128), dtype) for space in (pltpu.VMEM, pltpu.SMEM) for dtype in (jnp.int32, jnp.float32)]
    scratch += [pltpu.SemaphoreType.DMA((len(sources) + 5,))]
    return sums_call(kernel, [*flags, *asked], 3, sources, scratch, rows, half, entries, "lon_sums")


def edges_kernel(core_ref, *refs):
    rows, half = refs[0].shape[:2]
    per = 128 // 8
    lane = lax.broadcasted_iota(jnp.int32, (half, 128), 1)
    odd = core_ref[0] == 1
    for earlier_ref, out_ref in zip(refs[6:-2], refs[-2:]):
        out_ref[:, half:] = earlier_ref[...]
    for j in range(rows // per):
        ends = []
        for side in range(2):
            parts = refs[3 * side : 3 * side + 3]
            packed = jnp.zeros((half, 128), jnp.float32)
            for i in range(per):
                r = j * per + i
                cells = parts[0][r] + parts[1][r].astype(jnp.float32) + parts[2][r].astype(jnp.float32)
                at = 8 * i + 3 * (1 - side)
                spot = (lane >= at) & (lane < at + 3)
                packed = jnp.where(spot, pltpu.roll(cells, 8 * i + 3, 1), packed)
            ends.append(packed)
        for out_ref, value in zip(refs[-2:], (jnp.where(odd, *ends), jnp.where(odd, *ends[::-1]))):
            out_ref[j, :half] = value.astype(out_ref.dtype)


def edges(core, parts, earlier):
    rows, half, width = parts[0].shape
    specs = [
        pl.BlockSpec((rows, half, 128), lambda t, at=at: (0, 0, at)) for at in (0, width // 128 - 1) for _ in parts
    ]
    whole = lambda shape: pl.BlockSpec(shape, lambda t: (0,) * len(shape))
    packed = (rows // 16, half + sum(array.shape[1] for array in earlier[:1]), 128)
    return pl.pallas_call(
        edges_kernel,
        grid=(1,),
        in_specs=[in_smem()] + specs + [whole(array.shape) for array in earlier],
        out_specs=[whole(packed)] * 2,
        out_shape=[jax.ShapeDtypeStruct(packed, jnp.bfloat16)] * 2,
        compiler_params=pltpu.CompilerParams(vmem_limit_bytes=VMEM_BYTES),
        cost_estimate=pl.CostEstimate(flops=8 * half * 256 * rows, bytes_accessed=16 * half * 256 * rows, transcendentals=0),
        name="edges",
    )(core, *parts, *parts, *earlier)


def combine_kernel(own0, a0, b0, own1, a1, b1, out_ref):
    rows, half = own0.shape[:2]
    for r in range(rows):
        out_ref[r, :half] = own0[r] + a0[r].astype(jnp.float32) + b0[r].astype(jnp.float32)
        out_ref[r, half:] = own1[r] + a1[r].astype(jnp.float32) + b1[r].astype(jnp.float32)


def combine(parts0, parts1):
    rows, half, width = parts0[0].shape
    step = 8
    return pl.pallas_call(
        combine_kernel,
        grid=(rows // step,),
        in_specs=[pl.BlockSpec((step, half, width), lambda t: (t, 0, 0))] * 6,
        out_specs=pl.BlockSpec((step, 2 * half, width), lambda t: (t, 0, 0)),
        out_shape=jax.ShapeDtypeStruct((rows, 2 * half, width), jnp.float32),
        compiler_params=pltpu.CompilerParams(vmem_limit_bytes=VMEM_BYTES),
        cost_estimate=pl.CostEstimate(
            flops=4 * rows * half * width, bytes_accessed=24 * rows * half * width, transcendentals=0
        ),
        name="combine",
    )(*parts0, *parts1)


def shifted_by(row, edge, amount, lane):
    count = len(row)
    if amount == 0:
        return row
    if amount > 0:
        row = row[:-1] + [jnp.where(lane >= 128 - amount, edge, row[-1])]
        turned = [pltpu.roll(tile, amount, 1) for tile in row]
        return [jnp.where(lane < amount, turned[t - 1], turned[t]) for t in range(count)]
    row = [jnp.where(lane < -amount, edge, row[0])] + row[1:]
    turned = [pltpu.roll(tile, 128 + amount, 1) for tile in row]
    return [jnp.where(lane >= 128 + amount, turned[(t + 1) % count], turned[t]) for t in range(count)]


def edge_tile(west_ref, east_ref, r):
    per = 128 // 8
    both = west_ref[r // per].astype(jnp.float32) + east_ref[r // per].astype(jnp.float32)
    return pltpu.roll(both, (125 - 8 * (r % per)) % 128, 1)


def rows_kernel(lat_ref, offset_ref, first_row, last_row, one_ref, other_ref, *outs):
    bins, width = first_row.shape[1:]
    lane = lax.broadcasted_iota(jnp.int32, (bins, 128), 1)
    spots = [slice(128 * t, 128 * t + 128) for t in range(width // 128)]
    end = offset_ref.shape[0] - 1
    odd = lat_ref[0] == 1
    for out_ref, first in ((outs[0], odd), (outs[1], jnp.logical_not(odd))):
        offset = jnp.where(first, offset_ref[0], offset_ref[end])
        row = [jnp.where(first, first_row[0, :, at], last_row[0, :, at]) for at in spots]
        edge = jnp.where(first, edge_tile(one_ref, other_ref, 0), edge_tile(one_ref, other_ref, end))
        for amount in range(-REACH, REACH + 1):

            @pl.when(offset == amount)
            def _(out_ref=out_ref, row=row, edge=edge, amount=amount):
                for at, tile in zip(spots, shifted_by(row, edge, amount, lane)):
                    out_ref[0, :, at] = tile.astype(out_ref.dtype)


def outer_rows(lat, offset, remapped, one, other):
    rows, bins, width = remapped.shape
    row = lambda at: pl.BlockSpec((1, bins, width), lambda t: (at, 0, 0))
    whole = pl.BlockSpec(one.shape, lambda t: (0, 0, 0))
    return pl.pallas_call(
        rows_kernel,
        grid=(1,),
        in_specs=[in_smem()] * 2 + [row(0), row(rows - 1), whole, whole],
        out_specs=[row(0), row(0)],
        out_shape=[jax.ShapeDtypeStruct((1, bins, width), jnp.bfloat16)] * 2,
        compiler_params=pltpu.CompilerParams(vmem_limit_bytes=VMEM_BYTES),
        cost_estimate=pl.CostEstimate(flops=20 * bins * width, bytes_accessed=12 * bins * width, transcendentals=0),
        name="outer_rows",
    )(lat, offset, remapped, remapped, one, other)


def final_kernel(offset_ref, remap_ref, west_ref, east_ref, kappa_ref, local_ref, out_ref, outer_ref, edge_ref):
    rows, bins, width = remap_ref.shape
    count = width // 128
    lane = lax.broadcasted_iota(jnp.int32, (8, 128), 1)
    spots = [slice(128 * t, 128 * t + 128) for t in range(count)]
    for r in range(rows):
        edge_ref[r] = edge_tile(west_ref, east_ref, r)

    def moved(row, edge, amount):
        row = [jnp.where(lane < -amount, edge, row[0])] + row[1:]
        row = row[:-1] + [jnp.where(lane >= 128 - amount, edge, row[-1])]
        turned = [pltpu.roll(tile, (amount + 128) & 127, 1) for tile in row]
        before, after = lane < amount, lane >= 128 + amount
        return [
            jnp.where(before, turned[t - 1], jnp.where(after, turned[(t + 1) % count], turned[t])) for t in range(count)
        ]

    pieces = [slice(8 * b, 8 * b + 8) for b in range(bins // 8)]
    before, now, base = {}, {}, {}
    stores = []
    for r in range(rows):
        amount = offset_ref[r]
        kappa = [kappa_ref[r, :, spot] for spot in spots]
        above = [kappa_ref[max(r - 1, 0), :, spot] for spot in spots]
        for at in pieces:
            row = [remap_ref[r, at, spot] for spot in spots]
            edge = edge_ref[r, at]
            center = moved(row, edge, amount)
            east = moved(row, edge, amount - 1)
            west = moved(row, edge, amount + 1)
            key = at.start
            fresh = []
            for t, spot in enumerate(spots):
                around = kappa[t] * (east[t] + west[t] - 4.0 * center[t])
                fresh.append(local_ref[r, at, spot] + center[t] + around)
                if r == 1:
                    stores.append((r - 1, at, spot, base[key][t] + above[t] * center[t]))
                elif r:
                    stores.append((r - 1, at, spot, base[key][t] + above[t] * (before[key][t] + center[t])))
            if r:
                before[key] = now[key]
            now[key], base[key] = center, fresh
        if r % 2:
            for which, at, spot, value in stores:
                if which:
                    out_ref[which, at, spot] = value
                else:
                    outer_ref[0, at, spot] = value
            stores = []
    for at in pieces:
        for t, spot in enumerate(spots):
            outer_ref[1, at, spot] = base[at.start][t] + kappa_ref[rows - 1, :, spot] * before[at.start][t]


def final(offset, remapped, west, east, kappa, local):
    rows, bins, width = remapped.shape
    tile = bins // 2
    block = pl.BlockSpec((rows, tile, width), lambda t: (0, t, 0))
    packed = pl.BlockSpec((west.shape[0], tile, 128), lambda t: (0, t, 0))
    return pl.pallas_call(
        final_kernel,
        grid=(bins // tile,),
        in_specs=[in_smem(), block, packed, packed, pl.BlockSpec(kappa.shape, lambda t: (0, 0, 0)), block],
        out_specs=[block, pl.BlockSpec((2, tile, width), lambda t: (0, t, 0))],
        out_shape=[
            jax.ShapeDtypeStruct(local.shape, jnp.float32),
            jax.ShapeDtypeStruct((2, bins, width), jnp.float32),
        ],
        scratch_shapes=[pltpu.VMEM((rows, tile, 128), jnp.float32)],
        compiler_params=pltpu.CompilerParams(vmem_limit_bytes=VMEM_BYTES),
        cost_estimate=pl.CostEstimate(flops=30 * remapped.size, bytes_accessed=12 * remapped.size, transcendentals=0),
        name="final",
    )(offset, remapped, west, east, kappa, local)


def halo_kernel(lat_ref, one_ref, other_ref, kappa_ref, outer_ref, _, out_ref, sums_ref, sems):
    odd = lat_ref[0] == 1
    rows = out_ref.shape[0]
    copies = []
    for side, (first, at) in enumerate(((odd, 0), (jnp.logical_not(odd), rows - 1))):
        value = jnp.where(first, one_ref[0].astype(jnp.float32), other_ref[0].astype(jnp.float32))
        sums_ref[side] = outer_ref[side] + kappa_ref[at] * value
        copy = pltpu.make_async_copy(sums_ref.at[pl.ds(side, 1)], out_ref.at[pl.ds(at, 1)], sems.at[side])
        copy.start()
        copies.append(copy)
    for copy in copies:
        copy.wait()


def add_halo(lat, one, other, kappa, outer, partial):
    vmem = pl.BlockSpec(memory_space=pltpu.VMEM)
    return pl.pallas_call(
        halo_kernel,
        in_specs=[in_smem()] + [vmem] * 4 + [in_place()],
        out_specs=in_place(),
        out_shape=jax.ShapeDtypeStruct(partial.shape, jnp.float32),
        scratch_shapes=[pltpu.VMEM(outer.shape, jnp.float32), pltpu.SemaphoreType.DMA((2,))],
        input_output_aliases={5: 0},
        compiler_params=pltpu.CompilerParams(vmem_limit_bytes=VMEM_BYTES),
        cost_estimate=pl.CostEstimate(flops=4 * outer.size, bytes_accessed=20 * outer.size, transcendentals=0),
        name="add_halo",
    )(lat, one, other, kappa, outer, partial)


def body(
    conc,
    dep_owner,
    dep_row,
    dep_weight,
    dep_count,
    zonal_offset,
    agg_rates,
    toeplitz,
    settle,
    kappa,
):
    rows, bins, width = conc.shape
    entries = dep_owner.shape[2]
    my_lat, my_lon = lax.axis_index("lat"), lax.axis_index("lon")
    flags = [(value % 2).astype(jnp.int32).reshape(1) for value in (my_lon, my_lon // 2, my_lat)]
    half = bins // 2
    low, high, meta = messages(conc, dep_owner[0].T, dep_row[0].T, dep_weight[0].T, dep_count)
    lat1, lat2 = swap_lat(high, 0), swap_lat(high, 1)
    lon1, lon2 = swap_chip(low, 0), swap_chip(low, 1)
    beside = swap_core(conc)
    rates, meta = lax.optimization_barrier((agg_rates, meta))
    local = local_terms(conc, rates, toeplitz, settle)
    terms = decoded(flags, [lat1, meta, lat2], lat_slots, rows, half, entries)
    lat1, lat2, local, terms = lax.optimization_barrier((lat1, lat2, local, terms))

    to_lon1, own1, to_lon2 = lon_sums(
        flags,
        [lon1, meta, lon2],
        lon_slots,
        [(lat1, 0), (conc, half), (lat2, 0), (swap_core(lat1), 0), (beside, half), (swap_core(lat2), 0)],
        rows,
        half,
        entries,
    )
    parts1 = [swap_chip(to_lon1, 0), swap_chip(to_lon2, 1)]
    own1, later = lax.optimization_barrier((own1, flags))
    parts1 = [own1] + parts1

    to_lat1, own0, to_lat2 = lat_sums(
        later,
        terms,
        [(conc, 0), (beside, 0), (lon1, 0), (lon2, 0), (swap_core(lon1), 0), (swap_core(lon2), 0)],
        rows,
        half,
        entries,
    )
    parts0 = [own0, swap_lat(to_lat1, 0), swap_lat(to_lat2, 1)]

    kappa = kappa[:, None, :]

    earlier = edges(flags[0], parts1, [])
    parts0, earlier = lax.optimization_barrier((parts0, earlier))
    to_core, to_across = edges(flags[0], parts0, earlier)
    one, other = swap_core(to_core), swap_across(to_across)
    remapped = combine(parts0, parts1)
    row1, row2 = outer_rows(flags[2], zonal_offset, remapped, one, other)
    row1, row2 = swap_lat(row1, 0), swap_lat(row2, 1)
    partial, outer = final(zonal_offset, remapped, one, other, kappa, local)
    return add_halo(flags[2], row1, row2, kappa, outer, partial)


def solution(mesh):
    return jax.shard_map(
        body,
        mesh=mesh,
        in_specs=(
            P("lat", None, "lon"),
            P("lon", "lat", None),
            P("lon", "lat", None),
            P("lon", "lat", None),
            P("lon", "lat"),
            P("lat"),
            P(None, "lat", "lon"),
            P(),
            P(),
            P("lat", "lon"),
        ),
        out_specs=P("lat", None, "lon"),
        check_vma=False,
    )
```

```python
import functools

import jax
import jax.numpy as jnp
from jax import lax
from jax.experimental import pallas as pl
from jax.experimental.pallas import tpu as pltpu
from jax.sharding import PartitionSpec as P

REACH = 2
NEAR_LON = 5
UNROLL = 4
VMEM_BYTES = 12 * 1024 * 1024
MOST_BYTES = 60 * 1024 * 1024
TABLE_BYTES = 20 * 1024 * 1024
QUICK = 2
FIELDS = ((0, 0), (0, 128), (8, 0), (8, 128), (16, 0))


def exchange(value, axis, pairs):
    return lax.ppermute(value, axis, [(i, j) for i, j in pairs] + [(j, i) for i, j in pairs])


def swap_core(value):
    return exchange(value, "lon", [(i, i + 1) for i in range(0, lax.axis_size("lon"), 2)])


def swap_across(value):
    count = lax.axis_size("lon")
    return exchange(value, "lon", [(i, (i + 1) % count) for i in range(1, count, 2)])


def swap_chip(value, second):
    count = lax.axis_size("lon")
    firsts = [i for i in range(count) if (i // 2) % 2 != second]
    return exchange(value, "lon", [(i, (i + 2) % count) for i in firsts])


def swap_lat(value, second):
    count = lax.axis_size("lat")
    return exchange(value, "lat", [(i, i + 1) for i in range(1 - second, count - 1, 2)])


def in_smem():
    return pl.BlockSpec(memory_space=pltpu.SMEM)


def in_place():
    return pl.BlockSpec(memory_space=pl.ANY)


def for_rows(count, one):
    def some(g, carry):
        stores = []
        for u in range(UNROLL):
            stores += one(g * UNROLL + u)
        for ref, at, value in stores:
            ref[at] = value.astype(ref.dtype)
        return carry

    lax.fori_loop(0, count // UNROLL, some, 0)


def growth_kernel(flip_ref, settle_ref, conc_ref, rates_ref, out_ref, mat_ref):
    ranks, rows_step = rates_ref.shape[0], conc_ref.shape[0]
    bins, width = conc_ref.shape[1:]

    @pl.when(pl.program_id(0) == 0)
    def _():
        for q in range(ranks):
            spread = jnp.broadcast_to(flip_ref[q : q + 1, :], (bins, 2 * bins))
            turned = pltpu.roll(spread, bins + 1, 1, stride=1, stride_axis=0)
            mat_ref[q * bins : (q + 1) * bins, :] = turned[:, :bins].astype(jnp.bfloat16)

    settle = jnp.broadcast_to(settle_ref[...], (bins, width))
    for r in range(rows_step):
        cells = conc_ref[r]
        product = jnp.dot(mat_ref[...], cells, preferred_element_type=jnp.float32)
        total = -settle * cells.astype(jnp.float32)
        for q in range(ranks):
            total = total + rates_ref[q, r : r + 1, :] * product[q * bins : (q + 1) * bins]
        out_ref[r] = total


def local_terms(conc, agg_rates, toeplitz, settle):
    rows, bins, width = conc.shape
    ranks = agg_rates.shape[0]
    step = 8
    flipped = jnp.pad(toeplitz[:, ::-1].astype(jnp.float32), ((0, 0), (0, 1)))
    return pl.pallas_call(
        growth_kernel,
        grid=(rows // step,),
        in_specs=[
            pl.BlockSpec((ranks, 2 * bins), lambda i: (0, 0)),
            pl.BlockSpec((bins, 1), lambda i: (0, 0)),
            pl.BlockSpec((step, bins, width), lambda i: (i, 0, 0)),
            pl.BlockSpec((ranks, step, width), lambda i: (0, i, 0)),
        ],
        out_specs=pl.BlockSpec((step, bins, width), lambda i: (i, 0, 0)),
        out_shape=jax.ShapeDtypeStruct(conc.shape, jnp.float32),
        scratch_shapes=[pltpu.VMEM((ranks * bins, bins), jnp.bfloat16)],
        compiler_params=pltpu.CompilerParams(vmem_limit_bytes=VMEM_BYTES),
        cost_estimate=pl.CostEstimate(
            flops=2 * ranks * bins * bins * rows * width, bytes_accessed=8 * conc.size, transcendentals=0
        ),
        name="growth",
    )(flipped, settle[:, None], conc, agg_rates)


def messages_kernel(
    conc_ref, owner_hbm, source_hbm, weight_hbm, count_hbm, low_ref, high_ref, meta_ref,
    owner_ref, source_ref, weight_ref, count_ref, sems,
):
    rows = conc_ref.shape[0]
    half = low_ref.shape[1]
    entries = owner_ref.shape[0]
    small = [
        pltpu.make_async_copy(hbm, ref, sems.at[2 + i])
        for i, (hbm, ref) in enumerate(
            ((owner_hbm, owner_ref), (source_hbm, source_ref), (weight_hbm, weight_ref), (count_hbm, count_ref))
        )
    ]
    large = [
        pltpu.make_async_copy(conc_ref.at[:, pl.ds(i * half, half), :], ref.at[pl.ds(0, rows)], sems.at[i])
        for i, ref in enumerate((low_ref, high_ref))
    ]
    for copy in small + large:
        copy.start()
    meta_ref[...] = jnp.zeros(meta_ref.shape, meta_ref.dtype)
    for copy in small:
        copy.wait()
    wide = lambda value: value.astype(jnp.float32)
    entry = lax.broadcasted_iota(jnp.int32, owner_ref.shape, 0)
    live = jnp.where(entry < count_ref[...], weight_ref[...], 0.0)
    top = live.astype(jnp.bfloat16)
    middle = (live - wide(top)).astype(jnp.bfloat16)
    bottom = (live - wide(top) - wide(middle)).astype(jnp.bfloat16)
    fields = (wide(owner_ref[...]), wide(source_ref[...]), wide(top), wide(middle), wide(bottom))
    for field, (at, lane) in zip(fields, FIELDS):
        meta_ref[0, at : at + entries, lane : lane + rows] = field.astype(jnp.bfloat16)
    low_ref[rows] = meta_ref[0]
    high_ref[rows] = meta_ref[0]
    for copy in large:
        copy.wait()


def messages(conc, owner, source, weight, count):
    rows, bins, width = conc.shape
    half = bins // 2
    return pl.pallas_call(
        messages_kernel,
        in_specs=[in_place()] * 5,
        out_specs=[pl.BlockSpec(memory_space=pltpu.VMEM)] * 3,
        out_shape=[
            jax.ShapeDtypeStruct((rows + 1, half, width), conc.dtype),
            jax.ShapeDtypeStruct((rows + 1, half, width), conc.dtype),
            jax.ShapeDtypeStruct((1, half, width), conc.dtype),
        ],
        scratch_shapes=[pltpu.VMEM(small.shape, small.dtype) for small in (owner, source, weight, count)]
        + [pltpu.SemaphoreType.DMA((6,))],
        compiler_params=pltpu.CompilerParams(vmem_limit_bytes=MOST_BYTES),
        cost_estimate=pl.CostEstimate(flops=0, bytes_accessed=4 * conc.size, transcendentals=0),
        name="messages",
    )(conc, owner, source, weight, count)


def signs(flags):
    return [1.0 - 2.0 * ref[0].astype(jnp.float32) for ref in flags]


def lat_slots(rows, group, lat_step, lon_step, flags):
    core, chip, lat = signs(flags)
    far = jnp.where(core * chip < 0.0, 4.0, 5.0)
    slot = jnp.where(
        lon_step == 0.0,
        0.0,
        jnp.where(
            lon_step == 2.0 * chip, 2.0, jnp.where(lon_step == -2.0 * chip, 3.0, jnp.where(lon_step == core, 1.0, far))
        ),
    )
    return lat_step == (group - 1.0) * lat, slot * rows


def lon_slots(rows, group, lat_step, lon_step, flags):
    core, chip, lat = signs(flags)
    lon_from = 2.0 * (1.0 - group) * chip + lon_step
    slot = jnp.where(lon_from == 0.0, 1.0, 4.0) - lat_step * lat
    return (lon_from == 0.0) | (lon_from == core), slot * rows


def decode(slots, rows, entries, flags, meta_ref, index_ref, weight_ref):
    for g in range(3):
        owner, source, top, middle, bottom = [
            meta_ref[g, at : at + entries, lane : lane + 128].astype(jnp.float32) for at, lane in FIELDS
        ]
        weight = top + middle + bottom
        band = jnp.where(owner >= NEAR_LON, 1.0, 0.0) + jnp.where(owner >= 2 * NEAR_LON, 1.0, 0.0)
        here, base = slots(rows, float(g), band - 1.0, owner - NEAR_LON * band - REACH, flags)
        here = jnp.where(here & (weight != 0.0), 1.0, 0.0)
        index = base + source
        packed = [[jnp.zeros((1, 128), jnp.float32)] * 2 for _ in range(entries)]
        rank = jnp.zeros((1, 128), jnp.float32)
        for k in range(entries):
            taken = here[k : k + 1]
            for place in range(k + 1):
                spot = (taken > 0.0) & (rank == place)
                packed[place] = [
                    jnp.where(spot, index[k : k + 1], packed[place][0]),
                    jnp.where(spot, weight[k : k + 1], packed[place][1]),
                ]
            rank = rank + taken
        for place in range(entries):
            at = g * entries + place
            index_ref[at : at + 1, :] = packed[place][0].astype(jnp.int32)
            weight_ref[at : at + 1, :] = packed[place][1]
        at = 3 * entries + g
        index_ref[at : at + 1, :] = rank.astype(jnp.int32)


def read_metas(asked, meta_ref, sems, first):
    return [
        pltpu.make_async_copy(ref.at[pl.ds(ref.shape[0] - 1, 1)], meta_ref.at[pl.ds(g, 1)], sems.at[first + g])
        for g, ref in enumerate(asked)
    ]


def decode_kernel(slots, rows, entries, *refs):
    flags, asked, (index_ref, weight_ref, meta_ref, sems) = refs[:3], refs[3:6], refs[6:]
    copies = read_metas(asked, meta_ref, sems, 0)
    for copy in copies:
        copy.start()
    for copy in copies:
        copy.wait()
    decode(slots, rows, entries, flags, meta_ref, index_ref, weight_ref)


def decoded(flags, asked, slots, rows, half, entries):
    width = asked[1].shape[2]
    vectors = -(-3 * (entries + 1) // 8) * 8
    return pl.pallas_call(
        functools.partial(decode_kernel, slots, rows, entries),
        in_specs=[in_smem()] * 3 + [in_place()] * 3,
        out_specs=[pl.BlockSpec(memory_space=pltpu.VMEM)] * 2,
        out_shape=[
            jax.ShapeDtypeStruct((vectors, 128), jnp.int32),
            jax.ShapeDtypeStruct((vectors, 128), jnp.float32),
        ],
        scratch_shapes=[pltpu.VMEM((3, half, width), jnp.bfloat16), pltpu.SemaphoreType.DMA((3,))],
        compiler_params=pltpu.CompilerParams(vmem_limit_bytes=VMEM_BYTES),
        cost_estimate=pl.CostEstimate(flops=0, bytes_accessed=6 * half * width, transcendentals=0),
        name="decode",
    )(*flags, *asked)


def table_copies(bases, rows, sources, table, sems):
    half = table.shape[1]
    return [
        pltpu.make_async_copy(
            source.at[pl.ds(0, rows), pl.ds(base, half), :], table.at[pl.ds(i * rows, rows)], sems.at[i]
        )
        for i, (source, base) in enumerate(zip(sources, bases))
    ]


def add_terms(rows, entries, index_ref, weight_ref, table, outs):
    half, width = table.shape[1:]
    for group, out in enumerate(outs):

        def some(g, carry, group=group, out=out):
            def sums(terms):
                totals = []
                for u in range(UNROLL):
                    r = g * UNROLL + u
                    total = jnp.zeros((half, width), jnp.float32)
                    for k in range(terms):
                        row = group * entries + k
                        total = total + weight_ref[row, r] * table[index_ref[row, r]].astype(jnp.float32)
                    totals.append(total)
                for u in range(UNROLL):
                    out[g * UNROLL + u] = totals[u].astype(out.dtype)

            most = index_ref[3 * entries + group, g * UNROLL]
            for u in range(1, UNROLL):
                most = jnp.maximum(most, index_ref[3 * entries + group, g * UNROLL + u])
            sums(min(QUICK, entries))

            @pl.when(most > QUICK)
            def _():
                sums(entries)

            return carry

        lax.fori_loop(0, rows // UNROLL, some, 0)


def lat_sums_kernel(bases, entries, core_ref, chip_ref, index_ref, weight_ref, *refs):
    tables = len(bases)
    sources, outs = refs[:tables], refs[tables : tables + 3]
    table, sems = refs[tables + 3 :]
    rows = table.shape[0] // tables
    copies = table_copies(bases, rows, sources, table, sems)
    first = core_ref[0] != chip_ref[0]
    for copy in copies[:-2]:
        copy.start()
    pl.when(first)(copies[-2].start)
    pl.when(jnp.logical_not(first))(copies[-1].start)
    for copy in copies[:-2]:
        copy.wait()
    pl.when(first)(copies[-2].wait)
    pl.when(jnp.logical_not(first))(copies[-1].wait)
    add_terms(rows, entries, index_ref, weight_ref, table, outs)


def lon_sums_kernel(bases, slots, entries, *refs):
    tables = len(bases)
    flags, refs = refs[:3], refs[3:]
    asked, sources, outs = refs[:3], refs[3 : 3 + tables], refs[3 + tables : 6 + tables]
    table, meta_ref, index_vec, weight_vec, index_ref, weight_ref, sems = refs[6 + tables :]
    rows = table.shape[0] // tables
    metas = read_metas(asked, meta_ref, sems, tables)
    copies = table_copies(bases, rows, sources, table, sems)
    for copy in metas + copies:
        copy.start()
    for copy in metas:
        copy.wait()
    decode(slots, rows, entries, flags, meta_ref, index_vec, weight_vec)
    to_scalar = [
        pltpu.make_async_copy(index_vec, index_ref, sems.at[tables + 3]),
        pltpu.make_async_copy(weight_vec, weight_ref, sems.at[tables + 4]),
    ]
    for copy in to_scalar:
        copy.start()
    for copy in to_scalar + copies:
        copy.wait()
    add_terms(rows, entries, index_ref, weight_ref, table, outs)


def sums_call(kernel, operands, smem, sources, scratch, rows, half, entries, name):
    tables = len(sources)
    width = sources[0][0].shape[2]
    return pl.pallas_call(
        kernel,
        in_specs=[in_smem()] * smem + [in_place()] * (len(operands) - smem + tables),
        out_specs=[pl.BlockSpec(memory_space=pltpu.VMEM)] * 3,
        out_shape=[
            jax.ShapeDtypeStruct((rows, half, width), dtype) for dtype in (jnp.bfloat16, jnp.float32, jnp.bfloat16)
        ],
        scratch_shapes=[pltpu.VMEM((tables * rows, half, width), jnp.bfloat16)] + scratch,
        compiler_params=pltpu.CompilerParams(vmem_limit_bytes=TABLE_BYTES),
        cost_estimate=pl.CostEstimate(
            flops=6 * rows * entries * half * width,
            bytes_accessed=2 * (tables + 3) * rows * half * width,
            transcendentals=0,
        ),
        name=name,
    )(*operands, *[source for source, _ in sources])


def lat_sums(flags, terms, sources, rows, half, entries):
    kernel = functools.partial(lat_sums_kernel, tuple(base for _, base in sources), entries)
    scratch = [pltpu.SemaphoreType.DMA((len(sources),))]
    return sums_call(kernel, [*flags[:2], *terms], 4, sources, scratch, rows, half, entries, "lat_sums")


def lon_sums(flags, asked, slots, sources, rows, half, entries):
    kernel = functools.partial(lon_sums_kernel, tuple(base for _, base in sources), slots, entries)
    vectors = -(-3 * (entries + 1) // 8) * 8
    scratch = [pltpu.VMEM((3, half, asked[1].shape[2]), jnp.bfloat16)]
    scratch += [space((vectors, 128), dtype) for space in (pltpu.VMEM, pltpu.SMEM) for dtype in (jnp.int32, jnp.float32)]
    scratch += [pltpu.SemaphoreType.DMA((len(sources) + 5,))]
    return sums_call(kernel, [*flags, *asked], 3, sources, scratch, rows, half, entries, "lon_sums")


def edges_kernel(core_ref, *refs):
    rows, half = refs[0].shape[:2]
    per = 128 // 8
    lane = lax.broadcasted_iota(jnp.int32, (half, 128), 1)
    odd = core_ref[0] == 1
    for earlier_ref, out_ref in zip(refs[6:-2], refs[-2:]):
        out_ref[:, half:] = earlier_ref[...]
    for j in range(rows // per):
        ends = []
        for side in range(2):
            parts = refs[3 * side : 3 * side + 3]
            packed = jnp.zeros((half, 128), jnp.float32)
            for i in range(per):
                r = j * per + i
                cells = parts[0][r] + parts[1][r].astype(jnp.float32) + parts[2][r].astype(jnp.float32)
                at = 8 * i + 3 * (1 - side)
                spot = (lane >= at) & (lane < at + 3)
                packed = jnp.where(spot, pltpu.roll(cells, 8 * i + 3, 1), packed)
            ends.append(packed)
        for out_ref, value in zip(refs[-2:], (jnp.where(odd, *ends), jnp.where(odd, *ends[::-1]))):
            out_ref[j, :half] = value.astype(out_ref.dtype)


def edges(core, parts, earlier):
    rows, half, width = parts[0].shape
    specs = [
        pl.BlockSpec((rows, half, 128), lambda t, at=at: (0, 0, at)) for at in (0, width // 128 - 1) for _ in parts
    ]
    whole = lambda shape: pl.BlockSpec(shape, lambda t: (0,) * len(shape))
    packed = (rows // 16, half + sum(array.shape[1] for array in earlier[:1]), 128)
    return pl.pallas_call(
        edges_kernel,
        grid=(1,),
        in_specs=[in_smem()] + specs + [whole(array.shape) for array in earlier],
        out_specs=[whole(packed)] * 2,
        out_shape=[jax.ShapeDtypeStruct(packed, jnp.bfloat16)] * 2,
        compiler_params=pltpu.CompilerParams(vmem_limit_bytes=VMEM_BYTES),
        cost_estimate=pl.CostEstimate(flops=8 * half * 256 * rows, bytes_accessed=16 * half * 256 * rows, transcendentals=0),
        name="edges",
    )(core, *parts, *parts, *earlier)


def combine_kernel(own0, a0, b0, own1, a1, b1, out_ref):
    rows, half = own0.shape[:2]
    for r in range(rows):
        out_ref[r, :half] = own0[r] + a0[r].astype(jnp.float32) + b0[r].astype(jnp.float32)
        out_ref[r, half:] = own1[r] + a1[r].astype(jnp.float32) + b1[r].astype(jnp.float32)


def combine(parts0, parts1):
    rows, half, width = parts0[0].shape
    step = 8
    return pl.pallas_call(
        combine_kernel,
        grid=(rows // step,),
        in_specs=[pl.BlockSpec((step, half, width), lambda t: (t, 0, 0))] * 6,
        out_specs=pl.BlockSpec((step, 2 * half, width), lambda t: (t, 0, 0)),
        out_shape=jax.ShapeDtypeStruct((rows, 2 * half, width), jnp.float32),
        compiler_params=pltpu.CompilerParams(vmem_limit_bytes=VMEM_BYTES),
        cost_estimate=pl.CostEstimate(
            flops=4 * rows * half * width, bytes_accessed=24 * rows * half * width, transcendentals=0
        ),
        name="combine",
    )(*parts0, *parts1)


def shifted_by(row, edge, amount, lane):
    count = len(row)
    if amount == 0:
        return row
    if amount > 0:
        row = row[:-1] + [jnp.where(lane >= 128 - amount, edge, row[-1])]
        turned = [pltpu.roll(tile, amount, 1) for tile in row]
        return [jnp.where(lane < amount, turned[t - 1], turned[t]) for t in range(count)]
    row = [jnp.where(lane < -amount, edge, row[0])] + row[1:]
    turned = [pltpu.roll(tile, 128 + amount, 1) for tile in row]
    return [jnp.where(lane >= 128 + amount, turned[(t + 1) % count], turned[t]) for t in range(count)]


def edge_tile(west_ref, east_ref, r):
    per = 128 // 8
    both = west_ref[r // per].astype(jnp.float32) + east_ref[r // per].astype(jnp.float32)
    return pltpu.roll(both, (125 - 8 * (r % per)) % 128, 1)


def rows_kernel(lat_ref, offset_ref, first_row, last_row, one_ref, other_ref, *outs):
    bins, width = first_row.shape[1:]
    lane = lax.broadcasted_iota(jnp.int32, (bins, 128), 1)
    spots = [slice(128 * t, 128 * t + 128) for t in range(width // 128)]
    end = offset_ref.shape[0] - 1
    odd = lat_ref[0] == 1
    for out_ref, first in ((outs[0], odd), (outs[1], jnp.logical_not(odd))):
        offset = jnp.where(first, offset_ref[0], offset_ref[end])
        row = [jnp.where(first, first_row[0, :, at], last_row[0, :, at]) for at in spots]
        edge = jnp.where(first, edge_tile(one_ref, other_ref, 0), edge_tile(one_ref, other_ref, end))
        for amount in range(-REACH, REACH + 1):

            @pl.when(offset == amount)
            def _(out_ref=out_ref, row=row, edge=edge, amount=amount):
                for at, tile in zip(spots, shifted_by(row, edge, amount, lane)):
                    out_ref[0, :, at] = tile.astype(out_ref.dtype)


def outer_rows(lat, offset, remapped, one, other):
    rows, bins, width = remapped.shape
    row = lambda at: pl.BlockSpec((1, bins, width), lambda t: (at, 0, 0))
    whole = pl.BlockSpec(one.shape, lambda t: (0, 0, 0))
    return pl.pallas_call(
        rows_kernel,
        grid=(1,),
        in_specs=[in_smem()] * 2 + [row(0), row(rows - 1), whole, whole],
        out_specs=[row(0), row(0)],
        out_shape=[jax.ShapeDtypeStruct((1, bins, width), jnp.bfloat16)] * 2,
        compiler_params=pltpu.CompilerParams(vmem_limit_bytes=VMEM_BYTES),
        cost_estimate=pl.CostEstimate(flops=20 * bins * width, bytes_accessed=12 * bins * width, transcendentals=0),
        name="outer_rows",
    )(lat, offset, remapped, remapped, one, other)


def final_kernel(offset_ref, remap_ref, west_ref, east_ref, kappa_ref, local_ref, out_ref, outer_ref, edge_ref):
    rows, bins, width = remap_ref.shape
    count = width // 128
    lane = lax.broadcasted_iota(jnp.int32, (8, 128), 1)
    spots = [slice(128 * t, 128 * t + 128) for t in range(count)]
    for r in range(rows):
        edge_ref[r] = edge_tile(west_ref, east_ref, r)

    def moved(row, edge, amount):
        row = [jnp.where(lane < -amount, edge, row[0])] + row[1:]
        row = row[:-1] + [jnp.where(lane >= 128 - amount, edge, row[-1])]
        turned = [pltpu.roll(tile, (amount + 128) & 127, 1) for tile in row]
        before, after = lane < amount, lane >= 128 + amount
        return [
            jnp.where(before, turned[t - 1], jnp.where(after, turned[(t + 1) % count], turned[t])) for t in range(count)
        ]

    pieces = [slice(8 * b, 8 * b + 8) for b in range(bins // 8)]
    before, now, base = {}, {}, {}
    stores = []
    for r in range(rows):
        amount = offset_ref[r]
        kappa = [kappa_ref[r, :, spot] for spot in spots]
        above = [kappa_ref[max(r - 1, 0), :, spot] for spot in spots]
        for at in pieces:
            row = [remap_ref[r, at, spot] for spot in spots]
            edge = edge_ref[r, at]
            center = moved(row, edge, amount)
            east = moved(row, edge, amount - 1)
            west = moved(row, edge, amount + 1)
            key = at.start
            fresh = []
            for t, spot in enumerate(spots):
                around = kappa[t] * (east[t] + west[t] - 4.0 * center[t])
                fresh.append(local_ref[r, at, spot] + center[t] + around)
                if r == 1:
                    stores.append((r - 1, at, spot, base[key][t] + above[t] * center[t]))
                elif r:
                    stores.append((r - 1, at, spot, base[key][t] + above[t] * (before[key][t] + center[t])))
            if r:
                before[key] = now[key]
            now[key], base[key] = center, fresh
        if r % 2:
            for which, at, spot, value in stores:
                if which:
                    out_ref[which, at, spot] = value
                else:
                    outer_ref[0, at, spot] = value
            stores = []
    for at in pieces:
        for t, spot in enumerate(spots):
            outer_ref[1, at, spot] = base[at.start][t] + kappa_ref[rows - 1, :, spot] * before[at.start][t]


def final(offset, remapped, west, east, kappa, local):
    rows, bins, width = remapped.shape
    tile = bins // 2
    block = pl.BlockSpec((rows, tile, width), lambda t: (0, t, 0))
    packed = pl.BlockSpec((west.shape[0], tile, 128), lambda t: (0, t, 0))
    return pl.pallas_call(
        final_kernel,
        grid=(bins // tile,),
        in_specs=[in_smem(), block, packed, packed, pl.BlockSpec(kappa.shape, lambda t: (0, 0, 0)), block],
        out_specs=[block, pl.BlockSpec((2, tile, width), lambda t: (0, t, 0))],
        out_shape=[
            jax.ShapeDtypeStruct(local.shape, jnp.float32),
            jax.ShapeDtypeStruct((2, bins, width), jnp.float32),
        ],
        scratch_shapes=[pltpu.VMEM((rows, tile, 128), jnp.float32)],
        compiler_params=pltpu.CompilerParams(vmem_limit_bytes=VMEM_BYTES),
        cost_estimate=pl.CostEstimate(flops=30 * remapped.size, bytes_accessed=12 * remapped.size, transcendentals=0),
        name="final",
    )(offset, remapped, west, east, kappa, local)


def halo_kernel(lat_ref, one_ref, other_ref, kappa_ref, outer_ref, _, out_ref, sums_ref, sems):
    odd = lat_ref[0] == 1
    rows = out_ref.shape[0]
    copies = []
    for side, (first, at) in enumerate(((odd, 0), (jnp.logical_not(odd), rows - 1))):
        value = jnp.where(first, one_ref[0].astype(jnp.float32), other_ref[0].astype(jnp.float32))
        sums_ref[side] = outer_ref[side] + kappa_ref[at] * value
        copy = pltpu.make_async_copy(sums_ref.at[pl.ds(side, 1)], out_ref.at[pl.ds(at, 1)], sems.at[side])
        copy.start()
        copies.append(copy)
    for copy in copies:
        copy.wait()


def add_halo(lat, one, other, kappa, outer, partial):
    vmem = pl.BlockSpec(memory_space=pltpu.VMEM)
    return pl.pallas_call(
        halo_kernel,
        in_specs=[in_smem()] + [vmem] * 4 + [in_place()],
        out_specs=in_place(),
        out_shape=jax.ShapeDtypeStruct(partial.shape, jnp.float32),
        scratch_shapes=[pltpu.VMEM(outer.shape, jnp.float32), pltpu.SemaphoreType.DMA((2,))],
        input_output_aliases={5: 0},
        compiler_params=pltpu.CompilerParams(vmem_limit_bytes=VMEM_BYTES),
        cost_estimate=pl.CostEstimate(flops=4 * outer.size, bytes_accessed=20 * outer.size, transcendentals=0),
        name="add_halo",
    )(lat, one, other, kappa, outer, partial)


def body(
    conc,
    dep_owner,
    dep_row,
    dep_weight,
    dep_count,
    zonal_offset,
    agg_rates,
    toeplitz,
    settle,
    kappa,
):
    rows, bins, width = conc.shape
    entries = dep_owner.shape[2]
    my_lat, my_lon = lax.axis_index("lat"), lax.axis_index("lon")
    flags = [(value % 2).astype(jnp.int32).reshape(1) for value in (my_lon, my_lon // 2 + 1, my_lat + 1)]
    half = bins // 2
    low, high, meta = messages(conc, dep_owner[0].T, dep_row[0].T, dep_weight[0].T, dep_count)
    lat1, lat2 = swap_lat(high, 0), swap_lat(high, 1)
    lon1, lon2 = swap_chip(low, 0), swap_chip(low, 1)
    beside = swap_core(conc)
    rates, meta = lax.optimization_barrier((agg_rates, meta))
    local = local_terms(conc, rates, toeplitz, settle)
    terms = decoded(flags, [lat1, meta, lat2], lat_slots, rows, half, entries)
    lat1, lat2, local, terms = lax.optimization_barrier((lat1, lat2, local, terms))

    to_lon1, own1, to_lon2 = lon_sums(
        flags,
        [lon1, meta, lon2],
        lon_slots,
        [(lat1, 0), (conc, half), (lat2, 0), (swap_core(lat1), 0), (beside, half), (swap_core(lat2), 0)],
        rows,
        half,
        entries,
    )
    parts1 = [swap_chip(to_lon1, 0), swap_chip(to_lon2, 1)]
    own1, later = lax.optimization_barrier((own1, flags))
    parts1 = [own1] + parts1

    to_lat1, own0, to_lat2 = lat_sums(
        later,
        terms,
        [(conc, 0), (beside, 0), (lon1, 0), (lon2, 0), (swap_core(lon1), 0), (swap_core(lon2), 0)],
        rows,
        half,
        entries,
    )
    parts0 = [own0, swap_lat(to_lat1, 0), swap_lat(to_lat2, 1)]

    kappa = kappa[:, None, :]

    earlier = edges(flags[0], parts1, [])
    parts0, earlier = lax.optimization_barrier((parts0, earlier))
    to_core, to_across = edges(flags[0], parts0, earlier)
    one, other = swap_core(to_core), swap_across(to_across)
    remapped = combine(parts0, parts1)
    row1, row2 = outer_rows(flags[2], zonal_offset, remapped, one, other)
    row1, row2 = swap_lat(row1, 0), swap_lat(row2, 1)
    partial, outer = final(zonal_offset, remapped, one, other, kappa, local)
    return add_halo(flags[2], row1, row2, kappa, outer, partial)


def solution(mesh):
    return jax.shard_map(
        body,
        mesh=mesh,
        in_specs=(
            P("lat", None, "lon"),
            P("lon", "lat", None),
            P("lon", "lat", None),
            P("lon", "lat", None),
            P("lon", "lat"),
            P("lat"),
            P(None, "lat", "lon"),
            P(),
            P(),
            P("lat", "lon"),
        ),
        out_specs=P("lat", None, "lon"),
        check_vma=False,
    )
```

```python
import functools

import jax
import jax.numpy as jnp
from jax import lax
from jax.experimental import pallas as pl
from jax.experimental.pallas import tpu as pltpu
from jax.sharding import PartitionSpec as P

REACH = 2
NEAR_LON = 5
UNROLL = 4
VMEM_BYTES = 12 * 1024 * 1024
MOST_BYTES = 60 * 1024 * 1024
TABLE_BYTES = 20 * 1024 * 1024
QUICK = 2
FIELDS = ((0, 0), (0, 128), (8, 0), (8, 128), (16, 0))


def exchange(value, axis, pairs):
    return lax.ppermute(value, axis, [(i, j) for i, j in pairs] + [(j, i) for i, j in pairs])


def swap_core(value):
    return exchange(value, "lon", [(i, i + 1) for i in range(0, lax.axis_size("lon"), 2)])


def swap_across(value):
    count = lax.axis_size("lon")
    return exchange(value, "lon", [(i, (i + 1) % count) for i in range(1, count, 2)])


def swap_chip(value, second):
    count = lax.axis_size("lon")
    firsts = [i for i in range(count) if (i // 2) % 2 == second]
    return exchange(value, "lon", [(i, (i + 2) % count) for i in firsts])


def swap_lat(value, second):
    count = lax.axis_size("lat")
    return exchange(value, "lat", [(i, i + 1) for i in range(second, count - 1, 2)])


def in_smem():
    return pl.BlockSpec(memory_space=pltpu.SMEM)


def in_place():
    return pl.BlockSpec(memory_space=pl.ANY)


def for_rows(count, one):
    def some(g, carry):
        stores = []
        for u in range(UNROLL):
            stores += one(g * UNROLL + u)
        for ref, at, value in stores:
            ref[at] = value.astype(ref.dtype)
        return carry

    lax.fori_loop(0, count // UNROLL, some, 0)


def growth_kernel(flip_ref, settle_ref, conc_ref, rates_ref, out_ref, mat_ref):
    ranks, rows_step = rates_ref.shape[0], conc_ref.shape[0]
    bins, width = conc_ref.shape[1:]

    @pl.when(pl.program_id(0) == 0)
    def _():
        for q in range(ranks):
            spread = jnp.broadcast_to(flip_ref[q : q + 1, :], (bins, 2 * bins))
            turned = pltpu.roll(spread, bins + 1, 1, stride=1, stride_axis=0)
            mat_ref[q * bins : (q + 1) * bins, :] = turned[:, :bins].astype(jnp.bfloat16)

    settle = jnp.broadcast_to(settle_ref[...], (bins, width))
    for r in range(rows_step):
        cells = conc_ref[r]
        product = jnp.dot(mat_ref[...], cells, preferred_element_type=jnp.float32)
        total = -settle * cells.astype(jnp.float32)
        for q in range(ranks):
            total = total + rates_ref[q, r : r + 1, :] * product[q * bins : (q + 1) * bins]
        out_ref[r] = total


def local_terms(conc, agg_rates, toeplitz, settle):
    rows, bins, width = conc.shape
    ranks = agg_rates.shape[0]
    step = 8
    flipped = jnp.pad(toeplitz[:, ::-1].astype(jnp.float32), ((0, 0), (0, 1)))
    return pl.pallas_call(
        growth_kernel,
        grid=(rows // step,),
        in_specs=[
            pl.BlockSpec((ranks, 2 * bins), lambda i: (0, 0)),
            pl.BlockSpec((bins, 1), lambda i: (0, 0)),
            pl.BlockSpec((step, bins, width), lambda i: (i, 0, 0)),
            pl.BlockSpec((ranks, step, width), lambda i: (0, i, 0)),
        ],
        out_specs=pl.BlockSpec((step, bins, width), lambda i: (i, 0, 0)),
        out_shape=jax.ShapeDtypeStruct(conc.shape, jnp.float32),
        scratch_shapes=[pltpu.VMEM((ranks * bins, bins), jnp.bfloat16)],
        compiler_params=pltpu.CompilerParams(vmem_limit_bytes=VMEM_BYTES),
        cost_estimate=pl.CostEstimate(
            flops=2 * ranks * bins * bins * rows * width, bytes_accessed=8 * conc.size, transcendentals=0
        ),
        name="growth",
    )(flipped, settle[:, None], conc, agg_rates)


def messages_kernel(
    conc_ref, owner_hbm, source_hbm, weight_hbm, count_hbm, low_ref, high_ref, meta_ref,
    owner_ref, source_ref, weight_ref, count_ref, sems,
):
    rows = conc_ref.shape[0]
    half = low_ref.shape[1]
    entries = owner_ref.shape[0]
    small = [
        pltpu.make_async_copy(hbm, ref, sems.at[2 + i])
        for i, (hbm, ref) in enumerate(
            ((owner_hbm, owner_ref), (source_hbm, source_ref), (weight_hbm, weight_ref), (count_hbm, count_ref))
        )
    ]
    large = [
        pltpu.make_async_copy(conc_ref.at[:, pl.ds(i * half, half), :], ref.at[pl.ds(0, rows)], sems.at[i])
        for i, ref in enumerate((low_ref, high_ref))
    ]
    for copy in small + large:
        copy.start()
    meta_ref[...] = jnp.zeros(meta_ref.shape, meta_ref.dtype)
    for copy in small:
        copy.wait()
    wide = lambda value: value.astype(jnp.float32)
    entry = lax.broadcasted_iota(jnp.int32, owner_ref.shape, 0)
    live = jnp.where(entry < count_ref[...], weight_ref[...], 0.0)
    top = live.astype(jnp.bfloat16)
    middle = (live - wide(top)).astype(jnp.bfloat16)
    bottom = (live - wide(top) - wide(middle)).astype(jnp.bfloat16)
    fields = (wide(owner_ref[...]), wide(source_ref[...]), wide(top), wide(middle), wide(bottom))
    for field, (at, lane) in zip(fields, FIELDS):
        meta_ref[0, at : at + entries, lane : lane + rows] = field.astype(jnp.bfloat16)
    low_ref[rows] = meta_ref[0]
    high_ref[rows] = meta_ref[0]
    for copy in large:
        copy.wait()


def messages(conc, owner, source, weight, count):
    rows, bins, width = conc.shape
    half = bins // 2
    return pl.pallas_call(
        messages_kernel,
        in_specs=[in_place()] * 5,
        out_specs=[pl.BlockSpec(memory_space=pltpu.VMEM)] * 3,
        out_shape=[
            jax.ShapeDtypeStruct((rows + 1, half, width), conc.dtype),
            jax.ShapeDtypeStruct((rows + 1, half, width), conc.dtype),
            jax.ShapeDtypeStruct((1, half, width), conc.dtype),
        ],
        scratch_shapes=[pltpu.VMEM(small.shape, small.dtype) for small in (owner, source, weight, count)]
        + [pltpu.SemaphoreType.DMA((6,))],
        compiler_params=pltpu.CompilerParams(vmem_limit_bytes=MOST_BYTES),
        cost_estimate=pl.CostEstimate(flops=0, bytes_accessed=4 * conc.size, transcendentals=0),
        name="messages",
    )(conc, owner, source, weight, count)


def signs(flags):
    return [1.0 - 2.0 * ref[0].astype(jnp.float32) for ref in flags]


def lat_slots(rows, group, lat_step, lon_step, flags):
    core, chip, lat = signs(flags)
    far = jnp.where(core * chip < 0.0, 4.0, 5.0)
    slot = jnp.where(
        lon_step == 0.0,
        0.0,
        jnp.where(
            lon_step == 2.0 * chip, 2.0, jnp.where(lon_step == -2.0 * chip, 3.0, jnp.where(lon_step == core, 1.0, far))
        ),
    )
    return lat_step == (group - 1.0) * lat, slot * rows


def lon_slots(rows, group, lat_step, lon_step, flags):
    core, chip, lat = signs(flags)
    lon_from = 2.0 * (1.0 - group) * chip + lon_step
    slot = jnp.where(lon_from == 0.0, 1.0, 4.0) - lat_step * lat
    return (lon_from == 0.0) | (lon_from == core), slot * rows


def decode(slots, rows, entries, flags, meta_ref, index_ref, weight_ref):
    for g in range(3):
        owner, source, top, middle, bottom = [
            meta_ref[g, at : at + entries, lane : lane + 128].astype(jnp.float32) for at, lane in FIELDS
        ]
        weight = top + middle + bottom
        band = jnp.where(owner >= NEAR_LON, 1.0, 0.0) + jnp.where(owner >= 2 * NEAR_LON, 1.0, 0.0)
        here, base = slots(rows, float(g), band - 1.0, owner - NEAR_LON * band - REACH, flags)
        here = jnp.where(here & (weight != 0.0), 1.0, 0.0)
        index = base + source
        packed = [[jnp.zeros((1, 128), jnp.float32)] * 2 for _ in range(entries)]
        rank = jnp.zeros((1, 128), jnp.float32)
        for k in range(entries):
            taken = here[k : k + 1]
            for place in range(k + 1):
                spot = (taken > 0.0) & (rank == place)
                packed[place] = [
                    jnp.where(spot, index[k : k + 1], packed[place][0]),
                    jnp.where(spot, weight[k : k + 1], packed[place][1]),
                ]
            rank = rank + taken
        for place in range(entries):
            at = g * entries + place
            index_ref[at : at + 1, :] = packed[place][0].astype(jnp.int32)
            weight_ref[at : at + 1, :] = packed[place][1]
        at = 3 * entries + g
        index_ref[at : at + 1, :] = rank.astype(jnp.int32)


def read_metas(asked, meta_ref, sems, first):
    return [
        pltpu.make_async_copy(ref.at[pl.ds(ref.shape[0] - 1, 1)], meta_ref.at[pl.ds(g, 1)], sems.at[first + g])
        for g, ref in enumerate(asked)
    ]


def decode_kernel(slots, rows, entries, *refs):
    flags, asked, (index_ref, weight_ref, meta_ref, sems) = refs[:3], refs[3:6], refs[6:]
    copies = read_metas(asked, meta_ref, sems, 0)
    for copy in copies:
        copy.start()
    for copy in copies:
        copy.wait()
    decode(slots, rows, entries, flags, meta_ref, index_ref, weight_ref)


def decoded(flags, asked, slots, rows, half, entries):
    width = asked[1].shape[2]
    vectors = -(-3 * (entries + 1) // 8) * 8
    return pl.pallas_call(
        functools.partial(decode_kernel, slots, rows, entries),
        in_specs=[in_smem()] * 3 + [in_place()] * 3,
        out_specs=[pl.BlockSpec(memory_space=pltpu.VMEM)] * 2,
        out_shape=[
            jax.ShapeDtypeStruct((vectors, 128), jnp.int32),
            jax.ShapeDtypeStruct((vectors, 128), jnp.float32),
        ],
        scratch_shapes=[pltpu.VMEM((3, half, width), jnp.bfloat16), pltpu.SemaphoreType.DMA((3,))],
        compiler_params=pltpu.CompilerParams(vmem_limit_bytes=VMEM_BYTES),
        cost_estimate=pl.CostEstimate(flops=0, bytes_accessed=6 * half * width, transcendentals=0),
        name="decode",
    )(*flags, *asked)


def table_copies(bases, rows, sources, table, sems):
    half = table.shape[1]
    return [
        pltpu.make_async_copy(
            source.at[pl.ds(0, rows), pl.ds(base, half), :], table.at[pl.ds(i * rows, rows)], sems.at[i]
        )
        for i, (source, base) in enumerate(zip(sources, bases))
    ]


def add_terms(rows, entries, index_ref, weight_ref, table, outs):
    half, width = table.shape[1:]
    for group, out in enumerate(outs):

        def some(g, carry, group=group, out=out):
            def sums(terms):
                totals = []
                for u in range(UNROLL):
                    r = g * UNROLL + u
                    total = jnp.zeros((half, width), jnp.float32)
                    for k in range(terms):
                        row = group * entries + k
                        total = total + weight_ref[row, r] * table[index_ref[row, r]].astype(jnp.float32)
                    totals.append(total)
                for u in range(UNROLL):
                    out[g * UNROLL + u] = totals[u].astype(out.dtype)

            most = index_ref[3 * entries + group, g * UNROLL]
            for u in range(1, UNROLL):
                most = jnp.maximum(most, index_ref[3 * entries + group, g * UNROLL + u])
            sums(min(QUICK, entries))

            @pl.when(most > QUICK)
            def _():
                sums(entries)

            return carry

        lax.fori_loop(0, rows // UNROLL, some, 0)


def lat_sums_kernel(bases, entries, core_ref, chip_ref, index_ref, weight_ref, *refs):
    tables = len(bases)
    sources, outs = refs[:tables], refs[tables : tables + 3]
    table, sems = refs[tables + 3 :]
    rows = table.shape[0] // tables
    copies = table_copies(bases, rows, sources, table, sems)
    first = core_ref[0] != chip_ref[0]
    for copy in copies[:-2]:
        copy.start()
    pl.when(first)(copies[-2].start)
    pl.when(jnp.logical_not(first))(copies[-1].start)
    for copy in copies[:-2]:
        copy.wait()
    pl.when(first)(copies[-2].wait)
    pl.when(jnp.logical_not(first))(copies[-1].wait)
    add_terms(rows, entries, index_ref, weight_ref, table, outs)


def lon_sums_kernel(bases, slots, entries, *refs):
    tables = len(bases)
    flags, refs = refs[:3], refs[3:]
    asked, sources, outs = refs[:3], refs[3 : 3 + tables], refs[3 + tables : 6 + tables]
    table, meta_ref, index_vec, weight_vec, index_ref, weight_ref, sems = refs[6 + tables :]
    rows = table.shape[0] // tables
    metas = read_metas(asked, meta_ref, sems, tables)
    copies = table_copies(bases, rows, sources, table, sems)
    for copy in metas + copies:
        copy.start()
    for copy in metas:
        copy.wait()
    decode(slots, rows, entries, flags, meta_ref, index_vec, weight_vec)
    to_scalar = [
        pltpu.make_async_copy(index_vec, index_ref, sems.at[tables + 3]),
        pltpu.make_async_copy(weight_vec, weight_ref, sems.at[tables + 4]),
    ]
    for copy in to_scalar:
        copy.start()
    for copy in to_scalar + copies:
        copy.wait()
    add_terms(rows, entries, index_ref, weight_ref, table, outs)


def sums_call(kernel, operands, smem, sources, scratch, rows, half, entries, name):
    tables = len(sources)
    width = sources[0][0].shape[2]
    return pl.pallas_call(
        kernel,
        in_specs=[in_smem()] * smem + [in_place()] * (len(operands) - smem + tables),
        out_specs=[pl.BlockSpec(memory_space=pltpu.VMEM)] * 3,
        out_shape=[
            jax.ShapeDtypeStruct((rows, half, width), dtype) for dtype in (jnp.bfloat16, jnp.float32, jnp.bfloat16)
        ],
        scratch_shapes=[pltpu.VMEM((tables * rows, half, width), jnp.bfloat16)] + scratch,
        compiler_params=pltpu.CompilerParams(vmem_limit_bytes=TABLE_BYTES),
        cost_estimate=pl.CostEstimate(
            flops=6 * rows * entries * half * width,
            bytes_accessed=2 * (tables + 3) * rows * half * width,
            transcendentals=0,
        ),
        name=name,
    )(*operands, *[source for source, _ in sources])


def lat_sums(flags, terms, sources, rows, half, entries):
    kernel = functools.partial(lat_sums_kernel, tuple(base for _, base in sources), entries)
    scratch = [pltpu.SemaphoreType.DMA((len(sources),))]
    return sums_call(kernel, [*flags[:2], *terms], 4, sources, scratch, rows, half, entries, "lat_sums")


def lon_sums(flags, asked, slots, sources, rows, half, entries):
    kernel = functools.partial(lon_sums_kernel, tuple(base for _, base in sources), slots, entries)
    vectors = -(-3 * (entries + 1) // 8) * 8
    scratch = [pltpu.VMEM((3, half, asked[1].shape[2]), jnp.bfloat16)]
    scratch += [space((vectors, 128), dtype) for space in (pltpu.VMEM, pltpu.SMEM) for dtype in (jnp.int32, jnp.float32)]
    scratch += [pltpu.SemaphoreType.DMA((len(sources) + 5,))]
    return sums_call(kernel, [*flags, *asked], 3, sources, scratch, rows, half, entries, "lon_sums")


def edges_kernel(core_ref, *refs):
    rows, half = refs[0].shape[:2]
    per = 128 // 8
    lane = lax.broadcasted_iota(jnp.int32, (half, 128), 1)
    odd = core_ref[0] == 1
    for earlier_ref, out_ref in zip(refs[6:-2], refs[-2:]):
        out_ref[:, half:] = earlier_ref[...]
    for j in range(rows // per):
        ends = []
        for side in range(2):
            parts = refs[3 * side : 3 * side + 3]
            packed = jnp.zeros((half, 128), jnp.float32)
            for i in range(per):
                r = j * per + i
                cells = parts[0][r] + parts[1][r].astype(jnp.float32) + parts[2][r].astype(jnp.float32)
                at = 8 * i + 3 * (1 - side)
                spot = (lane >= at) & (lane < at + 3)
                packed = jnp.where(spot, pltpu.roll(cells, 8 * i + 3, 1), packed)
            ends.append(packed)
        for out_ref, value in zip(refs[-2:], (jnp.where(odd, *ends), jnp.where(odd, *ends[::-1]))):
            out_ref[j, :half] = value.astype(out_ref.dtype)


def edges(core, parts, earlier):
    rows, half, width = parts[0].shape
    specs = [
        pl.BlockSpec((rows, half, 128), lambda t, at=at: (0, 0, at)) for at in (0, width // 128 - 1) for _ in parts
    ]
    whole = lambda shape: pl.BlockSpec(shape, lambda t: (0,) * len(shape))
    packed = (rows // 16, half + sum(array.shape[1] for array in earlier[:1]), 128)
    return pl.pallas_call(
        edges_kernel,
        grid=(1,),
        in_specs=[in_smem()] + specs + [whole(array.shape) for array in earlier],
        out_specs=[whole(packed)] * 2,
        out_shape=[jax.ShapeDtypeStruct(packed, jnp.bfloat16)] * 2,
        compiler_params=pltpu.CompilerParams(vmem_limit_bytes=VMEM_BYTES),
        cost_estimate=pl.CostEstimate(flops=8 * half * 256 * rows, bytes_accessed=16 * half * 256 * rows, transcendentals=0),
        name="edges",
    )(core, *parts, *parts, *earlier)


def combine_kernel(own0, a0, b0, own1, a1, b1, out_ref):
    rows, half = own0.shape[:2]
    for r in range(rows):
        for first, parts in ((0, (own0, a0, b0)), (half, (own1, a1, b1))):
            total = parts[0][r] + parts[1][r].astype(jnp.float32) + parts[2][r].astype(jnp.float32)
            out_ref[r, first : first + half] = total.astype(out_ref.dtype)


def combine(parts0, parts1):
    rows, half, width = parts0[0].shape
    step = 8
    return pl.pallas_call(
        combine_kernel,
        grid=(rows // step,),
        in_specs=[pl.BlockSpec((step, half, width), lambda t: (t, 0, 0))] * 6,
        out_specs=pl.BlockSpec((step, 2 * half, width), lambda t: (t, 0, 0)),
        out_shape=jax.ShapeDtypeStruct((rows, 2 * half, width), jnp.bfloat16),
        compiler_params=pltpu.CompilerParams(vmem_limit_bytes=VMEM_BYTES),
        cost_estimate=pl.CostEstimate(
            flops=4 * rows * half * width, bytes_accessed=24 * rows * half * width, transcendentals=0
        ),
        name="combine",
    )(*parts0, *parts1)


def shifted_by(row, edge, amount, lane):
    count = len(row)
    if amount == 0:
        return row
    if amount > 0:
        row = row[:-1] + [jnp.where(lane >= 128 - amount, edge, row[-1])]
        turned = [pltpu.roll(tile, amount, 1) for tile in row]
        return [jnp.where(lane < amount, turned[t - 1], turned[t]) for t in range(count)]
    row = [jnp.where(lane < -amount, edge, row[0])] + row[1:]
    turned = [pltpu.roll(tile, 128 + amount, 1) for tile in row]
    return [jnp.where(lane >= 128 + amount, turned[(t + 1) % count], turned[t]) for t in range(count)]


def edge_tile(one_ref, other_ref, r):
    per = 128 // 8
    both = one_ref[r // per] + other_ref[r // per]
    return pltpu.roll(both, (125 - 8 * (r % per)) % 128, 1)


def rows_kernel(lat_ref, offset_ref, first_row, last_row, one_ref, other_ref, *outs):
    bins, width = first_row.shape[1:]
    lane = lax.broadcasted_iota(jnp.int32, (bins, 128), 1)
    spots = [slice(128 * t, 128 * t + 128) for t in range(width // 128)]
    end = offset_ref.shape[0] - 1
    odd = lat_ref[0] == 1
    for out_ref, first in ((outs[0], odd), (outs[1], jnp.logical_not(odd))):
        offset = jnp.where(first, offset_ref[0], offset_ref[end])
        row = [jnp.where(first, first_row[0, :, at], last_row[0, :, at]) for at in spots]
        edge = jnp.where(first, edge_tile(one_ref, other_ref, 0), edge_tile(one_ref, other_ref, end))
        for amount in range(-REACH, REACH + 1):

            @pl.when(offset == amount)
            def _(out_ref=out_ref, row=row, edge=edge, amount=amount):
                for at, tile in zip(spots, shifted_by(row, edge, amount, lane)):
                    out_ref[0, :, at] = tile.astype(out_ref.dtype)


def outer_rows(lat, offset, remapped, one, other):
    rows, bins, width = remapped.shape
    row = lambda at: pl.BlockSpec((1, bins, width), lambda t: (at, 0, 0))
    whole = pl.BlockSpec(one.shape, lambda t: (0, 0, 0))
    return pl.pallas_call(
        rows_kernel,
        grid=(1,),
        in_specs=[in_smem()] * 2 + [row(0), row(rows - 1), whole, whole],
        out_specs=[row(0), row(0)],
        out_shape=[jax.ShapeDtypeStruct((1, bins, width), jnp.bfloat16)] * 2,
        compiler_params=pltpu.CompilerParams(vmem_limit_bytes=VMEM_BYTES),
        cost_estimate=pl.CostEstimate(flops=20 * bins * width, bytes_accessed=12 * bins * width, transcendentals=0),
        name="outer_rows",
    )(lat, offset, remapped, remapped, one, other)


def final_kernel(offset_ref, remap_ref, one_ref, other_ref, kappa_ref, local_ref, out_ref, outer_ref, edge_ref):
    rows, bins, width = remap_ref.shape
    count = width // 128
    lane = lax.broadcasted_iota(jnp.int32, (16, 128), 1)
    spots = [slice(128 * t, 128 * t + 128) for t in range(count)]
    for r in range(rows):
        edge_ref[r] = edge_tile(one_ref, other_ref, r)

    def moved(row, edge, amount):
        row = [jnp.where(lane < -amount, edge, row[0])] + row[1:]
        row = row[:-1] + [jnp.where(lane >= 128 - amount, edge, row[-1])]
        turned = [pltpu.roll(tile, (amount + 128) & 127, 1) for tile in row]
        before, after = lane < amount, lane >= 128 + amount
        return [
            jnp.where(before, turned[t - 1], jnp.where(after, turned[(t + 1) % count], turned[t])).astype(jnp.float32)
            for t in range(count)
        ]

    pieces = [slice(16 * b, 16 * b + 16) for b in range(bins // 16)]
    before, now, base = {}, {}, {}
    stores = []
    for r in range(rows):
        amount = offset_ref[r]
        kappa = [kappa_ref[r, :, spot] for spot in spots]
        above = [kappa_ref[max(r - 1, 0), :, spot] for spot in spots]
        for at in pieces:
            row = [remap_ref[r, at, spot] for spot in spots]
            edge = edge_ref[r, at]
            center = moved(row, edge, amount)
            east = moved(row, edge, amount - 1)
            west = moved(row, edge, amount + 1)
            key = at.start
            fresh = []
            for t, spot in enumerate(spots):
                around = kappa[t] * (east[t] + west[t] - 4.0 * center[t])
                fresh.append(local_ref[r, at, spot] + center[t] + around)
                if r == 1:
                    stores.append((r - 1, at, spot, base[key][t] + above[t] * center[t]))
                elif r:
                    stores.append((r - 1, at, spot, base[key][t] + above[t] * (before[key][t] + center[t])))
            if r:
                before[key] = now[key]
            now[key], base[key] = center, fresh
        if r % 2:
            for which, at, spot, value in stores:
                if which:
                    out_ref[which, at, spot] = value
                else:
                    outer_ref[0, at, spot] = value
            stores = []
    for at in pieces:
        for t, spot in enumerate(spots):
            outer_ref[1, at, spot] = base[at.start][t] + kappa_ref[rows - 1, :, spot] * before[at.start][t]


def final(offset, remapped, west, east, kappa, local):
    rows, bins, width = remapped.shape
    tile = bins // 2
    block = pl.BlockSpec((rows, tile, width), lambda t: (0, t, 0))
    packed = pl.BlockSpec((west.shape[0], tile, 128), lambda t: (0, t, 0))
    return pl.pallas_call(
        final_kernel,
        grid=(bins // tile,),
        in_specs=[in_smem(), block, packed, packed, pl.BlockSpec(kappa.shape, lambda t: (0, 0, 0)), block],
        out_specs=[block, pl.BlockSpec((2, tile, width), lambda t: (0, t, 0))],
        out_shape=[
            jax.ShapeDtypeStruct(local.shape, jnp.float32),
            jax.ShapeDtypeStruct((2, bins, width), jnp.float32),
        ],
        scratch_shapes=[pltpu.VMEM((rows, tile, 128), jnp.bfloat16)],
        compiler_params=pltpu.CompilerParams(vmem_limit_bytes=VMEM_BYTES),
        cost_estimate=pl.CostEstimate(flops=30 * remapped.size, bytes_accessed=12 * remapped.size, transcendentals=0),
        name="final",
    )(offset, remapped, west, east, kappa, local)


def halo_kernel(lat_ref, one_ref, other_ref, kappa_ref, outer_ref, _, out_ref, sums_ref, sems):
    odd = lat_ref[0] == 1
    rows = out_ref.shape[0]
    copies = []
    for side, (first, at) in enumerate(((odd, 0), (jnp.logical_not(odd), rows - 1))):
        value = jnp.where(first, one_ref[0].astype(jnp.float32), other_ref[0].astype(jnp.float32))
        sums_ref[side] = outer_ref[side] + kappa_ref[at] * value
        copy = pltpu.make_async_copy(sums_ref.at[pl.ds(side, 1)], out_ref.at[pl.ds(at, 1)], sems.at[side])
        copy.start()
        copies.append(copy)
    for copy in copies:
        copy.wait()


def add_halo(lat, one, other, kappa, outer, partial):
    vmem = pl.BlockSpec(memory_space=pltpu.VMEM)
    return pl.pallas_call(
        halo_kernel,
        in_specs=[in_smem()] + [vmem] * 4 + [in_place()],
        out_specs=in_place(),
        out_shape=jax.ShapeDtypeStruct(partial.shape, jnp.float32),
        scratch_shapes=[pltpu.VMEM(outer.shape, jnp.float32), pltpu.SemaphoreType.DMA((2,))],
        input_output_aliases={5: 0},
        compiler_params=pltpu.CompilerParams(vmem_limit_bytes=VMEM_BYTES),
        cost_estimate=pl.CostEstimate(flops=4 * outer.size, bytes_accessed=20 * outer.size, transcendentals=0),
        name="add_halo",
    )(lat, one, other, kappa, outer, partial)


def body(
    conc,
    dep_owner,
    dep_row,
    dep_weight,
    dep_count,
    zonal_offset,
    agg_rates,
    toeplitz,
    settle,
    kappa,
):
    rows, bins, width = conc.shape
    entries = dep_owner.shape[2]
    my_lat, my_lon = lax.axis_index("lat"), lax.axis_index("lon")
    flags = [(value % 2).astype(jnp.int32).reshape(1) for value in (my_lon, my_lon // 2, my_lat)]
    half = bins // 2
    low, high, meta = messages(conc, dep_owner[0].T, dep_row[0].T, dep_weight[0].T, dep_count)
    lat1, lat2 = swap_lat(high, 0), swap_lat(high, 1)
    lon1, lon2 = swap_chip(low, 0), swap_chip(low, 1)
    beside = swap_core(conc)
    rates, meta = lax.optimization_barrier((agg_rates, meta))
    local = local_terms(conc, rates, toeplitz, settle)
    lat1, lat2, local = lax.optimization_barrier((lat1, lat2, local))
    terms = decoded(flags, [lat1, meta, lat2], lat_slots, rows, half, entries)

    to_lon1, own1, to_lon2 = lon_sums(
        flags,
        [lon1, meta, lon2],
        lon_slots,
        [(lat1, 0), (conc, half), (lat2, 0), (swap_core(lat1), 0), (beside, half), (swap_core(lat2), 0)],
        rows,
        half,
        entries,
    )
    parts1 = [swap_chip(to_lon1, 0), swap_chip(to_lon2, 1)]
    own1, later = lax.optimization_barrier((own1, flags))
    parts1 = [own1] + parts1

    to_lat1, own0, to_lat2 = lat_sums(
        later,
        terms,
        [(conc, 0), (beside, 0), (lon1, 0), (lon2, 0), (swap_core(lon1), 0), (swap_core(lon2), 0)],
        rows,
        half,
        entries,
    )
    parts0 = [own0, swap_lat(to_lat1, 0), swap_lat(to_lat2, 1)]

    kappa = kappa[:, None, :]

    earlier = edges(flags[0], parts1, [])
    parts0, earlier = lax.optimization_barrier((parts0, earlier))
    to_core, to_across = edges(flags[0], parts0, earlier)
    one, other = swap_core(to_core), swap_across(to_across)
    remapped = combine(parts0, parts1)
    row1, row2 = outer_rows(flags[2], zonal_offset, remapped, one, other)
    row1, row2 = swap_lat(row1, 0), swap_lat(row2, 1)
    partial, outer = final(zonal_offset, remapped, one, other, kappa, local)
    return add_halo(flags[2], row1, row2, kappa, outer, partial)


def solution(mesh):
    return jax.shard_map(
        body,
        mesh=mesh,
        in_specs=(
            P("lat", None, "lon"),
            P("lon", "lat", None),
            P("lon", "lat", None),
            P("lon", "lat", None),
            P("lon", "lat"),
            P("lat"),
            P(None, "lat", "lon"),
            P(),
            P(),
            P("lat", "lon"),
        ),
        out_specs=P("lat", None, "lon"),
        check_vma=False,
    )
```

```python
import functools

import jax
import jax.numpy as jnp
from jax import lax
from jax.experimental import pallas as pl
from jax.experimental.pallas import tpu as pltpu
from jax.sharding import PartitionSpec as P

REACH = 2
NEAR_LON = 5
UNROLL = 4
VMEM_BYTES = 12 * 1024 * 1024
MOST_BYTES = 60 * 1024 * 1024
TABLE_BYTES = 20 * 1024 * 1024
QUICK = 2
FIELDS = ((0, 0), (0, 128), (8, 0), (8, 128), (16, 0))


def exchange(value, axis, pairs):
    return lax.ppermute(value, axis, [(i, j) for i, j in pairs] + [(j, i) for i, j in pairs])


def swap_core(value):
    return exchange(value, "lon", [(i, i + 1) for i in range(0, lax.axis_size("lon"), 2)])


def swap_across(value):
    count = lax.axis_size("lon")
    return exchange(value, "lon", [(i, (i + 1) % count) for i in range(1, count, 2)])


def swap_chip(value, second):
    count = lax.axis_size("lon")
    firsts = [i for i in range(count) if (i // 2) % 2 == second]
    return exchange(value, "lon", [(i, (i + 2) % count) for i in firsts])


def swap_lat(value, second):
    count = lax.axis_size("lat")
    return exchange(value, "lat", [(i, i + 1) for i in range(second, count - 1, 2)])


def in_smem():
    return pl.BlockSpec(memory_space=pltpu.SMEM)


def in_place():
    return pl.BlockSpec(memory_space=pl.ANY)


def for_rows(count, one):
    def some(g, carry):
        stores = []
        for u in range(UNROLL):
            stores += one(g * UNROLL + u)
        for ref, at, value in stores:
            ref[at] = value.astype(ref.dtype)
        return carry

    lax.fori_loop(0, count // UNROLL, some, 0)


def growth_kernel(flip_ref, settle_ref, conc_ref, rates_ref, out_ref, mat_ref):
    ranks, rows_step = rates_ref.shape[0], conc_ref.shape[0]
    bins, width = conc_ref.shape[1:]

    @pl.when(pl.program_id(0) == 0)
    def _():
        for q in range(ranks):
            spread = jnp.broadcast_to(flip_ref[q : q + 1, :], (bins, 2 * bins))
            turned = pltpu.roll(spread, bins + 1, 1, stride=1, stride_axis=0)
            mat_ref[q * bins : (q + 1) * bins, :] = turned[:, :bins].astype(jnp.bfloat16)

    settle = jnp.broadcast_to(settle_ref[...], (bins, width))
    for r in range(rows_step):
        cells = conc_ref[r]
        product = jnp.dot(mat_ref[...], cells, preferred_element_type=jnp.float32)
        total = -settle * cells.astype(jnp.float32)
        for q in range(ranks):
            total = total + rates_ref[q, r : r + 1, :] * product[q * bins : (q + 1) * bins]
        out_ref[r] = total


def local_terms(conc, agg_rates, toeplitz, settle):
    rows, bins, width = conc.shape
    ranks = agg_rates.shape[0]
    step = 8
    flipped = jnp.pad(toeplitz[:, ::-1].astype(jnp.float32), ((0, 0), (0, 1)))
    return pl.pallas_call(
        growth_kernel,
        grid=(rows // step,),
        in_specs=[
            pl.BlockSpec((ranks, 2 * bins), lambda i: (0, 0)),
            pl.BlockSpec((bins, 1), lambda i: (0, 0)),
            pl.BlockSpec((step, bins, width), lambda i: (i, 0, 0)),
            pl.BlockSpec((ranks, step, width), lambda i: (0, i, 0)),
        ],
        out_specs=pl.BlockSpec((step, bins, width), lambda i: (i, 0, 0)),
        out_shape=jax.ShapeDtypeStruct(conc.shape, jnp.float32),
        scratch_shapes=[pltpu.VMEM((ranks * bins, bins), jnp.bfloat16)],
        compiler_params=pltpu.CompilerParams(vmem_limit_bytes=VMEM_BYTES),
        cost_estimate=pl.CostEstimate(
            flops=2 * ranks * bins * bins * rows * width, bytes_accessed=8 * conc.size, transcendentals=0
        ),
        name="growth",
    )(flipped, settle[:, None], conc, agg_rates)


def messages_kernel(
    conc_ref, owner_hbm, source_hbm, weight_hbm, count_hbm, low_ref, high_ref, meta_ref,
    owner_ref, source_ref, weight_ref, count_ref, sems,
):
    rows = conc_ref.shape[0]
    half = low_ref.shape[1]
    entries = owner_ref.shape[0]
    small = [
        pltpu.make_async_copy(hbm, ref, sems.at[2 + i])
        for i, (hbm, ref) in enumerate(
            ((owner_hbm, owner_ref), (source_hbm, source_ref), (weight_hbm, weight_ref), (count_hbm, count_ref))
        )
    ]
    large = [
        pltpu.make_async_copy(conc_ref.at[:, pl.ds(i * half, half), :], ref.at[pl.ds(0, rows)], sems.at[i])
        for i, ref in enumerate((low_ref, high_ref))
    ]
    for copy in small + large:
        copy.start()
    meta_ref[...] = jnp.zeros(meta_ref.shape, meta_ref.dtype)
    for copy in small:
        copy.wait()
    wide = lambda value: value.astype(jnp.float32)
    entry = lax.broadcasted_iota(jnp.int32, owner_ref.shape, 0)
    live = jnp.where(entry < count_ref[...], weight_ref[...], 0.0)
    top = live.astype(jnp.bfloat16)
    middle = (live - wide(top)).astype(jnp.bfloat16)
    bottom = (live - wide(top) - wide(middle)).astype(jnp.bfloat16)
    fields = (wide(owner_ref[...]), wide(source_ref[...]), wide(top), wide(middle), wide(bottom))
    for field, (at, lane) in zip(fields, FIELDS):
        meta_ref[0, at : at + entries, lane : lane + rows] = field.astype(jnp.bfloat16)
    low_ref[rows] = meta_ref[0]
    high_ref[rows] = meta_ref[0]
    for copy in large:
        copy.wait()


def messages(conc, owner, source, weight, count):
    rows, bins, width = conc.shape
    half = bins // 2
    return pl.pallas_call(
        messages_kernel,
        in_specs=[in_place()] * 5,
        out_specs=[pl.BlockSpec(memory_space=pltpu.VMEM)] * 3,
        out_shape=[
            jax.ShapeDtypeStruct((rows + 1, half, width), conc.dtype),
            jax.ShapeDtypeStruct((rows + 1, half, width), conc.dtype),
            jax.ShapeDtypeStruct((1, half, width), conc.dtype),
        ],
        scratch_shapes=[pltpu.VMEM(small.shape, small.dtype) for small in (owner, source, weight, count)]
        + [pltpu.SemaphoreType.DMA((6,))],
        compiler_params=pltpu.CompilerParams(vmem_limit_bytes=MOST_BYTES),
        cost_estimate=pl.CostEstimate(flops=0, bytes_accessed=4 * conc.size, transcendentals=0),
        name="messages",
    )(conc, owner, source, weight, count)


def signs(flags):
    return [1.0 - 2.0 * ref[0].astype(jnp.float32) for ref in flags]


def lat_slots(rows, group, lat_step, lon_step, flags):
    core, chip, lat = signs(flags)
    far = jnp.where(core * chip < 0.0, 4.0, 5.0)
    slot = jnp.where(
        lon_step == 0.0,
        0.0,
        jnp.where(
            lon_step == 2.0 * chip, 2.0, jnp.where(lon_step == -2.0 * chip, 3.0, jnp.where(lon_step == core, 1.0, far))
        ),
    )
    return lat_step == (group - 1.0) * lat, slot * rows


def lon_slots(rows, group, lat_step, lon_step, flags):
    core, chip, lat = signs(flags)
    lon_from = 2.0 * (1.0 - group) * chip + lon_step
    slot = jnp.where(lon_from == 0.0, 1.0, 4.0) - lat_step * lat
    return (lon_from == 0.0) | (lon_from == core), slot * rows


def decode(slots, rows, entries, flags, meta_ref, index_ref, weight_ref):
    for g in range(3):
        owner, source, top, middle, bottom = [
            meta_ref[g, at : at + entries, lane : lane + 128].astype(jnp.float32) for at, lane in FIELDS
        ]
        weight = top + middle + bottom
        band = jnp.where(owner >= NEAR_LON, 1.0, 0.0) + jnp.where(owner >= 2 * NEAR_LON, 1.0, 0.0)
        here, base = slots(rows, float(g), band - 1.0, owner - NEAR_LON * band - REACH, flags)
        here = jnp.where(here & (weight != 0.0), 1.0, 0.0)
        index = base + source
        packed = [[jnp.zeros((1, 128), jnp.float32)] * 2 for _ in range(entries)]
        rank = jnp.zeros((1, 128), jnp.float32)
        for k in range(entries):
            taken = here[k : k + 1]
            for place in range(k + 1):
                spot = (taken > 0.0) & (rank == place)
                packed[place] = [
                    jnp.where(spot, index[k : k + 1], packed[place][0]),
                    jnp.where(spot, weight[k : k + 1], packed[place][1]),
                ]
            rank = rank + taken
        for place in range(entries):
            at = g * entries + place
            index_ref[at : at + 1, :] = packed[place][0].astype(jnp.int32)
            weight_ref[at : at + 1, :] = packed[place][1]
        at = 3 * entries + g
        index_ref[at : at + 1, :] = rank.astype(jnp.int32)


def read_metas(asked, meta_ref, sems, first):
    return [
        pltpu.make_async_copy(ref.at[pl.ds(ref.shape[0] - 1, 1)], meta_ref.at[pl.ds(g, 1)], sems.at[first + g])
        for g, ref in enumerate(asked)
    ]


def decode_kernel(slots, rows, entries, *refs):
    flags, asked, (index_ref, weight_ref, meta_ref, sems) = refs[:3], refs[3:6], refs[6:]
    copies = read_metas(asked, meta_ref, sems, 0)
    for copy in copies:
        copy.start()
    for copy in copies:
        copy.wait()
    decode(slots, rows, entries, flags, meta_ref, index_ref, weight_ref)


def decoded(flags, asked, slots, rows, half, entries):
    width = asked[1].shape[2]
    vectors = -(-3 * (entries + 1) // 8) * 8
    return pl.pallas_call(
        functools.partial(decode_kernel, slots, rows, entries),
        in_specs=[in_smem()] * 3 + [in_place()] * 3,
        out_specs=[pl.BlockSpec(memory_space=pltpu.VMEM)] * 2,
        out_shape=[
            jax.ShapeDtypeStruct((vectors, 128), jnp.int32),
            jax.ShapeDtypeStruct((vectors, 128), jnp.float32),
        ],
        scratch_shapes=[pltpu.VMEM((3, half, width), jnp.bfloat16), pltpu.SemaphoreType.DMA((3,))],
        compiler_params=pltpu.CompilerParams(vmem_limit_bytes=VMEM_BYTES),
        cost_estimate=pl.CostEstimate(flops=0, bytes_accessed=6 * half * width, transcendentals=0),
        name="decode",
    )(*flags, *asked)


def table_copies(bases, rows, sources, table, sems):
    half = table.shape[1]
    return [
        pltpu.make_async_copy(
            source.at[pl.ds(0, rows), pl.ds(base, half), :], table.at[pl.ds(i * rows, rows)], sems.at[i]
        )
        for i, (source, base) in enumerate(zip(sources, bases))
    ]


def add_terms(rows, entries, index_ref, weight_ref, table, outs):
    half, width = table.shape[1:]
    for group, out in enumerate(outs):

        def some(g, carry, group=group, out=out):
            def sums(terms):
                totals = []
                for u in range(UNROLL):
                    r = g * UNROLL + u
                    total = jnp.zeros((half, width), jnp.float32)
                    for k in range(terms):
                        row = group * entries + k
                        total = total + weight_ref[row, r] * table[index_ref[row, r]].astype(jnp.float32)
                    totals.append(total)
                for u in range(UNROLL):
                    out[g * UNROLL + u] = totals[u].astype(out.dtype)

            most = index_ref[3 * entries + group, g * UNROLL]
            for u in range(1, UNROLL):
                most = jnp.maximum(most, index_ref[3 * entries + group, g * UNROLL + u])
            sums(min(QUICK, entries))

            @pl.when(most > QUICK)
            def _():
                sums(entries)

            return carry

        lax.fori_loop(0, rows // UNROLL, some, 0)


def lat_sums_kernel(bases, entries, core_ref, chip_ref, index_ref, weight_ref, *refs):
    tables = len(bases)
    sources, outs = refs[:tables], refs[tables : tables + 3]
    table, sems = refs[tables + 3 :]
    rows = table.shape[0] // tables
    copies = table_copies(bases, rows, sources, table, sems)
    first = core_ref[0] != chip_ref[0]
    for copy in copies[:-2]:
        copy.start()
    pl.when(first)(copies[-2].start)
    pl.when(jnp.logical_not(first))(copies[-1].start)
    for copy in copies[:-2]:
        copy.wait()
    pl.when(first)(copies[-2].wait)
    pl.when(jnp.logical_not(first))(copies[-1].wait)
    add_terms(rows, entries, index_ref, weight_ref, table, outs)


def lon_sums_kernel(bases, slots, entries, *refs):
    tables = len(bases)
    flags, refs = refs[:3], refs[3:]
    asked, sources, outs = refs[:3], refs[3 : 3 + tables], refs[3 + tables : 6 + tables]
    table, meta_ref, index_vec, weight_vec, index_ref, weight_ref, sems = refs[6 + tables :]
    rows = table.shape[0] // tables
    metas = read_metas(asked, meta_ref, sems, tables)
    copies = table_copies(bases, rows, sources, table, sems)
    for copy in metas + copies:
        copy.start()
    for copy in metas:
        copy.wait()
    decode(slots, rows, entries, flags, meta_ref, index_vec, weight_vec)
    to_scalar = [
        pltpu.make_async_copy(index_vec, index_ref, sems.at[tables + 3]),
        pltpu.make_async_copy(weight_vec, weight_ref, sems.at[tables + 4]),
    ]
    for copy in to_scalar:
        copy.start()
    for copy in to_scalar + copies:
        copy.wait()
    add_terms(rows, entries, index_ref, weight_ref, table, outs)


def sums_call(kernel, operands, smem, sources, scratch, rows, half, entries, name):
    tables = len(sources)
    width = sources[0][0].shape[2]
    return pl.pallas_call(
        kernel,
        in_specs=[in_smem()] * smem + [in_place()] * (len(operands) - smem + tables),
        out_specs=[pl.BlockSpec(memory_space=pltpu.VMEM)] * 3,
        out_shape=[
            jax.ShapeDtypeStruct((rows, half, width), dtype) for dtype in (jnp.bfloat16, jnp.float32, jnp.bfloat16)
        ],
        scratch_shapes=[pltpu.VMEM((tables * rows, half, width), jnp.bfloat16)] + scratch,
        compiler_params=pltpu.CompilerParams(vmem_limit_bytes=TABLE_BYTES),
        cost_estimate=pl.CostEstimate(
            flops=6 * rows * entries * half * width,
            bytes_accessed=2 * (tables + 3) * rows * half * width,
            transcendentals=0,
        ),
        name=name,
    )(*operands, *[source for source, _ in sources])


def lat_sums(flags, terms, sources, rows, half, entries):
    kernel = functools.partial(lat_sums_kernel, tuple(base for _, base in sources), entries)
    scratch = [pltpu.SemaphoreType.DMA((len(sources),))]
    return sums_call(kernel, [*flags[:2], *terms], 4, sources, scratch, rows, half, entries, "lat_sums")


def lon_sums(flags, asked, slots, sources, rows, half, entries):
    kernel = functools.partial(lon_sums_kernel, tuple(base for _, base in sources), slots, entries)
    vectors = -(-3 * (entries + 1) // 8) * 8
    scratch = [pltpu.VMEM((3, half, asked[1].shape[2]), jnp.bfloat16)]
    scratch += [space((vectors, 128), dtype) for space in (pltpu.VMEM, pltpu.SMEM) for dtype in (jnp.int32, jnp.float32)]
    scratch += [pltpu.SemaphoreType.DMA((len(sources) + 5,))]
    return sums_call(kernel, [*flags, *asked], 3, sources, scratch, rows, half, entries, "lon_sums")


def edges_kernel(core_ref, *refs):
    rows, half = refs[0].shape[:2]
    per = 128 // 8
    lane = lax.broadcasted_iota(jnp.int32, (half, 128), 1)
    odd = core_ref[0] == 1
    for earlier_ref, out_ref in zip(refs[6:-2], refs[-2:]):
        out_ref[:, half:] = earlier_ref[...]
    for j in range(rows // per):
        ends = []
        for side in range(2):
            parts = refs[3 * side : 3 * side + 3]
            packed = jnp.zeros((half, 128), jnp.float32)
            for i in range(per):
                r = j * per + i
                cells = parts[0][r] + parts[1][r].astype(jnp.float32) + parts[2][r].astype(jnp.float32)
                at = 8 * i + 3 * (1 - side)
                spot = (lane >= at) & (lane < at + 3)
                packed = jnp.where(spot, pltpu.roll(cells, 8 * i + 3, 1), packed)
            ends.append(packed)
        for out_ref, value in zip(refs[-2:], (jnp.where(odd, *ends), jnp.where(odd, *ends[::-1]))):
            out_ref[j, :half] = value.astype(out_ref.dtype)


def edges(core, parts, earlier):
    rows, half, width = parts[0].shape
    specs = [
        pl.BlockSpec((rows, half, 128), lambda t, at=at: (0, 0, at)) for at in (0, width // 128 - 1) for _ in parts
    ]
    whole = lambda shape: pl.BlockSpec(shape, lambda t: (0,) * len(shape))
    packed = (rows // 16, half + sum(array.shape[1] for array in earlier[:1]), 128)
    return pl.pallas_call(
        edges_kernel,
        grid=(1,),
        in_specs=[in_smem()] + specs + [whole(array.shape) for array in earlier],
        out_specs=[whole(packed)] * 2,
        out_shape=[jax.ShapeDtypeStruct(packed, jnp.bfloat16)] * 2,
        compiler_params=pltpu.CompilerParams(vmem_limit_bytes=VMEM_BYTES),
        cost_estimate=pl.CostEstimate(flops=8 * half * 256 * rows, bytes_accessed=16 * half * 256 * rows, transcendentals=0),
        name="edges",
    )(core, *parts, *parts, *earlier)


def combine_kernel(own0, a0, b0, own1, a1, b1, out_ref):
    rows, half = own0.shape[:2]
    for r in range(rows):
        out_ref[r, :half] = own0[r] + a0[r].astype(jnp.float32) + b0[r].astype(jnp.float32)
        out_ref[r, half:] = own1[r] + a1[r].astype(jnp.float32) + b1[r].astype(jnp.float32)


def combine(parts0, parts1):
    rows, half, width = parts0[0].shape
    step = 8
    return pl.pallas_call(
        combine_kernel,
        grid=(rows // step,),
        in_specs=[pl.BlockSpec((step, half, width), lambda t: (t, 0, 0))] * 6,
        out_specs=pl.BlockSpec((step, 2 * half, width), lambda t: (t, 0, 0)),
        out_shape=jax.ShapeDtypeStruct((rows, 2 * half, width), jnp.float32),
        compiler_params=pltpu.CompilerParams(vmem_limit_bytes=VMEM_BYTES),
        cost_estimate=pl.CostEstimate(
            flops=4 * rows * half * width, bytes_accessed=24 * rows * half * width, transcendentals=0
        ),
        name="combine",
    )(*parts0, *parts1)


def shifted_by(row, edge, amount, lane):
    count = len(row)
    if amount == 0:
        return row
    if amount > 0:
        row = row[:-1] + [jnp.where(lane >= 128 - amount, edge, row[-1])]
        turned = [pltpu.roll(tile, amount, 1) for tile in row]
        return [jnp.where(lane < amount, turned[t - 1], turned[t]) for t in range(count)]
    row = [jnp.where(lane < -amount, edge, row[0])] + row[1:]
    turned = [pltpu.roll(tile, 128 + amount, 1) for tile in row]
    return [jnp.where(lane >= 128 + amount, turned[(t + 1) % count], turned[t]) for t in range(count)]


def edge_tile(west_ref, east_ref, r):
    per = 128 // 8
    both = west_ref[r // per].astype(jnp.float32) + east_ref[r // per].astype(jnp.float32)
    return pltpu.roll(both, (125 - 8 * (r % per)) % 128, 1)


def rows_kernel(lat_ref, offset_ref, first_row, last_row, one_ref, other_ref, *outs):
    bins, width = first_row.shape[1:]
    lane = lax.broadcasted_iota(jnp.int32, (bins, 128), 1)
    spots = [slice(128 * t, 128 * t + 128) for t in range(width // 128)]
    end = offset_ref.shape[0] - 1
    odd = lat_ref[0] == 1
    for out_ref, first in ((outs[0], odd), (outs[1], jnp.logical_not(odd))):
        offset = jnp.broadcast_to(jnp.where(first, offset_ref[0], offset_ref[end]), (bins, 128))
        row = [jnp.where(first, first_row[0, :, at], last_row[0, :, at]) for at in spots]
        edge = jnp.where(first, edge_tile(one_ref, other_ref, 0), edge_tile(one_ref, other_ref, end))
        result = row
        for amount in (-2, -1, 1, 2):
            moved = shifted_by(row, edge, amount, lane)
            result = [jnp.where(offset == amount, tile, kept) for tile, kept in zip(moved, result)]
        for at, tile in zip(spots, result):
            out_ref[0, :, at] = tile.astype(out_ref.dtype)


def outer_rows(lat, offset, remapped, one, other):
    rows, bins, width = remapped.shape
    row = lambda at: pl.BlockSpec((1, bins, width), lambda t: (at, 0, 0))
    whole = lambda array: pl.BlockSpec(array.shape, lambda t: (0, 0, 0))
    return pl.pallas_call(
        rows_kernel,
        grid=(1,),
        in_specs=[in_smem(), whole(offset), row(0), row(rows - 1), whole(one), whole(other)],
        out_specs=[row(0), row(0)],
        out_shape=[jax.ShapeDtypeStruct((1, bins, width), jnp.bfloat16)] * 2,
        compiler_params=pltpu.CompilerParams(vmem_limit_bytes=VMEM_BYTES),
        cost_estimate=pl.CostEstimate(flops=20 * bins * width, bytes_accessed=12 * bins * width, transcendentals=0),
        name="outer_rows",
    )(lat, offset, remapped, remapped, one, other)


def final_kernel(
    offset_ref, remap_ref, one_ref, other_ref, kappa_ref, local_ref, out_ref, outer_ref, edge_ref, sums_ref, sems
):
    rows, bins, width = remap_ref.shape
    count = width // 128
    lane = lax.broadcasted_iota(jnp.int32, (8, 128), 1)
    spots = [slice(128 * t, 128 * t + 128) for t in range(count)]
    for r in range(rows):
        edge_ref[r] = edge_tile(one_ref, other_ref, r)

    def moved(row, edge, amount):
        row = [jnp.where(lane < -amount, edge, row[0])] + row[1:]
        row = row[:-1] + [jnp.where(lane >= 128 - amount, edge, row[-1])]
        turned = [pltpu.roll(tile, (amount + 128) & 127, 1) for tile in row]
        before, after = lane < amount, lane >= 128 + amount
        return [
            jnp.where(before, turned[t - 1], jnp.where(after, turned[(t + 1) % count], turned[t])) for t in range(count)
        ]

    copies = []
    for half in range(2):
        first = half * bins // 2
        pieces = [slice(b, b + 8) for b in range(first, first + bins // 2, 8)]
        before, now, base = {}, {}, {}
        stores = []
        sent = 1
        for r in range(rows):
            amount = offset_ref[r]
            kappa = [kappa_ref[r, :, spot] for spot in spots]
            above = [kappa_ref[max(r - 1, 0), :, spot] for spot in spots]
            for at in pieces:
                row = [remap_ref[r, at, spot] for spot in spots]
                edge = edge_ref[r, at]
                center = moved(row, edge, amount)
                east = moved(row, edge, amount - 1)
                west = moved(row, edge, amount + 1)
                key = at.start
                fresh = []
                for t, spot in enumerate(spots):
                    around = kappa[t] * (east[t] + west[t] - 4.0 * center[t])
                    fresh.append(local_ref[r, at, spot] + center[t] + around)
                    if r == 1:
                        stores.append((r - 1, at, spot, base[key][t] + above[t] * center[t]))
                    elif r:
                        stores.append((r - 1, at, spot, base[key][t] + above[t] * (before[key][t] + center[t])))
                if r:
                    before[key] = now[key]
                now[key], base[key] = center, fresh
            if r % 2:
                for which, at, spot, value in stores:
                    if which:
                        sums_ref[which, at, spot] = value
                    else:
                        outer_ref[0, at, spot] = value
                stores = []
            if r % 8 == 7:
                block = (pl.ds(sent, r - sent), pl.ds(first, bins // 2))
                copy = pltpu.make_async_copy(sums_ref.at[block], out_ref.at[block], sems.at[len(copies)])
                copy.start()
                copies.append(copy)
                sent = r
        for at in pieces:
            for t, spot in enumerate(spots):
                outer_ref[1, at, spot] = base[at.start][t] + kappa_ref[rows - 1, :, spot] * before[at.start][t]
    for copy in copies:
        copy.wait()


def final(offset, remapped, one, other, kappa, local):
    rows, bins, width = remapped.shape
    vmem = pl.BlockSpec(memory_space=pltpu.VMEM)
    return pl.pallas_call(
        final_kernel,
        in_specs=[in_smem()] + [vmem] * 5,
        out_specs=[in_place(), vmem],
        out_shape=[
            jax.ShapeDtypeStruct(local.shape, jnp.float32),
            jax.ShapeDtypeStruct((2, bins, width), jnp.float32),
        ],
        scratch_shapes=[
            pltpu.VMEM((rows, bins, 128), jnp.float32),
            pltpu.VMEM((rows, bins, width), jnp.float32),
            pltpu.SemaphoreType.DMA((2 * (rows // 8),)),
        ],
        compiler_params=pltpu.CompilerParams(vmem_limit_bytes=TABLE_BYTES),
        cost_estimate=pl.CostEstimate(flops=30 * remapped.size, bytes_accessed=12 * remapped.size, transcendentals=0),
        name="final",
    )(offset, remapped, one, other, kappa, local)


def halo_kernel(lat_ref, one_ref, other_ref, kappa_ref, outer_ref, _, out_ref, sums_ref, sems):
    odd = lat_ref[0] == 1
    rows = out_ref.shape[0]
    copies = []
    for side, (first, at) in enumerate(((odd, 0), (jnp.logical_not(odd), rows - 1))):
        value = jnp.where(first, one_ref[0].astype(jnp.float32), other_ref[0].astype(jnp.float32))
        sums_ref[side] = outer_ref[side] + kappa_ref[at] * value
        copy = pltpu.make_async_copy(sums_ref.at[pl.ds(side, 1)], out_ref.at[pl.ds(at, 1)], sems.at[side])
        copy.start()
        copies.append(copy)
    for copy in copies:
        copy.wait()


def add_halo(lat, one, other, kappa, outer, partial):
    vmem = pl.BlockSpec(memory_space=pltpu.VMEM)
    return pl.pallas_call(
        halo_kernel,
        in_specs=[in_smem()] + [vmem] * 4 + [in_place()],
        out_specs=in_place(),
        out_shape=jax.ShapeDtypeStruct(partial.shape, jnp.float32),
        scratch_shapes=[pltpu.VMEM(outer.shape, jnp.float32), pltpu.SemaphoreType.DMA((2,))],
        input_output_aliases={5: 0},
        compiler_params=pltpu.CompilerParams(vmem_limit_bytes=VMEM_BYTES),
        cost_estimate=pl.CostEstimate(flops=4 * outer.size, bytes_accessed=20 * outer.size, transcendentals=0),
        name="add_halo",
    )(lat, one, other, kappa, outer, partial)


def body(
    conc,
    dep_owner,
    dep_row,
    dep_weight,
    dep_count,
    zonal_offset,
    agg_rates,
    toeplitz,
    settle,
    kappa,
):
    rows, bins, width = conc.shape
    entries = dep_owner.shape[2]
    my_lat, my_lon = lax.axis_index("lat"), lax.axis_index("lon")
    flags = [(value % 2).astype(jnp.int32).reshape(1) for value in (my_lon, my_lon // 2, my_lat)]
    half = bins // 2
    low, high, meta = messages(conc, dep_owner[0].T, dep_row[0].T, dep_weight[0].T, dep_count)
    lat1, lat2 = swap_lat(high, 0), swap_lat(high, 1)
    lon1, lon2 = swap_chip(low, 0), swap_chip(low, 1)
    beside = swap_core(conc)
    rates, meta = lax.optimization_barrier((agg_rates, meta))
    local = local_terms(conc, rates, toeplitz, settle)
    terms = decoded(flags, [lat1, meta, lat2], lat_slots, rows, half, entries)
    spread = jnp.broadcast_to(zonal_offset[:, None, None], (rows, 1, 128))
    lat1, lat2, local, terms, spread = lax.optimization_barrier((lat1, lat2, local, terms, spread))

    to_lon1, own1, to_lon2 = lon_sums(
        flags,
        [lon1, meta, lon2],
        lon_slots,
        [(lat1, 0), (conc, half), (lat2, 0), (swap_core(lat1), 0), (beside, half), (swap_core(lat2), 0)],
        rows,
        half,
        entries,
    )
    parts1 = [swap_chip(to_lon1, 0), swap_chip(to_lon2, 1)]
    own1, later = lax.optimization_barrier((own1, flags))
    parts1 = [own1] + parts1

    to_lat1, own0, to_lat2 = lat_sums(
        later,
        terms,
        [(conc, 0), (beside, 0), (lon1, 0), (lon2, 0), (swap_core(lon1), 0), (swap_core(lon2), 0)],
        rows,
        half,
        entries,
    )
    parts0 = [own0, swap_lat(to_lat1, 0), swap_lat(to_lat2, 1)]

    kappa = kappa[:, None, :]

    earlier = edges(flags[0], parts1, [])
    parts0, earlier = lax.optimization_barrier((parts0, earlier))
    to_core, to_across = edges(flags[0], parts0, earlier)
    one, other = swap_core(to_core), swap_across(to_across)
    remapped = combine(parts0, parts1)
    row1, row2 = outer_rows(flags[2], spread, remapped, one, other)
    row1, row2 = swap_lat(row1, 0), swap_lat(row2, 1)
    partial, outer = final(zonal_offset, remapped, one, other, kappa, local)
    return add_halo(flags[2], row1, row2, kappa, outer, partial)


def solution(mesh):
    return jax.shard_map(
        body,
        mesh=mesh,
        in_specs=(
            P("lat", None, "lon"),
            P("lon", "lat", None),
            P("lon", "lat", None),
            P("lon", "lat", None),
            P("lon", "lat"),
            P("lat"),
            P(None, "lat", "lon"),
            P(),
            P(),
            P("lat", "lon"),
        ),
        out_specs=P("lat", None, "lon"),
        check_vma=False,
    )
```

```python
import functools

import jax
import jax.numpy as jnp
from jax import lax
from jax.experimental import pallas as pl
from jax.experimental.pallas import tpu as pltpu
from jax.sharding import PartitionSpec as P

REACH = 2
NEAR_LON = 5
UNROLL = 4
VMEM_BYTES = 12 * 1024 * 1024
MOST_BYTES = 60 * 1024 * 1024
TABLE_BYTES = 20 * 1024 * 1024
QUICK = 2
FIELDS = ((0, 0), (0, 128), (8, 0), (8, 128), (16, 0))


def exchange(value, axis, pairs):
    return lax.ppermute(value, axis, [(i, j) for i, j in pairs] + [(j, i) for i, j in pairs])


def swap_core(value):
    return exchange(value, "lon", [(i, i + 1) for i in range(0, lax.axis_size("lon"), 2)])


def swap_across(value):
    count = lax.axis_size("lon")
    return exchange(value, "lon", [(i, (i + 1) % count) for i in range(1, count, 2)])


def swap_chip(value, second):
    count = lax.axis_size("lon")
    firsts = [i for i in range(count) if (i // 2) % 2 == second]
    return exchange(value, "lon", [(i, (i + 2) % count) for i in firsts])


def swap_lat(value, second):
    count = lax.axis_size("lat")
    return exchange(value, "lat", [(i, i + 1) for i in range(second, count - 1, 2)])


def in_smem():
    return pl.BlockSpec(memory_space=pltpu.SMEM)


def in_place():
    return pl.BlockSpec(memory_space=pl.ANY)


def for_rows(count, one):
    def some(g, carry):
        stores = []
        for u in range(UNROLL):
            stores += one(g * UNROLL + u)
        for ref, at, value in stores:
            ref[at] = value.astype(ref.dtype)
        return carry

    lax.fori_loop(0, count // UNROLL, some, 0)


def growth_kernel(flip_ref, settle_ref, conc_ref, rates_ref, out_ref, mat_ref):
    ranks, rows_step = rates_ref.shape[0], conc_ref.shape[0]
    bins, width = conc_ref.shape[1:]

    @pl.when(pl.program_id(0) == 0)
    def _():
        for q in range(ranks):
            spread = jnp.broadcast_to(flip_ref[q : q + 1, :], (bins, 2 * bins))
            turned = pltpu.roll(spread, bins + 1, 1, stride=1, stride_axis=0)
            mat_ref[q * bins : (q + 1) * bins, :] = turned[:, :bins].astype(jnp.bfloat16)

    settle = jnp.broadcast_to(settle_ref[...], (bins, width))
    for r in range(rows_step):
        cells = conc_ref[r]
        product = jnp.dot(mat_ref[...], cells, preferred_element_type=jnp.float32)
        total = -settle * cells.astype(jnp.float32)
        for q in range(ranks):
            total = total + rates_ref[q, r : r + 1, :] * product[q * bins : (q + 1) * bins]
        out_ref[r] = total


def local_terms(conc, agg_rates, toeplitz, settle):
    rows, bins, width = conc.shape
    ranks = agg_rates.shape[0]
    step = 8
    flipped = jnp.pad(toeplitz[:, ::-1].astype(jnp.float32), ((0, 0), (0, 1)))
    return pl.pallas_call(
        growth_kernel,
        grid=(rows // step,),
        in_specs=[
            pl.BlockSpec((ranks, 2 * bins), lambda i: (0, 0)),
            pl.BlockSpec((bins, 1), lambda i: (0, 0)),
            pl.BlockSpec((step, bins, width), lambda i: (i, 0, 0)),
            pl.BlockSpec((ranks, step, width), lambda i: (0, i, 0)),
        ],
        out_specs=pl.BlockSpec((step, bins, width), lambda i: (i, 0, 0)),
        out_shape=jax.ShapeDtypeStruct(conc.shape, jnp.float32),
        scratch_shapes=[pltpu.VMEM((ranks * bins, bins), jnp.bfloat16)],
        compiler_params=pltpu.CompilerParams(vmem_limit_bytes=VMEM_BYTES),
        cost_estimate=pl.CostEstimate(
            flops=2 * ranks * bins * bins * rows * width, bytes_accessed=8 * conc.size, transcendentals=0
        ),
        name="growth",
    )(flipped, settle[:, None], conc, agg_rates)


def messages_kernel(
    conc_ref, owner_hbm, source_hbm, weight_hbm, count_hbm, low_ref, high_ref, meta_ref,
    owner_ref, source_ref, weight_ref, count_ref, sems,
):
    rows = conc_ref.shape[0]
    half = low_ref.shape[1]
    entries = owner_ref.shape[0]
    small = [
        pltpu.make_async_copy(hbm, ref, sems.at[2 + i])
        for i, (hbm, ref) in enumerate(
            ((owner_hbm, owner_ref), (source_hbm, source_ref), (weight_hbm, weight_ref), (count_hbm, count_ref))
        )
    ]
    large = [
        pltpu.make_async_copy(conc_ref.at[:, pl.ds(i * half, half), :], ref.at[pl.ds(0, rows)], sems.at[i])
        for i, ref in enumerate((low_ref, high_ref))
    ]
    for copy in small + large:
        copy.start()
    meta_ref[...] = jnp.zeros(meta_ref.shape, meta_ref.dtype)
    for copy in small:
        copy.wait()
    wide = lambda value: value.astype(jnp.float32)
    entry = lax.broadcasted_iota(jnp.int32, owner_ref.shape, 0)
    live = jnp.where(entry < count_ref[...], weight_ref[...], 0.0)
    top = live.astype(jnp.bfloat16)
    middle = (live - wide(top)).astype(jnp.bfloat16)
    bottom = (live - wide(top) - wide(middle)).astype(jnp.bfloat16)
    fields = (wide(owner_ref[...]), wide(source_ref[...]), wide(top), wide(middle), wide(bottom))
    for field, (at, lane) in zip(fields, FIELDS):
        meta_ref[0, at : at + entries, lane : lane + rows] = field.astype(jnp.bfloat16)
    low_ref[rows] = meta_ref[0]
    high_ref[rows] = meta_ref[0]
    for copy in large:
        copy.wait()


def messages(conc, owner, source, weight, count):
    rows, bins, width = conc.shape
    half = bins // 2
    return pl.pallas_call(
        messages_kernel,
        in_specs=[in_place()] * 5,
        out_specs=[pl.BlockSpec(memory_space=pltpu.VMEM)] * 3,
        out_shape=[
            jax.ShapeDtypeStruct((rows + 1, half, width), conc.dtype),
            jax.ShapeDtypeStruct((rows + 1, half, width), conc.dtype),
            jax.ShapeDtypeStruct((1, half, width), conc.dtype),
        ],
        scratch_shapes=[pltpu.VMEM(small.shape, small.dtype) for small in (owner, source, weight, count)]
        + [pltpu.SemaphoreType.DMA((6,))],
        compiler_params=pltpu.CompilerParams(vmem_limit_bytes=MOST_BYTES),
        cost_estimate=pl.CostEstimate(flops=0, bytes_accessed=4 * conc.size, transcendentals=0),
        name="messages",
    )(conc, owner, source, weight, count)


def signs(flags):
    return [1.0 - 2.0 * ref[0].astype(jnp.float32) for ref in flags]


def lat_slots(rows, group, lat_step, lon_step, flags):
    core, chip, lat = signs(flags)
    far = jnp.where(core * chip < 0.0, 4.0, 5.0)
    slot = jnp.where(
        lon_step == 0.0,
        0.0,
        jnp.where(
            lon_step == 2.0 * chip, 2.0, jnp.where(lon_step == -2.0 * chip, 3.0, jnp.where(lon_step == core, 1.0, far))
        ),
    )
    return lat_step == (group - 1.0) * lat, slot * rows


def lon_slots(rows, group, lat_step, lon_step, flags):
    core, chip, lat = signs(flags)
    lon_from = 2.0 * (1.0 - group) * chip + lon_step
    slot = jnp.where(lon_from == 0.0, 1.0, 4.0) - lat_step * lat
    return (lon_from == 0.0) | (lon_from == core), slot * rows


def decode(slots, rows, entries, flags, meta_ref, index_ref, weight_ref):
    for g in range(3):
        owner, source, top, middle, bottom = [
            meta_ref[g, at : at + entries, lane : lane + 128].astype(jnp.float32) for at, lane in FIELDS
        ]
        weight = top + middle + bottom
        band = jnp.where(owner >= NEAR_LON, 1.0, 0.0) + jnp.where(owner >= 2 * NEAR_LON, 1.0, 0.0)
        here, base = slots(rows, float(g), band - 1.0, owner - NEAR_LON * band - REACH, flags)
        here = jnp.where(here & (weight != 0.0), 1.0, 0.0)
        index = base + source
        packed = [[jnp.zeros((1, 128), jnp.float32)] * 2 for _ in range(entries)]
        rank = jnp.zeros((1, 128), jnp.float32)
        for k in range(entries):
            taken = here[k : k + 1]
            for place in range(k + 1):
                spot = (taken > 0.0) & (rank == place)
                packed[place] = [
                    jnp.where(spot, index[k : k + 1], packed[place][0]),
                    jnp.where(spot, weight[k : k + 1], packed[place][1]),
                ]
            rank = rank + taken
        for place in range(entries):
            at = g * entries + place
            index_ref[at : at + 1, :] = packed[place][0].astype(jnp.int32)
            weight_ref[at : at + 1, :] = packed[place][1]
        at = 3 * entries + g
        index_ref[at : at + 1, :] = rank.astype(jnp.int32)


def read_metas(asked, meta_ref, sems, first):
    return [
        pltpu.make_async_copy(ref.at[pl.ds(ref.shape[0] - 1, 1)], meta_ref.at[pl.ds(g, 1)], sems.at[first + g])
        for g, ref in enumerate(asked)
    ]


def decode_kernel(slots, rows, entries, *refs):
    flags, asked, (index_ref, weight_ref, meta_ref, sems) = refs[:3], refs[3:6], refs[6:]
    copies = read_metas(asked, meta_ref, sems, 0)
    for copy in copies:
        copy.start()
    for copy in copies:
        copy.wait()
    decode(slots, rows, entries, flags, meta_ref, index_ref, weight_ref)


def decoded(flags, asked, slots, rows, half, entries):
    width = asked[1].shape[2]
    vectors = -(-3 * (entries + 1) // 8) * 8
    return pl.pallas_call(
        functools.partial(decode_kernel, slots, rows, entries),
        in_specs=[in_smem()] * 3 + [in_place()] * 3,
        out_specs=[pl.BlockSpec(memory_space=pltpu.VMEM)] * 2,
        out_shape=[
            jax.ShapeDtypeStruct((vectors, 128), jnp.int32),
            jax.ShapeDtypeStruct((vectors, 128), jnp.float32),
        ],
        scratch_shapes=[pltpu.VMEM((3, half, width), jnp.bfloat16), pltpu.SemaphoreType.DMA((3,))],
        compiler_params=pltpu.CompilerParams(vmem_limit_bytes=VMEM_BYTES),
        cost_estimate=pl.CostEstimate(flops=0, bytes_accessed=6 * half * width, transcendentals=0),
        name="decode",
    )(*flags, *asked)


def table_copies(bases, rows, sources, table, sems):
    half = table.shape[1]
    return [
        pltpu.make_async_copy(
            source.at[pl.ds(0, rows), pl.ds(base, half), :], table.at[pl.ds(i * rows, rows)], sems.at[i]
        )
        for i, (source, base) in enumerate(zip(sources, bases))
    ]


def add_terms(rows, entries, index_ref, weight_ref, table, outs):
    half, width = table.shape[1:]
    for group, out in enumerate(outs):

        def some(g, carry, group=group, out=out):
            def sums(terms):
                totals = []
                for u in range(UNROLL):
                    r = g * UNROLL + u
                    total = jnp.zeros((half, width), jnp.float32)
                    for k in range(terms):
                        row = group * entries + k
                        total = total + weight_ref[row, r] * table[index_ref[row, r]].astype(jnp.float32)
                    totals.append(total)
                for u in range(UNROLL):
                    out[g * UNROLL + u] = totals[u].astype(out.dtype)

            most = index_ref[3 * entries + group, g * UNROLL]
            for u in range(1, UNROLL):
                most = jnp.maximum(most, index_ref[3 * entries + group, g * UNROLL + u])
            sums(min(QUICK, entries))

            @pl.when(most > QUICK)
            def _():
                sums(entries)

            return carry

        lax.fori_loop(0, rows // UNROLL, some, 0)


def lat_sums_kernel(bases, entries, core_ref, chip_ref, index_ref, weight_ref, *refs):
    tables = len(bases)
    sources, outs = refs[:tables], refs[tables : tables + 3]
    table, sems = refs[tables + 3 :]
    rows = table.shape[0] // tables
    copies = table_copies(bases, rows, sources, table, sems)
    first = core_ref[0] != chip_ref[0]
    for copy in copies[:-2]:
        copy.start()
    pl.when(first)(copies[-2].start)
    pl.when(jnp.logical_not(first))(copies[-1].start)
    for copy in copies[:-2]:
        copy.wait()
    pl.when(first)(copies[-2].wait)
    pl.when(jnp.logical_not(first))(copies[-1].wait)
    add_terms(rows, entries, index_ref, weight_ref, table, outs)


def lon_sums_kernel(bases, slots, entries, *refs):
    tables = len(bases)
    flags, refs = refs[:3], refs[3:]
    asked, sources, outs = refs[:3], refs[3 : 3 + tables], refs[3 + tables : 6 + tables]
    table, meta_ref, index_vec, weight_vec, index_ref, weight_ref, sems = refs[6 + tables :]
    rows = table.shape[0] // tables
    metas = read_metas(asked, meta_ref, sems, tables)
    copies = table_copies(bases, rows, sources, table, sems)
    for copy in metas + copies:
        copy.start()
    for copy in metas:
        copy.wait()
    decode(slots, rows, entries, flags, meta_ref, index_vec, weight_vec)
    to_scalar = [
        pltpu.make_async_copy(index_vec, index_ref, sems.at[tables + 3]),
        pltpu.make_async_copy(weight_vec, weight_ref, sems.at[tables + 4]),
    ]
    for copy in to_scalar:
        copy.start()
    for copy in to_scalar + copies:
        copy.wait()
    add_terms(rows, entries, index_ref, weight_ref, table, outs)


def sums_call(kernel, operands, smem, sources, scratch, rows, half, entries, name):
    tables = len(sources)
    width = sources[0][0].shape[2]
    return pl.pallas_call(
        kernel,
        in_specs=[in_smem()] * smem + [in_place()] * (len(operands) - smem + tables),
        out_specs=[pl.BlockSpec(memory_space=pltpu.VMEM)] * 3,
        out_shape=[
            jax.ShapeDtypeStruct((rows, half, width), dtype) for dtype in (jnp.bfloat16, jnp.float32, jnp.bfloat16)
        ],
        scratch_shapes=[pltpu.VMEM((tables * rows, half, width), jnp.bfloat16)] + scratch,
        compiler_params=pltpu.CompilerParams(vmem_limit_bytes=TABLE_BYTES),
        cost_estimate=pl.CostEstimate(
            flops=6 * rows * entries * half * width,
            bytes_accessed=2 * (tables + 3) * rows * half * width,
            transcendentals=0,
        ),
        name=name,
    )(*operands, *[source for source, _ in sources])


def lat_sums(flags, terms, sources, rows, half, entries):
    kernel = functools.partial(lat_sums_kernel, tuple(base for _, base in sources), entries)
    scratch = [pltpu.SemaphoreType.DMA((len(sources),))]
    return sums_call(kernel, [*flags[:2], *terms], 4, sources, scratch, rows, half, entries, "lat_sums")


def lon_sums(flags, asked, slots, sources, rows, half, entries):
    kernel = functools.partial(lon_sums_kernel, tuple(base for _, base in sources), slots, entries)
    vectors = -(-3 * (entries + 1) // 8) * 8
    scratch = [pltpu.VMEM((3, half, asked[1].shape[2]), jnp.bfloat16)]
    scratch += [space((vectors, 128), dtype) for space in (pltpu.VMEM, pltpu.SMEM) for dtype in (jnp.int32, jnp.float32)]
    scratch += [pltpu.SemaphoreType.DMA((len(sources) + 5,))]
    return sums_call(kernel, [*flags, *asked], 3, sources, scratch, rows, half, entries, "lon_sums")


def edges_kernel(core_ref, *refs):
    rows, half = refs[0].shape[:2]
    per = 128 // 8
    lane = lax.broadcasted_iota(jnp.int32, (half, 128), 1)
    odd = core_ref[0] == 1
    for earlier_ref, out_ref in zip(refs[6:-2], refs[-2:]):
        out_ref[:, half:] = earlier_ref[...]
    for j in range(rows // per):
        ends = []
        for side in range(2):
            parts = refs[3 * side : 3 * side + 3]
            packed = jnp.zeros((half, 128), jnp.float32)
            for i in range(per):
                r = j * per + i
                cells = parts[0][r] + parts[1][r].astype(jnp.float32) + parts[2][r].astype(jnp.float32)
                at = 8 * i + 3 * (1 - side)
                spot = (lane >= at) & (lane < at + 3)
                packed = jnp.where(spot, pltpu.roll(cells, 8 * i + 3, 1), packed)
            ends.append(packed)
        for out_ref, value in zip(refs[-2:], (jnp.where(odd, *ends), jnp.where(odd, *ends[::-1]))):
            out_ref[j, :half] = value.astype(out_ref.dtype)


def edges(core, parts, earlier):
    rows, half, width = parts[0].shape
    specs = [
        pl.BlockSpec((rows, half, 128), lambda t, at=at: (0, 0, at)) for at in (0, width // 128 - 1) for _ in parts
    ]
    whole = lambda shape: pl.BlockSpec(shape, lambda t: (0,) * len(shape))
    packed = (rows // 16, half + sum(array.shape[1] for array in earlier[:1]), 128)
    return pl.pallas_call(
        edges_kernel,
        grid=(1,),
        in_specs=[in_smem()] + specs + [whole(array.shape) for array in earlier],
        out_specs=[whole(packed)] * 2,
        out_shape=[jax.ShapeDtypeStruct(packed, jnp.bfloat16)] * 2,
        compiler_params=pltpu.CompilerParams(vmem_limit_bytes=VMEM_BYTES),
        cost_estimate=pl.CostEstimate(flops=8 * half * 256 * rows, bytes_accessed=16 * half * 256 * rows, transcendentals=0),
        name="edges",
    )(core, *parts, *parts, *earlier)


def combine_kernel(own0, a0, b0, own1, a1, b1, out_ref):
    rows, half = own0.shape[:2]
    for r in range(rows):
        out_ref[r, :half] = own0[r] + a0[r].astype(jnp.float32) + b0[r].astype(jnp.float32)
        out_ref[r, half:] = own1[r] + a1[r].astype(jnp.float32) + b1[r].astype(jnp.float32)


def combine(parts0, parts1):
    rows, half, width = parts0[0].shape
    step = 8
    return pl.pallas_call(
        combine_kernel,
        grid=(rows // step,),
        in_specs=[pl.BlockSpec((step, half, width), lambda t: (t, 0, 0))] * 6,
        out_specs=pl.BlockSpec((step, 2 * half, width), lambda t: (t, 0, 0)),
        out_shape=jax.ShapeDtypeStruct((rows, 2 * half, width), jnp.float32),
        compiler_params=pltpu.CompilerParams(vmem_limit_bytes=VMEM_BYTES),
        cost_estimate=pl.CostEstimate(
            flops=4 * rows * half * width, bytes_accessed=24 * rows * half * width, transcendentals=0
        ),
        name="combine",
    )(*parts0, *parts1)


def shifted_by(row, edge, amount, lane):
    count = len(row)
    if amount == 0:
        return row
    if amount > 0:
        row = row[:-1] + [jnp.where(lane >= 128 - amount, edge, row[-1])]
        turned = [pltpu.roll(tile, amount, 1) for tile in row]
        return [jnp.where(lane < amount, turned[t - 1], turned[t]) for t in range(count)]
    row = [jnp.where(lane < -amount, edge, row[0])] + row[1:]
    turned = [pltpu.roll(tile, 128 + amount, 1) for tile in row]
    return [jnp.where(lane >= 128 + amount, turned[(t + 1) % count], turned[t]) for t in range(count)]


def edge_tile(west_ref, east_ref, r):
    per = 128 // 8
    both = west_ref[r // per].astype(jnp.float32) + east_ref[r // per].astype(jnp.float32)
    return pltpu.roll(both, (125 - 8 * (r % per)) % 128, 1)


def rows_kernel(lat_ref, offset_ref, first_row, last_row, one_ref, other_ref, *outs):
    bins, width = first_row.shape[1:]
    lane = lax.broadcasted_iota(jnp.int32, (bins, 128), 1)
    spots = [slice(128 * t, 128 * t + 128) for t in range(width // 128)]
    end = offset_ref.shape[0] - 1
    odd = lat_ref[0] == 1
    for out_ref, first in ((outs[0], odd), (outs[1], jnp.logical_not(odd))):
        offset = jnp.broadcast_to(jnp.where(first, offset_ref[0], offset_ref[end]), (bins, 128))
        row = [jnp.where(first, first_row[0, :, at], last_row[0, :, at]) for at in spots]
        edge = jnp.where(first, edge_tile(one_ref, other_ref, 0), edge_tile(one_ref, other_ref, end))
        result = row
        for amount in (-2, -1, 1, 2):
            moved = shifted_by(row, edge, amount, lane)
            result = [jnp.where(offset == amount, tile, kept) for tile, kept in zip(moved, result)]
        for at, tile in zip(spots, result):
            out_ref[0, :, at] = tile.astype(out_ref.dtype)


def outer_rows(lat, offset, remapped, one, other):
    rows, bins, width = remapped.shape
    row = lambda at: pl.BlockSpec((1, bins, width), lambda t: (at, 0, 0))
    whole = lambda array: pl.BlockSpec(array.shape, lambda t: (0, 0, 0))
    return pl.pallas_call(
        rows_kernel,
        grid=(1,),
        in_specs=[in_smem(), whole(offset), row(0), row(rows - 1), whole(one), whole(other)],
        out_specs=[row(0), row(0)],
        out_shape=[jax.ShapeDtypeStruct((1, bins, width), jnp.bfloat16)] * 2,
        compiler_params=pltpu.CompilerParams(vmem_limit_bytes=VMEM_BYTES),
        cost_estimate=pl.CostEstimate(flops=20 * bins * width, bytes_accessed=12 * bins * width, transcendentals=0),
        name="outer_rows",
    )(lat, offset, remapped, remapped, one, other)


def final_kernel(
    spread_ref, remap_ref, one_ref, other_ref, kappa_ref, local_ref, out_ref, outer_ref,
    offset_ref, edge_ref, sums_ref, sems,
):
    rows, bins, width = remap_ref.shape
    offsets = pltpu.make_async_copy(spread_ref, offset_ref, sems.at[sems.shape[0] - 1])
    offsets.start()
    count = width // 128
    lane = lax.broadcasted_iota(jnp.int32, (8, 128), 1)
    spots = [slice(128 * t, 128 * t + 128) for t in range(count)]
    for r in range(rows):
        edge_ref[r] = edge_tile(one_ref, other_ref, r)
    offsets.wait()

    def moved(row, edge, amount):
        row = [jnp.where(lane < -amount, edge, row[0])] + row[1:]
        row = row[:-1] + [jnp.where(lane >= 128 - amount, edge, row[-1])]
        turned = [pltpu.roll(tile, (amount + 128) & 127, 1) for tile in row]
        before, after = lane < amount, lane >= 128 + amount
        return [
            jnp.where(before, turned[t - 1], jnp.where(after, turned[(t + 1) % count], turned[t])) for t in range(count)
        ]

    copies = []
    for half in range(2):
        first = half * bins // 2
        pieces = [slice(b, b + 8) for b in range(first, first + bins // 2, 8)]
        before, now, base = {}, {}, {}
        stores = []
        sent = 1
        for r in range(rows):
            amount = offset_ref[r, 0, 0]
            kappa = [kappa_ref[r, :, spot] for spot in spots]
            above = [kappa_ref[max(r - 1, 0), :, spot] for spot in spots]
            for at in pieces:
                row = [remap_ref[r, at, spot] for spot in spots]
                edge = edge_ref[r, at]
                center = moved(row, edge, amount)
                east = moved(row, edge, amount - 1)
                west = moved(row, edge, amount + 1)
                key = at.start
                fresh = []
                for t, spot in enumerate(spots):
                    around = kappa[t] * (east[t] + west[t] - 4.0 * center[t])
                    fresh.append(local_ref[r, at, spot] + center[t] + around)
                    if r == 1:
                        stores.append((r - 1, at, spot, base[key][t] + above[t] * center[t]))
                    elif r:
                        stores.append((r - 1, at, spot, base[key][t] + above[t] * (before[key][t] + center[t])))
                if r:
                    before[key] = now[key]
                now[key], base[key] = center, fresh
            if r % 2:
                for which, at, spot, value in stores:
                    if which:
                        sums_ref[which, at, spot] = value
                    else:
                        outer_ref[0, at, spot] = value
                stores = []
            if r % 8 == 7:
                block = (pl.ds(sent, r - sent), pl.ds(first, bins // 2))
                copy = pltpu.make_async_copy(sums_ref.at[block], out_ref.at[block], sems.at[len(copies)])
                copy.start()
                copies.append(copy)
                sent = r
        for at in pieces:
            for t, spot in enumerate(spots):
                outer_ref[1, at, spot] = base[at.start][t] + kappa_ref[rows - 1, :, spot] * before[at.start][t]
    for copy in copies:
        copy.wait()


def final(spread, remapped, one, other, kappa, local):
    rows, bins, width = remapped.shape
    vmem = pl.BlockSpec(memory_space=pltpu.VMEM)
    return pl.pallas_call(
        final_kernel,
        in_specs=[vmem] * 6,
        out_specs=[in_place(), vmem],
        out_shape=[
            jax.ShapeDtypeStruct(local.shape, jnp.float32),
            jax.ShapeDtypeStruct((2, bins, width), jnp.float32),
        ],
        scratch_shapes=[
            pltpu.SMEM(spread.shape, jnp.int32),
            pltpu.VMEM((rows, bins, 128), jnp.float32),
            pltpu.VMEM((rows, bins, width), jnp.float32),
            pltpu.SemaphoreType.DMA((2 * (rows // 8) + 1,)),
        ],
        compiler_params=pltpu.CompilerParams(vmem_limit_bytes=TABLE_BYTES),
        cost_estimate=pl.CostEstimate(flops=30 * remapped.size, bytes_accessed=12 * remapped.size, transcendentals=0),
        name="final",
    )(spread, remapped, one, other, kappa, local)


def halo_kernel(lat_ref, one_ref, other_ref, kappa_ref, outer_ref, _, out_ref, sums_ref, sems):
    odd = lat_ref[0] == 1
    rows = out_ref.shape[0]
    copies = []
    for side, (first, at) in enumerate(((odd, 0), (jnp.logical_not(odd), rows - 1))):
        value = jnp.where(first, one_ref[0].astype(jnp.float32), other_ref[0].astype(jnp.float32))
        sums_ref[side] = outer_ref[side] + kappa_ref[at] * value
        copy = pltpu.make_async_copy(sums_ref.at[pl.ds(side, 1)], out_ref.at[pl.ds(at, 1)], sems.at[side])
        copy.start()
        copies.append(copy)
    for copy in copies:
        copy.wait()


def add_halo(lat, one, other, kappa, outer, partial):
    vmem = pl.BlockSpec(memory_space=pltpu.VMEM)
    return pl.pallas_call(
        halo_kernel,
        in_specs=[in_smem()] + [vmem] * 4 + [in_place()],
        out_specs=in_place(),
        out_shape=jax.ShapeDtypeStruct(partial.shape, jnp.float32),
        scratch_shapes=[pltpu.VMEM(outer.shape, jnp.float32), pltpu.SemaphoreType.DMA((2,))],
        input_output_aliases={5: 0},
        compiler_params=pltpu.CompilerParams(vmem_limit_bytes=VMEM_BYTES),
        cost_estimate=pl.CostEstimate(flops=4 * outer.size, bytes_accessed=20 * outer.size, transcendentals=0),
        name="add_halo",
    )(lat, one, other, kappa, outer, partial)


def body(
    conc,
    dep_owner,
    dep_row,
    dep_weight,
    dep_count,
    zonal_offset,
    agg_rates,
    toeplitz,
    settle,
    kappa,
):
    rows, bins, width = conc.shape
    entries = dep_owner.shape[2]
    my_lat, my_lon = lax.axis_index("lat"), lax.axis_index("lon")
    flags = [(value % 2).astype(jnp.int32).reshape(1) for value in (my_lon, my_lon // 2, my_lat)]
    half = bins // 2
    low, high, meta = messages(conc, dep_owner[0].T, dep_row[0].T, dep_weight[0].T, dep_count)
    lat1, lat2 = swap_lat(high, 0), swap_lat(high, 1)
    lon1, lon2 = swap_chip(low, 0), swap_chip(low, 1)
    beside = swap_core(conc)
    rates, meta = lax.optimization_barrier((agg_rates, meta))
    local = local_terms(conc, rates, toeplitz, settle)
    spread = jnp.broadcast_to(zonal_offset[:, None, None], (rows, 1, 128))
    lat1, local, spread = lax.optimization_barrier((lat1, local, spread))
    beside_lat1, beside_lat2 = swap_core(lat1), swap_core(lat2)
    terms = decoded(flags, [lat1, meta, lat2], lat_slots, rows, half, entries)
    lon1, lon2, terms = lax.optimization_barrier((lon1, lon2, terms))

    to_lon1, own1, to_lon2 = lon_sums(
        flags,
        [lon1, meta, lon2],
        lon_slots,
        [(lat1, 0), (conc, half), (lat2, 0), (beside_lat1, 0), (beside, half), (beside_lat2, 0)],
        rows,
        half,
        entries,
    )
    parts1 = [swap_chip(to_lon1, 0), swap_chip(to_lon2, 1)]
    own1, later = lax.optimization_barrier((own1, flags))
    parts1 = [own1] + parts1

    to_lat1, own0, to_lat2 = lat_sums(
        later,
        terms,
        [(conc, 0), (beside, 0), (lon1, 0), (lon2, 0), (swap_core(lon1), 0), (swap_core(lon2), 0)],
        rows,
        half,
        entries,
    )
    parts0 = [own0, swap_lat(to_lat1, 0), swap_lat(to_lat2, 1)]

    kappa = kappa[:, None, :]

    earlier = edges(flags[0], parts1, [])
    parts0, earlier = lax.optimization_barrier((parts0, earlier))
    to_core, to_across = edges(flags[0], parts0, earlier)
    one, other = swap_core(to_core), swap_across(to_across)
    remapped = combine(parts0, parts1)
    row1, row2 = outer_rows(flags[2], spread, remapped, one, other)
    row1, row2 = swap_lat(row1, 0), swap_lat(row2, 1)
    partial, outer = final(spread, remapped, one, other, kappa, local)
    return add_halo(flags[2], row1, row2, kappa, outer, partial)


def solution(mesh):
    return jax.shard_map(
        body,
        mesh=mesh,
        in_specs=(
            P("lat", None, "lon"),
            P("lon", "lat", None),
            P("lon", "lat", None),
            P("lon", "lat", None),
            P("lon", "lat"),
            P("lat"),
            P(None, "lat", "lon"),
            P(),
            P(),
            P("lat", "lon"),
        ),
        out_specs=P("lat", None, "lon"),
        check_vma=False,
    )
```

```python
import functools

import jax
import jax.numpy as jnp
from jax import lax
from jax.experimental import pallas as pl
from jax.experimental.pallas import tpu as pltpu
from jax.sharding import PartitionSpec as P

REACH = 2
NEAR_LON = 5
UNROLL = 4
VMEM_BYTES = 12 * 1024 * 1024
MOST_BYTES = 60 * 1024 * 1024
TABLE_BYTES = 20 * 1024 * 1024
QUICK = 2
FIELDS = ((0, 0), (0, 128), (8, 0), (8, 128), (16, 0))


def exchange(value, axis, pairs):
    return lax.ppermute(value, axis, [(i, j) for i, j in pairs] + [(j, i) for i, j in pairs])


def swap_core(value):
    return exchange(value, "lon", [(i, i + 1) for i in range(0, lax.axis_size("lon"), 2)])


def swap_across(value):
    count = lax.axis_size("lon")
    return exchange(value, "lon", [(i, (i + 1) % count) for i in range(1, count, 2)])


def swap_chip(value, second):
    count = lax.axis_size("lon")
    firsts = [i for i in range(count) if (i // 2) % 2 == second]
    return exchange(value, "lon", [(i, (i + 2) % count) for i in firsts])


def swap_lat(value, second):
    count = lax.axis_size("lat")
    return exchange(value, "lat", [(i, i + 1) for i in range(second, count - 1, 2)])


def in_smem():
    return pl.BlockSpec(memory_space=pltpu.SMEM)


def in_place():
    return pl.BlockSpec(memory_space=pl.ANY)


def for_rows(count, one):
    def some(g, carry):
        stores = []
        for u in range(UNROLL):
            stores += one(g * UNROLL + u)
        for ref, at, value in stores:
            ref[at] = value.astype(ref.dtype)
        return carry

    lax.fori_loop(0, count // UNROLL, some, 0)


def growth_kernel(flip_ref, settle_ref, conc_ref, rates_ref, out_ref, mat_ref):
    ranks, rows_step = rates_ref.shape[0], conc_ref.shape[0]
    bins, width = conc_ref.shape[1:]

    @pl.when(pl.program_id(0) == 0)
    def _():
        for q in range(ranks):
            spread = jnp.broadcast_to(flip_ref[q : q + 1, :], (bins, 2 * bins))
            turned = pltpu.roll(spread, bins + 1, 1, stride=1, stride_axis=0)
            mat_ref[q * bins : (q + 1) * bins, :] = turned[:, :bins].astype(jnp.bfloat16)

    settle = jnp.broadcast_to(settle_ref[...], (bins, width))
    for r in range(rows_step):
        cells = conc_ref[r]
        product = jnp.dot(mat_ref[...], cells, preferred_element_type=jnp.float32)
        total = -settle * cells.astype(jnp.float32)
        for q in range(ranks):
            total = total + rates_ref[q, r : r + 1, :] * product[q * bins : (q + 1) * bins]
        out_ref[r] = total


def local_terms(conc, agg_rates, toeplitz, settle):
    rows, bins, width = conc.shape
    ranks = agg_rates.shape[0]
    step = 8
    flipped = jnp.pad(toeplitz[:, ::-1].astype(jnp.float32), ((0, 0), (0, 1)))
    return pl.pallas_call(
        growth_kernel,
        grid=(rows // step,),
        in_specs=[
            pl.BlockSpec((ranks, 2 * bins), lambda i: (0, 0)),
            pl.BlockSpec((bins, 1), lambda i: (0, 0)),
            pl.BlockSpec((step, bins, width), lambda i: (i, 0, 0)),
            pl.BlockSpec((ranks, step, width), lambda i: (0, i, 0)),
        ],
        out_specs=pl.BlockSpec((step, bins, width), lambda i: (i, 0, 0)),
        out_shape=jax.ShapeDtypeStruct(conc.shape, jnp.float32),
        scratch_shapes=[pltpu.VMEM((ranks * bins, bins), jnp.bfloat16)],
        compiler_params=pltpu.CompilerParams(vmem_limit_bytes=VMEM_BYTES),
        cost_estimate=pl.CostEstimate(
            flops=2 * ranks * bins * bins * rows * width, bytes_accessed=8 * conc.size, transcendentals=0
        ),
        name="growth",
    )(flipped, settle[:, None], conc, agg_rates)


def messages_kernel(
    conc_ref, owner_hbm, source_hbm, weight_hbm, count_hbm, low_ref, high_ref, meta_ref,
    owner_ref, source_ref, weight_ref, count_ref, sems,
):
    rows = conc_ref.shape[0]
    half = low_ref.shape[1]
    entries = owner_ref.shape[0]
    small = [
        pltpu.make_async_copy(hbm, ref, sems.at[2 + i])
        for i, (hbm, ref) in enumerate(
            ((owner_hbm, owner_ref), (source_hbm, source_ref), (weight_hbm, weight_ref), (count_hbm, count_ref))
        )
    ]
    large = [
        pltpu.make_async_copy(conc_ref.at[:, pl.ds(i * half, half), :], ref.at[pl.ds(0, rows)], sems.at[i])
        for i, ref in enumerate((low_ref, high_ref))
    ]
    for copy in small + large:
        copy.start()
    meta_ref[...] = jnp.zeros(meta_ref.shape, meta_ref.dtype)
    for copy in small:
        copy.wait()
    wide = lambda value: value.astype(jnp.float32)
    entry = lax.broadcasted_iota(jnp.int32, owner_ref.shape, 0)
    live = jnp.where(entry < count_ref[...], weight_ref[...], 0.0)
    top = live.astype(jnp.bfloat16)
    middle = (live - wide(top)).astype(jnp.bfloat16)
    bottom = (live - wide(top) - wide(middle)).astype(jnp.bfloat16)
    fields = (wide(owner_ref[...]), wide(source_ref[...]), wide(top), wide(middle), wide(bottom))
    for field, (at, lane) in zip(fields, FIELDS):
        meta_ref[0, at : at + entries, lane : lane + rows] = field.astype(jnp.bfloat16)
    low_ref[rows] = meta_ref[0]
    high_ref[rows] = meta_ref[0]
    for copy in large:
        copy.wait()


def messages(conc, owner, source, weight, count):
    rows, bins, width = conc.shape
    half = bins // 2
    return pl.pallas_call(
        messages_kernel,
        in_specs=[in_place()] * 5,
        out_specs=[pl.BlockSpec(memory_space=pltpu.VMEM)] * 3,
        out_shape=[
            jax.ShapeDtypeStruct((rows + 1, half, width), conc.dtype),
            jax.ShapeDtypeStruct((rows + 1, half, width), conc.dtype),
            jax.ShapeDtypeStruct((1, half, width), conc.dtype),
        ],
        scratch_shapes=[pltpu.VMEM(small.shape, small.dtype) for small in (owner, source, weight, count)]
        + [pltpu.SemaphoreType.DMA((6,))],
        compiler_params=pltpu.CompilerParams(vmem_limit_bytes=MOST_BYTES),
        cost_estimate=pl.CostEstimate(flops=0, bytes_accessed=4 * conc.size, transcendentals=0),
        name="messages",
    )(conc, owner, source, weight, count)


def signs(flags):
    return [1.0 - 2.0 * ref[0].astype(jnp.float32) for ref in flags]


def lat_slots(rows, group, lat_step, lon_step, flags):
    core, chip, lat = signs(flags)
    far = jnp.where(core * chip < 0.0, 4.0, 5.0)
    slot = jnp.where(
        lon_step == 0.0,
        0.0,
        jnp.where(
            lon_step == 2.0 * chip, 2.0, jnp.where(lon_step == -2.0 * chip, 3.0, jnp.where(lon_step == core, 1.0, far))
        ),
    )
    return lat_step == (group - 1.0) * lat, slot * rows


def lon_slots(rows, group, lat_step, lon_step, flags):
    core, chip, lat = signs(flags)
    lon_from = 2.0 * (1.0 - group) * chip + lon_step
    slot = jnp.where(lon_from == 0.0, 1.0, 4.0) - lat_step * lat
    return (lon_from == 0.0) | (lon_from == core), slot * rows


def decode(slots, rows, entries, flags, meta_ref, index_ref, weight_ref):
    for g in range(3):
        owner, source, top, middle, bottom = [
            meta_ref[g, at : at + entries, lane : lane + 128].astype(jnp.float32) for at, lane in FIELDS
        ]
        weight = top + middle + bottom
        band = jnp.where(owner >= NEAR_LON, 1.0, 0.0) + jnp.where(owner >= 2 * NEAR_LON, 1.0, 0.0)
        here, base = slots(rows, float(g), band - 1.0, owner - NEAR_LON * band - REACH, flags)
        here = jnp.where(here & (weight != 0.0), 1.0, 0.0)
        index = base + source
        packed = [[jnp.zeros((1, 128), jnp.float32)] * 2 for _ in range(entries)]
        rank = jnp.zeros((1, 128), jnp.float32)
        for k in range(entries):
            taken = here[k : k + 1]
            for place in range(k + 1):
                spot = (taken > 0.0) & (rank == place)
                packed[place] = [
                    jnp.where(spot, index[k : k + 1], packed[place][0]),
                    jnp.where(spot, weight[k : k + 1], packed[place][1]),
                ]
            rank = rank + taken
        for place in range(entries):
            at = g * entries + place
            index_ref[at : at + 1, :] = packed[place][0].astype(jnp.int32)
            weight_ref[at : at + 1, :] = packed[place][1]
        at = 3 * entries + g
        index_ref[at : at + 1, :] = rank.astype(jnp.int32)


def read_metas(asked, meta_ref, sems, first):
    return [
        pltpu.make_async_copy(ref.at[pl.ds(ref.shape[0] - 1, 1)], meta_ref.at[pl.ds(g, 1)], sems.at[first + g])
        for g, ref in enumerate(asked)
    ]


def decode_kernel(slots, rows, entries, *refs):
    flags, asked, (index_ref, weight_ref, meta_ref, sems) = refs[:3], refs[3:6], refs[6:]
    copies = read_metas(asked, meta_ref, sems, 0)
    for copy in copies:
        copy.start()
    for copy in copies:
        copy.wait()
    decode(slots, rows, entries, flags, meta_ref, index_ref, weight_ref)


def decoded(flags, asked, slots, rows, half, entries):
    width = asked[1].shape[2]
    vectors = -(-3 * (entries + 1) // 8) * 8
    return pl.pallas_call(
        functools.partial(decode_kernel, slots, rows, entries),
        in_specs=[in_smem()] * 3 + [in_place()] * 3,
        out_specs=[pl.BlockSpec(memory_space=pltpu.VMEM)] * 2,
        out_shape=[
            jax.ShapeDtypeStruct((vectors, 128), jnp.int32),
            jax.ShapeDtypeStruct((vectors, 128), jnp.float32),
        ],
        scratch_shapes=[pltpu.VMEM((3, half, width), jnp.bfloat16), pltpu.SemaphoreType.DMA((3,))],
        compiler_params=pltpu.CompilerParams(vmem_limit_bytes=VMEM_BYTES),
        cost_estimate=pl.CostEstimate(flops=0, bytes_accessed=6 * half * width, transcendentals=0),
        name="decode",
    )(*flags, *asked)


def table_copies(bases, rows, sources, table, sems):
    half = table.shape[1]
    return [
        pltpu.make_async_copy(
            source.at[pl.ds(0, rows), pl.ds(base, half), :], table.at[pl.ds(i * rows, rows)], sems.at[i]
        )
        for i, (source, base) in enumerate(zip(sources, bases))
    ]


def add_terms(rows, entries, index_ref, weight_ref, table, outs):
    half, width = table.shape[1:]
    for group, out in enumerate(outs):

        def some(g, carry, group=group, out=out):
            def sums(terms):
                totals = []
                for u in range(UNROLL):
                    r = g * UNROLL + u
                    total = jnp.zeros((half, width), jnp.float32)
                    for k in range(terms):
                        row = group * entries + k
                        total = total + weight_ref[row, r] * table[index_ref[row, r]].astype(jnp.float32)
                    totals.append(total)
                for u in range(UNROLL):
                    out[g * UNROLL + u] = totals[u].astype(out.dtype)

            most = index_ref[3 * entries + group, g * UNROLL]
            for u in range(1, UNROLL):
                most = jnp.maximum(most, index_ref[3 * entries + group, g * UNROLL + u])
            sums(min(QUICK, entries))

            @pl.when(most > QUICK)
            def _():
                sums(entries)

            return carry

        lax.fori_loop(0, rows // UNROLL, some, 0)


def lat_sums_kernel(bases, entries, core_ref, chip_ref, index_ref, weight_ref, *refs):
    tables = len(bases)
    sources, outs = refs[:tables], refs[tables : tables + 3]
    table, sems = refs[tables + 3 :]
    rows = table.shape[0] // tables
    copies = table_copies(bases, rows, sources, table, sems)
    first = core_ref[0] != chip_ref[0]
    for copy in copies[:-2]:
        copy.start()
    pl.when(first)(copies[-2].start)
    pl.when(jnp.logical_not(first))(copies[-1].start)
    for copy in copies[:-2]:
        copy.wait()
    pl.when(first)(copies[-2].wait)
    pl.when(jnp.logical_not(first))(copies[-1].wait)
    add_terms(rows, entries, index_ref, weight_ref, table, outs)


def lon_sums_kernel(bases, slots, entries, *refs):
    tables = len(bases)
    flags, refs = refs[:3], refs[3:]
    asked, sources, outs = refs[:3], refs[3 : 3 + tables], refs[3 + tables : 6 + tables]
    table, meta_ref, index_vec, weight_vec, index_ref, weight_ref, sems = refs[6 + tables :]
    rows = table.shape[0] // tables
    metas = read_metas(asked, meta_ref, sems, tables)
    copies = table_copies(bases, rows, sources, table, sems)
    for copy in metas + copies:
        copy.start()
    for copy in metas:
        copy.wait()
    decode(slots, rows, entries, flags, meta_ref, index_vec, weight_vec)
    to_scalar = [
        pltpu.make_async_copy(index_vec, index_ref, sems.at[tables + 3]),
        pltpu.make_async_copy(weight_vec, weight_ref, sems.at[tables + 4]),
    ]
    for copy in to_scalar:
        copy.start()
    for copy in to_scalar + copies:
        copy.wait()
    add_terms(rows, entries, index_ref, weight_ref, table, outs)


def sums_call(kernel, operands, smem, sources, scratch, rows, half, entries, name):
    tables = len(sources)
    width = sources[0][0].shape[2]
    return pl.pallas_call(
        kernel,
        in_specs=[in_smem()] * smem + [in_place()] * (len(operands) - smem + tables),
        out_specs=[pl.BlockSpec(memory_space=pltpu.VMEM)] * 3,
        out_shape=[
            jax.ShapeDtypeStruct((rows, half, width), dtype) for dtype in (jnp.bfloat16, jnp.float32, jnp.bfloat16)
        ],
        scratch_shapes=[pltpu.VMEM((tables * rows, half, width), jnp.bfloat16)] + scratch,
        compiler_params=pltpu.CompilerParams(vmem_limit_bytes=TABLE_BYTES),
        cost_estimate=pl.CostEstimate(
            flops=6 * rows * entries * half * width,
            bytes_accessed=2 * (tables + 3) * rows * half * width,
            transcendentals=0,
        ),
        name=name,
    )(*operands, *[source for source, _ in sources])


def lat_sums(flags, terms, sources, rows, half, entries):
    kernel = functools.partial(lat_sums_kernel, tuple(base for _, base in sources), entries)
    scratch = [pltpu.SemaphoreType.DMA((len(sources),))]
    return sums_call(kernel, [*flags[:2], *terms], 4, sources, scratch, rows, half, entries, "lat_sums")


def lon_sums(flags, asked, slots, sources, rows, half, entries):
    kernel = functools.partial(lon_sums_kernel, tuple(base for _, base in sources), slots, entries)
    vectors = -(-3 * (entries + 1) // 8) * 8
    scratch = [pltpu.VMEM((3, half, asked[1].shape[2]), jnp.bfloat16)]
    scratch += [space((vectors, 128), dtype) for space in (pltpu.VMEM, pltpu.SMEM) for dtype in (jnp.int32, jnp.float32)]
    scratch += [pltpu.SemaphoreType.DMA((len(sources) + 5,))]
    return sums_call(kernel, [*flags, *asked], 3, sources, scratch, rows, half, entries, "lon_sums")


def edges_kernel(core_ref, *refs):
    rows, half = refs[0].shape[:2]
    per = 128 // 8
    lane = lax.broadcasted_iota(jnp.int32, (half, 128), 1)
    odd = core_ref[0] == 1
    for earlier_ref, out_ref in zip(refs[6:-2], refs[-2:]):
        out_ref[:, half:] = earlier_ref[...]
    for j in range(rows // per):
        ends = []
        for side in range(2):
            parts = refs[3 * side : 3 * side + 3]
            packed = jnp.zeros((half, 128), jnp.float32)
            for i in range(per):
                r = j * per + i
                cells = parts[0][r] + parts[1][r].astype(jnp.float32) + parts[2][r].astype(jnp.float32)
                at = 8 * i + 3 * (1 - side)
                spot = (lane >= at) & (lane < at + 3)
                packed = jnp.where(spot, pltpu.roll(cells, 8 * i + 3, 1), packed)
            ends.append(packed)
        for out_ref, value in zip(refs[-2:], (jnp.where(odd, *ends), jnp.where(odd, *ends[::-1]))):
            out_ref[j, :half] = value.astype(out_ref.dtype)


def edges(core, parts, earlier):
    rows, half, width = parts[0].shape
    specs = [
        pl.BlockSpec((rows, half, 128), lambda t, at=at: (0, 0, at)) for at in (0, width // 128 - 1) for _ in parts
    ]
    whole = lambda shape: pl.BlockSpec(shape, lambda t: (0,) * len(shape))
    packed = (rows // 16, half + sum(array.shape[1] for array in earlier[:1]), 128)
    return pl.pallas_call(
        edges_kernel,
        grid=(1,),
        in_specs=[in_smem()] + specs + [whole(array.shape) for array in earlier],
        out_specs=[whole(packed)] * 2,
        out_shape=[jax.ShapeDtypeStruct(packed, jnp.bfloat16)] * 2,
        compiler_params=pltpu.CompilerParams(vmem_limit_bytes=VMEM_BYTES),
        cost_estimate=pl.CostEstimate(flops=8 * half * 256 * rows, bytes_accessed=16 * half * 256 * rows, transcendentals=0),
        name="edges",
    )(core, *parts, *parts, *earlier)


def combine_kernel(own0, a0, b0, own1, a1, b1, out_ref):
    rows, half = own0.shape[:2]
    for r in range(rows):
        out_ref[r, :half] = own0[r] + a0[r].astype(jnp.float32) + b0[r].astype(jnp.float32)
        out_ref[r, half:] = own1[r] + a1[r].astype(jnp.float32) + b1[r].astype(jnp.float32)


def combine(parts0, parts1):
    rows, half, width = parts0[0].shape
    step = 8
    return pl.pallas_call(
        combine_kernel,
        grid=(rows // step,),
        in_specs=[pl.BlockSpec((step, half, width), lambda t: (t, 0, 0))] * 6,
        out_specs=pl.BlockSpec((step, 2 * half, width), lambda t: (t, 0, 0)),
        out_shape=jax.ShapeDtypeStruct((rows, 2 * half, width), jnp.float32),
        compiler_params=pltpu.CompilerParams(vmem_limit_bytes=VMEM_BYTES),
        cost_estimate=pl.CostEstimate(
            flops=4 * rows * half * width, bytes_accessed=24 * rows * half * width, transcendentals=0
        ),
        name="combine",
    )(*parts0, *parts1)


def shifted_by(row, edge, amount, lane):
    count = len(row)
    if amount == 0:
        return row
    if amount > 0:
        row = row[:-1] + [jnp.where(lane >= 128 - amount, edge, row[-1])]
        turned = [pltpu.roll(tile, amount, 1) for tile in row]
        return [jnp.where(lane < amount, turned[t - 1], turned[t]) for t in range(count)]
    row = [jnp.where(lane < -amount, edge, row[0])] + row[1:]
    turned = [pltpu.roll(tile, 128 + amount, 1) for tile in row]
    return [jnp.where(lane >= 128 + amount, turned[(t + 1) % count], turned[t]) for t in range(count)]


def edge_tile(west_ref, east_ref, r):
    per = 128 // 8
    both = west_ref[r // per].astype(jnp.float32) + east_ref[r // per].astype(jnp.float32)
    return pltpu.roll(both, (125 - 8 * (r % per)) % 128, 1)


def rows_kernel(lat_ref, offset_ref, first_row, last_row, one_ref, other_ref, *outs):
    bins, width = first_row.shape[1:]
    lane = lax.broadcasted_iota(jnp.int32, (bins, 128), 1)
    spots = [slice(128 * t, 128 * t + 128) for t in range(width // 128)]
    end = offset_ref.shape[0] - 1
    odd = lat_ref[0] == 1
    for out_ref, first in ((outs[0], odd), (outs[1], jnp.logical_not(odd))):
        offset = jnp.broadcast_to(jnp.where(first, offset_ref[0], offset_ref[end]), (bins, 128))
        row = [jnp.where(first, first_row[0, :, at], last_row[0, :, at]) for at in spots]
        edge = jnp.where(first, edge_tile(one_ref, other_ref, 0), edge_tile(one_ref, other_ref, end))
        result = row
        for amount in (-2, -1, 1, 2):
            moved = shifted_by(row, edge, amount, lane)
            result = [jnp.where(offset == amount, tile, kept) for tile, kept in zip(moved, result)]
        for at, tile in zip(spots, result):
            out_ref[0, :, at] = tile.astype(out_ref.dtype)


def outer_rows(lat, offset, remapped, one, other):
    rows, bins, width = remapped.shape
    row = lambda at: pl.BlockSpec((1, bins, width), lambda t: (at, 0, 0))
    whole = lambda array: pl.BlockSpec(array.shape, lambda t: (0, 0, 0))
    return pl.pallas_call(
        rows_kernel,
        grid=(1,),
        in_specs=[in_smem(), whole(offset), row(0), row(rows - 1), whole(one), whole(other)],
        out_specs=[row(0), row(0)],
        out_shape=[jax.ShapeDtypeStruct((1, bins, width), jnp.bfloat16)] * 2,
        compiler_params=pltpu.CompilerParams(vmem_limit_bytes=VMEM_BYTES),
        cost_estimate=pl.CostEstimate(flops=20 * bins * width, bytes_accessed=12 * bins * width, transcendentals=0),
        name="outer_rows",
    )(lat, offset, remapped, remapped, one, other)


def final_kernel(
    offset_ref, remap_ref, one_ref, other_ref, kappa_ref, local_ref, out_ref, outer_ref, edge_ref, sums_ref, sems
):
    rows, bins, width = remap_ref.shape
    count = width // 128
    lane = lax.broadcasted_iota(jnp.int32, (8, 128), 1)
    spots = [slice(128 * t, 128 * t + 128) for t in range(count)]
    for r in range(rows):
        edge_ref[r] = edge_tile(one_ref, other_ref, r)

    def moved(row, edge, amount):
        row = [jnp.where(lane < -amount, edge, row[0])] + row[1:]
        row = row[:-1] + [jnp.where(lane >= 128 - amount, edge, row[-1])]
        turned = [pltpu.roll(tile, (amount + 128) & 127, 1) for tile in row]
        before, after = lane < amount, lane >= 128 + amount
        return [
            jnp.where(before, turned[t - 1], jnp.where(after, turned[(t + 1) % count], turned[t])) for t in range(count)
        ]

    copies = []
    for half in range(2):
        first = half * bins // 2
        pieces = [slice(b, b + 8) for b in range(first, first + bins // 2, 8)]
        before, now, base = {}, {}, {}
        stores = []
        sent = 1
        for r in range(rows):
            amount = offset_ref[r]
            kappa = [kappa_ref[r, :, spot] for spot in spots]
            above = [kappa_ref[max(r - 1, 0), :, spot] for spot in spots]
            for at in pieces:
                row = [remap_ref[r, at, spot] for spot in spots]
                edge = edge_ref[r, at]
                center = moved(row, edge, amount)
                east = moved(row, edge, amount - 1)
                west = moved(row, edge, amount + 1)
                key = at.start
                fresh = []
                for t, spot in enumerate(spots):
                    around = kappa[t] * (east[t] + west[t] - 4.0 * center[t])
                    fresh.append(local_ref[r, at, spot] + center[t] + around)
                    if r == 1:
                        stores.append((r - 1, at, spot, base[key][t] + above[t] * center[t]))
                    elif r:
                        stores.append((r - 1, at, spot, base[key][t] + above[t] * (before[key][t] + center[t])))
                if r:
                    before[key] = now[key]
                now[key], base[key] = center, fresh
            if r % 2:
                for which, at, spot, value in stores:
                    if which:
                        sums_ref[which, at, spot] = value
                    else:
                        outer_ref[0, at, spot] = value
                stores = []
            if r % 8 == 7:
                block = (pl.ds(sent, r - sent), pl.ds(first, bins // 2))
                copy = pltpu.make_async_copy(sums_ref.at[block], out_ref.at[block], sems.at[len(copies)])
                copy.start()
                copies.append(copy)
                sent = r
        for at in pieces:
            for t, spot in enumerate(spots):
                outer_ref[1, at, spot] = base[at.start][t] + kappa_ref[rows - 1, :, spot] * before[at.start][t]
    for copy in copies:
        copy.wait()


def final(offset, remapped, one, other, kappa, local):
    rows, bins, width = remapped.shape
    vmem = pl.BlockSpec(memory_space=pltpu.VMEM)
    return pl.pallas_call(
        final_kernel,
        in_specs=[in_smem()] + [vmem] * 5,
        out_specs=[in_place(), vmem],
        out_shape=[
            jax.ShapeDtypeStruct(local.shape, jnp.float32),
            jax.ShapeDtypeStruct((2, bins, width), jnp.float32),
        ],
        scratch_shapes=[
            pltpu.VMEM((rows, bins, 128), jnp.float32),
            pltpu.VMEM((rows, bins, width), jnp.float32),
            pltpu.SemaphoreType.DMA((2 * (rows // 8),)),
        ],
        compiler_params=pltpu.CompilerParams(vmem_limit_bytes=TABLE_BYTES),
        cost_estimate=pl.CostEstimate(flops=30 * remapped.size, bytes_accessed=12 * remapped.size, transcendentals=0),
        name="final",
    )(offset, remapped, one, other, kappa, local)


def halo_kernel(lat_ref, one_ref, other_ref, kappa_ref, outer_ref, _, out_ref, sums_ref, sems):
    odd = lat_ref[0] == 1
    rows = out_ref.shape[0]
    copies = []
    for side, (first, at) in enumerate(((odd, 0), (jnp.logical_not(odd), rows - 1))):
        value = jnp.where(first, one_ref[0].astype(jnp.float32), other_ref[0].astype(jnp.float32))
        sums_ref[side] = outer_ref[side] + kappa_ref[at] * value
        copy = pltpu.make_async_copy(sums_ref.at[pl.ds(side, 1)], out_ref.at[pl.ds(at, 1)], sems.at[side])
        copy.start()
        copies.append(copy)
    for copy in copies:
        copy.wait()


def add_halo(lat, one, other, kappa, outer, partial):
    vmem = pl.BlockSpec(memory_space=pltpu.VMEM)
    return pl.pallas_call(
        halo_kernel,
        in_specs=[in_smem()] + [vmem] * 4 + [in_place()],
        out_specs=in_place(),
        out_shape=jax.ShapeDtypeStruct(partial.shape, jnp.float32),
        scratch_shapes=[pltpu.VMEM(outer.shape, jnp.float32), pltpu.SemaphoreType.DMA((2,))],
        input_output_aliases={5: 0},
        compiler_params=pltpu.CompilerParams(vmem_limit_bytes=VMEM_BYTES),
        cost_estimate=pl.CostEstimate(flops=4 * outer.size, bytes_accessed=20 * outer.size, transcendentals=0),
        name="add_halo",
    )(lat, one, other, kappa, outer, partial)


def body(
    conc,
    dep_owner,
    dep_row,
    dep_weight,
    dep_count,
    zonal_offset,
    agg_rates,
    toeplitz,
    settle,
    kappa,
):
    rows, bins, width = conc.shape
    entries = dep_owner.shape[2]
    my_lat, my_lon = lax.axis_index("lat"), lax.axis_index("lon")
    flags = [(value % 2).astype(jnp.int32).reshape(1) for value in (my_lon, my_lon // 2, my_lat)]
    half = bins // 2
    low, high, meta = messages(conc, dep_owner[0].T, dep_row[0].T, dep_weight[0].T, dep_count)
    lat1, lat2 = swap_lat(high, 0), swap_lat(high, 1)
    lon1, lon2 = swap_chip(low, 0), swap_chip(low, 1)
    beside = swap_core(conc)
    rates, meta = lax.optimization_barrier((agg_rates, meta))
    local = local_terms(conc, rates, toeplitz, settle)
    terms = decoded(flags, [lat1, meta, lat2], lat_slots, rows, half, entries)
    spread = jnp.broadcast_to(zonal_offset[:, None, None], (rows, 1, 128))
    lat1, lat2, local, terms, spread = lax.optimization_barrier((lat1, lat2, local, terms, spread))

    to_lon1, own1, to_lon2 = lon_sums(
        flags,
        [lon1, meta, lon2],
        lon_slots,
        [(lat1, 0), (conc, half), (lat2, 0), (swap_core(lat1), 0), (beside, half), (swap_core(lat2), 0)],
        rows,
        half,
        entries,
    )
    parts1 = [swap_chip(to_lon1, 0), swap_chip(to_lon2, 1)]
    own1, later = lax.optimization_barrier((own1, flags))
    parts1 = [own1] + parts1

    to_lat1, own0, to_lat2 = lat_sums(
        later,
        terms,
        [(conc, 0), (beside, 0), (lon1, 0), (lon2, 0), (swap_core(lon1), 0), (swap_core(lon2), 0)],
        rows,
        half,
        entries,
    )
    parts0 = [own0, swap_lat(to_lat1, 0), swap_lat(to_lat2, 1)]

    kappa = kappa[:, None, :]

    earlier = edges(flags[0], parts1, [])
    parts0, earlier = lax.optimization_barrier((parts0, earlier))
    to_core, to_across = edges(flags[0], parts0, earlier)
    one, other = swap_core(to_core), swap_across(to_across)
    remapped = combine(parts0, parts1)
    lat = ((my_lat + 1) % 2).astype(jnp.int32).reshape(1)
    row1, row2 = outer_rows(lat, spread, remapped, one, other)
    row1, row2 = swap_lat(row1, 1), swap_lat(row2, 0)
    partial, outer = final(zonal_offset, remapped, one, other, kappa, local)
    return add_halo(lat, row1, row2, kappa, outer, partial)


def solution(mesh):
    return jax.shard_map(
        body,
        mesh=mesh,
        in_specs=(
            P("lat", None, "lon"),
            P("lon", "lat", None),
            P("lon", "lat", None),
            P("lon", "lat", None),
            P("lon", "lat"),
            P("lat"),
            P(None, "lat", "lon"),
            P(),
            P(),
            P("lat", "lon"),
        ),
        out_specs=P("lat", None, "lon"),
        check_vma=False,
    )
```

```python
import functools

import jax
import jax.numpy as jnp
from jax import lax
from jax.experimental import pallas as pl
from jax.experimental.pallas import tpu as pltpu
from jax.sharding import PartitionSpec as P

REACH = 2
NEAR_LON = 5
UNROLL = 4
VMEM_BYTES = 12 * 1024 * 1024
MOST_BYTES = 60 * 1024 * 1024
TABLE_BYTES = 20 * 1024 * 1024
QUICK = 2
FIELDS = ((0, 0), (0, 128), (8, 0), (8, 128), (16, 0))


def exchange(value, axis, pairs):
    return lax.ppermute(value, axis, [(i, j) for i, j in pairs] + [(j, i) for i, j in pairs])


def swap_core(value):
    return exchange(value, "lon", [(i, i + 1) for i in range(0, lax.axis_size("lon"), 2)])


def swap_across(value):
    count = lax.axis_size("lon")
    return exchange(value, "lon", [(i, (i + 1) % count) for i in range(1, count, 2)])


def swap_chip(value, second):
    count = lax.axis_size("lon")
    firsts = [i for i in range(count) if (i // 2) % 2 == second]
    return exchange(value, "lon", [(i, (i + 2) % count) for i in firsts])


def swap_lat(value, second):
    count = lax.axis_size("lat")
    return exchange(value, "lat", [(i, i + 1) for i in range(second, count - 1, 2)])


def in_smem():
    return pl.BlockSpec(memory_space=pltpu.SMEM)


def in_place():
    return pl.BlockSpec(memory_space=pl.ANY)


def for_rows(count, one):
    def some(g, carry):
        stores = []
        for u in range(UNROLL):
            stores += one(g * UNROLL + u)
        for ref, at, value in stores:
            ref[at] = value.astype(ref.dtype)
        return carry

    lax.fori_loop(0, count // UNROLL, some, 0)


def growth_kernel(flip_ref, settle_ref, conc_ref, rates_ref, out_ref, mat_ref):
    ranks, rows_step = rates_ref.shape[0], conc_ref.shape[0]
    bins, width = conc_ref.shape[1:]

    @pl.when(pl.program_id(0) == 0)
    def _():
        for q in range(ranks):
            spread = jnp.broadcast_to(flip_ref[q : q + 1, :], (bins, 2 * bins))
            turned = pltpu.roll(spread, bins + 1, 1, stride=1, stride_axis=0)
            mat_ref[q * bins : (q + 1) * bins, :] = turned[:, :bins].astype(jnp.bfloat16)

    settle = jnp.broadcast_to(settle_ref[...], (bins, width))
    for r in range(rows_step):
        cells = conc_ref[r]
        product = jnp.dot(mat_ref[...], cells, preferred_element_type=jnp.float32)
        total = -settle * cells.astype(jnp.float32)
        for q in range(ranks):
            total = total + rates_ref[q, r : r + 1, :] * product[q * bins : (q + 1) * bins]
        out_ref[r] = total


def local_terms(conc, agg_rates, toeplitz, settle):
    rows, bins, width = conc.shape
    ranks = agg_rates.shape[0]
    step = 8
    flipped = jnp.pad(toeplitz[:, ::-1].astype(jnp.float32), ((0, 0), (0, 1)))
    return pl.pallas_call(
        growth_kernel,
        grid=(rows // step,),
        in_specs=[
            pl.BlockSpec((ranks, 2 * bins), lambda i: (0, 0)),
            pl.BlockSpec((bins, 1), lambda i: (0, 0)),
            pl.BlockSpec((step, bins, width), lambda i: (i, 0, 0)),
            pl.BlockSpec((ranks, step, width), lambda i: (0, i, 0)),
        ],
        out_specs=pl.BlockSpec((step, bins, width), lambda i: (i, 0, 0)),
        out_shape=jax.ShapeDtypeStruct(conc.shape, jnp.float32),
        scratch_shapes=[pltpu.VMEM((ranks * bins, bins), jnp.bfloat16)],
        compiler_params=pltpu.CompilerParams(vmem_limit_bytes=VMEM_BYTES),
        cost_estimate=pl.CostEstimate(
            flops=2 * ranks * bins * bins * rows * width, bytes_accessed=8 * conc.size, transcendentals=0
        ),
        name="growth",
    )(flipped, settle[:, None], conc, agg_rates)


def messages_kernel(
    conc_ref, owner_hbm, source_hbm, weight_hbm, count_hbm, low_ref, high_ref, meta_ref,
    owner_ref, source_ref, weight_ref, count_ref, sems,
):
    rows = conc_ref.shape[0]
    half = low_ref.shape[1]
    entries = owner_ref.shape[0]
    small = [
        pltpu.make_async_copy(hbm, ref, sems.at[2 + i])
        for i, (hbm, ref) in enumerate(
            ((owner_hbm, owner_ref), (source_hbm, source_ref), (weight_hbm, weight_ref), (count_hbm, count_ref))
        )
    ]
    large = [
        pltpu.make_async_copy(conc_ref.at[:, pl.ds(i * half, half), :], ref.at[pl.ds(0, rows)], sems.at[i])
        for i, ref in enumerate((low_ref, high_ref))
    ]
    for copy in small + large:
        copy.start()
    meta_ref[...] = jnp.zeros(meta_ref.shape, meta_ref.dtype)
    for copy in small:
        copy.wait()
    wide = lambda value: value.astype(jnp.float32)
    entry = lax.broadcasted_iota(jnp.int32, owner_ref.shape, 0)
    live = jnp.where(entry < count_ref[...], weight_ref[...], 0.0)
    top = live.astype(jnp.bfloat16)
    middle = (live - wide(top)).astype(jnp.bfloat16)
    bottom = (live - wide(top) - wide(middle)).astype(jnp.bfloat16)
    fields = (wide(owner_ref[...]), wide(source_ref[...]), wide(top), wide(middle), wide(bottom))
    for field, (at, lane) in zip(fields, FIELDS):
        meta_ref[0, at : at + entries, lane : lane + rows] = field.astype(jnp.bfloat16)
    low_ref[rows] = meta_ref[0]
    high_ref[rows] = meta_ref[0]
    for copy in large:
        copy.wait()


def messages(conc, owner, source, weight, count):
    rows, bins, width = conc.shape
    half = bins // 2
    return pl.pallas_call(
        messages_kernel,
        in_specs=[in_place()] * 5,
        out_specs=[pl.BlockSpec(memory_space=pltpu.VMEM)] * 3,
        out_shape=[
            jax.ShapeDtypeStruct((rows + 1, half, width), conc.dtype),
            jax.ShapeDtypeStruct((rows + 1, half, width), conc.dtype),
            jax.ShapeDtypeStruct((1, half, width), conc.dtype),
        ],
        scratch_shapes=[pltpu.VMEM(small.shape, small.dtype) for small in (owner, source, weight, count)]
        + [pltpu.SemaphoreType.DMA((6,))],
        compiler_params=pltpu.CompilerParams(vmem_limit_bytes=MOST_BYTES),
        cost_estimate=pl.CostEstimate(flops=0, bytes_accessed=4 * conc.size, transcendentals=0),
        name="messages",
    )(conc, owner, source, weight, count)


def signs(flags):
    return [1.0 - 2.0 * ref[0].astype(jnp.float32) for ref in flags]


def lat_slots(rows, group, lat_step, lon_step, flags):
    core, chip, lat = signs(flags)
    far = jnp.where(core * chip < 0.0, 4.0, 5.0)
    slot = jnp.where(
        lon_step == 0.0,
        0.0,
        jnp.where(
            lon_step == 2.0 * chip, 2.0, jnp.where(lon_step == -2.0 * chip, 3.0, jnp.where(lon_step == core, 1.0, far))
        ),
    )
    return lat_step == (group - 1.0) * lat, slot * rows


def lon_slots(rows, group, lat_step, lon_step, flags):
    core, chip, lat = signs(flags)
    lon_from = 2.0 * (1.0 - group) * chip + lon_step
    slot = jnp.where(lon_from == 0.0, 1.0, 4.0) - lat_step * lat
    return (lon_from == 0.0) | (lon_from == core), slot * rows


def decode(slots, rows, entries, flags, meta_ref, index_ref, weight_ref):
    for g in range(3):
        owner, source, top, middle, bottom = [
            meta_ref[g, at : at + entries, lane : lane + 128].astype(jnp.float32) for at, lane in FIELDS
        ]
        weight = top + middle + bottom
        band = jnp.where(owner >= NEAR_LON, 1.0, 0.0) + jnp.where(owner >= 2 * NEAR_LON, 1.0, 0.0)
        here, base = slots(rows, float(g), band - 1.0, owner - NEAR_LON * band - REACH, flags)
        here = jnp.where(here & (weight != 0.0), 1.0, 0.0)
        index = base + source
        packed = [[jnp.zeros((1, 128), jnp.float32)] * 2 for _ in range(entries)]
        rank = jnp.zeros((1, 128), jnp.float32)
        for k in range(entries):
            taken = here[k : k + 1]
            for place in range(k + 1):
                spot = (taken > 0.0) & (rank == place)
                packed[place] = [
                    jnp.where(spot, index[k : k + 1], packed[place][0]),
                    jnp.where(spot, weight[k : k + 1], packed[place][1]),
                ]
            rank = rank + taken
        for place in range(entries):
            at = g * entries + place
            index_ref[at : at + 1, :] = packed[place][0].astype(jnp.int32)
            weight_ref[at : at + 1, :] = packed[place][1]
        at = 3 * entries + g
        index_ref[at : at + 1, :] = rank.astype(jnp.int32)


def read_metas(asked, meta_ref, sems, first):
    return [
        pltpu.make_async_copy(ref.at[pl.ds(ref.shape[0] - 1, 1)], meta_ref.at[pl.ds(g, 1)], sems.at[first + g])
        for g, ref in enumerate(asked)
    ]


def decode_kernel(slots, rows, entries, *refs):
    flags, asked, (index_ref, weight_ref, meta_ref, sems) = refs[:3], refs[3:6], refs[6:]
    copies = read_metas(asked, meta_ref, sems, 0)
    for copy in copies:
        copy.start()
    for copy in copies:
        copy.wait()
    decode(slots, rows, entries, flags, meta_ref, index_ref, weight_ref)


def decoded(flags, asked, slots, rows, half, entries):
    width = asked[1].shape[2]
    vectors = -(-3 * (entries + 1) // 8) * 8
    return pl.pallas_call(
        functools.partial(decode_kernel, slots, rows, entries),
        in_specs=[in_smem()] * 3 + [in_place()] * 3,
        out_specs=[pl.BlockSpec(memory_space=pltpu.VMEM)] * 2,
        out_shape=[
            jax.ShapeDtypeStruct((vectors, 128), jnp.int32),
            jax.ShapeDtypeStruct((vectors, 128), jnp.float32),
        ],
        scratch_shapes=[pltpu.VMEM((3, half, width), jnp.bfloat16), pltpu.SemaphoreType.DMA((3,))],
        compiler_params=pltpu.CompilerParams(vmem_limit_bytes=VMEM_BYTES),
        cost_estimate=pl.CostEstimate(flops=0, bytes_accessed=6 * half * width, transcendentals=0),
        name="decode",
    )(*flags, *asked)


def table_copies(bases, rows, sources, table, sems):
    half = table.shape[1]
    return [
        pltpu.make_async_copy(
            source.at[pl.ds(0, rows), pl.ds(base, half), :], table.at[pl.ds(i * rows, rows)], sems.at[i]
        )
        for i, (source, base) in enumerate(zip(sources, bases))
    ]


def add_terms(rows, entries, index_ref, weight_ref, table, outs):
    half, width = table.shape[1:]
    for group, out in enumerate(outs):

        def some(g, carry, group=group, out=out):
            def sums(terms):
                totals = []
                for u in range(UNROLL):
                    r = g * UNROLL + u
                    total = jnp.zeros((half, width), jnp.float32)
                    for k in range(terms):
                        row = group * entries + k
                        total = total + weight_ref[row, r] * table[index_ref[row, r]].astype(jnp.float32)
                    totals.append(total)
                for u in range(UNROLL):
                    out[g * UNROLL + u] = totals[u].astype(out.dtype)

            most = index_ref[3 * entries + group, g * UNROLL]
            for u in range(1, UNROLL):
                most = jnp.maximum(most, index_ref[3 * entries + group, g * UNROLL + u])
            sums(min(QUICK, entries))

            @pl.when(most > QUICK)
            def _():
                sums(entries)

            return carry

        lax.fori_loop(0, rows // UNROLL, some, 0)


def lat_sums_kernel(bases, entries, core_ref, chip_ref, index_ref, weight_ref, *refs):
    tables = len(bases)
    sources, outs = refs[:tables], refs[tables : tables + 3]
    table, sems = refs[tables + 3 :]
    rows = table.shape[0] // tables
    copies = table_copies(bases, rows, sources, table, sems)
    first = core_ref[0] != chip_ref[0]
    for copy in copies[:-2]:
        copy.start()
    pl.when(first)(copies[-2].start)
    pl.when(jnp.logical_not(first))(copies[-1].start)
    for copy in copies[:-2]:
        copy.wait()
    pl.when(first)(copies[-2].wait)
    pl.when(jnp.logical_not(first))(copies[-1].wait)
    add_terms(rows, entries, index_ref, weight_ref, table, outs)


def lon_sums_kernel(bases, slots, entries, *refs):
    tables = len(bases)
    flags, refs = refs[:3], refs[3:]
    asked, sources, outs = refs[:3], refs[3 : 3 + tables], refs[3 + tables : 6 + tables]
    table, meta_ref, index_vec, weight_vec, index_ref, weight_ref, sems = refs[6 + tables :]
    rows = table.shape[0] // tables
    metas = read_metas(asked, meta_ref, sems, tables)
    copies = table_copies(bases, rows, sources, table, sems)
    for copy in metas + copies:
        copy.start()
    for copy in metas:
        copy.wait()
    decode(slots, rows, entries, flags, meta_ref, index_vec, weight_vec)
    to_scalar = [
        pltpu.make_async_copy(index_vec, index_ref, sems.at[tables + 3]),
        pltpu.make_async_copy(weight_vec, weight_ref, sems.at[tables + 4]),
    ]
    for copy in to_scalar:
        copy.start()
    for copy in to_scalar + copies:
        copy.wait()
    add_terms(rows, entries, index_ref, weight_ref, table, outs)


def sums_call(kernel, operands, smem, sources, scratch, rows, half, entries, name):
    tables = len(sources)
    width = sources[0][0].shape[2]
    return pl.pallas_call(
        kernel,
        in_specs=[in_smem()] * smem + [in_place()] * (len(operands) - smem + tables),
        out_specs=[pl.BlockSpec(memory_space=pltpu.VMEM)] * 3,
        out_shape=[
            jax.ShapeDtypeStruct((rows, half, width), dtype) for dtype in (jnp.bfloat16, jnp.float32, jnp.bfloat16)
        ],
        scratch_shapes=[pltpu.VMEM((tables * rows, half, width), jnp.bfloat16)] + scratch,
        compiler_params=pltpu.CompilerParams(vmem_limit_bytes=TABLE_BYTES),
        cost_estimate=pl.CostEstimate(
            flops=6 * rows * entries * half * width,
            bytes_accessed=2 * (tables + 3) * rows * half * width,
            transcendentals=0,
        ),
        name=name,
    )(*operands, *[source for source, _ in sources])


def lat_sums(flags, terms, sources, rows, half, entries):
    kernel = functools.partial(lat_sums_kernel, tuple(base for _, base in sources), entries)
    scratch = [pltpu.SemaphoreType.DMA((len(sources),))]
    return sums_call(kernel, [*flags[:2], *terms], 4, sources, scratch, rows, half, entries, "lat_sums")


def lon_sums(flags, asked, slots, sources, rows, half, entries):
    kernel = functools.partial(lon_sums_kernel, tuple(base for _, base in sources), slots, entries)
    vectors = -(-3 * (entries + 1) // 8) * 8
    scratch = [pltpu.VMEM((3, half, asked[1].shape[2]), jnp.bfloat16)]
    scratch += [space((vectors, 128), dtype) for space in (pltpu.VMEM, pltpu.SMEM) for dtype in (jnp.int32, jnp.float32)]
    scratch += [pltpu.SemaphoreType.DMA((len(sources) + 5,))]
    return sums_call(kernel, [*flags, *asked], 3, sources, scratch, rows, half, entries, "lon_sums")


def edges_kernel(core_ref, *refs):
    rows, half = refs[0].shape[:2]
    per = 128 // 8
    lane = lax.broadcasted_iota(jnp.int32, (half, 128), 1)
    odd = core_ref[0] == 1
    for earlier_ref, out_ref in zip(refs[6:-2], refs[-2:]):
        out_ref[:, half:] = earlier_ref[...]
    for j in range(rows // per):
        ends = []
        for side in range(2):
            parts = refs[3 * side : 3 * side + 3]
            packed = jnp.zeros((half, 128), jnp.float32)
            for i in range(per):
                r = j * per + i
                cells = parts[0][r] + parts[1][r].astype(jnp.float32) + parts[2][r].astype(jnp.float32)
                at = 8 * i + 3 * (1 - side)
                spot = (lane >= at) & (lane < at + 3)
                packed = jnp.where(spot, pltpu.roll(cells, 8 * i + 3, 1), packed)
            ends.append(packed)
        for out_ref, value in zip(refs[-2:], (jnp.where(odd, *ends), jnp.where(odd, *ends[::-1]))):
            out_ref[j, :half] = value.astype(out_ref.dtype)


def edges(core, parts, earlier):
    rows, half, width = parts[0].shape
    specs = [
        pl.BlockSpec((rows, half, 128), lambda t, at=at: (0, 0, at)) for at in (0, width // 128 - 1) for _ in parts
    ]
    whole = lambda shape: pl.BlockSpec(shape, lambda t: (0,) * len(shape))
    packed = (rows // 16, half + sum(array.shape[1] for array in earlier[:1]), 128)
    return pl.pallas_call(
        edges_kernel,
        grid=(1,),
        in_specs=[in_smem()] + specs + [whole(array.shape) for array in earlier],
        out_specs=[whole(packed)] * 2,
        out_shape=[jax.ShapeDtypeStruct(packed, jnp.bfloat16)] * 2,
        compiler_params=pltpu.CompilerParams(vmem_limit_bytes=VMEM_BYTES),
        cost_estimate=pl.CostEstimate(flops=8 * half * 256 * rows, bytes_accessed=16 * half * 256 * rows, transcendentals=0),
        name="edges",
    )(core, *parts, *parts, *earlier)


def combine_kernel(own0, a0, b0, own1, a1, b1, out_ref):
    rows, half = own0.shape[:2]
    for r in range(rows):
        out_ref[r, :half] = own0[r] + a0[r].astype(jnp.float32) + b0[r].astype(jnp.float32)
        out_ref[r, half:] = own1[r] + a1[r].astype(jnp.float32) + b1[r].astype(jnp.float32)


def combine(parts0, parts1):
    rows, half, width = parts0[0].shape
    step = 8
    return pl.pallas_call(
        combine_kernel,
        grid=(rows // step,),
        in_specs=[pl.BlockSpec((step, half, width), lambda t: (t, 0, 0))] * 6,
        out_specs=pl.BlockSpec((step, 2 * half, width), lambda t: (t, 0, 0)),
        out_shape=jax.ShapeDtypeStruct((rows, 2 * half, width), jnp.float32),
        compiler_params=pltpu.CompilerParams(vmem_limit_bytes=VMEM_BYTES),
        cost_estimate=pl.CostEstimate(
            flops=4 * rows * half * width, bytes_accessed=24 * rows * half * width, transcendentals=0
        ),
        name="combine",
    )(*parts0, *parts1)


def shifted_by(row, edge, amount, lane):
    count = len(row)
    if amount == 0:
        return row
    if amount > 0:
        row = row[:-1] + [jnp.where(lane >= 128 - amount, edge, row[-1])]
        turned = [pltpu.roll(tile, amount, 1) for tile in row]
        return [jnp.where(lane < amount, turned[t - 1], turned[t]) for t in range(count)]
    row = [jnp.where(lane < -amount, edge, row[0])] + row[1:]
    turned = [pltpu.roll(tile, 128 + amount, 1) for tile in row]
    return [jnp.where(lane >= 128 + amount, turned[(t + 1) % count], turned[t]) for t in range(count)]


def edge_tile(west_ref, east_ref, r):
    per = 128 // 8
    both = west_ref[r // per].astype(jnp.float32) + east_ref[r // per].astype(jnp.float32)
    return pltpu.roll(both, (125 - 8 * (r % per)) % 128, 1)


def rows_kernel(lat_ref, offset_ref, first_row, last_row, one_ref, other_ref, *outs):
    bins, width = first_row.shape[1:]
    lane = lax.broadcasted_iota(jnp.int32, (bins, 128), 1)
    spots = [slice(128 * t, 128 * t + 128) for t in range(width // 128)]
    end = offset_ref.shape[0] - 1
    odd = lat_ref[0] == 1
    for out_ref, first in ((outs[0], odd), (outs[1], jnp.logical_not(odd))):
        offset = jnp.broadcast_to(jnp.where(first, offset_ref[0], offset_ref[end]), (bins, 128))
        row = [jnp.where(first, first_row[0, :, at], last_row[0, :, at]) for at in spots]
        edge = jnp.where(first, edge_tile(one_ref, other_ref, 0), edge_tile(one_ref, other_ref, end))
        result = row
        for amount in (-2, -1, 1, 2):
            moved = shifted_by(row, edge, amount, lane)
            result = [jnp.where(offset == amount, tile, kept) for tile, kept in zip(moved, result)]
        for at, tile in zip(spots, result):
            out_ref[0, :, at] = tile.astype(out_ref.dtype)


def outer_rows(lat, offset, remapped, one, other):
    rows, bins, width = remapped.shape
    row = lambda at: pl.BlockSpec((1, bins, width), lambda t: (at, 0, 0))
    whole = lambda array: pl.BlockSpec(array.shape, lambda t: (0, 0, 0))
    return pl.pallas_call(
        rows_kernel,
        grid=(1,),
        in_specs=[in_smem(), whole(offset), row(0), row(rows - 1), whole(one), whole(other)],
        out_specs=[row(0), row(0)],
        out_shape=[jax.ShapeDtypeStruct((1, bins, width), jnp.bfloat16)] * 2,
        compiler_params=pltpu.CompilerParams(vmem_limit_bytes=VMEM_BYTES),
        cost_estimate=pl.CostEstimate(flops=20 * bins * width, bytes_accessed=12 * bins * width, transcendentals=0),
        name="outer_rows",
    )(lat, offset, remapped, remapped, one, other)


def final_kernel(
    offset_ref, remap_ref, one_ref, other_ref, kappa_ref, local_ref, out_ref, outer_ref, sums_ref, sems
):
    rows, bins, width = remap_ref.shape
    count = width // 128
    lane = lax.broadcasted_iota(jnp.int32, (8, 128), 1)
    spots = [slice(128 * t, 128 * t + 128) for t in range(count)]

    def moved(row, edge, amount):
        row = [jnp.where(lane < -amount, edge, row[0])] + row[1:]
        row = row[:-1] + [jnp.where(lane >= 128 - amount, edge, row[-1])]
        turned = [pltpu.roll(tile, (amount + 128) & 127, 1) for tile in row]
        before, after = lane < amount, lane >= 128 + amount
        return [
            jnp.where(before, turned[t - 1], jnp.where(after, turned[(t + 1) % count], turned[t])) for t in range(count)
        ]

    copies = []
    for half in range(2):
        first = half * bins // 2
        pieces = [slice(b, b + 8) for b in range(first, first + bins // 2, 8)]
        before, now, base = {}, {}, {}
        stores = []
        sent = 1
        for r in range(rows):
            amount = offset_ref[r]
            kappa = [kappa_ref[r, :, spot] for spot in spots]
            above = [kappa_ref[max(r - 1, 0), :, spot] for spot in spots]
            for at in pieces:
                row = [remap_ref[r, at, spot] for spot in spots]
                both = one_ref[r // 16, at].astype(jnp.float32) + other_ref[r // 16, at].astype(jnp.float32)
                edge = pltpu.roll(both, (125 - 8 * (r % 16)) % 128, 1)
                center = moved(row, edge, amount)
                east = moved(row, edge, amount - 1)
                west = moved(row, edge, amount + 1)
                key = at.start
                fresh = []
                for t, spot in enumerate(spots):
                    around = kappa[t] * (east[t] + west[t] - 4.0 * center[t])
                    fresh.append(local_ref[r, at, spot] + center[t] + around)
                    if r == 1:
                        stores.append((r - 1, at, spot, base[key][t] + above[t] * center[t]))
                    elif r:
                        stores.append((r - 1, at, spot, base[key][t] + above[t] * (before[key][t] + center[t])))
                if r:
                    before[key] = now[key]
                now[key], base[key] = center, fresh
            if r % 2:
                for which, at, spot, value in stores:
                    if which:
                        sums_ref[which, at, spot] = value
                    else:
                        outer_ref[0, at, spot] = value
                stores = []
            if r % 8 == 7:
                block = (pl.ds(sent, r - sent), pl.ds(first, bins // 2))
                copy = pltpu.make_async_copy(sums_ref.at[block], out_ref.at[block], sems.at[len(copies)])
                copy.start()
                copies.append(copy)
                sent = r
        for at in pieces:
            for t, spot in enumerate(spots):
                outer_ref[1, at, spot] = base[at.start][t] + kappa_ref[rows - 1, :, spot] * before[at.start][t]
    for copy in copies:
        copy.wait()


def final(offset, remapped, one, other, kappa, local):
    rows, bins, width = remapped.shape
    vmem = pl.BlockSpec(memory_space=pltpu.VMEM)
    return pl.pallas_call(
        final_kernel,
        in_specs=[in_smem()] + [vmem] * 5,
        out_specs=[in_place(), vmem],
        out_shape=[
            jax.ShapeDtypeStruct(local.shape, jnp.float32),
            jax.ShapeDtypeStruct((2, bins, width), jnp.float32),
        ],
        scratch_shapes=[
            pltpu.VMEM((rows, bins, width), jnp.float32),
            pltpu.SemaphoreType.DMA((2 * (rows // 8),)),
        ],
        compiler_params=pltpu.CompilerParams(vmem_limit_bytes=TABLE_BYTES),
        cost_estimate=pl.CostEstimate(flops=30 * remapped.size, bytes_accessed=12 * remapped.size, transcendentals=0),
        name="final",
    )(offset, remapped, one, other, kappa, local)


def halo_kernel(lat_ref, one_ref, other_ref, kappa_ref, outer_ref, _, out_ref, sums_ref, sems):
    odd = lat_ref[0] == 1
    rows = out_ref.shape[0]
    copies = []
    for side, (first, at) in enumerate(((odd, 0), (jnp.logical_not(odd), rows - 1))):
        value = jnp.where(first, one_ref[0].astype(jnp.float32), other_ref[0].astype(jnp.float32))
        sums_ref[side] = outer_ref[side] + kappa_ref[at] * value
        copy = pltpu.make_async_copy(sums_ref.at[pl.ds(side, 1)], out_ref.at[pl.ds(at, 1)], sems.at[side])
        copy.start()
        copies.append(copy)
    for copy in copies:
        copy.wait()


def add_halo(lat, one, other, kappa, outer, partial):
    vmem = pl.BlockSpec(memory_space=pltpu.VMEM)
    return pl.pallas_call(
        halo_kernel,
        in_specs=[in_smem()] + [vmem] * 4 + [in_place()],
        out_specs=in_place(),
        out_shape=jax.ShapeDtypeStruct(partial.shape, jnp.float32),
        scratch_shapes=[pltpu.VMEM(outer.shape, jnp.float32), pltpu.SemaphoreType.DMA((2,))],
        input_output_aliases={5: 0},
        compiler_params=pltpu.CompilerParams(vmem_limit_bytes=VMEM_BYTES),
        cost_estimate=pl.CostEstimate(flops=4 * outer.size, bytes_accessed=20 * outer.size, transcendentals=0),
        name="add_halo",
    )(lat, one, other, kappa, outer, partial)


def body(
    conc,
    dep_owner,
    dep_row,
    dep_weight,
    dep_count,
    zonal_offset,
    agg_rates,
    toeplitz,
    settle,
    kappa,
):
    rows, bins, width = conc.shape
    entries = dep_owner.shape[2]
    my_lat, my_lon = lax.axis_index("lat"), lax.axis_index("lon")
    flags = [(value % 2).astype(jnp.int32).reshape(1) for value in (my_lon, my_lon // 2, my_lat)]
    half = bins // 2
    low, high, meta = messages(conc, dep_owner[0].T, dep_row[0].T, dep_weight[0].T, dep_count)
    lat1, lat2 = swap_lat(high, 0), swap_lat(high, 1)
    lon1, lon2 = swap_chip(low, 0), swap_chip(low, 1)
    beside = swap_core(conc)
    rates, meta = lax.optimization_barrier((agg_rates, meta))
    local = local_terms(conc, rates, toeplitz, settle)
    terms = decoded(flags, [lat1, meta, lat2], lat_slots, rows, half, entries)
    spread = jnp.broadcast_to(zonal_offset[:, None, None], (rows, 1, 128))
    lat1, lat2, local, terms, spread = lax.optimization_barrier((lat1, lat2, local, terms, spread))

    to_lon1, own1, to_lon2 = lon_sums(
        flags,
        [lon1, meta, lon2],
        lon_slots,
        [(lat1, 0), (conc, half), (lat2, 0), (swap_core(lat1), 0), (beside, half), (swap_core(lat2), 0)],
        rows,
        half,
        entries,
    )
    parts1 = [swap_chip(to_lon1, 0), swap_chip(to_lon2, 1)]
    own1, later = lax.optimization_barrier((own1, flags))
    parts1 = [own1] + parts1

    to_lat1, own0, to_lat2 = lat_sums(
        later,
        terms,
        [(conc, 0), (beside, 0), (lon1, 0), (lon2, 0), (swap_core(lon1), 0), (swap_core(lon2), 0)],
        rows,
        half,
        entries,
    )
    parts0 = [own0, swap_lat(to_lat1, 0), swap_lat(to_lat2, 1)]

    kappa = kappa[:, None, :]

    earlier = edges(flags[0], parts1, [])
    parts0, earlier = lax.optimization_barrier((parts0, earlier))
    to_core, to_across = edges(flags[0], parts0, earlier)
    one, other = swap_core(to_core), swap_across(to_across)
    remapped = combine(parts0, parts1)
    row1, row2 = outer_rows(flags[2], spread, remapped, one, other)
    row1, row2 = swap_lat(row1, 0), swap_lat(row2, 1)
    partial, outer = final(zonal_offset, remapped, one, other, kappa, local)
    return add_halo(flags[2], row1, row2, kappa, outer, partial)


def solution(mesh):
    return jax.shard_map(
        body,
        mesh=mesh,
        in_specs=(
            P("lat", None, "lon"),
            P("lon", "lat", None),
            P("lon", "lat", None),
            P("lon", "lat", None),
            P("lon", "lat"),
            P("lat"),
            P(None, "lat", "lon"),
            P(),
            P(),
            P("lat", "lon"),
        ),
        out_specs=P("lat", None, "lon"),
        check_vma=False,
    )
```
